128 devices in a mesh: dp: 16 (over z, x_lo, core), row: 4 (over y), col: 2 (over x_hi).
Axes of the slice: x: 4 (x_hi: 2, x_lo: 2; x = x_hi * 2 + x_lo), y: 4, z: 4, core: 2. Of those that a mesh axis runs over, the one named last changes fastest.
Arguments:
- tokens: bfloat16 [16384, 1536], P(('dp', 'col'), 'row'), may hold values from -6 to 6
- cotangent: bfloat16 [16384, 1536], P(('dp', 'col'), 'row'), may hold values from -6 to 6
- lengths: int32 [16, 3], P('dp'), may hold values from 1 to 896, 1024 in all within a row
- gain_attn: float32 [1536], P('row'), may hold values from 0.5 to 1.5
- w_query: bfloat16 [1536, 1536], P('row', 'col'), may hold values from -0.15625 to 0.15625
- key_projection: bfloat16 [1536, 256], P('row', 'col'), may hold values from -0.15625 to 0.15625
- value_projection: bfloat16 [1536, 256], P('row', 'col'), may hold values from -0.15625 to 0.15625
- bias_query: float32 [1536], P('col'), may hold values from -3 to 3
- key_bias_vector: float32 [256], P('col'), may hold values from -3 to 3
- value_bias_vector: float32 [256], P('col'), may hold values from -3 to 3
- w_out: bfloat16 [1536, 1536], P('col', 'row'), may hold values from -1.25 to 1.25
- gain_ffn: float32 [1536], P('row'), may hold values from 0.5 to 1.5
- w_gate: bfloat16 [1536, 8960], P('row', 'col'), may hold values from -0.15625 to 0.15625
- w_up: bfloat16 [1536, 8960], P('row', 'col'), may hold values from -0.15625 to 0.15625
- w_down: bfloat16 [8960, 1536], P('col', 'row'), may hold values from -0.0625 to 0.0625
Outputs:
- result: float32 [16384, 1536], P(('dp', 'col'), 'row')
- grad_tokens: float32 [16384, 1536], P(('dp', 'col'), 'row')
- grad_gain_attn: float32 [1536], P('row')
- grad_w_query: float32 [1536, 1536], P('row', 'col')
- grad_w_key: float32 [1536, 256], P('row', 'col')
- grad_w_value: float32 [1536, 256], P('row', 'col')
- grad_bias_query: float32 [1536], P('col')
- grad_bias_key: float32 [256], P('col')
- grad_bias_value: float32 [256], P('col')
- grad_w_out: float32 [1536, 1536], P('col', 'row')
- grad_gain_ffn: float32 [1536], P('row')
- grad_w_gate: float32 [1536, 8960], P('row', 'col')
- grad_w_up: float32 [1536, 8960], P('row', 'col')
- grad_w_down: float32 [8960, 1536], P('col', 'row')
The draws below stay inside these ranges and needn't reach their ends.
Inputs may be any that keep to these rules, and one draw needn't show every extreme that they name: In each group the 3 lengths sum to 1024 and the longest is 896.
All inputs are finite; a program needn't handle non-finite values.
Results may differ from the reference program's by a relative error of at most 0.04.
Values may be sent and summed in bfloat16 or wider, within the bound.
A program may use at most 192 MiB of HBM per device.

```python
import math
import jax
import jax.numpy as jnp
import numpy as np
from jax import lax

MODEL_WIDTH = 1536
QUERY_HEADS = 12
KEY_VALUE_HEADS = 2
HEAD_SIZE = 128
FF = 8960
SLOTS = 3
CAP = 1024
LONGEST = 896
GROUPS = 16
TOKENS = 16384
N_DP = 16


def steps_of(own_key, shape, cuts, smallest, high):
    gain, own = 1.0, jax.random.fold_in(own_key, 6)
    for dim, blocks in cuts:
        heights = jnp.exp(jax.random.uniform(jax.random.fold_in(own, dim), (blocks,), jnp.float32, smallest / len(cuts), high / len(cuts)))
        gain = gain * jnp.repeat(heights, shape[dim] // blocks).reshape([-1 if axis == dim else 1 for axis in range(len(shape))])
    return gain


def split_up(number_of, total, limit, slope):
    portions = [(1 << 20) // math.isqrt(standing ** slope) + 1 for standing in range(2, number_of + 1)]
    surplus, given = total - limit - (number_of - 1), [1] * (number_of - 1)
    while surplus > 0:
        free = [i for i in range(number_of - 1) if given[i] < limit]
        whole, left = sum([portions[i] for i in free]), surplus
        for i in free:
            more = min(limit - given[i], max(1, left * portions[i] // whole), surplus)
            given[i] = given[i] + more
            surplus = surplus - more
    return np.array([limit] + given)


def ragged_sizes(rng, amount, total, bound, lean):
    if amount == 2:
        one = jax.random.randint(rng, (), max(1, total - bound), min(bound, total - 1) + 1)
        return jnp.stack([one, total - one])
    tallies = jnp.asarray(split_up(amount, total, bound, lean), jnp.int32)
    twos = (amount - 1) // 2
    giver, taker = tallies[1:1 + 2 * twos:2], tallies[2:2 + 2 * twos:2]
    room = jnp.minimum(giver - 1, bound - taker)
    shifted = jax.random.randint(jax.random.fold_in(rng, 1), (twos,), 0, 1 << 20) % (room + 1)
    tallies = tallies.at[1:1 + 2 * twos:2].set(giver - shifted).at[2:2 + 2 * twos:2].set(taker + shifted)
    return tallies[jax.random.permutation(jax.random.fold_in(rng, 2), amount)]


def bell_draw(own_key, extent, scale, bound, shards=(), kind=jnp.bfloat16):
    array = scale * jax.random.normal(own_key, extent, jnp.float32)
    if shards:
        array = array * steps_of(own_key, extent, shards, -0.22, 0.18)
    return jnp.clip(array, -bound, bound).astype(kind)


def setup_inputs(seed: int = 0) -> dict:
    key_list = jax.random.split(jax.random.key(seed), 16)
    return {
        "tokens": bell_draw(key_list[0], (TOKENS, MODEL_WIDTH), 1.0, 6.0, ((0, 32), (1, 4))),
        "cotangent": bell_draw(key_list[1], (TOKENS, MODEL_WIDTH), 1.0, 6.0, ((0, 32), (1, 4))),
        "lengths": jax.vmap(lambda own: ragged_sizes(own, SLOTS, CAP, LONGEST, 2))(jax.random.split(key_list[2], GROUPS)).reshape((GROUPS, SLOTS)).astype(jnp.int32),
        "gain_attn": jnp.clip(1.0 + 0.1 * jax.random.normal(key_list[3], (MODEL_WIDTH,), jnp.float32), 0.5, 1.5),
        "w_query": bell_draw(key_list[4], (MODEL_WIDTH, QUERY_HEADS * HEAD_SIZE), MODEL_WIDTH ** -0.5, 0.15625, ((0, 4), (1, 2))),
        "key_projection": bell_draw(key_list[5], (MODEL_WIDTH, KEY_VALUE_HEADS * HEAD_SIZE), MODEL_WIDTH ** -0.5, 0.15625, ((0, 4), (1, 2))),
        "value_projection": bell_draw(key_list[6], (MODEL_WIDTH, KEY_VALUE_HEADS * HEAD_SIZE), MODEL_WIDTH ** -0.5, 0.15625, ((0, 4), (1, 2))),
        "bias_query": bell_draw(key_list[7], (QUERY_HEADS * HEAD_SIZE,), 0.5, 3.0, ((0, 2),), jnp.float32),
        "key_bias_vector": bell_draw(key_list[8], (KEY_VALUE_HEADS * HEAD_SIZE,), 0.5, 3.0, ((0, 2),), jnp.float32),
        "value_bias_vector": bell_draw(key_list[9], (KEY_VALUE_HEADS * HEAD_SIZE,), 0.5, 3.0, ((0, 2),), jnp.float32),
        "w_out": bell_draw(key_list[10], (QUERY_HEADS * HEAD_SIZE, MODEL_WIDTH), (QUERY_HEADS * HEAD_SIZE // 64) ** -0.5, 1.25, ((0, 2), (1, 4))),
        "gain_ffn": jnp.clip(1.0 + 0.1 * jax.random.normal(key_list[11], (MODEL_WIDTH,), jnp.float32), 0.5, 1.5),
        "w_gate": bell_draw(key_list[12], (MODEL_WIDTH, FF), MODEL_WIDTH ** -0.5, 0.15625, ((0, 4), (1, 2))),
        "w_up": bell_draw(key_list[13], (MODEL_WIDTH, FF), MODEL_WIDTH ** -0.5, 0.15625, ((0, 4), (1, 2))),
        "w_down": bell_draw(key_list[14], (FF, MODEL_WIDTH), FF ** -0.5, 0.0625, ((0, 2), (1, 4))),
    }


EPS = 1e-06
THETA = 1000000.0

@jax.custom_vjp
def lower_precision(v):
    return lax.optimization_barrier(v.astype(jnp.bfloat16)).astype(jnp.float32)

@jax.custom_vjp
def low_back(v):
    return v

def low_keep(v):
    return (lower_precision(v), None)

def low_pass(kept, grad):
    return (grad,)

def back_keep(v):
    return (v, None)

def back_low(kept, grad):
    return (lower_precision(grad),)
lower_precision.defvjp(low_keep, low_pass)
low_back.defvjp(back_keep, back_low)

def matmul(left, right):
    return jnp.dot(left, right, precision=lax.Precision.HIGHEST, preferred_element_type=jnp.float32)

def apply_rotation(vector, cosine_table, sine_table):
    middle_index = vector.shape[-1] // 2
    turned = jnp.concatenate([-vector[..., middle_index:], vector[..., :middle_index]], -1)
    return vector * cosine_table + turned * sine_table

def layout(lengths_row, first, entry_count):
    index = first + jnp.arange(entry_count, dtype=jnp.int32)
    ends = jnp.cumsum(lengths_row).astype(jnp.int32)
    starts = (ends - lengths_row).astype(jnp.int32)
    segment = lax.optimization_barrier(jnp.sum((index[:, None] >= ends[None, :]).astype(jnp.int32), -1)).astype(jnp.int32)
    chosen = segment[:, None] == jnp.arange(lengths_row.shape[0], dtype=jnp.int32)[None, :]
    position = (index - lax.optimization_barrier(jnp.sum(jnp.where(chosen, starts[None, :], 0), -1))).astype(jnp.int32)
    return (index, segment, position)

def angles(position):
    steps_half = jnp.arange(HEAD_SIZE // 2, dtype=jnp.float32)
    inverse = jnp.exp(-jnp.log(THETA) * 2.0 * steps_half / HEAD_SIZE)
    turn = position.astype(jnp.float32)[:, None] * inverse[None, :]
    turn = jnp.concatenate([turn, turn], -1)[:, None, :]
    return (jnp.cos(turn), jnp.sin(turn))

def norm_scale(vector):
    return vector * lax.rsqrt(lax.optimization_barrier(jnp.mean(vector * vector, -1, keepdims=True)) + EPS)

def layer(stream, gain_attn, w_query, key_projection, value_projection, bias_query, key_bias_vector, value_bias_vector, w_out, gain_ffn, w_gate, w_up, w_down, cosine_table, sine_table, allowed):
    entry_count = stream.shape[0]
    head_group = QUERY_HEADS // KEY_VALUE_HEADS
    normed = lower_precision(norm_scale(stream) * gain_attn)
    query_before_rotation = low_back(matmul(normed, w_query) + bias_query)
    key_before_rotation = low_back(matmul(normed, key_projection) + key_bias_vector)
    value_before_repeat = low_back(matmul(normed, value_projection) + value_bias_vector)
    query_rows = lower_precision(apply_rotation(query_before_rotation.reshape(entry_count, QUERY_HEADS, HEAD_SIZE), cosine_table, sine_table)).reshape(entry_count, KEY_VALUE_HEADS, head_group, HEAD_SIZE)
    key = lower_precision(apply_rotation(key_before_rotation.reshape(entry_count, KEY_VALUE_HEADS, HEAD_SIZE), cosine_table, sine_table))
    value_rows = lower_precision(value_before_repeat.reshape(entry_count, KEY_VALUE_HEADS, HEAD_SIZE))
    scores = low_back(jnp.einsum('qhgd,khd->hgqk', query_rows, key, precision=lax.Precision.HIGHEST) * HEAD_SIZE ** (-0.5))
    scores = jnp.where(allowed[None, None], scores, -1e+30)
    probs = lower_precision(jax.nn.softmax(scores, axis=-1))
    attended = jnp.einsum('hgqk,khd->qhgd', probs, value_rows, precision=lax.Precision.HIGHEST).reshape(entry_count, QUERY_HEADS * HEAD_SIZE)
    attended = lower_precision(low_back(attended))
    middle = stream + low_back(matmul(attended, w_out))
    normed_ffn = lower_precision(norm_scale(middle) * gain_ffn)
    gate = low_back(matmul(normed_ffn, w_gate))
    up_value = low_back(matmul(normed_ffn, w_up))
    activated = lower_precision(jax.nn.silu(gate) * up_value)
    return middle + low_back(matmul(activated, w_down))

def reference(tokens, cotangent, lengths, gain_attn, w_query, key_projection, value_projection, bias_query, key_bias_vector, value_bias_vector, w_out, gain_ffn, w_gate, w_up, w_down):
    params = tuple((p.astype(jnp.float32) for p in (gain_attn, w_query, key_projection, value_projection, bias_query, key_bias_vector, value_bias_vector, w_out, gain_ffn, w_gate, w_up, w_down)))
    streams = tokens.astype(jnp.float32).reshape(N_DP, CAP, MODEL_WIDTH)
    cotangents = cotangent.astype(jnp.float32).reshape(N_DP, CAP, MODEL_WIDTH)

    def one_group(totals, item):
        stream, grad_out, lengths_row = item
        index, segment, position = layout(lengths_row, jnp.int32(0), CAP)
        cosine_table, sine_table = angles(position)
        allowed = (segment[:, None] == segment[None, :]) & (index[None, :] <= index[:, None])

        def forward(stream_in, *weights):
            return layer(stream_in, *weights, cosine_table, sine_table, allowed)
        output, pullback = jax.vjp(forward, stream, *params)
        grads = pullback(grad_out)
        totals = tuple((a + b for a, b in zip(totals, grads[1:])))
        return (totals, (output, grads[0]))
    start = tuple((jnp.zeros_like(p) for p in params))
    totals, (outputs, grad_streams) = lax.scan(one_group, start, (streams, cotangents, lengths))
    return (outputs.reshape(N_DP * CAP, MODEL_WIDTH), grad_streams.reshape(N_DP * CAP, MODEL_WIDTH), totals[0], totals[1], totals[2], totals[3], totals[4], totals[5], totals[6], totals[7], totals[8], totals[9], totals[10], totals[11])
```

```python
import functools

import jax
import jax.numpy as jnp
from jax import lax
from jax.experimental import pallas as pl
from jax.experimental.pallas import tpu as pltpu
from jax.sharding import PartitionSpec as P

HEAD_SIZE = 128
EPS = 1e-06
THETA = 1000000.0
LANES = 128
MESH = pl.DeviceIdType.MESH
BF16 = jnp.bfloat16
F32 = jnp.float32
ANY = pl.BlockSpec(memory_space=pl.ANY)
VMEM = pl.BlockSpec(memory_space=pltpu.VMEM)

Z_STEP = 4
Z_GROUPS = [[z * Z_STEP + i for z in range(4)] for i in range(Z_STEP)]


def here():
    return lax.axis_index("dp"), lax.axis_index("row"), lax.axis_index("col")


def flip_near(dp):
    return dp + 2 - 4 * ((dp // 2) % 2)


def pair_of(place, row=None):
    dp, own, col = place
    return flip_near(dp), own if row is None else row, 1 - col


def near_of(place, row=None):
    dp, own, col = place
    return flip_near(dp), own if row is None else row, col


def twin_of(place):
    dp, row, col = place
    return dp + 1 - 2 * (dp % 2), row, col


def along_z(place, step):
    dp, row, col = place
    return (dp + Z_STEP * step) % (4 * Z_STEP), row, col


def along_y(place, step):
    dp, row, col = place
    return dp, (row + step) % 4, col


def meet(peers):
    barrier = pltpu.get_barrier_semaphore()
    for peer in peers:
        pl.semaphore_signal(barrier, inc=1, device_id=peer, device_id_type=MESH)
    pl.semaphore_wait(barrier, len(peers))


class Mail:
    def __init__(self, send, recv):
        self.send, self.recv, self.count, self.sent = send, recv, 0, []

    def post(self, source, target, device):
        index = self.count
        self.count += 1
        copy = pltpu.make_async_remote_copy(
            src_ref=source,
            dst_ref=target,
            send_sem=self.send.at[index],
            recv_sem=self.recv.at[index],
            device_id=device,
            device_id_type=MESH,
        )
        copy.start()
        self.sent.append(copy)
        return copy

    def finish(self):
        assert self.count == self.send.shape[0], self.count
        for copy in self.sent:
            copy.wait_send()


def talk(body, ident, copies, local, outs, in_specs, out_specs, scratch=(), limit=32):
    return pl.pallas_call(
        body,
        out_shape=[jax.ShapeDtypeStruct(*out) for out in outs],
        in_specs=in_specs,
        out_specs=out_specs,
        scratch_shapes=[
            *scratch,
            pltpu.SemaphoreType.DMA((copies,)),
            pltpu.SemaphoreType.DMA((copies,)),
            pltpu.SemaphoreType.DMA((max(local, 1),)),
        ],
        compiler_params=pltpu.CompilerParams(
            collective_id=ident, has_side_effects=True, vmem_limit_bytes=limit << 20
        ),
    )


def start_kernel(tok, cot, lens, wqkv, wout, tok2, cot2, lens2, qkv_full, out_full, send, recv, local):
    place = here()
    dp, row, col = place
    twin, pair = twin_of(place), pair_of(place)
    core = dp % 2
    right, left = along_y(place, 1), along_y(place, 3)
    peers = [along_y(place, s) for s in (1, 2, 3)]
    peers += [pair_of(place, (row + s) % 4) for s in range(4)] + [twin]
    meet(peers)
    mail = Mail(send, recv)
    rows = tok.shape[0] // 4
    piece = tok.shape[1]
    lanes = pl.ds(pl.multiple_of(row * piece, LANES), piece)
    arrivals = []
    kept = []

    def spread(source, target):
        for step in range(4):
            other = (row + step) % 4
            part = source.at[pl.ds(pl.multiple_of(other * rows, rows), rows), :]
            room = target.at[col, :, lanes]
            if step:
                arrivals.append(mail.post(part, room, along_y(place, step)))
            else:
                kept.append(pltpu.make_async_copy(part, room, local.at[len(kept)]))
                kept[-1].start()
            arrivals.append(mail.post(part, room, pair_of(place, other)))

    spread(tok, tok2)
    arrivals.append(mail.post(lens, lens2.at[col], pair))
    kept.append(pltpu.make_async_copy(lens, lens2.at[col], local.at[len(kept)]))
    kept[-1].start()

    def qkv_part(owner, quarter):
        height = wqkv.shape[0] // 4
        start = (core * 2 + quarter) * height
        return (
            lambda: wqkv.at[pl.ds(pl.multiple_of(start, 16), height), :],
            qkv_full.at[pl.ds(pl.multiple_of(owner * wqkv.shape[0] + start, 16), height), :],
        )

    def out_part(owner, quarter):
        height = wout.shape[0] // 4
        start = (core * 2 + quarter) * height
        rows_here = pl.ds(pl.multiple_of(start, 16), height)
        return (
            lambda: wout.at[rows_here, :],
            out_full.at[rows_here, pl.ds(pl.multiple_of(owner * wout.shape[1], LANES), wout.shape[1])],
        )

    parts = (qkv_part, out_part)
    hops = {}
    for part in parts:
        for turn in range(2):
            for name, device, quarter in (("r", right, turn), ("l", left, 1 - turn)):
                source, target = part(row, quarter)
                hops[part, name, quarter] = mail.post(source(), target, device)
    kept.append(
        pltpu.make_async_copy(
            wqkv,
            qkv_full.at[pl.ds(pl.multiple_of(row * wqkv.shape[0], 16), wqkv.shape[0]), :],
            local.at[len(kept)],
        )
    )
    kept[-1].start()
    kept.append(
        pltpu.make_async_copy(
            wout,
            out_full.at[:, pl.ds(pl.multiple_of(row * wout.shape[1], LANES), wout.shape[1])],
            local.at[len(kept)],
        )
    )
    kept[-1].start()
    spread(cot, cot2)
    before, after, across = (row + 3) % 4, (row + 1) % 4, (row + 2) % 4

    def share(part, owner, quarter):
        block = part(owner, quarter)[1]
        arrivals.append(mail.post(block, block, twin))

    for part in parts:
        hops[part, "r", 0].wait_recv()
        block = part(before, 0)[1]
        hops[part, "fr"] = mail.post(block, block, right)
        share(part, before, 0)
        hops[part, "l", 1].wait_recv()
        block = part(after, 1)[1]
        hops[part, "fl"] = mail.post(block, block, left)
        share(part, after, 1)
        hops[part, "r", 1].wait_recv()
        share(part, before, 1)
        hops[part, "l", 0].wait_recv()
        share(part, after, 0)
    for part in parts:
        hops[part, "fr"].wait_recv()
        share(part, across, 0)
        hops[part, "fl"].wait_recv()
        share(part, across, 1)
    for copy in arrivals:
        copy.wait_recv()
    for copy in kept:
        copy.wait()
    mail.finish()


def keys_kernel(kv, near_low, own, send, recv, local):
    place = here()
    dp, row, col = place
    meet([along_y(place, s) for s in (1, 2, 3)] + [near_of(place, (row + s) % 4) for s in range(4)])
    mail = Mail(send, recv)
    rows = kv.shape[1]
    spot = pl.ds(pl.multiple_of(row * rows, rows), rows)
    kept = pltpu.make_async_copy(kv, own.at[:, spot, :], local.at[0])
    kept.start()
    arrivals = []
    for step in range(4):
        if step:
            arrivals.append(mail.post(kv, own.at[:, spot, :], along_y(place, step)))
        arrivals.append(mail.post(kv.at[0], near_low.at[spot, :], near_of(place, (row + step) % 4)))
    for copy in arrivals:
        copy.wait_recv()
    kept.wait()
    mail.finish()


def pair_kernel(mine, theirs, send, recv, local):
    place = here()
    pair = pair_of(place)
    meet([pair])
    mail = Mail(send, recv)
    mail.post(mine, theirs, pair).wait_recv()
    mail.finish()


def gather_z_kernel(block, full, send, recv, local):
    place = here()
    dp, row, col = place
    z = dp // Z_STEP
    up, down = along_z(place, 1), along_z(place, 3)
    meet([up, down])
    mail = Mail(send, recv)
    half = block.shape[0] // 2

    def part(owner, which):
        return full.at[owner, pl.ds(which * half, half), :]

    got = {}
    for turn in range(2):
        for name, device, which in (("u", up, turn), ("d", down, 1 - turn)):
            got[name, which] = mail.post(block.at[pl.ds(which * half, half), :], part(z, which), device)
    kept = pltpu.make_async_copy(block, full.at[z], local.at[0])
    kept.start()
    got["u", 0].wait_recv()
    last_up = mail.post(part((z + 3) % 4, 0), part((z + 3) % 4, 0), up)
    got["d", 1].wait_recv()
    last_down = mail.post(part((z + 1) % 4, 1), part((z + 1) % 4, 1), down)
    for copy in (got["u", 1], got["d", 0], last_up, last_down):
        copy.wait_recv()
    kept.wait()
    mail.finish()


def reduce_z_kernel(parts, total, up1, down1, up2, down2, other, stage_up, stage_down, stage, send, recv, local):
    place = here()
    dp, row, col = place
    z = dp // Z_STEP
    up, down, pair = along_z(place, 1), along_z(place, 3), pair_of(place)
    meet([up, down, pair])
    mail = Mail(send, recv)
    above, below, across = (z + 1) % 4, (z + 3) % 4, (z + 2) % 4
    size = parts.shape[1] // 4

    def chunk(ref, owner, index):
        return ref.at[owner, pl.ds(index * size, size), :]

    first, second = {}, {}
    for i in range(2):
        first["u", i] = mail.post(chunk(parts, across, i), up1.at[i], up)
        first["d", i] = mail.post(chunk(parts, across, 2 + i), down1.at[i], down)
    for i in range(2):
        second["u", 2 + i] = mail.post(chunk(parts, above, 2 + i), up2.at[2 + i], up)
        second["d", i] = mail.post(chunk(parts, below, i), down2.at[i], down)
    for i in range(2):
        first["u", i].wait_recv()
        stage_up[i] = (chunk(parts, above, i)[...].astype(F32) + up1[i].astype(F32)).astype(BF16)
        second["u", i] = mail.post(stage_up.at[i], up2.at[i], up)
        first["d", i].wait_recv()
        stage_down[i] = (chunk(parts, below, 2 + i)[...].astype(F32) + down1[i].astype(F32)).astype(BF16)
        second["d", 2 + i] = mail.post(stage_down.at[i], down2.at[2 + i], down)
    swaps = {}
    for i in (0, 2, 1, 3):
        second["u", i].wait_recv()
        second["d", i].wait_recv()
        stage[i] = (
            chunk(parts, z, i)[...].astype(F32) + up2[i].astype(F32) + down2[i].astype(F32)
        ).astype(BF16)
        swaps[i] = mail.post(stage.at[i], other.at[i], pair)
    for i in (0, 2, 1, 3):
        swaps[i].wait_recv()
        total[pl.ds(i * size, size), :] = stage[i].astype(F32) + other[i].astype(F32)
    mail.finish()


def reduce_y_kernel(parts, total, up1, down1, up2, down2, stage_up, stage_down, send, recv, local):
    place = here()
    dp, row, col = place
    up, down = along_y(place, 1), along_y(place, 3)
    meet([up, down])
    mail = Mail(send, recv)
    above, below, across = (row + 1) % 4, (row + 3) % 4, (row + 2) % 4
    size = parts.shape[1] // 4

    def chunk(ref, owner, index):
        return ref.at[owner, pl.ds(index * size, size), :]

    first, second = {}, {}
    for i in range(2):
        first["u", i] = mail.post(chunk(parts, across, i), up1.at[i], up)
        first["d", i] = mail.post(chunk(parts, across, 2 + i), down1.at[i], down)
    for i in range(2):
        second["u", 2 + i] = mail.post(chunk(parts, above, 2 + i), up2.at[2 + i], up)
        second["d", i] = mail.post(chunk(parts, below, i), down2.at[i], down)
    for i in range(2):
        first["u", i].wait_recv()
        stage_up[i] = (chunk(parts, above, i)[...].astype(F32) + up1[i].astype(F32)).astype(BF16)
        second["u", i] = mail.post(stage_up.at[i], up2.at[i], up)
        first["d", i].wait_recv()
        stage_down[i] = (chunk(parts, below, 2 + i)[...].astype(F32) + down1[i].astype(F32)).astype(BF16)
        second["d", 2 + i] = mail.post(stage_down.at[i], down2.at[2 + i], down)
    for i in (0, 2, 1, 3):
        second["u", i].wait_recv()
        second["d", i].wait_recv()
        total[pl.ds(i * size, size), :] = (
            chunk(parts, row, i)[...].astype(F32) + up2[i].astype(F32) + down2[i].astype(F32)
        ).astype(BF16)
    mail.finish()


def keys_back_kernel(low, own, total, from_own, from_near, send, recv, local):
    place = here()
    dp, row, col = place
    meet([along_y(place, s) for s in (1, 2, 3)] + [near_of(place, (row + s) % 4) for s in range(4)])
    mail = Mail(send, recv)
    rows = total.shape[1]

    def spot(owner):
        return pl.ds(pl.multiple_of(owner * rows, rows), rows)

    arrivals = []
    for step in range(4):
        other = (row + step) % 4
        if step:
            arrivals.append(mail.post(own.at[:, spot(other), :], from_own.at[step - 1], along_y(place, step)))
        arrivals.append(mail.post(low.at[spot(other), :], from_near.at[step], near_of(place, other)))
    for copy in arrivals:
        copy.wait_recv()
    for half in range(2):
        value = own[half, spot(row), :].astype(F32)
        for step in range(3):
            value = value + from_own[step, half].astype(F32)
        if half == 0:
            for step in range(4):
                value = value + from_near[step].astype(F32)
        total[half] = value
    mail.finish()


def halves_kernel(first, second, first_in, second_in, send, recv, local):
    place = here()
    dp, row, col = place
    pair = pair_of(place)
    meet([pair])
    mail = Mail(send, recv)
    copies = [mail.post(first.at[1 - col], first_in, pair), mail.post(second.at[1 - col], second_in, pair)]
    for copy in copies:
        copy.wait_recv()
    mail.finish()


def end_kernel(one, two, bias, gains, one_out, two_out, bias_out, gains_out, send, recv, local):
    place = here()
    dp, row, col = place
    meet([along_y(place, s) for s in (1, 2, 3)] + [pair_of(place, (row + s) % 4) for s in range(4)])
    mail = Mail(send, recv)
    rows = one.shape[0]
    piece = one.shape[1] // 4
    spot = pl.ds(pl.multiple_of(row * rows, rows), rows)
    kept, arrivals = [], []

    def keep(source, target):
        kept.append(pltpu.make_async_copy(source, target, local.at[len(kept)]))
        kept[-1].start()

    for step in range(4):
        other = (row + step) % 4
        lanes = pl.ds(pl.multiple_of(other * piece, LANES), piece)
        device = along_y(place, step)
        mine = gains_out.at[col * 4 + row]
        moves = [
            (one.at[:, lanes], one_out.at[spot, :]),
            (two.at[:, lanes], two_out.at[spot, :]),
            (bias, bias_out.at[row]),
            (gains.at[other], mine),
        ]
        for source, target in moves:
            if step:
                arrivals.append(mail.post(source, target, device))
            else:
                keep(source, target)
        arrivals.append(mail.post(gains.at[other], mine, pair_of(place, other)))
    for copy in arrivals:
        copy.wait_recv()
    for copy in kept:
        copy.wait()
    mail.finish()


def tail_kernel(
    gu, dn, qkv, small, gu_out, dn_out, qkv_out, small_out, *scratch
):
    (gu_t, dn_t, qkv_t, small_t, gu_n, dn_n, qkv_n, small_n, gu_h, dn_h, qkv_h, small_h, send, recv, local) = scratch
    place = here()
    dp, row, col = place
    z = dp // Z_STEP
    core = dp % 2
    twin, near, up, down = twin_of(place), near_of(place), along_z(place, 1), along_z(place, 3)
    meet([twin, near, up, down])
    mail = Mail(send, recv)
    large = ((gu, gu_t, gu_n, gu_h, gu_out), (dn, dn_t, dn_n, dn_h, dn_out), (qkv, qkv_t, qkv_n, qkv_h, qkv_out))

    def half_of(ref, which):
        half = ref.shape[0] // 2
        return ref.at[pl.ds(pl.multiple_of(which * half, 16), half), :]

    first = [mail.post(half_of(ref, 1 - core), got, twin) for ref, got, _, _, _ in large]
    first_small = mail.post(small, small_t, twin)
    second = []
    for (ref, got, theirs, held, _), copy in zip(large, first):
        copy.wait_recv()
        held[...] = (half_of(ref, core)[...].astype(F32) + got[...].astype(F32)).astype(BF16)
        second.append(mail.post(held, theirs, near))
    first_small.wait_recv()
    small_h[0] = small[...] + small_t[...]
    second_small = mail.post(small_h.at[0], small_n, near)

    def room(out, owner, which):
        half = out.shape[1] // 2
        return out.at[owner, pl.ds(pl.multiple_of(which * half, 16), half), :]

    def quarter(out, owner, which):
        size = out.shape[1] // 4
        return out.at[owner, pl.ds(pl.multiple_of((core * 2 + which) * size, 16), size), :]

    kept, arrivals, hops = [], [], []
    sums = []
    for (ref, got, theirs, held, out), copy in zip(large, second):
        copy.wait_recv()
        got[...] = (held[...].astype(F32) + theirs[...].astype(F32)).astype(BF16)
        size = out.shape[1] // 4
        posts = {}
        for turn in range(2):
            for name, device, which in (("u", up, turn), ("d", down, 1 - turn)):
                posts[name, which] = mail.post(got.at[pl.ds(which * size, size), :], quarter(out, z, which), device)
        hops.append(posts)
        kept.append(pltpu.make_async_copy(got, room(out, z, core), local.at[len(kept)]))
        kept[-1].start()
        arrivals.append(mail.post(got, room(out, z, core), twin))
    second_small.wait_recv()
    small_t[...] = small_h[0] + small_n[...]
    small_up = mail.post(small_t, small_out.at[z], up)
    arrivals.append(mail.post(small_t, small_out.at[z], down))
    kept.append(pltpu.make_async_copy(small_t, small_out.at[z], local.at[len(kept)]))
    kept[-1].start()

    above, below, across = (z + 1) % 4, (z + 3) % 4, (z + 2) % 4
    lasts = []
    for (_, _, _, _, out), posts in zip(large, hops):
        posts["u", 0].wait_recv()
        one = mail.post(quarter(out, below, 0), quarter(out, below, 0), up)
        arrivals.append(mail.post(quarter(out, below, 0), quarter(out, below, 0), twin))
        posts["d", 1].wait_recv()
        two = mail.post(quarter(out, above, 1), quarter(out, above, 1), down)
        arrivals.append(mail.post(quarter(out, above, 1), quarter(out, above, 1), twin))
        posts["u", 1].wait_recv()
        arrivals.append(mail.post(quarter(out, below, 1), quarter(out, below, 1), twin))
        posts["d", 0].wait_recv()
        arrivals.append(mail.post(quarter(out, above, 0), quarter(out, above, 0), twin))
        lasts.append((out, one, two))
    small_up.wait_recv()
    arrivals.append(mail.post(small_out.at[below], small_out.at[below], up))
    for out, one, two in lasts:
        one.wait_recv()
        arrivals.append(mail.post(quarter(out, across, 0), quarter(out, across, 0), twin))
        two.wait_recv()
        arrivals.append(mail.post(quarter(out, across, 1), quarter(out, across, 1), twin))
    for copy in arrivals:
        copy.wait_recv()
    for copy in kept:
        copy.wait()
    mail.finish()


def rotated(vector):
    middle = vector.shape[-1] // 2
    return jnp.concatenate([-vector[..., middle:], vector[..., :middle]], -1)


def apply_rotation(vector, cosine, sine):
    return vector * cosine + rotated(vector) * sine


def undo_rotation(vector, cosine, sine):
    turned = vector * sine
    middle = vector.shape[-1] // 2
    return vector * cosine + jnp.concatenate([turned[..., middle:], -turned[..., :middle]], -1)


def layout(lengths_row, index):
    ends = jnp.cumsum(lengths_row)
    starts = ends - lengths_row
    segment = jnp.sum((index[:, None] >= ends[None, :]).astype(jnp.int32), -1)
    chosen = segment[:, None] == jnp.arange(lengths_row.shape[0], dtype=jnp.int32)[None, :]
    position = index - jnp.sum(jnp.where(chosen, starts[None, :], 0), -1)
    return segment, position


def angles(position):
    steps_half = jnp.arange(HEAD_SIZE // 2, dtype=F32)
    inverse = jnp.exp(-jnp.log(THETA) * 2.0 * steps_half / HEAD_SIZE)
    turn = position.astype(F32)[:, None] * inverse[None, :]
    turn = jnp.concatenate([turn, turn], -1)[:, None, :]
    return jnp.cos(turn), jnp.sin(turn)


def dot_plain(left, right):
    return jnp.dot(left, right, preferred_element_type=F32)


def dot_rows(left, right):
    return lax.dot_general(left, right, (((1,), (1,)), ((), ())), preferred_element_type=F32)


def dot_cols(left, right):
    return lax.dot_general(left, right, (((0,), (0,)), ((), ())), preferred_element_type=F32)


def norm_inverse(stream):
    return lax.rsqrt(jnp.mean(stream * stream, -1, keepdims=True) + EPS)


def norm_back(stream, inverse, gain, incoming):
    scaled = incoming * gain
    inner = jnp.mean(scaled * stream, -1, keepdims=True)
    back = inverse * scaled - stream * (inverse**3 * inner)
    return back, jnp.sum(incoming * stream * inverse, 0)


def attend(query, key, value, allowed, factor):
    raw = jnp.einsum("qhd,kd->hqk", query, key, preferred_element_type=F32) * factor
    scores = jnp.where(allowed[None], raw, -1e30)
    peak = jnp.max(scores, -1, keepdims=True)
    raised = jnp.exp(scores - peak)
    probs = raised / jnp.sum(raised, -1, keepdims=True)
    out = jnp.einsum("hqk,kd->qhd", probs.astype(BF16), value, preferred_element_type=F32)
    return out.astype(BF16), probs


def attend_back(query, key, value, probs, grad, factor):
    grad_probs = jnp.einsum("qhd,kd->hqk", grad, value, preferred_element_type=F32)
    inner = jnp.sum(grad_probs * probs, -1, keepdims=True)
    grad_scores = (probs * (grad_probs - inner)).astype(BF16)
    grad_query = jnp.einsum("hqk,kd->qhd", grad_scores, key, preferred_element_type=F32) * factor
    grad_key = jnp.einsum("hqk,qhd->kd", grad_scores, query, preferred_element_type=F32) * factor
    grad_value = jnp.einsum("hqk,qhd->kd", probs.astype(BF16), grad, preferred_element_type=F32)
    return grad_query, jnp.concatenate([grad_key, grad_value], 1).astype(BF16)


def on_device(
    tokens,
    cotangent,
    lengths,
    gain_attn,
    w_query,
    key_projection,
    value_projection,
    bias_query,
    key_bias_vector,
    value_bias_vector,
    w_out,
    gain_ffn,
    w_gate,
    w_up,
    w_down,
):
    dp, row, col = here()
    z = dp // Z_STEP
    half_rows, piece = tokens.shape
    width = 4 * piece
    rows = half_rows // 4
    q_width = w_query.shape[1]
    kv_width = key_projection.shape[1]
    heads = q_width // HEAD_SIZE
    hidden = w_gate.shape[1]
    share = -(-hidden // (4 * LANES)) * LANES
    factor = HEAD_SIZE ** (-0.5)
    spare = 4 * share - hidden
    take = z * share

    w_in = jnp.concatenate([w_query, key_projection, value_projection], 1)
    in_width = w_in.shape[1]
    lens = jnp.pad(lengths, ((0, 7), (0, LANES - lengths.shape[1])))
    tok2, cot2, lens2, w_in_full, w_out_full = talk(
        start_kernel,
        0,
        39,
        5,
        [
            ((2, rows, width), BF16),
            ((2, rows, width), BF16),
            ((2, 8, LANES), jnp.int32),
            ((width, in_width), BF16),
            ((q_width, width), BF16),
        ],
        [ANY] * 5,
        [ANY] * 5,
    )(tokens, cotangent, lens, w_in, w_out)

    w_both = jnp.concatenate(
        [
            lax.dynamic_slice(jnp.pad(w_gate, ((0, 0), (0, spare))), (0, take), (piece, share)),
            lax.dynamic_slice(jnp.pad(w_up, ((0, 0), (0, spare))), (0, take), (piece, share)),
        ],
        1,
    )
    w_down_t = lax.dynamic_slice(jnp.pad(w_down, ((0, spare), (0, 0))), (take, 0), (share, piece)).T
    w_both, w_down_t, _ = lax.optimization_barrier((w_both, w_down_t, lens2))
    w_both_full = lax.all_gather(w_both, "row", axis=0, tiled=True)
    w_down_full = lax.all_gather(w_down_t, "row", axis=0, tiled=True)
    cot_rows = cot2.reshape(2 * rows, width)
    cot_full = lax.all_gather(cot_rows, "dp", axis=0, tiled=True, axis_index_groups=Z_GROUPS)

    gain_attn_full = lax.all_gather(gain_attn, "row", axis=0, tiled=True)
    gain_ffn_full = lax.all_gather(gain_ffn, "row", axis=0, tiled=True)

    lens_a, lens_b = lens2[0, 0, :3], lens2[1, 0, :3]
    count = jnp.arange(rows, dtype=jnp.int32) + row * rows
    index_a, index_b = count, count + half_rows
    keys_a = jnp.arange(half_rows, dtype=jnp.int32)
    keys_b = jnp.arange(2 * half_rows, dtype=jnp.int32)
    segment_a, position_a = layout(lens_a, index_a)
    segment_b, position_b = layout(lens_b, index_b)
    allowed_a = (segment_a[:, None] == layout(lens_a, keys_a)[0][None, :]) & (keys_a[None, :] <= index_a[:, None])
    allowed_b = (segment_b[:, None] == layout(lens_b, keys_b)[0][None, :]) & (keys_b[None, :] <= index_b[:, None])
    cosine, sine = angles(jnp.concatenate([position_a, position_b]))

    stream = tok2.reshape(2 * rows, width).astype(F32)
    inverse_attn = norm_inverse(stream)
    normed = (stream * inverse_attn * gain_attn_full).astype(BF16)
    pre = dot_plain(normed, w_in_full) + jnp.concatenate([bias_query, key_bias_vector, value_bias_vector])
    query = apply_rotation(pre[:, :q_width].reshape(2 * rows, heads, HEAD_SIZE), cosine, sine).astype(BF16)
    key = apply_rotation(pre[:, q_width : q_width + kv_width], cosine[:, 0], sine[:, 0]).astype(BF16)
    key_value = jnp.concatenate([key, pre[:, q_width + kv_width :].astype(BF16)], 1)
    near_low, own_keys = talk(
        keys_kernel,
        1,
        7,
        1,
        [((half_rows, 2 * kv_width), BF16), ((2, half_rows, 2 * kv_width), BF16)],
        [ANY],
        [ANY] * 2,
    )(key_value.reshape(2, rows, 2 * kv_width))
    kv_a = own_keys[0]
    kv_b = jnp.concatenate([near_low, own_keys[1]], 0)
    query_a, query_b = query[:rows], query[rows:]
    out_a, probs_a = attend(query_a, kv_a[:, :kv_width], kv_a[:, kv_width:], allowed_a, factor)
    out_b, probs_b = attend(query_b, kv_b[:, :kv_width], kv_b[:, kv_width:], allowed_b, factor)
    attended = jnp.concatenate([out_a, out_b], 0).reshape(2 * rows, q_width)
    branch = dot_plain(attended, w_out_full).astype(BF16)
    (branch_other,) = talk(pair_kernel, 2, 1, 0, [((2 * rows, width), BF16)], [ANY], [ANY])(branch)
    middle = stream + (branch.astype(F32) + branch_other.astype(F32))
    inverse_ffn = norm_inverse(middle)
    normed_ffn = (middle * inverse_ffn * gain_ffn_full).astype(BF16)

    (ffn_in,) = talk(gather_z_kernel, 3, 6, 1, [((4, 2 * rows, width), BF16)], [ANY], [ANY])(normed_ffn)
    ffn_in = ffn_in.reshape(8 * rows, width)
    both = dot_plain(ffn_in, w_both_full)
    gate, up_value = both[:, :share], both[:, share:]
    grad_act = dot_plain(cot_full, w_down_full)
    spread = 1.0 / (1.0 + jnp.exp(-gate))
    smooth = gate * spread
    activated = (smooth * up_value).astype(BF16)
    grad_gate = grad_act * up_value * (spread * (1.0 + gate * (1.0 - spread)))
    grad_both = jnp.concatenate([grad_gate, grad_act * smooth], 1).astype(BF16)
    grad_in_parts = dot_rows(grad_both, w_both_full).astype(BF16).reshape(4, 2 * rows, width)
    chunk = (2, rows // 2, width)
    chunks = (4, rows // 2, width)
    (grad_normed_ffn,) = talk(
        reduce_z_kernel,
        4,
        16,
        0,
        [((2 * rows, width), F32)],
        [VMEM],
        [VMEM],
        [
            pltpu.VMEM(chunk, BF16),
            pltpu.VMEM(chunk, BF16),
            pltpu.VMEM(chunks, BF16),
            pltpu.VMEM(chunks, BF16),
            pltpu.VMEM(chunks, BF16),
            pltpu.VMEM(chunk, BF16),
            pltpu.VMEM(chunk, BF16),
            pltpu.VMEM(chunks, BF16),
        ],
    )(grad_in_parts)
    down_parts = dot_rows(activated, w_down_full).astype(BF16)
    down_part = lax.psum_scatter(down_parts, "dp", scatter_dimension=0, tiled=True, axis_index_groups=Z_GROUPS)
    grad_both_w = dot_cols(ffn_in, grad_both).astype(BF16)
    grad_down_w = jnp.concatenate(
        [dot_cols(activated, cot_full[:, r * piece : (r + 1) * piece]).astype(BF16) for r in range(4)], 0
    )
    both_sum = lax.psum_scatter(grad_both_w, "row", scatter_dimension=0, tiled=True)
    down_sum = lax.psum_scatter(grad_down_w, "row", scatter_dimension=0, tiled=True)

    back_mid, gain_ffn_part = norm_back(middle, inverse_ffn, gain_ffn_full, grad_normed_ffn)
    grad_middle = cot_rows.astype(F32) + back_mid
    grad_mid_low = grad_middle.astype(BF16)
    grad_att = dot_rows(grad_mid_low, w_out_full).astype(BF16).reshape(2 * rows, heads, HEAD_SIZE)
    out_w = jnp.concatenate(
        [dot_cols(attended, grad_mid_low[:, r * piece : (r + 1) * piece]).astype(BF16) for r in range(4)], 0
    )
    out_sum = lax.psum(lax.psum_scatter(out_w, "row", scatter_dimension=0, tiled=True), "dp")
    gq_a, gkv_a = attend_back(query_a, kv_a[:, :kv_width], kv_a[:, kv_width:], probs_a, grad_att[:rows], factor)
    gq_b, gkv_b = attend_back(query_b, kv_b[:, :kv_width], kv_b[:, kv_width:], probs_b, grad_att[rows:], factor)
    (grad_kv,) = talk(
        keys_back_kernel,
        5,
        7,
        0,
        [((2, rows, 2 * kv_width), F32)],
        [VMEM] * 2,
        [VMEM],
        [pltpu.VMEM((3, 2, rows, 2 * kv_width), BF16), pltpu.VMEM((4, rows, 2 * kv_width), BF16)],
    )(gkv_b[:half_rows], jnp.stack([gkv_a, gkv_b[half_rows:]]))
    grad_kv = grad_kv.reshape(2 * rows, 2 * kv_width)
    grad_query = undo_rotation(jnp.concatenate([gq_a, gq_b], 0), cosine, sine).reshape(2 * rows, q_width)
    grad_key = undo_rotation(grad_kv[:, :kv_width], cosine[:, 0], sine[:, 0])
    grad_pre = jnp.concatenate([grad_query, grad_key, grad_kv[:, kv_width:]], 1).astype(BF16)
    grad_normed_part = dot_rows(grad_pre, w_in_full).astype(BF16).reshape(2, rows, width)
    grad_normed_in, down_in = talk(
        halves_kernel,
        6,
        2,
        0,
        [((rows, width), BF16)] * 2,
        [ANY] * 2,
        [ANY] * 2,
    )(grad_normed_part, down_part.reshape(2, rows, width))

    def own(array):
        return lax.dynamic_index_in_dim(array.reshape(2, rows, -1), col, 0, keepdims=False)

    grad_normed = own(grad_normed_part).astype(F32) + grad_normed_in.astype(F32)
    result_rows = own(middle) + (own(down_part).astype(F32) + down_in.astype(F32))
    back_in, gain_attn_part = norm_back(own(stream), own(inverse_attn), gain_attn_full, grad_normed)
    grad_rows = own(grad_middle) + back_in
    grad_bias = jnp.sum(grad_pre.astype(F32), 0)
    gains = jnp.stack([gain_attn_part, 0.5 * gain_ffn_part]).reshape(2, 4, piece).transpose(1, 0, 2)
    result, grad_tokens, bias_all, gains_all = talk(
        end_kernel,
        7,
        16,
        4,
        [
            ((half_rows, piece), BF16),
            ((half_rows, piece), BF16),
            ((4, 8, in_width), F32),
            ((8, 8, piece), F32),
        ],
        [ANY] * 4,
        [ANY] * 4,
    )(
        result_rows.astype(BF16),
        grad_rows.astype(BF16),
        jnp.pad(grad_bias[None], ((0, 7), (0, 0))),
        jnp.pad(gains, ((0, 0), (0, 6), (0, 0))),
    )
    in_w = dot_cols(normed, grad_pre).astype(BF16).reshape(4, piece, in_width)
    size = piece // 4
    (in_sum,) = talk(
        reduce_y_kernel,
        8,
        12,
        0,
        [((piece, in_width), BF16)],
        [VMEM],
        [VMEM],
        [
            pltpu.VMEM((2, size, in_width), BF16),
            pltpu.VMEM((2, size, in_width), BF16),
            pltpu.VMEM((4, size, in_width), BF16),
            pltpu.VMEM((4, size, in_width), BF16),
            pltpu.VMEM((2, size, in_width), BF16),
            pltpu.VMEM((2, size, in_width), BF16),
        ],
    )(in_w)
    bias_sum = jnp.sum(bias_all, 0)[0]
    gains_sum = jnp.sum(gains_all, 0)[:2].reshape(2 * piece)
    small = jnp.stack([bias_sum, jnp.pad(gains_sum, (0, in_width - 2 * piece))])
    small = jnp.pad(small, ((0, 6), (0, 0)))
    gu_half, dn_half, in_half = (piece // 2, 2 * share), (share // 2, piece), (piece // 2, in_width)
    both_all, down_all, in_all, small_all = talk(
        tail_kernel,
        9,
        50,
        4,
        [
            ((4, piece, 2 * share), BF16),
            ((4, share, piece), BF16),
            ((4, piece, in_width), BF16),
            ((4, 8, in_width), F32),
        ],
        [VMEM] * 4,
        [ANY] * 4,
        [pltpu.VMEM(s, BF16) for s in (gu_half, dn_half, in_half)]
        + [pltpu.VMEM((8, in_width), F32)]
        + [pltpu.VMEM(s, BF16) for s in (gu_half, dn_half, in_half)]
        + [pltpu.VMEM((8, in_width), F32)]
        + [pltpu.VMEM(s, BF16) for s in (gu_half, dn_half, in_half)]
        + [pltpu.VMEM((1, 8, in_width), F32)],
    )(both_sum, down_sum, in_sum, small)
    in_total = in_all[0].astype(F32) + in_all[1].astype(F32) + in_all[2].astype(F32) + in_all[3].astype(F32)
    small_total = small_all[0] + small_all[1] + small_all[2] + small_all[3]
    bias_total, gains_total = small_total[0], small_total[1]
    gate_total = jnp.concatenate([both_all[i, :, :share] for i in range(4)], 1)[:, :hidden].astype(F32)
    up_total = jnp.concatenate([both_all[i, :, share:] for i in range(4)], 1)[:, :hidden].astype(F32)
    down_total = down_all.reshape(4 * share, piece)[:hidden].astype(F32)
    upper = q_width + kv_width
    return (
        result.astype(F32),
        grad_tokens.astype(F32),
        gains_total[:piece],
        in_total[:, :q_width],
        in_total[:, q_width:upper],
        in_total[:, upper:],
        bias_total[:q_width],
        bias_total[q_width:upper],
        bias_total[upper:],
        out_sum.astype(F32),
        gains_total[piece : 2 * piece],
        gate_total,
        up_total,
        down_total,
    )


def solution(mesh):
    placed = (
        P(("dp", "col"), "row"),
        P(("dp", "col"), "row"),
        P("dp", None),
        P("row"),
        P("row", "col"),
        P("row", "col"),
        P("row", "col"),
        P("col"),
        P("col"),
        P("col"),
        P("col", "row"),
        P("row"),
        P("row", "col"),
        P("row", "col"),
        P("col", "row"),
    )
    return jax.shard_map(
        on_device,
        mesh=mesh,
        in_specs=placed,
        out_specs=(
            P(("dp", "col"), "row"),
            P(("dp", "col"), "row"),
            P("row"),
            P("row", "col"),
            P("row", "col"),
            P("row", "col"),
            P("col"),
            P("col"),
            P("col"),
            P("col", "row"),
            P("row"),
            P("row", "col"),
            P("row", "col"),
            P("col", "row"),
        ),
        check_vma=False,
    )
```

```python
import functools

import jax
import jax.numpy as jnp
from jax import lax
from jax.experimental import pallas as pl
from jax.experimental.pallas import tpu as pltpu
from jax.sharding import PartitionSpec as P

HEAD_SIZE = 128
EPS = 1e-06
THETA = 1000000.0
LANES = 128
MESH = pl.DeviceIdType.MESH
BF16 = jnp.bfloat16
F32 = jnp.float32
ANY = pl.BlockSpec(memory_space=pl.ANY)
VMEM = pl.BlockSpec(memory_space=pltpu.VMEM)

Z_STEP = 4
TAIL_COPIES = 113
TAIL_LOCAL = 11


def here():
    return lax.axis_index("dp"), lax.axis_index("row"), lax.axis_index("col")


def flip_near(dp):
    return dp + 2 - 4 * ((dp // 2) % 2)


def pair_of(place, row=None):
    dp, own, col = place
    return flip_near(dp), own if row is None else row, 1 - col


def near_of(place, row=None):
    dp, own, col = place
    return flip_near(dp), own if row is None else row, col


def twin_of(place):
    dp, row, col = place
    return dp + 1 - 2 * (dp % 2), row, col


def along_z(place, step):
    dp, row, col = place
    return (dp + Z_STEP * step) % (4 * Z_STEP), row, col


def along_y(place, step):
    dp, row, col = place
    return dp, (row + step) % 4, col


def meet(peers):
    barrier = pltpu.get_barrier_semaphore()
    for peer in peers:
        pl.semaphore_signal(barrier, inc=1, device_id=peer, device_id_type=MESH)
    pl.semaphore_wait(barrier, len(peers))


class Mail:
    def __init__(self, send, recv):
        self.send, self.recv, self.count, self.sent = send, recv, 0, []

    def post(self, source, target, device):
        index = self.count
        self.count += 1
        copy = pltpu.make_async_remote_copy(
            src_ref=source,
            dst_ref=target,
            send_sem=self.send.at[index],
            recv_sem=self.recv.at[index],
            device_id=device,
            device_id_type=MESH,
        )
        copy.start()
        self.sent.append(copy)
        return copy

    def finish(self):
        assert self.count == self.send.shape[0], (self.count, self.send.shape)
        for copy in self.sent:
            copy.wait_send()


def talk(body, ident, copies, local, outs, in_specs, out_specs, scratch=(), limit=32):
    return pl.pallas_call(
        body,
        out_shape=[jax.ShapeDtypeStruct(*out) for out in outs],
        in_specs=in_specs,
        out_specs=out_specs,
        scratch_shapes=[
            *scratch,
            pltpu.SemaphoreType.DMA((copies,)),
            pltpu.SemaphoreType.DMA((copies,)),
            pltpu.SemaphoreType.DMA((max(local, 1),)),
        ],
        compiler_params=pltpu.CompilerParams(
            collective_id=ident, has_side_effects=True, vmem_limit_bytes=limit << 20
        ),
    )


def start_kernel(
    tok, cot, lens, gains, wqkv, wout, tok2, cot2, lens2, gains4, qkv_full, out_full, send, recv, local
):
    place = here()
    dp, row, col = place
    twin, pair = twin_of(place), pair_of(place)
    core = dp % 2
    right, left = along_y(place, 1), along_y(place, 3)
    meet([along_y(place, s) for s in (1, 2, 3)] + [pair, twin])
    mail = Mail(send, recv)
    rows = tok.shape[0] // 4
    piece = tok.shape[1]
    lanes = pl.ds(pl.multiple_of(row * piece, LANES), piece)
    kept = []

    def keep(source, target):
        kept.append(pltpu.make_async_copy(source, target, local.at[len(kept)]))
        kept[-1].start()
        return len(kept) - 1

    def spread(source, target):
        got = []
        for step in range(4):
            other = (row + step) % 4
            part = source.at[pl.ds(pl.multiple_of(other * rows, rows), rows), :]
            room = target.at[col, :, lanes]
            if step:
                got.append(mail.post(part, room, along_y(place, step)))
            else:
                mine = keep(part, room)
        return got, mine

    tokens = spread(tok, tok2)
    arrivals = [mail.post(lens, lens2.at[col], pair)]
    keep(lens, lens2.at[col])
    keep(gains, gains4.at[row])
    for step in (1, 2, 3):
        arrivals.append(mail.post(gains, gains4.at[row], along_y(place, step)))

    def qkv_part(owner, quarter):
        height = wqkv.shape[0] // 4
        start = (core * 2 + quarter) * height
        return (
            lambda: wqkv.at[pl.ds(pl.multiple_of(start, 16), height), :],
            qkv_full.at[pl.ds(pl.multiple_of(owner * wqkv.shape[0] + start, 16), height), :],
        )

    def out_part(owner, quarter):
        height = wout.shape[0] // 4
        start = (core * 2 + quarter) * height
        rows_here = pl.ds(pl.multiple_of(start, 16), height)
        return (
            lambda: wout.at[rows_here, :],
            out_full.at[rows_here, pl.ds(pl.multiple_of(owner * wout.shape[1], LANES), wout.shape[1])],
        )

    parts = (qkv_part, out_part)
    hops = {}
    for part in parts:
        for turn in range(2):
            for name, device, quarter in (("r", right, turn), ("l", left, 1 - turn)):
                source, target = part(row, quarter)
                hops[part, name, quarter] = mail.post(source(), target, device)
    keep(wqkv, qkv_full.at[pl.ds(pl.multiple_of(row * wqkv.shape[0], 16), wqkv.shape[0]), :])
    keep(wout, out_full.at[:, pl.ds(pl.multiple_of(row * wout.shape[1], LANES), wout.shape[1])])
    cotangents = spread(cot, cot2)
    before, after, across = (row + 3) % 4, (row + 1) % 4, (row + 2) % 4

    def to_pair(spreading, target):
        got, mine = spreading
        kept[mine].wait()
        kept[mine] = None
        for copy in got:
            copy.wait_recv()
        arrivals.append(mail.post(target.at[col], target.at[col], pair))

    to_pair(tokens, tok2)

    def share(part, owner, quarter):
        block = part(owner, quarter)[1]
        arrivals.append(mail.post(block, block, twin))

    for part in parts:
        hops[part, "r", 0].wait_recv()
        block = part(before, 0)[1]
        hops[part, "fr"] = mail.post(block, block, right)
        share(part, before, 0)
        hops[part, "l", 1].wait_recv()
        block = part(after, 1)[1]
        hops[part, "fl"] = mail.post(block, block, left)
        share(part, after, 1)
        hops[part, "r", 1].wait_recv()
        share(part, before, 1)
        hops[part, "l", 0].wait_recv()
        share(part, after, 0)
    to_pair(cotangents, cot2)
    for part in parts:
        hops[part, "fr"].wait_recv()
        share(part, across, 0)
        hops[part, "fl"].wait_recv()
        share(part, across, 1)
    for copy in arrivals:
        copy.wait_recv()
    for copy in kept:
        if copy is not None:
            copy.wait()
    mail.finish()


def keys_kernel(kv, near_low, own, send, recv, local):
    place = here()
    dp, row, col = place
    meet([along_y(place, s) for s in (1, 2, 3)] + [near_of(place, (row + s) % 4) for s in range(4)])
    mail = Mail(send, recv)
    rows = kv.shape[1]
    spot = pl.ds(pl.multiple_of(row * rows, rows), rows)
    kept = pltpu.make_async_copy(kv, own.at[:, spot, :], local.at[0])
    kept.start()
    arrivals = []
    for step in range(4):
        if step:
            arrivals.append(mail.post(kv, own.at[:, spot, :], along_y(place, step)))
        arrivals.append(mail.post(kv.at[0], near_low.at[spot, :], near_of(place, (row + step) % 4)))
    for copy in arrivals:
        copy.wait_recv()
    kept.wait()
    mail.finish()


def pair_kernel(mine, theirs, send, recv, local):
    place = here()
    pair = pair_of(place)
    meet([pair])
    mail = Mail(send, recv)
    mail.post(mine, theirs, pair).wait_recv()
    mail.finish()


def gather_z_kernel(block, weights, full, weights_full, send, recv, local):
    place = here()
    dp, row, col = place
    core = dp % 2
    up, down, twin = along_z(place, 1), along_z(place, 3), twin_of(place)
    meet([up, down, twin])
    mail = Mail(send, recv)
    half = block.shape[0] // 2

    def part(slot, which):
        return full.at[slot, pl.ds(which * half, half), :]

    got = {}
    for turn in range(2):
        for name, device, slot, which in (("u", up, 1, turn), ("d", down, 3, 1 - turn)):
            got[name, which] = mail.post(block.at[pl.ds(which * half, half), :], part(slot, which), device)
    shared = [mail.post(weights.at[r], weights_full.at[r, core], twin) for r in range(4)]
    kept = [pltpu.make_async_copy(block, full.at[0], local.at[0])]
    kept += [pltpu.make_async_copy(weights.at[r], weights_full.at[r, core], local.at[1 + r]) for r in range(4)]
    for copy in kept:
        copy.start()
    got["u", 0].wait_recv()
    last_up = mail.post(part(1, 0), part(2, 0), up)
    got["d", 1].wait_recv()
    last_down = mail.post(part(3, 1), part(2, 1), down)
    for copy in [got["u", 1], got["d", 0], last_up, last_down] + shared:
        copy.wait_recv()
    for copy in kept:
        copy.wait()
    mail.finish()


def middle_kernel(
    parts,
    x,
    gb,
    act,
    cot,
    total,
    gu_half,
    dn_half,
    parts_v,
    x_v,
    gb_v,
    act_v,
    cot_v,
    turned,
    gu_w,
    dn_w,
    gu_in,
    dn_in,
    up1,
    down1,
    up2,
    down2,
    other,
    stage_up,
    stage_down,
    stage,
    send,
    recv,
    local,
):
    place = here()
    dp, row, col = place
    core = dp % 2
    up, down, pair, twin = along_z(place, 1), along_z(place, 3), pair_of(place), twin_of(place)
    meet([up, down, pair, twin])
    mail = Mail(send, recv)
    above, below, across = 3, 1, 2
    size = parts.shape[1] // 4

    loads = [
        pltpu.make_async_copy(source, target, local.at[i])
        for i, (source, target) in enumerate(((x, x_v), (gb, gb_v), (parts, parts_v), (act, act_v), (cot, cot_v)))
    ]

    def chunk(ref, owner, index):
        return ref.at[owner, pl.ds(index * size, size), :]

    first, second = {}, {}
    for i in range(2):
        first["u", i] = mail.post(chunk(parts, across, i), up1.at[i], up)
        first["d", i] = mail.post(chunk(parts, across, 2 + i), down1.at[i], down)
    for copy in loads:
        copy.start()
    for i in range(2):
        second["u", 2 + i] = mail.post(chunk(parts, above, 2 + i), up2.at[2 + i], up)
        second["d", i] = mail.post(chunk(parts, below, i), down2.at[i], down)

    def turn(source, target):
        @pl.loop(0, source.shape[1] // LANES)
        def _(t):
            lanes = pl.ds(pl.multiple_of(t * LANES, LANES), LANES)
            target[lanes, :] = source[:, lanes].T

    def forward(i):
        first["u", i].wait_recv()
        stage_up[i] = (chunk(parts_v, above, i)[...].astype(F32) + up1[i].astype(F32)).astype(BF16)
        second["u", i] = mail.post(stage_up.at[i], up2.at[i], up)
        first["d", i].wait_recv()
        stage_down[i] = (chunk(parts_v, below, 2 + i)[...].astype(F32) + down1[i].astype(F32)).astype(BF16)
        second["d", 2 + i] = mail.post(stage_down.at[i], down2.at[2 + i], down)

    piece = gu_w.shape[2]
    share = gu_w.shape[3]
    steps = share // piece
    shared = []

    def up_block(r):
        @pl.loop(0, 2 * steps)
        def _(n):
            lanes = pl.ds(pl.multiple_of(n * piece, LANES), piece)
            tile = jnp.dot(turned[pl.ds(r * piece, piece), :], gb_v[:, lanes], preferred_element_type=F32)
            gu_w[r, n // steps, :, pl.ds(pl.multiple_of((n % steps) * piece, LANES), piece)] = tile.astype(BF16)

        shared.append(mail.post(gu_w.at[r, 1 - core], gu_in.at[r], twin))

    def down_block(r):
        @pl.loop(0, steps)
        def _(n):
            rows = pl.ds(pl.multiple_of(n * piece, LANES), piece)
            tile = jnp.dot(turned[rows, :], cot_v[:, r * piece : (r + 1) * piece], preferred_element_type=F32)
            dn_w[r, rows, :] = tile.astype(BF16)

        half = share // 2
        there = pl.ds(pl.multiple_of((1 - core) * half, 16), half)
        shared.append(mail.post(dn_w.at[r, there, :], dn_in.at[r], twin))

    loads[0].wait()
    turn(x_v, turned)
    loads[2].wait()
    forward(0)
    loads[1].wait()
    up_block(0)
    forward(1)
    up_block(1)
    up_block(2)
    up_block(3)
    swaps = {}

    def settle(i):
        second["u", i].wait_recv()
        second["d", i].wait_recv()
        stage[i] = (chunk(parts_v, 0, i)[...].astype(F32) + up2[i].astype(F32) + down2[i].astype(F32)).astype(BF16)
        swaps[i] = mail.post(stage.at[i], other.at[i], pair)

    loads[3].wait()
    turn(act_v, turned)
    loads[4].wait()
    settle(0)
    settle(2)
    down_block(0)
    down_block(1)
    settle(1)
    settle(3)
    down_block(2)
    down_block(3)
    for i in (0, 2, 1, 3):
        swaps[i].wait_recv()
        total[pl.ds(i * size, size), :] = stage[i].astype(F32) + other[i].astype(F32)
    half = share // 2
    mine = pl.ds(pl.multiple_of(core * half, 16), half)
    stores = []
    for r in range(4):
        shared[r].wait_recv()
        gu_in[r] = (gu_w[r, core].astype(F32) + gu_in[r].astype(F32)).astype(BF16)
        stores.append(pltpu.make_async_copy(gu_in.at[r], gu_half.at[r], local.at[5 + r]))
        stores[-1].start()
    for r in range(4):
        shared[4 + r].wait_recv()
        dn_in[r] = (dn_w[r, mine, :].astype(F32) + dn_in[r].astype(F32)).astype(BF16)
        stores.append(pltpu.make_async_copy(dn_in.at[r], dn_half.at[r], local.at[9 + r]))
        stores[-1].start()
    for copy in stores:
        copy.wait()
    mail.finish()


def keys_back_kernel(low, own, total, from_own, from_near, send, recv, local):
    place = here()
    dp, row, col = place
    meet([along_y(place, s) for s in (1, 2, 3)] + [near_of(place, (row + s) % 4) for s in range(4)])
    mail = Mail(send, recv)
    rows = total.shape[1]

    def spot(owner):
        return pl.ds(pl.multiple_of(owner * rows, rows), rows)

    arrivals = []
    for step in range(4):
        other = (row + step) % 4
        if step:
            arrivals.append(mail.post(own.at[:, spot(other), :], from_own.at[step - 1], along_y(place, step)))
        arrivals.append(mail.post(low.at[spot(other), :], from_near.at[step], near_of(place, other)))
    for copy in arrivals:
        copy.wait_recv()
    for half in range(2):
        value = own[half, spot(row), :].astype(F32)
        for step in range(3):
            value = value + from_own[step, half].astype(F32)
        if half == 0:
            for step in range(4):
                value = value + from_near[step].astype(F32)
        total[half] = value
    mail.finish()


def halves_kernel(first, second, first_in, second_in, send, recv, local):
    place = here()
    dp, row, col = place
    pair = pair_of(place)
    meet([pair])
    mail = Mail(send, recv)
    copies = [mail.post(first.at[1 - col], first_in, pair), mail.post(second.at[1 - col], second_in, pair)]
    for copy in copies:
        copy.wait_recv()
    mail.finish()


def tail_kernel(
    gu,
    dn,
    qkv,
    wo,
    one,
    two,
    bias,
    gains,
    gu_out,
    dn_out,
    qkv_out,
    wo_out,
    one_out,
    two_out,
    small_out,
    gu_n,
    dn_n,
    gu_s,
    dn_s,
    q_t,
    w_t,
    q_h,
    w_h,
    q_up1,
    q_down1,
    q_up2,
    q_down2,
    w_up1,
    w_down1,
    w_up2,
    w_down2,
    q_s,
    w_s,
    q_n,
    w_n,
    q_z,
    w_z,
    bias_in,
    gains_in,
    small_a,
    small_b,
    small_t,
    small_n,
    send,
    recv,
    local,
):
    place = here()
    dp, row, col = place
    core = dp % 2
    z = dp // Z_STEP
    twin, near, up, down = twin_of(place), near_of(place), along_z(place, 1), along_z(place, 3)
    far_z = along_z(place, 2)
    right, left = along_y(place, 1), along_y(place, 3)
    meet(
        [along_y(place, s) for s in (1, 2, 3)]
        + [pair_of(place, (row + s) % 4) for s in range(4)]
        + [twin, near, up, down, far_z]
    )
    mail = Mail(send, recv)
    kept, arrivals = [], []

    def keep(source, target):
        kept.append(pltpu.make_async_copy(source, target, local.at[len(kept)]))
        kept[-1].start()
        return len(kept) - 1

    def even(start, size):
        return pl.ds(pl.multiple_of(start, 16), size)

    q_rows, w_rows = q_t.shape[1], w_t.shape[0]
    q_first = mail.post(qkv.at[:, even((1 - core) * q_rows, q_rows), :], q_t, twin)
    w_first = mail.post(wo.at[even((1 - core) * w_rows, w_rows), :], w_t, twin)

    thirds = gu.shape[0] // 3
    near_copies = []
    for i in range(3):
        near_copies.append(mail.post(gu.at[pl.ds(i * thirds, thirds), :], gu_n.at[i], near))
    near_copies.append(mail.post(dn, dn_n, near))

    rows, piece = one.shape[0], one.shape[1] // 4
    spot = pl.ds(pl.multiple_of(row * rows, rows), rows)
    small_copies, small_kept = [], []
    for step in range(4):
        other = (row + step) % 4
        device = along_y(place, step)
        mine = gains_in.at[col * 4 + row]
        if step:
            small_copies.append(mail.post(bias, bias_in.at[row], device))
            small_copies.append(mail.post(gains.at[other], mine, device))
        else:
            small_kept.append(keep(bias, bias_in.at[row]))
            small_kept.append(keep(gains.at[other], mine))
        small_copies.append(mail.post(gains.at[other], mine, pair_of(place, other)))
    for step in range(4):
        lanes = pl.ds(pl.multiple_of(((row + step) % 4) * piece, LANES), piece)
        for source, target in ((one, one_out), (two, two_out)):
            if step:
                arrivals.append(mail.post(source.at[:, lanes], target.at[spot, :], along_y(place, step)))
            else:
                keep(source.at[:, lanes], target.at[spot, :])

    q_first.wait_recv()
    for r in range(4):
        q_h[r] = (qkv[r, even(core * q_rows, q_rows), :].astype(F32) + q_t[r].astype(F32)).astype(BF16)
    w_first.wait_recv()
    for r in range(4):
        lanes = pl.ds(r * piece, piece)
        w_h[r] = (wo[even(core * w_rows, w_rows), lanes].astype(F32) + w_t[:, lanes].astype(F32)).astype(BF16)
    above, below, across = (row + 1) % 4, (row + 3) % 4, (row + 2) % 4
    pieces = ((q_h, q_up1, q_down1, q_up2, q_down2, q_s, q_n, q_z), (w_h, w_up1, w_down1, w_up2, w_down2, w_s, w_n, w_z))
    ring = []
    for held, up1, down1, up2, down2, _, _, _ in pieces:
        half = held.shape[1] // 2
        low, high = pl.ds(0, half), pl.ds(half, half)
        ring.append((mail.post(held.at[across, low, :], up1, right), mail.post(held.at[across, high, :], down1, left)))
    straight = []
    for held, up1, down1, up2, down2, _, _, _ in pieces:
        half = held.shape[1] // 2
        low, high = pl.ds(0, half), pl.ds(half, half)
        straight.append(
            (mail.post(held.at[above, high, :], up2.at[1], right), mail.post(held.at[below, low, :], down2.at[0], left))
        )

    for copy in small_copies:
        copy.wait_recv()
    for index in small_kept:
        kept[index].wait()
        kept[index] = None
    small_a[...] = jnp.zeros_like(small_a)
    small_a[0:8, :] = bias_in[0] + bias_in[1] + bias_in[2] + bias_in[3]
    small_a[8:16, 0:piece] = (
        gains_in[0] + gains_in[1] + gains_in[2] + gains_in[3] + gains_in[4] + gains_in[5] + gains_in[6] + gains_in[7]
    )
    small_first = mail.post(small_a, small_t, twin)

    half_dn = dn.shape[0]
    hops = []

    def ring_z(i):
        near_copies[i].wait_recv()
        if i < 3:
            gu_s[i] = (gu[pl.ds(i * thirds, thirds), :].astype(F32) + gu_n[i].astype(F32)).astype(BF16)
            held, size = gu_s.at[i], thirds // 2

            def room(slot, which=None):
                start, height = (i * thirds, thirds) if which is None else (i * thirds + which * size, size)
                return gu_out.at[slot, core, pl.ds(start, height), :]

        else:
            dn_s[...] = (dn[...].astype(F32) + dn_n[...].astype(F32)).astype(BF16)
            held, size = dn_s, half_dn // 2

            def room(slot, which=None):
                start, height = (0, half_dn) if which is None else (which * size, size)
                return dn_out.at[slot, core, pl.ds(start, height), :]

        posts = {}
        for turn in range(2):
            for name, device, which in (("u", up, turn), ("d", down, 1 - turn)):
                posts[name, which] = mail.post(held.at[pl.ds(which * size, size), :], room(z, which), device)
        keep(held, room(z))
        arrivals.append(mail.post(held, room(z), twin))
        hops.append((room, posts))

    def ring_z_on(i):
        room, posts = hops[i]
        posts["u", 0].wait_recv()
        block = room((z + 3) % 4, 0)
        one_more = mail.post(block, block, up)
        arrivals.append(mail.post(block, block, twin))
        posts["d", 1].wait_recv()
        block = room((z + 1) % 4, 1)
        two_more = mail.post(block, block, down)
        arrivals.append(mail.post(block, block, twin))
        posts["u", 1].wait_recv()
        block = room((z + 3) % 4, 1)
        arrivals.append(mail.post(block, block, twin))
        posts["d", 0].wait_recv()
        block = room((z + 1) % 4, 0)
        arrivals.append(mail.post(block, block, twin))
        hops[i] = (room, one_more, two_more)

    def ring_z_end(i):
        room, one_more, two_more = hops[i]
        for which, copy in ((0, one_more), (1, two_more)):
            copy.wait_recv()
            block = room((z + 2) % 4, which)
            arrivals.append(mail.post(block, block, twin))

    ring_z(0)
    lasts = []
    for (held, up1, down1, up2, down2, _, _, _), (from_left, from_right) in zip(pieces, ring):
        half = held.shape[1] // 2
        from_left.wait_recv()
        up1[...] = (held[above, 0:half, :].astype(F32) + up1[...].astype(F32)).astype(BF16)
        one_more = mail.post(up1, up2.at[0], right)
        from_right.wait_recv()
        down1[...] = (held[below, half : 2 * half, :].astype(F32) + down1[...].astype(F32)).astype(BF16)
        lasts.append((one_more, mail.post(down1, down2.at[1], left)))
    ring_z(1)
    small_first.wait_recv()
    small_b[...] = small_a[...] + small_t[...]
    small_second = mail.post(small_b, small_n, near)
    ring_z(2)
    ring_z(3)
    near_second = []
    for (held, up1, down1, up2, down2, total, theirs, _), pair_first, pair_last in zip(pieces, straight, lasts):
        half = held.shape[1] // 2
        for copy in pair_first + pair_last:
            copy.wait_recv()
        for i in range(2):
            part = pl.ds(i * half, half)
            total[part, :] = (
                held[row, part, :].astype(F32) + up2[i].astype(F32) + down2[i].astype(F32)
            ).astype(BF16)
        near_second.append(mail.post(total, theirs, near))
    ring_z_on(0)
    small_second.wait_recv()
    small_t[...] = small_b[...] + small_n[...]
    for device in (up, down, far_z):
        arrivals.append(mail.post(small_t, small_out.at[z], device))
    keep(small_t, small_out.at[z])
    z_copies = []
    for (held, _, _, _, _, total, theirs, quarter), copy in zip(pieces, near_second):
        copy.wait_recv()
        held[row] = (total[...].astype(F32) + theirs[...].astype(F32)).astype(BF16)
        size = quarter.shape[1]
        for step, device in ((1, up), (3, down), (2, far_z)):
            source = held.at[row, even(((z + step) % 4) * size, size), :]
            z_copies.append(mail.post(source, quarter.at[step - 1], device))
    ring_z_on(1)
    ring_z_on(2)
    ring_z_end(0)
    for copy in z_copies:
        copy.wait_recv()
    q_last = []
    for (held, _, _, _, _, _, theirs, quarter), out in zip(pieces, (qkv_out, wo_out)):
        size = quarter.shape[1]
        mine = even(z * size, size)
        height = held.shape[1]
        theirs[0:size, :] = (
            held[row, mine, :].astype(F32)
            + quarter[0].astype(F32)
            + quarter[1].astype(F32)
            + quarter[2].astype(F32)
        ).astype(BF16)
        room = out.at[even(core * height + z * size, size), :]
        for device in (up, down, far_z):
            q_last.append(mail.post(theirs.at[0:size, :], room, device))
        arrivals.append(mail.post(theirs.at[0:size, :], room, twin))
        keep(theirs.at[0:size, :], room)
    ring_z_on(3)
    ring_z_end(1)
    ring_z_end(2)
    for copy in q_last:
        copy.wait_recv()
    for total, quarter, out in ((q_s, q_z, qkv_out), (w_s, w_z, wo_out)):
        size, height = quarter.shape[1], total.shape[0]
        for step in (1, 2, 3):
            room = out.at[even(core * height + ((z + step) % 4) * size, size), :]
            arrivals.append(mail.post(room, room, twin))
    ring_z_end(3)
    for copy in arrivals:
        copy.wait_recv()
    for copy in kept:
        if copy is not None:
            copy.wait()
    mail.finish()


def rotated(vector):
    middle = vector.shape[-1] // 2
    return jnp.concatenate([-vector[..., middle:], vector[..., :middle]], -1)


def apply_rotation(vector, cosine, sine):
    return vector * cosine + rotated(vector) * sine


def undo_rotation(vector, cosine, sine):
    turned = vector * sine
    middle = vector.shape[-1] // 2
    return vector * cosine + jnp.concatenate([turned[..., middle:], -turned[..., :middle]], -1)


def layout(lengths_row, index):
    ends = jnp.cumsum(lengths_row)
    starts = ends - lengths_row
    segment = jnp.sum((index[:, None] >= ends[None, :]).astype(jnp.int32), -1)
    chosen = segment[:, None] == jnp.arange(lengths_row.shape[0], dtype=jnp.int32)[None, :]
    position = index - jnp.sum(jnp.where(chosen, starts[None, :], 0), -1)
    return segment, position


def angles(position):
    steps_half = jnp.arange(HEAD_SIZE // 2, dtype=F32)
    inverse = jnp.exp(-jnp.log(THETA) * 2.0 * steps_half / HEAD_SIZE)
    turn = position.astype(F32)[:, None] * inverse[None, :]
    turn = jnp.concatenate([turn, turn], -1)[:, None, :]
    return jnp.cos(turn), jnp.sin(turn)


def dot_plain(left, right):
    return jnp.dot(left, right, preferred_element_type=F32)


def dot_rows(left, right):
    return lax.dot_general(left, right, (((1,), (1,)), ((), ())), preferred_element_type=F32)


def dot_cols(left, right):
    return lax.dot_general(left, right, (((0,), (0,)), ((), ())), preferred_element_type=F32)


def norm_inverse(stream):
    return lax.rsqrt(jnp.mean(stream * stream, -1, keepdims=True) + EPS)


def norm_back(stream, inverse, gain, incoming):
    scaled = incoming * gain
    inner = jnp.mean(scaled * stream, -1, keepdims=True)
    back = inverse * scaled - stream * (inverse**3 * inner)
    return back, jnp.sum(incoming * stream * inverse, 0)


def attend(query, key, value, allowed, factor):
    raw = jnp.einsum("qhd,kd->hqk", query, key, preferred_element_type=F32) * factor
    scores = jnp.where(allowed[None], raw, -1e30)
    peak = jnp.max(scores, -1, keepdims=True)
    raised = jnp.exp(scores - peak)
    probs = raised / jnp.sum(raised, -1, keepdims=True)
    out = jnp.einsum("hqk,kd->qhd", probs.astype(BF16), value, preferred_element_type=F32)
    return out.astype(BF16), probs


def attend_back(query, key, value, probs, grad, factor):
    grad_probs = jnp.einsum("qhd,kd->hqk", grad, value, preferred_element_type=F32)
    inner = jnp.sum(grad_probs * probs, -1, keepdims=True)
    grad_scores = (probs * (grad_probs - inner)).astype(BF16)
    grad_query = jnp.einsum("hqk,kd->qhd", grad_scores, key, preferred_element_type=F32) * factor
    grad_key = jnp.einsum("hqk,qhd->kd", grad_scores, query, preferred_element_type=F32) * factor
    grad_value = jnp.einsum("hqk,qhd->kd", probs.astype(BF16), grad, preferred_element_type=F32)
    return grad_query, jnp.concatenate([grad_key, grad_value], 1).astype(BF16)


def on_device(
    tokens,
    cotangent,
    lengths,
    gain_attn,
    w_query,
    key_projection,
    value_projection,
    bias_query,
    key_bias_vector,
    value_bias_vector,
    w_out,
    gain_ffn,
    w_gate,
    w_up,
    w_down,
):
    dp, row, col = here()
    z = dp // Z_STEP
    half_rows, piece = tokens.shape
    width = 4 * piece
    rows = half_rows // 4
    q_width = w_query.shape[1]
    kv_width = key_projection.shape[1]
    heads = q_width // HEAD_SIZE
    hidden = w_gate.shape[1]
    share = -(-hidden // (4 * LANES)) * LANES
    factor = HEAD_SIZE ** (-0.5)
    spare = 4 * share - hidden
    take = z * share

    w_in = jnp.concatenate([w_query, key_projection, value_projection], 1)
    in_width = w_in.shape[1]
    lens = jnp.pad(lengths, ((0, 7), (0, LANES - lengths.shape[1])))
    gains = jnp.pad(jnp.stack([gain_attn, gain_ffn]), ((0, 6), (0, 0)))
    tok2, cot2, lens2, gains4, w_in_full, w_out_full = talk(
        start_kernel,
        0,
        36,
        6,
        [
            ((2, rows, width), BF16),
            ((2, rows, width), BF16),
            ((2, 8, LANES), jnp.int32),
            ((4, 8, piece), F32),
            ((width, in_width), BF16),
            ((q_width, width), BF16),
        ],
        [ANY] * 6,
        [ANY] * 6,
    )(tokens, cotangent, lens, gains, w_in, w_out)

    core = dp % 2
    thin = piece // 2
    cut = (core * thin, take)
    w_ffn = jnp.concatenate(
        [
            lax.dynamic_slice(jnp.pad(w_gate, ((0, 0), (0, spare))), cut, (thin, share)),
            lax.dynamic_slice(jnp.pad(w_up, ((0, 0), (0, spare))), cut, (thin, share)),
            lax.dynamic_slice(
                lax.dynamic_slice(jnp.pad(w_down, ((0, spare), (0, 0))), (take, 0), (share, piece)).T,
                (core * thin, 0),
                (thin, share),
            ),
        ],
        1,
    )
    w_ffn, _ = lax.optimization_barrier((w_ffn, lens2))
    w_ffn = lax.all_gather(w_ffn, "row", axis=0, tiled=False)
    cot_rows = cot2.reshape(2 * rows, width)

    def shift_z(array, step):
        count = 4 * Z_STEP
        return lax.ppermute(array, "dp", [(d, (d + Z_STEP * step) % count) for d in range(count)])

    cot_full = jnp.concatenate([cot_rows] + [shift_z(cot_rows, step) for step in (1, 2, 3)], 0)
    gain_attn_full, gain_ffn_full = gains4[:, 0].reshape(width), gains4[:, 1].reshape(width)

    lens_a, lens_b = lens2[0, 0, :3], lens2[1, 0, :3]
    count = jnp.arange(rows, dtype=jnp.int32) + row * rows
    index_a, index_b = count, count + half_rows
    keys_a = jnp.arange(half_rows, dtype=jnp.int32)
    keys_b = jnp.arange(2 * half_rows, dtype=jnp.int32)
    segment_a, position_a = layout(lens_a, index_a)
    segment_b, position_b = layout(lens_b, index_b)
    allowed_a = (segment_a[:, None] == layout(lens_a, keys_a)[0][None, :]) & (keys_a[None, :] <= index_a[:, None])
    allowed_b = (segment_b[:, None] == layout(lens_b, keys_b)[0][None, :]) & (keys_b[None, :] <= index_b[:, None])
    cosine, sine = angles(jnp.concatenate([position_a, position_b]))

    stream = tok2.reshape(2 * rows, width).astype(F32)
    inverse_attn = norm_inverse(stream)
    normed = (stream * inverse_attn * gain_attn_full).astype(BF16)
    pre = dot_plain(normed, w_in_full) + jnp.concatenate([bias_query, key_bias_vector, value_bias_vector])
    query = apply_rotation(pre[:, :q_width].reshape(2 * rows, heads, HEAD_SIZE), cosine, sine).astype(BF16)
    key = apply_rotation(pre[:, q_width : q_width + kv_width], cosine[:, 0], sine[:, 0]).astype(BF16)
    key_value = jnp.concatenate([key, pre[:, q_width + kv_width :].astype(BF16)], 1)
    near_low, own_keys = talk(
        keys_kernel,
        1,
        7,
        1,
        [((half_rows, 2 * kv_width), BF16), ((2, half_rows, 2 * kv_width), BF16)],
        [ANY],
        [ANY] * 2,
    )(key_value.reshape(2, rows, 2 * kv_width))
    kv_a = own_keys[0]
    kv_b = jnp.concatenate([near_low, own_keys[1]], 0)
    query_a, query_b = query[:rows], query[rows:]
    out_a, probs_a = attend(query_a, kv_a[:, :kv_width], kv_a[:, kv_width:], allowed_a, factor)
    out_b, probs_b = attend(query_b, kv_b[:, :kv_width], kv_b[:, kv_width:], allowed_b, factor)
    attended = jnp.concatenate([out_a, out_b], 0).reshape(2 * rows, q_width)
    branch = dot_plain(attended, w_out_full).astype(BF16)
    (branch_other,) = talk(pair_kernel, 2, 1, 0, [((2 * rows, width), BF16)], [ANY], [ANY])(branch)
    middle = stream + (branch.astype(F32) + branch_other.astype(F32))
    inverse_ffn = norm_inverse(middle)
    normed_ffn = (middle * inverse_ffn * gain_ffn_full).astype(BF16)

    ffn_in, w_ffn_full = talk(
        gather_z_kernel,
        3,
        10,
        5,
        [((4, 2 * rows, width), BF16), ((4, 2, thin, 3 * share), BF16)],
        [ANY] * 2,
        [ANY] * 2,
    )(normed_ffn, w_ffn)
    ffn_in = ffn_in.reshape(8 * rows, width)
    w_ffn_full = w_ffn_full.reshape(width, 3 * share)
    w_both_full, w_down_full = w_ffn_full[:, : 2 * share], w_ffn_full[:, 2 * share :]
    both = dot_plain(ffn_in, w_both_full)
    gate, up_value = both[:, :share], both[:, share:]
    grad_act = dot_plain(cot_full, w_down_full)
    spread = 1.0 / (1.0 + jnp.exp(-gate))
    smooth = gate * spread
    activated = (smooth * up_value).astype(BF16)
    grad_gate = grad_act * up_value * (spread * (1.0 + gate * (1.0 - spread)))
    grad_both = jnp.concatenate([grad_gate, grad_act * smooth], 1).astype(BF16)
    grad_in_parts = dot_rows(grad_both, w_both_full).astype(BF16).reshape(4, 2 * rows, width)
    chunk = (2, rows // 2, width)
    chunks = (4, rows // 2, width)
    grad_normed_ffn, both_half, down_half = talk(
        middle_kernel,
        4,
        24,
        13,
        [((2 * rows, width), F32), ((4, piece, share), BF16), ((4, share // 2, piece), BF16)],
        [ANY] * 5,
        [VMEM, ANY, ANY],
        [
            pltpu.VMEM(shape, BF16)
            for shape in (
                (4, 2 * rows, width),
                (8 * rows, width),
                (8 * rows, 2 * share),
                (8 * rows, share),
                (8 * rows, width),
                (width, 8 * rows),
                (4, 2, piece, share),
                (4, share, piece),
                (4, piece, share),
                (4, share // 2, piece),
                chunk,
                chunk,
                chunks,
                chunks,
                chunks,
                chunk,
                chunk,
                chunks,
            )
        ],
        limit=56,
    )(grad_in_parts, ffn_in, grad_both, activated, cot_full)
    down_parts = dot_rows(activated, w_down_full).astype(BF16).reshape(4, 2 * rows, width)
    down_part = down_parts[0].astype(F32)
    for step in (1, 2, 3):
        down_part = down_part + shift_z(down_parts[step], 4 - step).astype(F32)
    down_part = down_part.astype(BF16)
    both_sum = lax.psum_scatter(both_half, "row", scatter_dimension=0, tiled=False)
    down_sum = lax.psum_scatter(down_half, "row", scatter_dimension=0, tiled=False)

    back_mid, gain_ffn_part = norm_back(middle, inverse_ffn, gain_ffn_full, grad_normed_ffn)
    grad_middle = cot_rows.astype(F32) + back_mid
    grad_mid_low = grad_middle.astype(BF16)
    grad_att = dot_rows(grad_mid_low, w_out_full).astype(BF16).reshape(2 * rows, heads, HEAD_SIZE)
    out_w = dot_cols(attended, grad_mid_low).astype(BF16)
    gq_a, gkv_a = attend_back(query_a, kv_a[:, :kv_width], kv_a[:, kv_width:], probs_a, grad_att[:rows], factor)
    gq_b, gkv_b = attend_back(query_b, kv_b[:, :kv_width], kv_b[:, kv_width:], probs_b, grad_att[rows:], factor)
    (grad_kv,) = talk(
        keys_back_kernel,
        5,
        7,
        0,
        [((2, rows, 2 * kv_width), F32)],
        [VMEM] * 2,
        [VMEM],
        [pltpu.VMEM((3, 2, rows, 2 * kv_width), BF16), pltpu.VMEM((4, rows, 2 * kv_width), BF16)],
    )(gkv_b[:half_rows], jnp.stack([gkv_a, gkv_b[half_rows:]]))
    grad_kv = grad_kv.reshape(2 * rows, 2 * kv_width)
    grad_query = undo_rotation(jnp.concatenate([gq_a, gq_b], 0), cosine, sine).reshape(2 * rows, q_width)
    grad_key = undo_rotation(grad_kv[:, :kv_width], cosine[:, 0], sine[:, 0])
    grad_pre = jnp.concatenate([grad_query, grad_key, grad_kv[:, kv_width:]], 1).astype(BF16)
    grad_normed_part = dot_rows(grad_pre, w_in_full).astype(BF16).reshape(2, rows, width)
    grad_normed_in, down_in = talk(
        halves_kernel,
        6,
        2,
        0,
        [((rows, width), BF16)] * 2,
        [ANY] * 2,
        [ANY] * 2,
    )(grad_normed_part, down_part.reshape(2, rows, width))

    def own(array):
        return lax.dynamic_index_in_dim(array.reshape(2, rows, -1), col, 0, keepdims=False)

    grad_normed = own(grad_normed_part).astype(F32) + grad_normed_in.astype(F32)
    result_rows = own(middle) + (own(down_part).astype(F32) + down_in.astype(F32))
    back_in, gain_attn_part = norm_back(own(stream), own(inverse_attn), gain_attn_full, grad_normed)
    grad_rows = own(grad_middle) + back_in
    grad_bias = jnp.sum(grad_pre.astype(F32), 0)
    gains = jnp.stack([gain_attn_part, 0.5 * gain_ffn_part]).reshape(2, 4, piece).transpose(1, 0, 2)
    in_w = dot_cols(normed, grad_pre).astype(BF16).reshape(4, piece, in_width)
    thirds = piece // 3
    q_half, w_half = (thin, in_width), (q_width // 2, piece)
    gate_up, down_all, in_total, out_total, result, grad_tokens, small_all = talk(
        tail_kernel,
        8,
        TAIL_COPIES,
        TAIL_LOCAL,
        [
            ((4, 2, piece, share), BF16),
            ((4, 2, share // 2, piece), BF16),
            ((piece, in_width), BF16),
            ((q_width, piece), BF16),
            ((half_rows, piece), BF16),
            ((half_rows, piece), BF16),
            ((4, 16, in_width), F32),
        ],
        [VMEM] * 4 + [ANY] * 4,
        [ANY] * 7,
        [
            pltpu.VMEM(shape, BF16)
            for shape in (
                (3, thirds, share),
                (share // 2, piece),
                (3, thirds, share),
                (share // 2, piece),
                (4, *q_half),
                (q_width // 2, width),
                (4, *q_half),
                (4, *w_half),
                (thin // 2, in_width),
                (thin // 2, in_width),
                (2, thin // 2, in_width),
                (2, thin // 2, in_width),
                (q_width // 4, piece),
                (q_width // 4, piece),
                (2, q_width // 4, piece),
                (2, q_width // 4, piece),
                q_half,
                w_half,
                q_half,
                w_half,
                (3, thin // 4, in_width),
                (3, q_width // 8, piece),
            )
        ]
        + [pltpu.VMEM((4, 8, in_width), F32), pltpu.VMEM((8, 8, piece), F32)]
        + [pltpu.VMEM((16, in_width), F32)] * 4,
        limit=56,
    )(
        both_sum,
        down_sum,
        in_w,
        out_w,
        result_rows.astype(BF16),
        grad_rows.astype(BF16),
        jnp.pad(grad_bias[None], ((0, 7), (0, 0))),
        jnp.pad(gains, ((0, 0), (0, 6), (0, 0))),
    )
    small_total = small_all[0] + small_all[1] + small_all[2] + small_all[3]
    bias_total = small_total[0]
    in_total = in_total.astype(F32)
    gate_total = jnp.concatenate([gate_up[i, 0] for i in range(4)], 1)[:, :hidden].astype(F32)
    up_total = jnp.concatenate([gate_up[i, 1] for i in range(4)], 1)[:, :hidden].astype(F32)
    down_total = down_all.reshape(4 * share, piece)[:hidden].astype(F32)
    upper = q_width + kv_width
    return (
        result.astype(F32),
        grad_tokens.astype(F32),
        small_total[8, :piece],
        in_total[:, :q_width],
        in_total[:, q_width:upper],
        in_total[:, upper:],
        bias_total[:q_width],
        bias_total[q_width:upper],
        bias_total[upper:],
        out_total.astype(F32),
        small_total[9, :piece],
        gate_total,
        up_total,
        down_total,
    )


def solution(mesh):
    placed = (
        P(("dp", "col"), "row"),
        P(("dp", "col"), "row"),
        P("dp", None),
        P("row"),
        P("row", "col"),
        P("row", "col"),
        P("row", "col"),
        P("col"),
        P("col"),
        P("col"),
        P("col", "row"),
        P("row"),
        P("row", "col"),
        P("row", "col"),
        P("col", "row"),
    )
    return jax.shard_map(
        on_device,
        mesh=mesh,
        in_specs=placed,
        out_specs=(
            P(("dp", "col"), "row"),
            P(("dp", "col"), "row"),
            P("row"),
            P("row", "col"),
            P("row", "col"),
            P("row", "col"),
            P("col"),
            P("col"),
            P("col"),
            P("col", "row"),
            P("row"),
            P("row", "col"),
            P("row", "col"),
            P("col", "row"),
        ),
        check_vma=False,
    )
```

```python
import math

import jax
import jax.numpy as jnp
from jax import lax
from jax.experimental import pallas as pl
from jax.experimental.pallas import tpu as pltpu
from jax.sharding import PartitionSpec as P

HEAD_SIZE = 128
EPS = 1e-06
THETA = 1000000.0
LANES = 128
MESH = pl.DeviceIdType.MESH
BF16 = jnp.bfloat16
F32 = jnp.float32
ANY = pl.BlockSpec(memory_space=pl.ANY)
VMEM = pl.BlockSpec(memory_space=pltpu.VMEM)

Z_STEP = 4
FRONT_COPIES = 74
FRONT_LOCAL = 27
TAIL_COPIES = 113
TAIL_LOCAL = 11


def here():
    return lax.axis_index("dp"), lax.axis_index("row"), lax.axis_index("col")


def flip_near(dp):
    return dp + 2 - 4 * ((dp // 2) % 2)


def pair_of(place, row=None):
    dp, own, col = place
    return flip_near(dp), own if row is None else row, 1 - col


def near_of(place, row=None):
    dp, own, col = place
    return flip_near(dp), own if row is None else row, col


def twin_of(place):
    dp, row, col = place
    return dp + 1 - 2 * (dp % 2), row, col


def along_z(place, step):
    dp, row, col = place
    return (dp + Z_STEP * step) % (4 * Z_STEP), row, col


def along_y(place, step):
    dp, row, col = place
    return dp, (row + step) % 4, col


def meet(peers):
    barrier = pltpu.get_barrier_semaphore()
    for peer in peers:
        pl.semaphore_signal(barrier, inc=1, device_id=peer, device_id_type=MESH)
    pl.semaphore_wait(barrier, len(peers))


class Mail:
    def __init__(self, send, recv):
        self.send, self.recv, self.count, self.sent = send, recv, 0, []

    def post(self, source, target, device):
        index = self.count
        self.count += 1
        copy = pltpu.make_async_remote_copy(
            src_ref=source,
            dst_ref=target,
            send_sem=self.send.at[index],
            recv_sem=self.recv.at[index],
            device_id=device,
            device_id_type=MESH,
        )
        copy.start()
        self.sent.append(copy)
        return copy

    def finish(self):
        assert self.count == self.send.shape[0], (self.count, self.send.shape)
        for copy in self.sent:
            copy.wait_send()


def talk(body, ident, copies, local, outs, in_specs, out_specs, scratch=(), limit=32):
    return pl.pallas_call(
        body,
        out_shape=[jax.ShapeDtypeStruct(*out) for out in outs],
        in_specs=in_specs,
        out_specs=out_specs,
        scratch_shapes=[
            *scratch,
            pltpu.SemaphoreType.DMA((copies,)),
            pltpu.SemaphoreType.DMA((copies,)),
            pltpu.SemaphoreType.DMA((max(local, 1),)),
        ],
        compiler_params=pltpu.CompilerParams(
            collective_id=ident, has_side_effects=True, vmem_limit_bytes=limit << 20
        ),
    )


def front_kernel(
    tok,
    cot,
    lens,
    gains,
    bias,
    wq,
    wk,
    wv,
    wo,
    wg,
    wu,
    wd,
    tok_out,
    cot_full,
    gains_out,
    normed,
    query,
    kva_out,
    kvb_out,
    logs,
    attended,
    tables,
    middle,
    bias_a,
    bias_b,
    ffn_in,
    w_in_out,
    w_out_out,
    wgu_full,
    wd_full,
    tok_v,
    lens_v,
    gains_v,
    w_in,
    w_out,
    gu_own,
    wd_own,
    blank_gu,
    blank_wd,
    kv,
    kva,
    kvb,
    branch,
    branch_in,
    normed_ffn,
    send,
    recv,
    local,
):
    place = here()
    dp, row, col = place
    z, core = dp // Z_STEP, dp % 2
    twin, pair, up, down = twin_of(place), pair_of(place), along_z(place, 1), along_z(place, 3)
    right, left = along_y(place, 1), along_y(place, 3)
    meet(
        [along_y(place, s) for s in (1, 2, 3)]
        + [near_of(place, (row + s) % 4) for s in range(4)]
        + [pair, twin, up, down]
    )
    mail = Mail(send, recv)
    kept = []

    def keep(source, target):
        kept.append(pltpu.make_async_copy(source, target, local.at[len(kept)]))
        kept[-1].start()
        return len(kept) - 1

    def kept_wait(index):
        kept[index].wait()
        kept[index] = None

    def even(start, size):
        return pl.ds(pl.multiple_of(start, 16), size)

    rows, piece = tok.shape[0] // 4, tok.shape[1]
    width = 4 * piece
    own_rows = even(col * rows, rows)
    spot = even(row * rows, rows)

    def spread(source, target):
        got = []
        for step in range(4):
            part = source.at[even(((row + step) % 4) * rows, rows), :]
            lanes = pl.ds(((4 - step) % 4) * piece, piece)
            if step:
                got.append(mail.post(part, target.at[own_rows, lanes], along_y(place, step)))
            else:
                mine = keep(part, target.at[own_rows, lanes])
        return got, mine

    tokens = spread(tok, tok_v)
    lens_got = mail.post(lens, lens_v.at[col], pair)
    lens_kept = keep(lens, lens_v.at[col])
    gains_kept = keep(gains, gains_v.at[0])
    gains_got = [mail.post(gains, gains_v.at[4 - s], along_y(place, s)) for s in (1, 2, 3)]

    q_width, kv_width = wq.shape[1], wk.shape[1]
    stages = [
        keep(wq, w_in.at[0, :, pl.ds(0, q_width)]),
        keep(wk, w_in.at[0, :, pl.ds(q_width, kv_width)]),
        keep(wv, w_in.at[0, :, pl.ds(q_width + kv_width, kv_width)]),
        keep(wo, w_out.at[:, pl.ds(0, piece)]),
    ]
    share = wd_own.shape[0]
    thin = piece // 2
    sure = share - LANES
    take = pl.multiple_of(z * share, LANES)
    big = []
    for k in range(2):
        for i, source in enumerate((wg, wu)):
            from_rows = pl.ds(k * thin, thin)
            big.append(keep(source.at[from_rows, pl.ds(take, sure)], gu_own.at[k, :, pl.ds(i * share, sure)]))
    big.append(keep(wd.at[pl.ds(take, sure), :], wd_own.at[pl.ds(0, sure), :]))
    blank_gu[...] = jnp.zeros_like(blank_gu)
    blank_wd[...] = jnp.zeros_like(blank_wd)
    first_edge = len(kept)
    edges = []
    for k in range(2):
        for i, source in enumerate((wg, wu)):
            target = gu_own.at[k, :, pl.ds(i * share + sure, LANES)]
            edges.append((source, pl.ds(k * thin, thin), None, target, blank_gu))
    edges.append((wd, None, slice(None), wd_own.at[pl.ds(sure, LANES), :], blank_wd))

    def edge(index, last):
        source, from_rows, _, target, blank = edges[index]
        if last:
            origin = blank
        elif from_rows is None:
            origin = source.at[pl.ds(pl.multiple_of(take + sure, LANES), LANES), :]
        else:
            origin = source.at[from_rows, pl.ds(pl.multiple_of(take + sure, LANES), LANES)]
        return pltpu.make_async_copy(origin, target, local.at[first_edge + index])

    @pl.when(z < 3)
    def _():
        for index in range(len(edges)):
            edge(index, False).start()

    @pl.when(z == 3)
    def _():
        for index in range(len(edges)):
            edge(index, True).start()

    for index in range(len(edges)):
        kept.append(edge(index, True))
        big.append(first_edge + index)

    q_rows, o_rows = thin // 4, w_out.shape[0] // 8

    def in_part(j, owner_z):
        return w_in.at[j, even(core * thin + owner_z * q_rows, q_rows), :]

    def in_parts(owner_z):
        return w_in.at[pl.ds(1, 3), even(core * thin + owner_z * q_rows, q_rows), :]

    def out_part(j, owner_z):
        return w_out.at[even(core * 4 * o_rows + owner_z * o_rows, o_rows), pl.ds(j * piece, piece)]

    def out_parts(owner_z):
        return w_out.at[even(core * 4 * o_rows + owner_z * o_rows, o_rows), pl.ds(piece, 3 * piece)]

    for index in stages:
        kept_wait(index)
    y_got = []
    for step in (1, 3, 2):
        y_got.append(mail.post(in_part(0, z), in_part(4 - step, z), along_y(place, step)))
        y_got.append(mail.post(out_part(0, z), out_part(4 - step, z), along_y(place, step)))

    for index in big:
        kept_wait(index)
    gu_half, wd_half = thin // 2, share // 4

    def gu_part(j, which=None):
        start, size = (0, thin) if which is None else (which * gu_half, gu_half)
        return wgu_full.at[j, core, pl.ds(start, size), :]

    def wd_part(j, which=None):
        start, size = (0, 2 * wd_half) if which is None else (which * wd_half, wd_half)
        return wd_full.at[even(core * 2 * wd_half + start, size), pl.ds(j * piece, piece)]

    def gu_source(which):
        return gu_own.at[core, pl.ds(which * gu_half, gu_half), :]

    def wd_source(which):
        return wd_own.at[even((core * 2 + which) * wd_half, wd_half), :]

    y_ring = {}
    for name, source, part in (("gu", gu_source, gu_part), ("wd", wd_source, wd_part)):
        for turn in range(2):
            y_ring[name, "r", turn] = mail.post(source(turn), part(3, turn), right)
            y_ring[name, "l", 1 - turn] = mail.post(source(1 - turn), part(1, 1 - turn), left)
    keep(gu_own, wgu_full.at[0])
    keep(wd_own, wd_full.at[:, pl.ds(0, piece)])
    twins = []

    def y_forward(name, part):
        y_ring[name, "r", 0].wait_recv()
        y_ring[name, "fr"] = mail.post(part(3, 0), part(2, 0), right)
        y_ring[name, "l", 1].wait_recv()
        y_ring[name, "fl"] = mail.post(part(1, 1), part(2, 1), left)

    def y_share(name, part):
        y_ring[name, "r", 1].wait_recv()
        twins.append(mail.post(part(3), part(3), twin))
        y_ring[name, "l", 0].wait_recv()
        twins.append(mail.post(part(1), part(1), twin))

    def y_end(name, part):
        y_ring[name, "fr"].wait_recv()
        y_ring[name, "fl"].wait_recv()
        twins.append(mail.post(part(2), part(2), twin))

    cotangents = spread(cot, cot_full.at[0])

    def to_pair(spreading, target):
        got, mine = spreading
        kept_wait(mine)
        for copy in got:
            copy.wait_recv()
        return mail.post(target.at[own_rows, :], target.at[own_rows, :], pair)

    tokens_pair = to_pair(tokens, tok_v)
    shares = []

    def give(part):
        shares.append(mail.post(part, part, twin))

    for copy in y_got:
        copy.wait_recv()
    in_up = mail.post(in_parts(z), in_parts(z), up)
    out_down = mail.post(out_parts(z), out_parts(z), down)
    out_up = mail.post(out_parts(z), out_parts(z), up)
    in_down = mail.post(in_parts(z), in_parts(z), down)
    give(in_parts(z))
    give(out_parts(z))

    kept_wait(lens_kept)
    lens_got.wait_recv()
    half_rows = 4 * rows

    def segment_of(which, index):
        end_0 = lens_v[which, 0:1, 0:1]
        end_1 = end_0 + lens_v[which, 0:1, 1:2]
        past_0 = (index >= end_0).astype(jnp.int32)
        past_1 = (index >= end_1).astype(jnp.int32)
        start = jnp.where(past_1 > 0, end_1, jnp.where(past_0 > 0, end_0, 0))
        return past_0 + past_1, start

    lane = lax.broadcasted_iota(jnp.int32, (rows, HEAD_SIZE), 1)
    half_lane = jnp.where(lane >= HEAD_SIZE // 2, lane - HEAD_SIZE // 2, lane).astype(F32)
    inverse = jnp.exp(half_lane * (-2.0 * math.log(THETA) / HEAD_SIZE))
    for which, mask, key_count in ((0, bias_a, half_rows), (1, bias_b, 2 * half_rows)):
        index = lax.broadcasted_iota(jnp.int32, (rows, HEAD_SIZE), 0) + (row * rows + which * half_rows)
        _, start = segment_of(which, index)
        turn = (index - start).astype(F32) * inverse
        tables[0, which * rows : (which + 1) * rows, :] = jnp.cos(turn)
        sine = jnp.sin(turn)
        tables[1, which * rows : (which + 1) * rows, :] = jnp.where(lane >= HEAD_SIZE // 2, sine, -sine)
        at = lax.broadcasted_iota(jnp.int32, (rows, key_count), 0) + (row * rows + which * half_rows)
        keys = lax.broadcasted_iota(jnp.int32, (rows, key_count), 1)
        allowed = jnp.logical_and(segment_of(which, at)[0] == segment_of(which, keys)[0], keys <= at)
        mask[...] = jnp.where(allowed, 0.0, -1e30)

    cot_pair = to_pair(cotangents, cot_full.at[0])
    kept_wait(gains_kept)
    for copy in gains_got:
        copy.wait_recv()
    keep(gains_v, gains_out)
    tokens_pair.wait_recv()
    keep(tok_v, tok_out)

    def normalise(value, which):
        scale = lax.rsqrt(jnp.sum(value * value, -1, keepdims=True) * (1.0 / width) + EPS)
        return [
            (value[:, j * piece : (j + 1) * piece] * scale * gains_v[j, which : which + 1, :]).astype(BF16)
            for j in range(4)
        ]

    for half in range(2):
        part = pl.ds(half * rows, rows)
        for j, block in enumerate(normalise(tok_v[part, :].astype(F32), 0)):
            normed[part, pl.ds(j * piece, piece)] = block

    in_up.wait_recv()
    in_far = mail.post(in_parts((z + 3) % 4), in_parts((z + 3) % 4), up)
    give(in_parts((z + 3) % 4))
    out_down.wait_recv()
    out_far = mail.post(out_parts((z + 1) % 4), out_parts((z + 1) % 4), down)
    give(out_parts((z + 1) % 4))
    in_down.wait_recv()
    give(in_parts((z + 1) % 4))
    out_up.wait_recv()
    give(out_parts((z + 3) % 4))
    cot_pair.wait_recv()

    def z_send(source, target, half):
        part = pl.ds(half * rows, rows)
        return (
            mail.post(source.at[part, :], target.at[1, part, :], up),
            mail.post(source.at[part, :], target.at[3, part, :], down),
        )

    def z_forward(target, half, copies):
        part = pl.ds(half * rows, rows)
        if half == 0:
            copies[0].wait_recv()
            return copies[1], mail.post(target.at[1, part, :], target.at[2, part, :], up)
        copies[1].wait_recv()
        return copies[0], mail.post(target.at[3, part, :], target.at[2, part, :], down)

    cot_z = [z_send(cot_full.at[0], cot_full, half) for half in range(2)]
    in_far.wait_recv()
    give(in_parts((z + 2) % 4))
    out_far.wait_recv()
    give(out_parts((z + 2) % 4))
    for copy in shares:
        copy.wait_recv()
    keep(w_in, w_in_out)
    keep(w_out, w_out_out)

    in_width = w_in.shape[2]

    def project(lanes):
        value = jnp.dot(normed[:, 0:piece], w_in[0, :, lanes], preferred_element_type=F32)
        for j in range(1, 4):
            value = value + jnp.dot(
                normed[:, j * piece : (j + 1) * piece], w_in[j, :, lanes], preferred_element_type=F32
            )
        return value + bias[0:1, lanes]

    def rotate(value):
        return value * tables[0] + pltpu.roll(value, HEAD_SIZE // 2, 1) * tables[1]

    key_value = project(slice(q_width, in_width))
    kv[:, 0:kv_width] = rotate(key_value[:, 0:kv_width]).astype(BF16)
    kv[:, kv_width : 2 * kv_width] = key_value[:, kv_width : 2 * kv_width].astype(BF16)
    a_rows, b_rows = pl.ds(0, rows), pl.ds(rows, rows)
    high_spot = even(half_rows + row * rows, rows)
    a_got, b_got = [], []
    for step in (1, 2, 3):
        a_got.append(mail.post(kv.at[a_rows, :], kva.at[spot, :], along_y(place, step)))
    for step in range(4):
        b_got.append(mail.post(kv.at[a_rows, :], kvb.at[spot, :], near_of(place, (row + step) % 4)))
        if step:
            b_got.append(mail.post(kv.at[b_rows, :], kvb.at[high_spot, :], along_y(place, step)))
    kva[spot, :] = kv[a_rows, :]
    kvb[high_spot, :] = kv[b_rows, :]
    for first in range(0, q_width, 2 * HEAD_SIZE):
        value = project(slice(first, first + 2 * HEAD_SIZE))
        for i in range(2):
            lanes = slice(first + i * HEAD_SIZE, first + (i + 1) * HEAD_SIZE)
            query[:, lanes] = rotate(value[:, i * HEAD_SIZE : (i + 1) * HEAD_SIZE]).astype(BF16)

    heads = q_width // HEAD_SIZE
    factor = HEAD_SIZE ** (-0.5)

    def attend(half, keys, mask):
        part = slice(half * rows, (half + 1) * rows)

        @pl.loop(0, heads)
        def _(h):
            lanes = pl.ds(pl.multiple_of(h * HEAD_SIZE, LANES), HEAD_SIZE)
            raw = lax.dot_general(
                query[part, lanes], keys[:, 0:HEAD_SIZE], (((1,), (1,)), ((), ())), preferred_element_type=F32
            )
            scores = raw * factor + mask[...]
            peak = jnp.max(scores, -1, keepdims=True)
            raised = jnp.exp(scores - peak)
            total = jnp.sum(raised, -1, keepdims=True)
            probs = (raised * (1.0 / total)).astype(BF16)
            out = jnp.dot(probs, keys[:, HEAD_SIZE : 2 * HEAD_SIZE], preferred_element_type=F32)
            attended[part, lanes] = out.astype(BF16)
            logs[half * heads + h] = jnp.broadcast_to(peak + jnp.log(total), (rows, LANES))

        for first in range(0, width, piece):
            lanes = slice(first, first + piece)
            branch[part, lanes] = jnp.dot(
                attended[part, :], w_out[:, lanes], preferred_element_type=F32
            ).astype(BF16)
        return mail.post(branch.at[part, :], branch_in.at[part, :], pair)

    def finish_half(half, copy):
        part = slice(half * rows, (half + 1) * rows)
        copy.wait_recv()
        value = tok_v[part, :].astype(F32) + (branch[part, :].astype(F32) + branch_in[part, :].astype(F32))
        middle[part, :] = value
        for j, block in enumerate(normalise(value, 1)):
            normed_ffn[part, j * piece : (j + 1) * piece] = block
        return z_send(normed_ffn, ffn_in, half)

    for copy in a_got:
        copy.wait_recv()
    keep(kva, kva_out)
    swap_a = attend(0, kva, bias_a)
    y_forward("gu", gu_part)
    cot_last = [z_forward(cot_full, half, cot_z[half]) for half in range(2)]
    for copy in b_got:
        copy.wait_recv()
    keep(kvb, kvb_out)
    swap_b = attend(1, kvb, bias_b)
    y_forward("wd", wd_part)
    ffn_z = [finish_half(0, swap_a)]
    y_share("gu", gu_part)
    ffn_z.append(finish_half(1, swap_b))
    keep(normed_ffn, ffn_in.at[0])
    y_share("wd", wd_part)
    y_end("gu", gu_part)
    ffn_last = [z_forward(ffn_in, half, ffn_z[half]) for half in range(2)]
    y_end("wd", wd_part)
    for copies in cot_last + ffn_last:
        for copy in copies:
            copy.wait_recv()
    for copy in twins:
        copy.wait_recv()
    for copy in kept:
        if copy is not None:
            copy.wait()
    mail.finish()


def middle_kernel(
    parts,
    x,
    gb,
    act,
    cot,
    total,
    gu_half,
    dn_half,
    parts_v,
    x_v,
    gb_v,
    act_v,
    cot_v,
    turned,
    gu_w,
    dn_w,
    gu_in,
    dn_in,
    up1,
    down1,
    up2,
    down2,
    other,
    stage_up,
    stage_down,
    stage,
    send,
    recv,
    local,
):
    place = here()
    dp, row, col = place
    core = dp % 2
    up, down, pair, twin = along_z(place, 1), along_z(place, 3), pair_of(place), twin_of(place)
    meet([up, down, pair, twin])
    mail = Mail(send, recv)
    above, below, across = 3, 1, 2
    size = parts.shape[1] // 4

    loads = [
        pltpu.make_async_copy(source, target, local.at[i])
        for i, (source, target) in enumerate(((x, x_v), (gb, gb_v), (parts, parts_v), (act, act_v), (cot, cot_v)))
    ]

    def chunk(ref, owner, index):
        return ref.at[owner, pl.ds(index * size, size), :]

    first, second = {}, {}
    for i in range(2):
        first["u", i] = mail.post(chunk(parts, across, i), up1.at[i], up)
        first["d", i] = mail.post(chunk(parts, across, 2 + i), down1.at[i], down)
    for copy in loads:
        copy.start()
    for i in range(2):
        second["u", 2 + i] = mail.post(chunk(parts, above, 2 + i), up2.at[2 + i], up)
        second["d", i] = mail.post(chunk(parts, below, i), down2.at[i], down)

    def turn(source, target):
        @pl.loop(0, source.shape[1] // LANES)
        def _(t):
            lanes = pl.ds(pl.multiple_of(t * LANES, LANES), LANES)
            target[lanes, :] = source[:, lanes].T

    def forward(i):
        first["u", i].wait_recv()
        stage_up[i] = (chunk(parts_v, above, i)[...].astype(F32) + up1[i].astype(F32)).astype(BF16)
        second["u", i] = mail.post(stage_up.at[i], up2.at[i], up)
        first["d", i].wait_recv()
        stage_down[i] = (chunk(parts_v, below, 2 + i)[...].astype(F32) + down1[i].astype(F32)).astype(BF16)
        second["d", 2 + i] = mail.post(stage_down.at[i], down2.at[2 + i], down)

    piece = gu_w.shape[2]
    share = gu_w.shape[3]
    steps = share // piece
    shared = []

    def up_block(r):
        @pl.loop(0, 2 * steps)
        def _(n):
            lanes = pl.ds(pl.multiple_of(n * piece, LANES), piece)
            tile = jnp.dot(turned[pl.ds(r * piece, piece), :], gb_v[:, lanes], preferred_element_type=F32)
            gu_w[r, n // steps, :, pl.ds(pl.multiple_of((n % steps) * piece, LANES), piece)] = tile.astype(BF16)

        shared.append(mail.post(gu_w.at[r, 1 - core], gu_in.at[r], twin))

    def down_block(r):
        @pl.loop(0, steps)
        def _(n):
            rows = pl.ds(pl.multiple_of(n * piece, LANES), piece)
            tile = jnp.dot(turned[rows, :], cot_v[:, r * piece : (r + 1) * piece], preferred_element_type=F32)
            dn_w[r, rows, :] = tile.astype(BF16)

        half = share // 2
        there = pl.ds(pl.multiple_of((1 - core) * half, 16), half)
        shared.append(mail.post(dn_w.at[r, there, :], dn_in.at[r], twin))

    loads[0].wait()
    turn(x_v, turned)
    loads[2].wait()
    forward(0)
    loads[1].wait()
    up_block(0)
    forward(1)
    up_block(1)
    up_block(2)
    up_block(3)
    swaps = {}

    def settle(i):
        second["u", i].wait_recv()
        second["d", i].wait_recv()
        stage[i] = (chunk(parts_v, 0, i)[...].astype(F32) + up2[i].astype(F32) + down2[i].astype(F32)).astype(BF16)
        swaps[i] = mail.post(stage.at[i], other.at[i], pair)

    loads[3].wait()
    turn(act_v, turned)
    loads[4].wait()
    settle(0)
    settle(2)
    down_block(0)
    down_block(1)
    settle(1)
    settle(3)
    down_block(2)
    down_block(3)
    for i in (0, 2, 1, 3):
        swaps[i].wait_recv()
        total[pl.ds(i * size, size), :] = stage[i].astype(F32) + other[i].astype(F32)
    half = share // 2
    mine = pl.ds(pl.multiple_of(core * half, 16), half)
    stores = []
    for r in range(4):
        shared[r].wait_recv()
        gu_in[r] = (gu_w[r, core].astype(F32) + gu_in[r].astype(F32)).astype(BF16)
        stores.append(pltpu.make_async_copy(gu_in.at[r], gu_half.at[(row + r) % 4], local.at[5 + r]))
        stores[-1].start()
    for r in range(4):
        shared[4 + r].wait_recv()
        dn_in[r] = (dn_w[r, mine, :].astype(F32) + dn_in[r].astype(F32)).astype(BF16)
        stores.append(pltpu.make_async_copy(dn_in.at[r], dn_half.at[(row + r) % 4], local.at[9 + r]))
        stores[-1].start()
    for copy in stores:
        copy.wait()
    mail.finish()


def keys_back_kernel(low, own, total, from_own, from_near, send, recv, local):
    place = here()
    dp, row, col = place
    meet([along_y(place, s) for s in (1, 2, 3)] + [near_of(place, (row + s) % 4) for s in range(4)])
    mail = Mail(send, recv)
    rows = total.shape[1]

    def spot(owner):
        return pl.ds(pl.multiple_of(owner * rows, rows), rows)

    arrivals = []
    for step in range(4):
        other = (row + step) % 4
        if step:
            arrivals.append(mail.post(own.at[:, spot(other), :], from_own.at[step - 1], along_y(place, step)))
        arrivals.append(mail.post(low.at[spot(other), :], from_near.at[step], near_of(place, other)))
    for copy in arrivals:
        copy.wait_recv()
    for half in range(2):
        value = own[half, spot(row), :].astype(F32)
        for step in range(3):
            value = value + from_own[step, half].astype(F32)
        if half == 0:
            for step in range(4):
                value = value + from_near[step].astype(F32)
        total[half] = value
    mail.finish()


def halves_kernel(first, second, first_in, second_in, send, recv, local):
    place = here()
    dp, row, col = place
    pair = pair_of(place)
    meet([pair])
    mail = Mail(send, recv)
    copies = [mail.post(first.at[1 - col], first_in, pair), mail.post(second.at[1 - col], second_in, pair)]
    for copy in copies:
        copy.wait_recv()
    mail.finish()


def tail_kernel(
    gu,
    dn,
    qkv,
    wo,
    one,
    two,
    bias,
    gains,
    gu_out,
    dn_out,
    qkv_out,
    wo_out,
    one_out,
    two_out,
    small_out,
    gu_n,
    dn_n,
    gu_s,
    dn_s,
    q_t,
    w_t,
    q_h,
    w_h,
    q_up1,
    q_down1,
    q_up2,
    q_down2,
    w_up1,
    w_down1,
    w_up2,
    w_down2,
    q_s,
    w_s,
    q_n,
    w_n,
    q_z,
    w_z,
    bias_in,
    gains_in,
    small_a,
    small_b,
    small_t,
    small_n,
    send,
    recv,
    local,
):
    place = here()
    dp, row, col = place
    core = dp % 2
    z = dp // Z_STEP
    twin, near, up, down = twin_of(place), near_of(place), along_z(place, 1), along_z(place, 3)
    far_z = along_z(place, 2)
    right, left = along_y(place, 1), along_y(place, 3)
    meet(
        [along_y(place, s) for s in (1, 2, 3)]
        + [pair_of(place, (row + s) % 4) for s in range(4)]
        + [twin, near, up, down, far_z]
    )
    mail = Mail(send, recv)
    kept, arrivals = [], []

    def keep(source, target):
        kept.append(pltpu.make_async_copy(source, target, local.at[len(kept)]))
        kept[-1].start()
        return len(kept) - 1

    def even(start, size):
        return pl.ds(pl.multiple_of(start, 16), size)

    q_rows, w_rows = q_t.shape[1], w_t.shape[0]
    q_first = mail.post(qkv.at[:, even((1 - core) * q_rows, q_rows), :], q_t, twin)
    w_first = mail.post(wo.at[even((1 - core) * w_rows, w_rows), :], w_t, twin)

    thirds = gu.shape[0] // 3
    near_copies = []
    for i in range(3):
        near_copies.append(mail.post(gu.at[pl.ds(i * thirds, thirds), :], gu_n.at[i], near))
    near_copies.append(mail.post(dn, dn_n, near))

    rows, piece = one.shape[0], one.shape[1] // 4
    spot = pl.ds(pl.multiple_of(row * rows, rows), rows)
    small_copies, small_kept = [], []
    for step in range(4):
        other = (row + step) % 4
        device = along_y(place, step)
        mine = gains_in.at[col * 4 + row]
        if step:
            small_copies.append(mail.post(bias, bias_in.at[row], device))
            small_copies.append(mail.post(gains.at[step], mine, device))
        else:
            small_kept.append(keep(bias, bias_in.at[row]))
            small_kept.append(keep(gains.at[step], mine))
        small_copies.append(mail.post(gains.at[step], mine, pair_of(place, other)))
    for step in range(4):
        lanes = pl.ds(step * piece, piece)
        for source, target in ((one, one_out), (two, two_out)):
            if step:
                arrivals.append(mail.post(source.at[:, lanes], target.at[spot, :], along_y(place, step)))
            else:
                keep(source.at[:, lanes], target.at[spot, :])

    q_first.wait_recv()
    for r in range(4):
        q_h[r] = (qkv[r, even(core * q_rows, q_rows), :].astype(F32) + q_t[r].astype(F32)).astype(BF16)
    w_first.wait_recv()
    for r in range(4):
        lanes = pl.ds(r * piece, piece)
        w_h[r] = (wo[even(core * w_rows, w_rows), lanes].astype(F32) + w_t[:, lanes].astype(F32)).astype(BF16)
    above, below, across = 1, 3, 2
    pieces = ((q_h, q_up1, q_down1, q_up2, q_down2, q_s, q_n, q_z), (w_h, w_up1, w_down1, w_up2, w_down2, w_s, w_n, w_z))
    ring = []
    for held, up1, down1, up2, down2, _, _, _ in pieces:
        half = held.shape[1] // 2
        low, high = pl.ds(0, half), pl.ds(half, half)
        ring.append((mail.post(held.at[across, low, :], up1, right), mail.post(held.at[across, high, :], down1, left)))
    straight = []
    for held, up1, down1, up2, down2, _, _, _ in pieces:
        half = held.shape[1] // 2
        low, high = pl.ds(0, half), pl.ds(half, half)
        straight.append(
            (mail.post(held.at[above, high, :], up2.at[1], right), mail.post(held.at[below, low, :], down2.at[0], left))
        )

    for copy in small_copies:
        copy.wait_recv()
    for index in small_kept:
        kept[index].wait()
        kept[index] = None
    small_a[...] = jnp.zeros_like(small_a)
    small_a[0:8, :] = bias_in[0] + bias_in[1] + bias_in[2] + bias_in[3]
    small_a[8:16, 0:piece] = (
        gains_in[0] + gains_in[1] + gains_in[2] + gains_in[3] + gains_in[4] + gains_in[5] + gains_in[6] + gains_in[7]
    )
    small_first = mail.post(small_a, small_t, twin)

    half_dn = dn.shape[0]
    hops = []

    def ring_z(i):
        near_copies[i].wait_recv()
        if i < 3:
            gu_s[i] = (gu[pl.ds(i * thirds, thirds), :].astype(F32) + gu_n[i].astype(F32)).astype(BF16)
            held, size = gu_s.at[i], thirds // 2

            def room(slot, which=None):
                start, height = (i * thirds, thirds) if which is None else (i * thirds + which * size, size)
                return gu_out.at[slot, core, pl.ds(start, height), :]

        else:
            dn_s[...] = (dn[...].astype(F32) + dn_n[...].astype(F32)).astype(BF16)
            held, size = dn_s, half_dn // 2

            def room(slot, which=None):
                start, height = (0, half_dn) if which is None else (which * size, size)
                return dn_out.at[slot, core, pl.ds(start, height), :]

        posts = {}
        for turn in range(2):
            for name, device, which in (("u", up, turn), ("d", down, 1 - turn)):
                posts[name, which] = mail.post(held.at[pl.ds(which * size, size), :], room(z, which), device)
        keep(held, room(z))
        arrivals.append(mail.post(held, room(z), twin))
        hops.append((room, posts))

    def ring_z_on(i):
        room, posts = hops[i]
        posts["u", 0].wait_recv()
        block = room((z + 3) % 4, 0)
        one_more = mail.post(block, block, up)
        arrivals.append(mail.post(block, block, twin))
        posts["d", 1].wait_recv()
        block = room((z + 1) % 4, 1)
        two_more = mail.post(block, block, down)
        arrivals.append(mail.post(block, block, twin))
        posts["u", 1].wait_recv()
        block = room((z + 3) % 4, 1)
        arrivals.append(mail.post(block, block, twin))
        posts["d", 0].wait_recv()
        block = room((z + 1) % 4, 0)
        arrivals.append(mail.post(block, block, twin))
        hops[i] = (room, one_more, two_more)

    def ring_z_end(i):
        room, one_more, two_more = hops[i]
        for which, copy in ((0, one_more), (1, two_more)):
            copy.wait_recv()
            block = room((z + 2) % 4, which)
            arrivals.append(mail.post(block, block, twin))

    ring_z(0)
    lasts = []
    for (held, up1, down1, up2, down2, _, _, _), (from_left, from_right) in zip(pieces, ring):
        half = held.shape[1] // 2
        from_left.wait_recv()
        up1[...] = (held[above, 0:half, :].astype(F32) + up1[...].astype(F32)).astype(BF16)
        one_more = mail.post(up1, up2.at[0], right)
        from_right.wait_recv()
        down1[...] = (held[below, half : 2 * half, :].astype(F32) + down1[...].astype(F32)).astype(BF16)
        lasts.append((one_more, mail.post(down1, down2.at[1], left)))
    ring_z(1)
    small_first.wait_recv()
    small_b[...] = small_a[...] + small_t[...]
    small_second = mail.post(small_b, small_n, near)
    ring_z(2)
    ring_z(3)
    near_second = []
    for (held, up1, down1, up2, down2, total, theirs, _), pair_first, pair_last in zip(pieces, straight, lasts):
        half = held.shape[1] // 2
        for copy in pair_first + pair_last:
            copy.wait_recv()
        for i in range(2):
            part = pl.ds(i * half, half)
            total[part, :] = (
                held[0, part, :].astype(F32) + up2[i].astype(F32) + down2[i].astype(F32)
            ).astype(BF16)
        near_second.append(mail.post(total, theirs, near))
    ring_z_on(0)
    small_second.wait_recv()
    small_t[...] = small_b[...] + small_n[...]
    for device in (up, down, far_z):
        arrivals.append(mail.post(small_t, small_out.at[z], device))
    keep(small_t, small_out.at[z])
    z_copies = []
    for (held, _, _, _, _, total, theirs, quarter), copy in zip(pieces, near_second):
        copy.wait_recv()
        held[0] = (total[...].astype(F32) + theirs[...].astype(F32)).astype(BF16)
        size = quarter.shape[1]
        for step, device in ((1, up), (3, down), (2, far_z)):
            source = held.at[0, even(((z + step) % 4) * size, size), :]
            z_copies.append(mail.post(source, quarter.at[step - 1], device))
    ring_z_on(1)
    ring_z_on(2)
    ring_z_end(0)
    for copy in z_copies:
        copy.wait_recv()
    q_last = []
    for (held, _, _, _, _, _, theirs, quarter), out in zip(pieces, (qkv_out, wo_out)):
        size = quarter.shape[1]
        mine = even(z * size, size)
        height = held.shape[1]
        theirs[0:size, :] = (
            held[0, mine, :].astype(F32)
            + quarter[0].astype(F32)
            + quarter[1].astype(F32)
            + quarter[2].astype(F32)
        ).astype(BF16)
        room = out.at[even(core * height + z * size, size), :]
        for device in (up, down, far_z):
            q_last.append(mail.post(theirs.at[0:size, :], room, device))
        arrivals.append(mail.post(theirs.at[0:size, :], room, twin))
        keep(theirs.at[0:size, :], room)
    ring_z_on(3)
    ring_z_end(1)
    ring_z_end(2)
    for copy in q_last:
        copy.wait_recv()
    for total, quarter, out in ((q_s, q_z, qkv_out), (w_s, w_z, wo_out)):
        size, height = quarter.shape[1], total.shape[0]
        for step in (1, 2, 3):
            room = out.at[even(core * height + ((z + step) % 4) * size, size), :]
            arrivals.append(mail.post(room, room, twin))
    ring_z_end(3)
    for copy in arrivals:
        copy.wait_recv()
    for copy in kept:
        if copy is not None:
            copy.wait()
    mail.finish()


def undo_rotation(vector, cosine, sine):
    turned = vector * sine
    middle = vector.shape[-1] // 2
    return vector * cosine + jnp.concatenate([turned[..., middle:], turned[..., :middle]], -1)


def dot_plain(left, right):
    return jnp.dot(left, right, preferred_element_type=F32)


def dot_rows(left, right):
    return lax.dot_general(left, right, (((1,), (1,)), ((), ())), preferred_element_type=F32)


def dot_cols(left, right):
    return lax.dot_general(left, right, (((0,), (0,)), ((), ())), preferred_element_type=F32)


def norm_inverse(stream):
    return lax.rsqrt(jnp.mean(stream * stream, -1, keepdims=True) + EPS)


def norm_back(stream, inverse, gain, incoming):
    scaled = incoming * gain
    inner = jnp.mean(scaled * stream, -1, keepdims=True)
    back = inverse * scaled - stream * (inverse**3 * inner)
    return back, jnp.sum(incoming * stream * inverse, 0)


def attend_back(query, key_value, logs, mask, grad, factor):
    key, value = key_value[:, :HEAD_SIZE], key_value[:, HEAD_SIZE:]
    raw = jnp.einsum("qhd,kd->hqk", query, key, preferred_element_type=F32)
    probs = jnp.exp(raw * factor + mask[None] - logs)
    grad_probs = jnp.einsum("qhd,kd->hqk", grad, value, preferred_element_type=F32)
    inner = jnp.sum(grad_probs * probs, -1, keepdims=True)
    grad_scores = (probs * (grad_probs - inner)).astype(BF16)
    grad_query = jnp.einsum("hqk,kd->qhd", grad_scores, key, preferred_element_type=F32) * factor
    grad_key = jnp.einsum("hqk,qhd->kd", grad_scores, query, preferred_element_type=F32) * factor
    grad_value = jnp.einsum("hqk,qhd->kd", probs.astype(BF16), grad, preferred_element_type=F32)
    return grad_query, jnp.concatenate([grad_key, grad_value], 1).astype(BF16)


def on_device(
    tokens,
    cotangent,
    lengths,
    gain_attn,
    w_query,
    key_projection,
    value_projection,
    bias_query,
    key_bias_vector,
    value_bias_vector,
    w_out,
    gain_ffn,
    w_gate,
    w_up,
    w_down,
):
    dp, row, col = here()
    z = dp // Z_STEP
    half_rows, piece = tokens.shape
    width = 4 * piece
    rows = half_rows // 4
    q_width = w_query.shape[1]
    kv_width = key_projection.shape[1]
    heads = q_width // HEAD_SIZE
    hidden = w_gate.shape[1]
    share = -(-hidden // (4 * LANES)) * LANES
    factor = HEAD_SIZE ** (-0.5)
    spare = 4 * share - hidden
    take = z * share

    in_width = q_width + 2 * kv_width
    thin = piece // 2
    lens = jnp.pad(lengths, ((0, 7), (0, LANES - lengths.shape[1])))
    gains = jnp.pad(jnp.stack([gain_attn, gain_ffn]), ((0, 6), (0, 0)))
    bias = jnp.concatenate([bias_query, key_bias_vector, value_bias_vector])
    bias = jnp.broadcast_to(bias[None], (8, in_width))
    (
        tok_rows,
        cot_full,
        gains4,
        normed,
        query,
        kv_a,
        kv_b,
        logs,
        attended,
        tables,
        middle,
        mask_a,
        mask_b,
        ffn_in,
        w_in_full,
        w_out_full,
        w_gu_full,
        w_down_full,
    ) = talk(
        front_kernel,
        0,
        FRONT_COPIES,
        FRONT_LOCAL,
        [
            ((2 * rows, width), BF16),
            ((4, 2 * rows, width), BF16),
            ((4, 8, piece), F32),
            ((2 * rows, width), BF16),
            ((2 * rows, q_width), BF16),
            ((half_rows, 2 * kv_width), BF16),
            ((2 * half_rows, 2 * kv_width), BF16),
            ((2 * heads, rows, LANES), F32),
            ((2 * rows, q_width), BF16),
            ((2, 2 * rows, HEAD_SIZE), F32),
            ((2 * rows, width), F32),
            ((rows, half_rows), F32),
            ((rows, 2 * half_rows), F32),
            ((4, 2 * rows, width), BF16),
            ((4, piece, in_width), BF16),
            ((q_width, width), BF16),
            ((4, 2, thin, 2 * share), BF16),
            ((share, width), BF16),
        ],
        [ANY] * 4 + [VMEM] + [ANY] * 7,
        [ANY] * 3 + [VMEM] * 2 + [ANY] * 2 + [VMEM] * 6 + [ANY] * 5,
        [
            pltpu.VMEM((2 * rows, width), BF16),
            pltpu.VMEM((2, 8, LANES), jnp.int32),
            pltpu.VMEM((4, 8, piece), F32),
            pltpu.VMEM((4, piece, in_width), BF16),
            pltpu.VMEM((q_width, width), BF16),
            pltpu.VMEM((2, thin, 2 * share), BF16),
            pltpu.VMEM((share, piece), BF16),
            pltpu.VMEM((thin, LANES), BF16),
            pltpu.VMEM((LANES, piece), BF16),
            pltpu.VMEM((2 * rows, 2 * kv_width), BF16),
            pltpu.VMEM((half_rows, 2 * kv_width), BF16),
            pltpu.VMEM((2 * half_rows, 2 * kv_width), BF16),
            pltpu.VMEM((2 * rows, width), BF16),
            pltpu.VMEM((2 * rows, width), BF16),
            pltpu.VMEM((2 * rows, width), BF16),
        ],
        limit=56,
    )(
        tokens,
        cotangent,
        lens,
        gains,
        bias,
        w_query,
        key_projection,
        value_projection,
        w_out,
        w_gate,
        w_up,
        w_down,
    )

    def shift_z(array, step):
        count = 4 * Z_STEP
        return lax.ppermute(array, "dp", [(d, (d + Z_STEP * step) % count) for d in range(count)])

    gain_attn_full, gain_ffn_full = gains4[:, 0].reshape(width), gains4[:, 1].reshape(width)
    cosine, sine = tables[0], tables[1]
    stream = tok_rows.astype(F32)
    inverse_attn = norm_inverse(stream)
    inverse_ffn = norm_inverse(middle)
    cot_rows = cot_full[0]
    cot_full = cot_full.reshape(8 * rows, width)
    ffn_in = ffn_in.reshape(8 * rows, width)
    w_in_full = w_in_full.reshape(width, in_width)
    w_both_full = w_gu_full.reshape(width, 2 * share)
    both = dot_plain(ffn_in, w_both_full)
    gate, up_value = both[:, :share], both[:, share:]
    grad_act = dot_rows(cot_full, w_down_full)
    spread = 1.0 / (1.0 + jnp.exp(-gate))
    smooth = gate * spread
    activated = (smooth * up_value).astype(BF16)
    grad_gate = grad_act * up_value * (spread * (1.0 + gate * (1.0 - spread)))
    grad_both = jnp.concatenate([grad_gate, grad_act * smooth], 1).astype(BF16)
    grad_in_parts = dot_rows(grad_both, w_both_full).astype(BF16).reshape(4, 2 * rows, width)
    chunk = (2, rows // 2, width)
    chunks = (4, rows // 2, width)
    grad_normed_ffn, both_half, down_half = talk(
        middle_kernel,
        4,
        24,
        13,
        [((2 * rows, width), F32), ((4, piece, share), BF16), ((4, share // 2, piece), BF16)],
        [ANY] * 5,
        [VMEM, ANY, ANY],
        [
            pltpu.VMEM(shape, BF16)
            for shape in (
                (4, 2 * rows, width),
                (8 * rows, width),
                (8 * rows, 2 * share),
                (8 * rows, share),
                (8 * rows, width),
                (width, 8 * rows),
                (4, 2, piece, share),
                (4, share, piece),
                (4, piece, share),
                (4, share // 2, piece),
                chunk,
                chunk,
                chunks,
                chunks,
                chunks,
                chunk,
                chunk,
                chunks,
            )
        ],
        limit=56,
    )(grad_in_parts, ffn_in, grad_both, activated, cot_full)
    down_parts = dot_plain(activated, w_down_full).astype(BF16).reshape(4, 2 * rows, width)
    down_part = down_parts[0].astype(F32)
    for step in (1, 2, 3):
        down_part = down_part + shift_z(down_parts[step], 4 - step).astype(F32)
    down_part = down_part.astype(BF16)
    both_sum = lax.psum_scatter(both_half, "row", scatter_dimension=0, tiled=False)
    down_sum = lax.psum_scatter(down_half, "row", scatter_dimension=0, tiled=False)

    back_mid, gain_ffn_part = norm_back(middle, inverse_ffn, gain_ffn_full, grad_normed_ffn)
    grad_middle = cot_rows.astype(F32) + back_mid
    grad_mid_low = grad_middle.astype(BF16)
    grad_att = dot_rows(grad_mid_low, w_out_full).astype(BF16).reshape(2 * rows, heads, HEAD_SIZE)
    out_w = dot_cols(attended, grad_mid_low).astype(BF16)
    queries = query.reshape(2, rows, heads, HEAD_SIZE)
    gq_a, gkv_a = attend_back(queries[0], kv_a, logs[:heads, :, :1], mask_a, grad_att[:rows], factor)
    gq_b, gkv_b = attend_back(queries[1], kv_b, logs[heads:, :, :1], mask_b, grad_att[rows:], factor)
    (grad_kv,) = talk(
        keys_back_kernel,
        5,
        7,
        0,
        [((2, rows, 2 * kv_width), F32)],
        [VMEM] * 2,
        [VMEM],
        [pltpu.VMEM((3, 2, rows, 2 * kv_width), BF16), pltpu.VMEM((4, rows, 2 * kv_width), BF16)],
    )(gkv_b[:half_rows], jnp.stack([gkv_a, gkv_b[half_rows:]]))
    grad_kv = grad_kv.reshape(2 * rows, 2 * kv_width)
    grad_query = undo_rotation(jnp.concatenate([gq_a, gq_b], 0), cosine[:, None], sine[:, None]).reshape(2 * rows, q_width)
    grad_key = undo_rotation(grad_kv[:, :kv_width], cosine, sine)
    grad_pre = jnp.concatenate([grad_query, grad_key, grad_kv[:, kv_width:]], 1).astype(BF16)
    grad_normed_part = dot_rows(grad_pre, w_in_full).astype(BF16).reshape(2, rows, width)
    grad_normed_in, down_in = talk(
        halves_kernel,
        6,
        2,
        0,
        [((rows, width), BF16)] * 2,
        [ANY] * 2,
        [ANY] * 2,
    )(grad_normed_part, down_part.reshape(2, rows, width))

    def own(array):
        return lax.dynamic_index_in_dim(array.reshape(2, rows, -1), col, 0, keepdims=False)

    grad_normed = own(grad_normed_part).astype(F32) + grad_normed_in.astype(F32)
    result_rows = own(middle) + (own(down_part).astype(F32) + down_in.astype(F32))
    back_in, gain_attn_part = norm_back(own(stream), own(inverse_attn), gain_attn_full, grad_normed)
    grad_rows = own(grad_middle) + back_in
    grad_bias = jnp.sum(grad_pre.astype(F32), 0)
    gains = jnp.stack([gain_attn_part, 0.5 * gain_ffn_part]).reshape(2, 4, piece).transpose(1, 0, 2)
    in_w = dot_cols(normed, grad_pre).astype(BF16).reshape(4, piece, in_width)
    thirds = piece // 3
    q_half, w_half = (thin, in_width), (q_width // 2, piece)
    gate_up, down_all, in_total, out_total, result, grad_tokens, small_all = talk(
        tail_kernel,
        8,
        TAIL_COPIES,
        TAIL_LOCAL,
        [
            ((4, 2, piece, share), BF16),
            ((4, 2, share // 2, piece), BF16),
            ((piece, in_width), BF16),
            ((q_width, piece), BF16),
            ((half_rows, piece), BF16),
            ((half_rows, piece), BF16),
            ((4, 16, in_width), F32),
        ],
        [VMEM] * 4 + [ANY] * 4,
        [ANY] * 7,
        [
            pltpu.VMEM(shape, BF16)
            for shape in (
                (3, thirds, share),
                (share // 2, piece),
                (3, thirds, share),
                (share // 2, piece),
                (4, *q_half),
                (q_width // 2, width),
                (4, *q_half),
                (4, *w_half),
                (thin // 2, in_width),
                (thin // 2, in_width),
                (2, thin // 2, in_width),
                (2, thin // 2, in_width),
                (q_width // 4, piece),
                (q_width // 4, piece),
                (2, q_width // 4, piece),
                (2, q_width // 4, piece),
                q_half,
                w_half,
                q_half,
                w_half,
                (3, thin // 4, in_width),
                (3, q_width // 8, piece),
            )
        ]
        + [pltpu.VMEM((4, 8, in_width), F32), pltpu.VMEM((8, 8, piece), F32)]
        + [pltpu.VMEM((16, in_width), F32)] * 4,
        limit=56,
    )(
        both_sum,
        down_sum,
        in_w,
        out_w,
        result_rows.astype(BF16),
        grad_rows.astype(BF16),
        jnp.pad(grad_bias[None], ((0, 7), (0, 0))),
        jnp.pad(gains, ((0, 0), (0, 6), (0, 0))),
    )
    small_total = small_all[0] + small_all[1] + small_all[2] + small_all[3]
    bias_total = small_total[0]
    in_total = in_total.astype(F32)
    gate_total = jnp.concatenate([gate_up[i, 0] for i in range(4)], 1)[:, :hidden].astype(F32)
    up_total = jnp.concatenate([gate_up[i, 1] for i in range(4)], 1)[:, :hidden].astype(F32)
    down_total = down_all.reshape(4 * share, piece)[:hidden].astype(F32)
    upper = q_width + kv_width
    return (
        result.astype(F32),
        grad_tokens.astype(F32),
        small_total[8, :piece],
        in_total[:, :q_width],
        in_total[:, q_width:upper],
        in_total[:, upper:],
        bias_total[:q_width],
        bias_total[q_width:upper],
        bias_total[upper:],
        out_total.astype(F32),
        small_total[9, :piece],
        gate_total,
        up_total,
        down_total,
    )


def solution(mesh):
    placed = (
        P(("dp", "col"), "row"),
        P(("dp", "col"), "row"),
        P("dp", None),
        P("row"),
        P("row", "col"),
        P("row", "col"),
        P("row", "col"),
        P("col"),
        P("col"),
        P("col"),
        P("col", "row"),
        P("row"),
        P("row", "col"),
        P("row", "col"),
        P("col", "row"),
    )
    return jax.shard_map(
        on_device,
        mesh=mesh,
        in_specs=placed,
        out_specs=(
            P(("dp", "col"), "row"),
            P(("dp", "col"), "row"),
            P("row"),
            P("row", "col"),
            P("row", "col"),
            P("row", "col"),
            P("col"),
            P("col"),
            P("col"),
            P("col", "row"),
            P("row"),
            P("row", "col"),
            P("row", "col"),
            P("col", "row"),
        ),
        check_vma=False,
    )
```

```python
import math

import jax
import jax.numpy as jnp
from jax import lax
from jax.experimental import pallas as pl
from jax.experimental.pallas import tpu as pltpu
from jax.sharding import PartitionSpec as P

HEAD_SIZE = 128
EPS = 1e-06
THETA = 1000000.0
LANES = 128
MESH = pl.DeviceIdType.MESH
BF16 = jnp.bfloat16
F32 = jnp.float32
ANY = pl.BlockSpec(memory_space=pl.ANY)
VMEM = pl.BlockSpec(memory_space=pltpu.VMEM)

Z_STEP = 4
FRONT_COPIES = 74
FRONT_LOCAL = 27
TAIL_COPIES = 113
TAIL_LOCAL = 11


def here():
    return lax.axis_index("dp"), lax.axis_index("row"), lax.axis_index("col")


def flip_near(dp):
    return dp + 2 - 4 * ((dp // 2) % 2)


def pair_of(place, row=None):
    dp, own, col = place
    return flip_near(dp), own if row is None else row, 1 - col


def near_of(place, row=None):
    dp, own, col = place
    return flip_near(dp), own if row is None else row, col


def twin_of(place):
    dp, row, col = place
    return dp + 1 - 2 * (dp % 2), row, col


def along_z(place, step):
    dp, row, col = place
    return (dp + Z_STEP * step) % (4 * Z_STEP), row, col


def along_y(place, step):
    dp, row, col = place
    return dp, (row + step) % 4, col


def meet(peers):
    barrier = pltpu.get_barrier_semaphore()
    for peer in peers:
        pl.semaphore_signal(barrier, inc=1, device_id=peer, device_id_type=MESH)
    pl.semaphore_wait(barrier, len(peers))


class Mail:
    def __init__(self, send, recv):
        self.send, self.recv, self.count, self.sent = send, recv, 0, []

    def post(self, source, target, device):
        index = self.count
        self.count += 1
        copy = pltpu.make_async_remote_copy(
            src_ref=source,
            dst_ref=target,
            send_sem=self.send.at[index],
            recv_sem=self.recv.at[index],
            device_id=device,
            device_id_type=MESH,
        )
        copy.start()
        self.sent.append(copy)
        return copy

    def finish(self):
        assert self.count == self.send.shape[0], (self.count, self.send.shape)
        for copy in self.sent:
            copy.wait_send()


def talk(body, ident, copies, local, outs, in_specs, out_specs, scratch=(), limit=32):
    return pl.pallas_call(
        body,
        out_shape=[jax.ShapeDtypeStruct(*out) for out in outs],
        in_specs=in_specs,
        out_specs=out_specs,
        scratch_shapes=[
            *scratch,
            pltpu.SemaphoreType.DMA((copies,)),
            pltpu.SemaphoreType.DMA((copies,)),
            pltpu.SemaphoreType.DMA((max(local, 1),)),
        ],
        compiler_params=pltpu.CompilerParams(
            collective_id=ident, has_side_effects=True, vmem_limit_bytes=limit << 20
        ),
    )


def front_kernel(
    tok,
    cot,
    lens,
    gains,
    bias,
    wq,
    wk,
    wv,
    wo,
    wg,
    wu,
    wd,
    tok_out,
    cot_full,
    gains_out,
    normed,
    query,
    kva_out,
    kvb_out,
    logs,
    attended,
    tables,
    middle,
    bias_a,
    bias_b,
    normed_ffn,
    w_in_out,
    w_out_out,
    wgu_full,
    wd_full,
    tok_v,
    lens_v,
    gains_v,
    w_in,
    w_out,
    gu_own,
    wd_own,
    blank_gu,
    blank_wd,
    kv,
    kva,
    kvb,
    branch,
    branch_in,
    send,
    recv,
    local,
):
    place = here()
    dp, row, col = place
    z, core = dp // Z_STEP, dp % 2
    twin, pair, up, down = twin_of(place), pair_of(place), along_z(place, 1), along_z(place, 3)
    right, left = along_y(place, 1), along_y(place, 3)
    meet(
        [along_y(place, s) for s in (1, 2, 3)]
        + [near_of(place, (row + s) % 4) for s in range(4)]
        + [pair, twin, up, down]
    )
    mail = Mail(send, recv)
    kept = []

    def keep(source, target):
        kept.append(pltpu.make_async_copy(source, target, local.at[len(kept)]))
        kept[-1].start()
        return len(kept) - 1

    def kept_wait(index):
        kept[index].wait()
        kept[index] = None

    def even(start, size):
        return pl.ds(pl.multiple_of(start, 16), size)

    rows, piece = tok.shape[0] // 4, tok.shape[1]
    width = 4 * piece
    own_rows = even(col * rows, rows)
    spot = even(row * rows, rows)

    def spread(source, target):
        got = []
        for step in range(4):
            part = source.at[even(((row + step) % 4) * rows, rows), :]
            lanes = pl.ds(((4 - step) % 4) * piece, piece)
            if step:
                got.append(mail.post(part, target.at[own_rows, lanes], along_y(place, step)))
            else:
                mine = keep(part, target.at[own_rows, lanes])
        return got, mine

    tokens = spread(tok, tok_v)
    lens_got = mail.post(lens, lens_v.at[col], pair)
    lens_kept = keep(lens, lens_v.at[col])
    gains_kept = keep(gains, gains_v.at[0])
    gains_got = [mail.post(gains, gains_v.at[4 - s], along_y(place, s)) for s in (1, 2, 3)]

    q_width, kv_width = wq.shape[1], wk.shape[1]
    stages = [
        keep(wq, w_in.at[0, :, pl.ds(0, q_width)]),
        keep(wk, w_in.at[0, :, pl.ds(q_width, kv_width)]),
        keep(wv, w_in.at[0, :, pl.ds(q_width + kv_width, kv_width)]),
        keep(wo, w_out.at[:, pl.ds(0, piece)]),
    ]
    share = wd_own.shape[0]
    thin = piece // 2
    sure = share - LANES
    take = pl.multiple_of(z * share, LANES)
    big = []
    for k in range(2):
        for i, source in enumerate((wg, wu)):
            from_rows = pl.ds(k * thin, thin)
            big.append(keep(source.at[from_rows, pl.ds(take, sure)], gu_own.at[k, :, pl.ds(i * share, sure)]))
    big.append(keep(wd.at[pl.ds(take, sure), :], wd_own.at[pl.ds(0, sure), :]))
    blank_gu[...] = jnp.zeros_like(blank_gu)
    blank_wd[...] = jnp.zeros_like(blank_wd)
    first_edge = len(kept)
    edges = []
    for k in range(2):
        for i, source in enumerate((wg, wu)):
            target = gu_own.at[k, :, pl.ds(i * share + sure, LANES)]
            edges.append((source, pl.ds(k * thin, thin), None, target, blank_gu))
    edges.append((wd, None, slice(None), wd_own.at[pl.ds(sure, LANES), :], blank_wd))

    def edge(index, last):
        source, from_rows, _, target, blank = edges[index]
        if last:
            origin = blank
        elif from_rows is None:
            origin = source.at[pl.ds(pl.multiple_of(take + sure, LANES), LANES), :]
        else:
            origin = source.at[from_rows, pl.ds(pl.multiple_of(take + sure, LANES), LANES)]
        return pltpu.make_async_copy(origin, target, local.at[first_edge + index])

    @pl.when(z < 3)
    def _():
        for index in range(len(edges)):
            edge(index, False).start()

    @pl.when(z == 3)
    def _():
        for index in range(len(edges)):
            edge(index, True).start()

    for index in range(len(edges)):
        kept.append(edge(index, True))
        big.append(first_edge + index)

    q_rows, o_rows = thin // 4, w_out.shape[0] // 8

    def in_part(j, owner_z):
        return w_in.at[j, even(core * thin + owner_z * q_rows, q_rows), :]

    def in_parts(owner_z):
        return w_in.at[pl.ds(1, 3), even(core * thin + owner_z * q_rows, q_rows), :]

    def in_side(owner_z, side):
        lanes = pl.ds(side * (w_in.shape[2] // 2), w_in.shape[2] // 2)
        return w_in.at[pl.ds(1, 3), even(core * thin + owner_z * q_rows, q_rows), lanes]

    def out_part(j, owner_z):
        return w_out.at[even(core * 4 * o_rows + owner_z * o_rows, o_rows), pl.ds(j * piece, piece)]

    def out_parts(owner_z):
        return w_out.at[even(core * 4 * o_rows + owner_z * o_rows, o_rows), pl.ds(piece, 3 * piece)]

    def out_side(owner_z, side):
        start = core * 4 * o_rows + owner_z * o_rows + side * (o_rows // 2)
        return w_out.at[even(start, o_rows // 2), pl.ds(piece, 3 * piece)]

    for index in stages:
        kept_wait(index)
    in_got = [mail.post(in_part(0, z), in_part(4 - step, z), along_y(place, step)) for step in (1, 3, 2)]
    out_got = [mail.post(out_part(0, z), out_part(4 - step, z), along_y(place, step)) for step in (1, 3, 2)]
    cotangents = spread(cot, cot_full.at[0])

    def to_pair(spreading, target):
        got, mine = spreading
        kept_wait(mine)
        for copy in got:
            copy.wait_recv()
        return mail.post(target.at[own_rows, :], target.at[own_rows, :], pair)

    tokens_pair = to_pair(tokens, tok_v)
    shares = []

    def give(part):
        shares.append(mail.post(part, part, twin))

    def z_first(side):
        copies = {}
        for turn in range(2):
            copies["u", turn] = mail.post(side(z, turn), side(z, turn), up)
            copies["d", 1 - turn] = mail.post(side(z, 1 - turn), side(z, 1 - turn), down)
        return copies

    below, above, across = (z + 3) % 4, (z + 1) % 4, (z + 2) % 4

    def z_second(side, whole, copies):
        copies["u", 0].wait_recv()
        far_up = mail.post(side(below, 0), side(below, 0), up)
        copies["d", 1].wait_recv()
        far_down = mail.post(side(above, 1), side(above, 1), down)
        copies["u", 1].wait_recv()
        give(whole(below))
        copies["d", 0].wait_recv()
        give(whole(above))
        return far_up, far_down

    def z_third(whole, copies):
        for copy in copies:
            copy.wait_recv()
        give(whole(across))

    for copy in in_got:
        copy.wait_recv()
    in_z = z_first(in_side)
    give(in_parts(z))
    for copy in out_got:
        copy.wait_recv()
    give(out_parts(z))

    for index in big:
        kept_wait(index)
    gu_half, wd_half = thin // 2, share // 4

    def gu_part(j, which=None):
        start, size = (0, thin) if which is None else (which * gu_half, gu_half)
        return wgu_full.at[j, core, pl.ds(start, size), :]

    def wd_part(j, which=None):
        start, size = (0, 2 * wd_half) if which is None else (which * wd_half, wd_half)
        return wd_full.at[even(core * 2 * wd_half + start, size), pl.ds(j * piece, piece)]

    def gu_source(which):
        return gu_own.at[core, pl.ds(which * gu_half, gu_half), :]

    def wd_source(which):
        return wd_own.at[even((core * 2 + which) * wd_half, wd_half), :]

    y_ring = {}
    for name, source, part in (("gu", gu_source, gu_part), ("wd", wd_source, wd_part)):
        for turn in range(2):
            y_ring[name, "r", turn] = mail.post(source(turn), part(3, turn), right)
            y_ring[name, "l", 1 - turn] = mail.post(source(1 - turn), part(1, 1 - turn), left)
    keep(gu_own, wgu_full.at[0])
    keep(wd_own, wd_full.at[:, pl.ds(0, piece)])
    twins = []

    def y_forward(name, part):
        y_ring[name, "r", 0].wait_recv()
        y_ring[name, "fr"] = mail.post(part(3, 0), part(2, 0), right)
        y_ring[name, "l", 1].wait_recv()
        y_ring[name, "fl"] = mail.post(part(1, 1), part(2, 1), left)

    def y_share(name, part):
        y_ring[name, "r", 1].wait_recv()
        twins.append(mail.post(part(3), part(3), twin))
        y_ring[name, "l", 0].wait_recv()
        twins.append(mail.post(part(1), part(1), twin))

    def y_end(name, part):
        y_ring[name, "fr"].wait_recv()
        y_ring[name, "fl"].wait_recv()
        twins.append(mail.post(part(2), part(2), twin))

    kept_wait(lens_kept)
    lens_got.wait_recv()
    half_rows = 4 * rows

    def segment_of(which, index):
        end_0 = lens_v[which, 0:1, 0:1]
        end_1 = end_0 + lens_v[which, 0:1, 1:2]
        past_0 = (index >= end_0).astype(jnp.int32)
        past_1 = (index >= end_1).astype(jnp.int32)
        start = jnp.where(past_1 > 0, end_1, jnp.where(past_0 > 0, end_0, 0))
        return past_0 + past_1, start

    lane = lax.broadcasted_iota(jnp.int32, (rows, HEAD_SIZE), 1)
    half_lane = jnp.where(lane >= HEAD_SIZE // 2, lane - HEAD_SIZE // 2, lane).astype(F32)
    inverse = jnp.exp(half_lane * (-2.0 * math.log(THETA) / HEAD_SIZE))
    for which, mask, key_count in ((0, bias_a, half_rows), (1, bias_b, 2 * half_rows)):
        index = lax.broadcasted_iota(jnp.int32, (rows, HEAD_SIZE), 0) + (row * rows + which * half_rows)
        _, start = segment_of(which, index)
        turn = (index - start).astype(F32) * inverse
        tables[0, which * rows : (which + 1) * rows, :] = jnp.cos(turn)
        sine = jnp.sin(turn)
        tables[1, which * rows : (which + 1) * rows, :] = jnp.where(lane >= HEAD_SIZE // 2, sine, -sine)
        at = lax.broadcasted_iota(jnp.int32, (rows, key_count), 0) + (row * rows + which * half_rows)
        keys = lax.broadcasted_iota(jnp.int32, (rows, key_count), 1)
        allowed = jnp.logical_and(segment_of(which, at)[0] == segment_of(which, keys)[0], keys <= at)
        mask[...] = jnp.where(allowed, 0.0, -1e30)

    kept_wait(gains_kept)
    for copy in gains_got:
        copy.wait_recv()
    keep(gains_v, gains_out)

    def normalise(value, which):
        scale = lax.rsqrt(jnp.sum(value * value, -1, keepdims=True) * (1.0 / width) + EPS)
        return [
            (value[:, j * piece : (j + 1) * piece] * scale * gains_v[j, which : which + 1, :]).astype(BF16)
            for j in range(4)
        ]

    def norm_rows(which):
        part = pl.ds(pl.multiple_of(which * rows, rows), rows)
        for j, block in enumerate(normalise(tok_v[part, :].astype(F32), 0)):
            normed[part, pl.ds(j * piece, piece)] = block

    norm_rows(col)
    in_far = z_second(in_side, in_parts, in_z)
    out_z = z_first(out_side)
    tokens_pair.wait_recv()
    keep(tok_v, tok_out)
    norm_rows(1 - col)
    cot_pair = to_pair(cotangents, cot_full.at[0])
    z_third(in_parts, in_far)
    for copy in shares:
        copy.wait_recv()
    shares.clear()
    keep(w_in, w_in_out)

    in_width = w_in.shape[2]

    def project(lanes):
        value = jnp.dot(normed[:, 0:piece], w_in[0, :, lanes], preferred_element_type=F32)
        for j in range(1, 4):
            value = value + jnp.dot(
                normed[:, j * piece : (j + 1) * piece], w_in[j, :, lanes], preferred_element_type=F32
            )
        return value + bias[0:1, lanes]

    def rotate(value):
        return value * tables[0] + pltpu.roll(value, HEAD_SIZE // 2, 1) * tables[1]

    key_value = project(slice(q_width, in_width))
    kv[:, 0:kv_width] = rotate(key_value[:, 0:kv_width]).astype(BF16)
    kv[:, kv_width : 2 * kv_width] = key_value[:, kv_width : 2 * kv_width].astype(BF16)
    a_rows, b_rows = pl.ds(0, rows), pl.ds(rows, rows)
    high_spot = even(half_rows + row * rows, rows)
    a_got, b_got = [], []
    for step in (1, 2, 3):
        a_got.append(mail.post(kv.at[a_rows, :], kva.at[spot, :], along_y(place, step)))
    for step in range(4):
        b_got.append(mail.post(kv.at[a_rows, :], kvb.at[spot, :], near_of(place, (row + step) % 4)))
        if step:
            b_got.append(mail.post(kv.at[b_rows, :], kvb.at[high_spot, :], along_y(place, step)))
    kva[spot, :] = kv[a_rows, :]
    kvb[high_spot, :] = kv[b_rows, :]
    for first in range(0, q_width, 2 * HEAD_SIZE):
        value = project(slice(first, first + 2 * HEAD_SIZE))
        for i in range(2):
            lanes = slice(first + i * HEAD_SIZE, first + (i + 1) * HEAD_SIZE)
            query[:, lanes] = rotate(value[:, i * HEAD_SIZE : (i + 1) * HEAD_SIZE]).astype(BF16)

    out_far = z_second(out_side, out_parts, out_z)
    heads = q_width // HEAD_SIZE
    factor = HEAD_SIZE ** (-0.5)

    def attend(half, keys, mask):
        part = slice(half * rows, (half + 1) * rows)

        @pl.loop(0, heads)
        def _(h):
            lanes = pl.ds(pl.multiple_of(h * HEAD_SIZE, LANES), HEAD_SIZE)
            raw = lax.dot_general(
                query[part, lanes], keys[:, 0:HEAD_SIZE], (((1,), (1,)), ((), ())), preferred_element_type=F32
            )
            scores = raw * factor + mask[...]
            peak = jnp.max(scores, -1, keepdims=True)
            raised = jnp.exp(scores - peak)
            total = jnp.sum(raised, -1, keepdims=True)
            probs = (raised * (1.0 / total)).astype(BF16)
            out = jnp.dot(probs, keys[:, HEAD_SIZE : 2 * HEAD_SIZE], preferred_element_type=F32)
            attended[part, lanes] = out.astype(BF16)
            logs[half * heads + h] = jnp.broadcast_to(peak + jnp.log(total), (rows, LANES))

        for first in range(0, width, piece):
            lanes = slice(first, first + piece)
            branch[part, lanes] = jnp.dot(
                attended[part, :], w_out[:, lanes], preferred_element_type=F32
            ).astype(BF16)
        return mail.post(branch.at[part, :], branch_in.at[part, :], pair)

    def finish_half(half, copy):
        part = slice(half * rows, (half + 1) * rows)
        copy.wait_recv()
        value = tok_v[part, :].astype(F32) + (branch[part, :].astype(F32) + branch_in[part, :].astype(F32))
        middle[part, :] = value
        for j, block in enumerate(normalise(value, 1)):
            normed_ffn[part, j * piece : (j + 1) * piece] = block

    def z_send(source, target, half):
        part = pl.ds(half * rows, rows)
        return (
            mail.post(source.at[part, :], target.at[1, part, :], up),
            mail.post(source.at[part, :], target.at[3, part, :], down),
        )

    def z_forward(target, half, copies):
        part = pl.ds(half * rows, rows)
        if half == 0:
            copies[0].wait_recv()
            return copies[1], mail.post(target.at[1, part, :], target.at[2, part, :], up)
        copies[1].wait_recv()
        return copies[0], mail.post(target.at[3, part, :], target.at[2, part, :], down)

    for copy in a_got:
        copy.wait_recv()
    keep(kva, kva_out)
    z_third(out_parts, out_far)
    for copy in shares:
        copy.wait_recv()
    keep(w_out, w_out_out)
    cot_pair.wait_recv()
    cot_z = [z_send(cot_full.at[0], cot_full, half) for half in range(2)]
    swap_a = attend(0, kva, bias_a)
    y_forward("gu", gu_part)
    for copy in b_got:
        copy.wait_recv()
    keep(kvb, kvb_out)
    swap_b = attend(1, kvb, bias_b)
    cot_last = [z_forward(cot_full, half, cot_z[half]) for half in range(2)]
    y_forward("wd", wd_part)
    finish_half(0, swap_a)
    y_share("gu", gu_part)
    finish_half(1, swap_b)
    y_share("wd", wd_part)
    y_end("gu", gu_part)
    y_end("wd", wd_part)
    for copies in cot_last:
        for copy in copies:
            copy.wait_recv()
    for copy in twins:
        copy.wait_recv()
    for copy in kept:
        if copy is not None:
            copy.wait()
    mail.finish()


def ffn_kernel(
    normed,
    cot,
    wgu,
    wd,
    total,
    gu_half,
    dn_half,
    down_out,
    x,
    cot_v,
    wgu_v,
    wd_v,
    gb,
    act,
    parts,
    turned,
    down_v,
    gu_in,
    dn_in,
    up1,
    down1,
    up2,
    down2,
    other,
    stage_up,
    stage_down,
    stage,
    send,
    recv,
    local,
):
    place = here()
    dp, row, col = place
    core = dp % 2
    up, down, pair, twin = along_z(place, 1), along_z(place, 3), pair_of(place), twin_of(place)
    meet([up, down, pair, twin])
    mail = Mail(send, recv)
    order = ((0, 0), (0, 1), (1, 0), (3, 1), (1, 1), (3, 0), (2, 0), (2, 1))
    spots = {half: i for i, half in enumerate(order)}
    rows = normed.shape[0] // 2
    size = rows // 2

    def block(ref, slot, half):
        return ref.at[pl.ds(spots[slot, half] * rows, rows), :]

    def halves(ref, half):
        return ref.at[pl.ds(half * rows, rows), :]

    kept = []

    def keep(source, target):
        kept.append(pltpu.make_async_copy(source, target, local.at[len(kept)]))
        kept[-1].start()
        return len(kept) - 1

    def kept_wait(index):
        kept[index].wait()
        kept[index] = None

    got = {}
    for turn in range(2):
        got["u", turn] = mail.post(halves(normed, turn), block(x, 1, turn), up)
        got["d", 1 - turn] = mail.post(halves(normed, 1 - turn), block(x, 3, 1 - turn), down)
    share = wd.shape[0]
    early = [keep(normed, x.at[pl.ds(0, 2 * rows), :]), keep(wgu, wgu_v)]
    early.append(keep(cot.at[0], cot_v.at[pl.ds(0, 2 * rows), :]))
    early.append(keep(wd, wd_v))
    later = [keep(cot.at[slot, pl.ds(half * rows, rows), :], block(cot_v, slot, half)) for slot, half in order[2:]]
    width = normed.shape[1]
    piece = width // 4

    def dot_nt(left, right):
        return lax.dot_general(left, right, (((1,), (1,)), ((), ())), preferred_element_type=F32)

    def compute(c):
        part = slice(2 * rows * c, 2 * rows * (c + 1))
        for start, size in ((0, 512), (512, share - 512)):
            lanes, above = slice(start, start + size), slice(share + start, share + start + size)
            gate = jnp.dot(x[part, :], wgu_v[:, lanes], preferred_element_type=F32)
            value = jnp.dot(x[part, :], wgu_v[:, above], preferred_element_type=F32)
            grad = dot_nt(cot_v[part, :], wd_v[lanes, :])
            spread = 1.0 / (1.0 + jnp.exp(-gate))
            smooth = gate * spread
            act[part, lanes] = (smooth * value).astype(BF16)
            gb[part, lanes] = (grad * value * (spread * (1.0 + gate * (1.0 - spread)))).astype(BF16)
            gb[part, above] = (grad * smooth).astype(BF16)
        for m in range(3):
            lanes = slice(512 * m, 512 * (m + 1))
            parts[part, lanes] = dot_nt(gb[part, :], wgu_v[lanes, :]).astype(BF16)

    for index in early:
        kept_wait(index)
    compute(0)
    got["u", 0].wait_recv()
    far_up = mail.post(block(x, 1, 0), block(x, 2, 0), up)
    got["d", 1].wait_recv()
    far_down = mail.post(block(x, 3, 1), block(x, 2, 1), down)
    for index in later:
        kept_wait(index)
    compute(1)
    got["u", 1].wait_recv()
    got["d", 0].wait_recv()
    compute(2)
    far_up.wait_recv()
    far_down.wait_recv()
    second = {
        ("d", 0): mail.post(block(parts, 1, 0), down2.at[0], down),
        ("u", 1): mail.post(block(parts, 3, 1), up2.at[1], up),
    }
    compute(3)
    first = {}
    for i in range(2):
        rows_i = pl.ds(i * size, size)
        first["u", i] = mail.post(block(parts, 2, 0).at[rows_i, :], up1.at[i], up)
        first["d", i] = mail.post(block(parts, 2, 1).at[rows_i, :], down1.at[i], down)

    def turn_over(source, target):
        @pl.loop(0, source.shape[1] // LANES)
        def _(t):
            lanes = pl.ds(pl.multiple_of(t * LANES, LANES), LANES)
            target[lanes, :] = source[:, lanes].T

    def forward(i):
        rows_i = pl.ds(i * size, size)
        first["u", i].wait_recv()
        stage_up[i] = (block(parts, 3, 0).at[rows_i, :][...].astype(F32) + up1[i].astype(F32)).astype(BF16)
        second["u", 0, i] = mail.post(stage_up.at[i], up2.at[0, rows_i, :], up)
        first["d", i].wait_recv()
        stage_down[i] = (block(parts, 1, 1).at[rows_i, :][...].astype(F32) + down1[i].astype(F32)).astype(BF16)
        second["d", 1, i] = mail.post(stage_down.at[i], down2.at[1, rows_i, :], down)

    turn_over(x, turned)
    forward(0)
    for m in range(3):
        lanes = slice(512 * m, 512 * (m + 1))

        @pl.loop(0, 4)
        def _(c):
            part = pl.ds(pl.multiple_of(c * 2 * rows, 2 * rows), 2 * rows)
            down_v[part, lanes] = jnp.dot(act[part, :], wd_v[:, lanes], preferred_element_type=F32).astype(BF16)

    forward(1)
    for slot, half in order:
        keep(block(down_v, slot, half), down_out.at[slot, pl.ds(half * rows, rows), :])
    tile = 256
    tiles = 2 * share // tile

    def gu_tiles(first_tile, last_tile):
        @pl.loop(first_tile, last_tile)
        def _(n):
            lanes = pl.ds(pl.multiple_of(((n + (tiles // 2) * (1 - core)) % tiles) * tile, tile), tile)
            wgu_v[:, lanes] = jnp.dot(turned[...], gb[:, lanes], preferred_element_type=F32).astype(BF16)

    swaps = {}

    def settle(i):
        rows_i = pl.ds(i * size, size)
        if i == 0:
            second["d", 0].wait_recv()
            second["u", 1].wait_recv()
        second["u", 0, i].wait_recv()
        second["d", 1, i].wait_recv()
        for half in range(2):
            value = block(parts, 0, half).at[rows_i, :][...].astype(F32)
            value = value + up2[half, rows_i, :].astype(F32) + down2[half, rows_i, :].astype(F32)
            stage[half, rows_i, :] = value.astype(BF16)
            swaps[half, i] = mail.post(stage.at[half, rows_i, :], other.at[half, rows_i, :], pair)

    there = pl.ds(pl.multiple_of((1 - core) * share, LANES), share)
    mine = pl.ds(pl.multiple_of(core * share, LANES), share)
    gu_tiles(0, tiles // 2 + 1)
    shared = [
        mail.post(wgu_v.at[pl.ds(j * piece, piece), there], gu_in.at[j], twin) for j in range(4)
    ]
    settle(0)
    gu_tiles(tiles // 2 + 1, tiles)
    settle(1)
    turn_over(act, turned)

    @pl.loop(0, width // tile)
    def _(n):
        lanes = pl.ds(pl.multiple_of(n * tile, tile), tile)
        wd_v[:, lanes] = jnp.dot(
            turned[0:share, :], cot_v[:, lanes], preferred_element_type=F32
        ).astype(BF16)

    half_share = share // 2
    rows_there = pl.ds(pl.multiple_of((1 - core) * half_share, 16), half_share)
    rows_mine = pl.ds(pl.multiple_of(core * half_share, 16), half_share)
    shared += [
        mail.post(wd_v.at[rows_there, pl.ds(j * piece, piece)], dn_in.at[j], twin) for j in range(4)
    ]
    for j in range(4):
        shared[j].wait_recv()
        gu_in[j] = (wgu_v[pl.ds(j * piece, piece), mine].astype(F32) + gu_in[j].astype(F32)).astype(BF16)
        keep(gu_in.at[j], gu_half.at[(row + j) % 4])
    for j in range(4):
        shared[4 + j].wait_recv()
        dn_in[j] = (wd_v[rows_mine, pl.ds(j * piece, piece)].astype(F32) + dn_in[j].astype(F32)).astype(BF16)
        keep(dn_in.at[j], dn_half.at[(row + j) % 4])
    for half, i in ((0, 0), (1, 0), (0, 1), (1, 1)):
        rows_i = pl.ds(i * size, size)
        swaps[half, i].wait_recv()
        total[pl.ds(half * rows + i * size, size), :] = stage[half, rows_i, :].astype(F32) + other[
            half, rows_i, :
        ].astype(F32)
    for copy in kept:
        if copy is not None:
            copy.wait()
    mail.finish()


def keys_back_kernel(low, own, total, from_own, from_near, send, recv, local):
    place = here()
    dp, row, col = place
    meet([along_y(place, s) for s in (1, 2, 3)] + [near_of(place, (row + s) % 4) for s in range(4)])
    mail = Mail(send, recv)
    rows = total.shape[1]

    def spot(owner):
        return pl.ds(pl.multiple_of(owner * rows, rows), rows)

    arrivals = []
    for step in range(4):
        other = (row + step) % 4
        if step:
            arrivals.append(mail.post(own.at[:, spot(other), :], from_own.at[step - 1], along_y(place, step)))
        arrivals.append(mail.post(low.at[spot(other), :], from_near.at[step], near_of(place, other)))
    for copy in arrivals:
        copy.wait_recv()
    for half in range(2):
        value = own[half, spot(row), :].astype(F32)
        for step in range(3):
            value = value + from_own[step, half].astype(F32)
        if half == 0:
            for step in range(4):
                value = value + from_near[step].astype(F32)
        total[half] = value
    mail.finish()


def halves_kernel(first, second, first_in, second_in, send, recv, local):
    place = here()
    dp, row, col = place
    pair = pair_of(place)
    meet([pair])
    mail = Mail(send, recv)
    copies = [mail.post(first.at[1 - col], first_in, pair), mail.post(second.at[1 - col], second_in, pair)]
    for copy in copies:
        copy.wait_recv()
    mail.finish()


def tail_kernel(
    gu,
    dn,
    qkv,
    wo,
    one,
    two,
    bias,
    gains,
    gu_out,
    dn_out,
    qkv_out,
    wo_out,
    one_out,
    two_out,
    small_out,
    gu_n,
    dn_n,
    gu_s,
    dn_s,
    q_t,
    w_t,
    q_h,
    w_h,
    q_up1,
    q_down1,
    q_up2,
    q_down2,
    w_up1,
    w_down1,
    w_up2,
    w_down2,
    q_s,
    w_s,
    q_n,
    w_n,
    q_z,
    w_z,
    bias_in,
    gains_in,
    small_a,
    small_b,
    small_t,
    small_n,
    send,
    recv,
    local,
):
    place = here()
    dp, row, col = place
    core = dp % 2
    z = dp // Z_STEP
    twin, near, up, down = twin_of(place), near_of(place), along_z(place, 1), along_z(place, 3)
    far_z = along_z(place, 2)
    right, left = along_y(place, 1), along_y(place, 3)
    meet(
        [along_y(place, s) for s in (1, 2, 3)]
        + [pair_of(place, (row + s) % 4) for s in range(4)]
        + [twin, near, up, down, far_z]
    )
    mail = Mail(send, recv)
    kept, arrivals = [], []

    def keep(source, target):
        kept.append(pltpu.make_async_copy(source, target, local.at[len(kept)]))
        kept[-1].start()
        return len(kept) - 1

    def even(start, size):
        return pl.ds(pl.multiple_of(start, 16), size)

    q_rows, w_rows = q_t.shape[1], w_t.shape[0]
    q_first = mail.post(qkv.at[:, even((1 - core) * q_rows, q_rows), :], q_t, twin)
    w_first = mail.post(wo.at[even((1 - core) * w_rows, w_rows), :], w_t, twin)

    thirds = gu.shape[0] // 3
    near_copies = []
    for i in range(3):
        near_copies.append(mail.post(gu.at[pl.ds(i * thirds, thirds), :], gu_n.at[i], near))
    near_copies.append(mail.post(dn, dn_n, near))

    rows, piece = one.shape[0], one.shape[1] // 4
    spot = pl.ds(pl.multiple_of(row * rows, rows), rows)
    small_copies, small_kept = [], []
    for step in range(4):
        other = (row + step) % 4
        device = along_y(place, step)
        mine = gains_in.at[col * 4 + row]
        if step:
            small_copies.append(mail.post(bias, bias_in.at[row], device))
            small_copies.append(mail.post(gains.at[step], mine, device))
        else:
            small_kept.append(keep(bias, bias_in.at[row]))
            small_kept.append(keep(gains.at[step], mine))
        small_copies.append(mail.post(gains.at[step], mine, pair_of(place, other)))
    for step in range(4):
        lanes = pl.ds(step * piece, piece)
        for source, target in ((one, one_out), (two, two_out)):
            if step:
                arrivals.append(mail.post(source.at[:, lanes], target.at[spot, :], along_y(place, step)))
            else:
                keep(source.at[:, lanes], target.at[spot, :])

    q_first.wait_recv()
    for r in range(4):
        q_h[r] = (qkv[r, even(core * q_rows, q_rows), :].astype(F32) + q_t[r].astype(F32)).astype(BF16)
    w_first.wait_recv()
    for r in range(4):
        lanes = pl.ds(r * piece, piece)
        w_h[r] = (wo[even(core * w_rows, w_rows), lanes].astype(F32) + w_t[:, lanes].astype(F32)).astype(BF16)
    above, below, across = 1, 3, 2
    pieces = ((q_h, q_up1, q_down1, q_up2, q_down2, q_s, q_n, q_z), (w_h, w_up1, w_down1, w_up2, w_down2, w_s, w_n, w_z))
    ring = []
    for held, up1, down1, up2, down2, _, _, _ in pieces:
        half = held.shape[1] // 2
        low, high = pl.ds(0, half), pl.ds(half, half)
        ring.append((mail.post(held.at[across, low, :], up1, right), mail.post(held.at[across, high, :], down1, left)))
    straight = []
    for held, up1, down1, up2, down2, _, _, _ in pieces:
        half = held.shape[1] // 2
        low, high = pl.ds(0, half), pl.ds(half, half)
        straight.append(
            (mail.post(held.at[above, high, :], up2.at[1], right), mail.post(held.at[below, low, :], down2.at[0], left))
        )

    for copy in small_copies:
        copy.wait_recv()
    for index in small_kept:
        kept[index].wait()
        kept[index] = None
    small_a[...] = jnp.zeros_like(small_a)
    small_a[0:8, :] = bias_in[0] + bias_in[1] + bias_in[2] + bias_in[3]
    small_a[8:16, 0:piece] = (
        gains_in[0] + gains_in[1] + gains_in[2] + gains_in[3] + gains_in[4] + gains_in[5] + gains_in[6] + gains_in[7]
    )
    small_first = mail.post(small_a, small_t, twin)

    half_dn = dn.shape[0]
    hops = []

    def ring_z(i):
        near_copies[i].wait_recv()
        if i < 3:
            gu_s[i] = (gu[pl.ds(i * thirds, thirds), :].astype(F32) + gu_n[i].astype(F32)).astype(BF16)
            held, size = gu_s.at[i], thirds // 2

            def room(slot, which=None):
                start, height = (i * thirds, thirds) if which is None else (i * thirds + which * size, size)
                return gu_out.at[slot, core, pl.ds(start, height), :]

        else:
            dn_s[...] = (dn[...].astype(F32) + dn_n[...].astype(F32)).astype(BF16)
            held, size = dn_s, half_dn // 2

            def room(slot, which=None):
                start, height = (0, half_dn) if which is None else (which * size, size)
                return dn_out.at[slot, core, pl.ds(start, height), :]

        posts = {}
        for turn in range(2):
            for name, device, which in (("u", up, turn), ("d", down, 1 - turn)):
                posts[name, which] = mail.post(held.at[pl.ds(which * size, size), :], room(z, which), device)
        keep(held, room(z))
        arrivals.append(mail.post(held, room(z), twin))
        hops.append((room, posts))

    def ring_z_on(i):
        room, posts = hops[i]
        posts["u", 0].wait_recv()
        block = room((z + 3) % 4, 0)
        one_more = mail.post(block, block, up)
        arrivals.append(mail.post(block, block, twin))
        posts["d", 1].wait_recv()
        block = room((z + 1) % 4, 1)
        two_more = mail.post(block, block, down)
        arrivals.append(mail.post(block, block, twin))
        posts["u", 1].wait_recv()
        block = room((z + 3) % 4, 1)
        arrivals.append(mail.post(block, block, twin))
        posts["d", 0].wait_recv()
        block = room((z + 1) % 4, 0)
        arrivals.append(mail.post(block, block, twin))
        hops[i] = (room, one_more, two_more)

    def ring_z_end(i):
        room, one_more, two_more = hops[i]
        for which, copy in ((0, one_more), (1, two_more)):
            copy.wait_recv()
            block = room((z + 2) % 4, which)
            arrivals.append(mail.post(block, block, twin))

    ring_z(0)
    lasts = []
    for (held, up1, down1, up2, down2, _, _, _), (from_left, from_right) in zip(pieces, ring):
        half = held.shape[1] // 2
        from_left.wait_recv()
        up1[...] = (held[above, 0:half, :].astype(F32) + up1[...].astype(F32)).astype(BF16)
        one_more = mail.post(up1, up2.at[0], right)
        from_right.wait_recv()
        down1[...] = (held[below, half : 2 * half, :].astype(F32) + down1[...].astype(F32)).astype(BF16)
        lasts.append((one_more, mail.post(down1, down2.at[1], left)))
    ring_z(1)
    small_first.wait_recv()
    small_b[...] = small_a[...] + small_t[...]
    small_second = mail.post(small_b, small_n, near)
    ring_z(2)
    ring_z(3)
    near_second = []
    for (held, up1, down1, up2, down2, total, theirs, _), pair_first, pair_last in zip(pieces, straight, lasts):
        half = held.shape[1] // 2
        for copy in pair_first + pair_last:
            copy.wait_recv()
        for i in range(2):
            part = pl.ds(i * half, half)
            total[part, :] = (
                held[0, part, :].astype(F32) + up2[i].astype(F32) + down2[i].astype(F32)
            ).astype(BF16)
        near_second.append(mail.post(total, theirs, near))
    ring_z_on(0)
    small_second.wait_recv()
    small_t[...] = small_b[...] + small_n[...]
    for device in (up, down, far_z):
        arrivals.append(mail.post(small_t, small_out.at[z], device))
    keep(small_t, small_out.at[z])
    z_copies = []
    for (held, _, _, _, _, total, theirs, quarter), copy in zip(pieces, near_second):
        copy.wait_recv()
        held[0] = (total[...].astype(F32) + theirs[...].astype(F32)).astype(BF16)
        size = quarter.shape[1]
        for step, device in ((1, up), (3, down), (2, far_z)):
            source = held.at[0, even(((z + step) % 4) * size, size), :]
            z_copies.append(mail.post(source, quarter.at[step - 1], device))
    ring_z_on(1)
    ring_z_on(2)
    ring_z_end(0)
    for copy in z_copies:
        copy.wait_recv()
    q_last = []
    for (held, _, _, _, _, _, theirs, quarter), out in zip(pieces, (qkv_out, wo_out)):
        size = quarter.shape[1]
        mine = even(z * size, size)
        height = held.shape[1]
        theirs[0:size, :] = (
            held[0, mine, :].astype(F32)
            + quarter[0].astype(F32)
            + quarter[1].astype(F32)
            + quarter[2].astype(F32)
        ).astype(BF16)
        room = out.at[even(core * height + z * size, size), :]
        for device in (up, down, far_z):
            q_last.append(mail.post(theirs.at[0:size, :], room, device))
        arrivals.append(mail.post(theirs.at[0:size, :], room, twin))
        keep(theirs.at[0:size, :], room)
    ring_z_on(3)
    ring_z_end(1)
    ring_z_end(2)
    for copy in q_last:
        copy.wait_recv()
    for total, quarter, out in ((q_s, q_z, qkv_out), (w_s, w_z, wo_out)):
        size, height = quarter.shape[1], total.shape[0]
        for step in (1, 2, 3):
            room = out.at[even(core * height + ((z + step) % 4) * size, size), :]
            arrivals.append(mail.post(room, room, twin))
    ring_z_end(3)
    for copy in arrivals:
        copy.wait_recv()
    for copy in kept:
        if copy is not None:
            copy.wait()
    mail.finish()


def undo_rotation(vector, cosine, sine):
    turned = vector * sine
    middle = vector.shape[-1] // 2
    return vector * cosine + jnp.concatenate([turned[..., middle:], turned[..., :middle]], -1)


def dot_plain(left, right):
    return jnp.dot(left, right, preferred_element_type=F32)


def dot_rows(left, right):
    return lax.dot_general(left, right, (((1,), (1,)), ((), ())), preferred_element_type=F32)


def dot_cols(left, right):
    return lax.dot_general(left, right, (((0,), (0,)), ((), ())), preferred_element_type=F32)


def norm_inverse(stream):
    return lax.rsqrt(jnp.mean(stream * stream, -1, keepdims=True) + EPS)


def norm_back(stream, inverse, gain, incoming):
    scaled = incoming * gain
    inner = jnp.mean(scaled * stream, -1, keepdims=True)
    back = inverse * scaled - stream * (inverse**3 * inner)
    return back, jnp.sum(incoming * stream * inverse, 0)


def attend_back(query, key_value, logs, mask, grad, factor):
    key, value = key_value[:, :HEAD_SIZE], key_value[:, HEAD_SIZE:]
    raw = jnp.einsum("qhd,kd->hqk", query, key, preferred_element_type=F32)
    probs = jnp.exp(raw * factor + mask[None] - logs)
    grad_probs = jnp.einsum("qhd,kd->hqk", grad, value, preferred_element_type=F32)
    inner = jnp.sum(grad_probs * probs, -1, keepdims=True)
    grad_scores = (probs * (grad_probs - inner)).astype(BF16)
    grad_query = jnp.einsum("hqk,kd->qhd", grad_scores, key, preferred_element_type=F32) * factor
    grad_key = jnp.einsum("hqk,qhd->kd", grad_scores, query, preferred_element_type=F32) * factor
    grad_value = jnp.einsum("hqk,qhd->kd", probs.astype(BF16), grad, preferred_element_type=F32)
    return grad_query, jnp.concatenate([grad_key, grad_value], 1).astype(BF16)


def on_device(
    tokens,
    cotangent,
    lengths,
    gain_attn,
    w_query,
    key_projection,
    value_projection,
    bias_query,
    key_bias_vector,
    value_bias_vector,
    w_out,
    gain_ffn,
    w_gate,
    w_up,
    w_down,
):
    dp, row, col = here()
    z = dp // Z_STEP
    half_rows, piece = tokens.shape
    width = 4 * piece
    rows = half_rows // 4
    q_width = w_query.shape[1]
    kv_width = key_projection.shape[1]
    heads = q_width // HEAD_SIZE
    hidden = w_gate.shape[1]
    share = -(-hidden // (4 * LANES)) * LANES
    factor = HEAD_SIZE ** (-0.5)
    spare = 4 * share - hidden
    take = z * share

    in_width = q_width + 2 * kv_width
    thin = piece // 2
    lens = jnp.pad(lengths, ((0, 7), (0, LANES - lengths.shape[1])))
    gains = jnp.pad(jnp.stack([gain_attn, gain_ffn]), ((0, 6), (0, 0)))
    bias = jnp.concatenate([bias_query, key_bias_vector, value_bias_vector])
    bias = jnp.broadcast_to(bias[None], (8, in_width))
    (
        tok_rows,
        cot_full,
        gains4,
        normed,
        query,
        kv_a,
        kv_b,
        logs,
        attended,
        tables,
        middle,
        mask_a,
        mask_b,
        normed_ffn,
        w_in_full,
        w_out_full,
        w_gu_full,
        w_down_full,
    ) = talk(
        front_kernel,
        0,
        FRONT_COPIES,
        FRONT_LOCAL,
        [
            ((2 * rows, width), BF16),
            ((4, 2 * rows, width), BF16),
            ((4, 8, piece), F32),
            ((2 * rows, width), BF16),
            ((2 * rows, q_width), BF16),
            ((half_rows, 2 * kv_width), BF16),
            ((2 * half_rows, 2 * kv_width), BF16),
            ((2 * heads, rows, LANES), F32),
            ((2 * rows, q_width), BF16),
            ((2, 2 * rows, HEAD_SIZE), F32),
            ((2 * rows, width), F32),
            ((rows, half_rows), F32),
            ((rows, 2 * half_rows), F32),
            ((2 * rows, width), BF16),
            ((4, piece, in_width), BF16),
            ((q_width, width), BF16),
            ((4, 2, thin, 2 * share), BF16),
            ((share, width), BF16),
        ],
        [ANY] * 4 + [VMEM] + [ANY] * 7,
        [ANY] * 3 + [VMEM] * 2 + [ANY] * 2 + [VMEM] * 7 + [ANY] * 4,
        [
            pltpu.VMEM((2 * rows, width), BF16),
            pltpu.VMEM((2, 8, LANES), jnp.int32),
            pltpu.VMEM((4, 8, piece), F32),
            pltpu.VMEM((4, piece, in_width), BF16),
            pltpu.VMEM((q_width, width), BF16),
            pltpu.VMEM((2, thin, 2 * share), BF16),
            pltpu.VMEM((share, piece), BF16),
            pltpu.VMEM((thin, LANES), BF16),
            pltpu.VMEM((LANES, piece), BF16),
            pltpu.VMEM((2 * rows, 2 * kv_width), BF16),
            pltpu.VMEM((half_rows, 2 * kv_width), BF16),
            pltpu.VMEM((2 * half_rows, 2 * kv_width), BF16),
            pltpu.VMEM((2 * rows, width), BF16),
            pltpu.VMEM((2 * rows, width), BF16),
        ],
        limit=56,
    )(
        tokens,
        cotangent,
        lens,
        gains,
        bias,
        w_query,
        key_projection,
        value_projection,
        w_out,
        w_gate,
        w_up,
        w_down,
    )

    def shift_z(array, step):
        count = 4 * Z_STEP
        return lax.ppermute(array, "dp", [(d, (d + Z_STEP * step) % count) for d in range(count)])

    gain_attn_full, gain_ffn_full = gains4[:, 0].reshape(width), gains4[:, 1].reshape(width)
    cosine, sine = tables[0], tables[1]
    stream = tok_rows.astype(F32)
    inverse_attn = norm_inverse(stream)
    inverse_ffn = norm_inverse(middle)
    cot_rows = cot_full[0]
    w_in_full = w_in_full.reshape(width, in_width)
    w_both_full = w_gu_full.reshape(width, 2 * share)
    half_block = (2, rows, width)
    grad_normed_ffn, both_half, down_half, down_parts = talk(
        ffn_kernel,
        4,
        28,
        26,
        [
            ((2 * rows, width), F32),
            ((4, piece, share), BF16),
            ((4, share // 2, piece), BF16),
            ((4, 2 * rows, width), BF16),
        ],
        [ANY] * 4,
        [VMEM, ANY, ANY, ANY],
        [
            pltpu.VMEM(shape, BF16)
            for shape in (
                (8 * rows, width),
                (8 * rows, width),
                (width, 2 * share),
                (share, width),
                (8 * rows, 2 * share),
                (8 * rows, share),
                (8 * rows, width),
                (width, 8 * rows),
                (8 * rows, width),
                (4, piece, share),
                (4, share // 2, piece),
                (2, rows // 2, width),
                (2, rows // 2, width),
                half_block,
                half_block,
                half_block,
                (2, rows // 2, width),
                (2, rows // 2, width),
                half_block,
            )
        ],
        limit=60,
    )(normed_ffn, cot_full, w_both_full, w_down_full)
    down_part = down_parts[0].astype(F32)
    for step in (1, 2, 3):
        down_part = down_part + shift_z(down_parts[step], 4 - step).astype(F32)
    down_part = down_part.astype(BF16)
    both_sum = lax.psum_scatter(both_half, "row", scatter_dimension=0, tiled=False)
    down_sum = lax.psum_scatter(down_half, "row", scatter_dimension=0, tiled=False)

    back_mid, gain_ffn_part = norm_back(middle, inverse_ffn, gain_ffn_full, grad_normed_ffn)
    grad_middle = cot_rows.astype(F32) + back_mid
    grad_mid_low = grad_middle.astype(BF16)
    grad_att = dot_rows(grad_mid_low, w_out_full).astype(BF16).reshape(2 * rows, heads, HEAD_SIZE)
    out_w = dot_cols(attended, grad_mid_low).astype(BF16)
    queries = query.reshape(2, rows, heads, HEAD_SIZE)
    gq_a, gkv_a = attend_back(queries[0], kv_a, logs[:heads, :, :1], mask_a, grad_att[:rows], factor)
    gq_b, gkv_b = attend_back(queries[1], kv_b, logs[heads:, :, :1], mask_b, grad_att[rows:], factor)
    (grad_kv,) = talk(
        keys_back_kernel,
        5,
        7,
        0,
        [((2, rows, 2 * kv_width), F32)],
        [VMEM] * 2,
        [VMEM],
        [pltpu.VMEM((3, 2, rows, 2 * kv_width), BF16), pltpu.VMEM((4, rows, 2 * kv_width), BF16)],
    )(gkv_b[:half_rows], jnp.stack([gkv_a, gkv_b[half_rows:]]))
    grad_kv = grad_kv.reshape(2 * rows, 2 * kv_width)
    grad_query = undo_rotation(jnp.concatenate([gq_a, gq_b], 0), cosine[:, None], sine[:, None]).reshape(2 * rows, q_width)
    grad_key = undo_rotation(grad_kv[:, :kv_width], cosine, sine)
    grad_pre = jnp.concatenate([grad_query, grad_key, grad_kv[:, kv_width:]], 1).astype(BF16)
    grad_normed_part = dot_rows(grad_pre, w_in_full).astype(BF16).reshape(2, rows, width)
    grad_normed_in, down_in = talk(
        halves_kernel,
        6,
        2,
        0,
        [((rows, width), BF16)] * 2,
        [ANY] * 2,
        [ANY] * 2,
    )(grad_normed_part, down_part.reshape(2, rows, width))

    def own(array):
        return lax.dynamic_index_in_dim(array.reshape(2, rows, -1), col, 0, keepdims=False)

    grad_normed = own(grad_normed_part).astype(F32) + grad_normed_in.astype(F32)
    result_rows = own(middle) + (own(down_part).astype(F32) + down_in.astype(F32))
    back_in, gain_attn_part = norm_back(own(stream), own(inverse_attn), gain_attn_full, grad_normed)
    grad_rows = own(grad_middle) + back_in
    grad_bias = jnp.sum(grad_pre.astype(F32), 0)
    gains = jnp.stack([gain_attn_part, 0.5 * gain_ffn_part]).reshape(2, 4, piece).transpose(1, 0, 2)
    in_w = dot_cols(normed, grad_pre).astype(BF16).reshape(4, piece, in_width)
    thirds = piece // 3
    q_half, w_half = (thin, in_width), (q_width // 2, piece)
    gate_up, down_all, in_total, out_total, result, grad_tokens, small_all = talk(
        tail_kernel,
        8,
        TAIL_COPIES,
        TAIL_LOCAL,
        [
            ((4, 2, piece, share), BF16),
            ((4, 2, share // 2, piece), BF16),
            ((piece, in_width), BF16),
            ((q_width, piece), BF16),
            ((half_rows, piece), BF16),
            ((half_rows, piece), BF16),
            ((4, 16, in_width), F32),
        ],
        [VMEM] * 4 + [ANY] * 4,
        [ANY] * 7,
        [
            pltpu.VMEM(shape, BF16)
            for shape in (
                (3, thirds, share),
                (share // 2, piece),
                (3, thirds, share),
                (share // 2, piece),
                (4, *q_half),
                (q_width // 2, width),
                (4, *q_half),
                (4, *w_half),
                (thin // 2, in_width),
                (thin // 2, in_width),
                (2, thin // 2, in_width),
                (2, thin // 2, in_width),
                (q_width // 4, piece),
                (q_width // 4, piece),
                (2, q_width // 4, piece),
                (2, q_width // 4, piece),
                q_half,
                w_half,
                q_half,
                w_half,
                (3, thin // 4, in_width),
                (3, q_width // 8, piece),
            )
        ]
        + [pltpu.VMEM((4, 8, in_width), F32), pltpu.VMEM((8, 8, piece), F32)]
        + [pltpu.VMEM((16, in_width), F32)] * 4,
        limit=56,
    )(
        both_sum,
        down_sum,
        in_w,
        out_w,
        result_rows.astype(BF16),
        grad_rows.astype(BF16),
        jnp.pad(grad_bias[None], ((0, 7), (0, 0))),
        jnp.pad(gains, ((0, 0), (0, 6), (0, 0))),
    )
    small_total = small_all[0] + small_all[1] + small_all[2] + small_all[3]
    bias_total = small_total[0]
    in_total = in_total.astype(F32)
    gate_total = jnp.concatenate([gate_up[i, 0] for i in range(4)], 1)[:, :hidden].astype(F32)
    up_total = jnp.concatenate([gate_up[i, 1] for i in range(4)], 1)[:, :hidden].astype(F32)
    down_total = down_all.reshape(4 * share, piece)[:hidden].astype(F32)
    upper = q_width + kv_width
    return (
        result.astype(F32),
        grad_tokens.astype(F32),
        small_total[8, :piece],
        in_total[:, :q_width],
        in_total[:, q_width:upper],
        in_total[:, upper:],
        bias_total[:q_width],
        bias_total[q_width:upper],
        bias_total[upper:],
        out_total.astype(F32),
        small_total[9, :piece],
        gate_total,
        up_total,
        down_total,
    )


def solution(mesh):
    placed = (
        P(("dp", "col"), "row"),
        P(("dp", "col"), "row"),
        P("dp", None),
        P("row"),
        P("row", "col"),
        P("row", "col"),
        P("row", "col"),
        P("col"),
        P("col"),
        P("col"),
        P("col", "row"),
        P("row"),
        P("row", "col"),
        P("row", "col"),
        P("col", "row"),
    )
    return jax.shard_map(
        on_device,
        mesh=mesh,
        in_specs=placed,
        out_specs=(
            P(("dp", "col"), "row"),
            P(("dp", "col"), "row"),
            P("row"),
            P("row", "col"),
            P("row", "col"),
            P("row", "col"),
            P("col"),
            P("col"),
            P("col"),
            P("col", "row"),
            P("row"),
            P("row", "col"),
            P("row", "col"),
            P("col", "row"),
        ),
        check_vma=False,
    )
```

```python
import math

import jax
import jax.numpy as jnp
from jax import lax
from jax.experimental import pallas as pl
from jax.experimental.pallas import tpu as pltpu
from jax.sharding import PartitionSpec as P

HEAD_SIZE = 128
EPS = 1e-06
THETA = 1000000.0
LANES = 128
MESH = pl.DeviceIdType.MESH
BF16 = jnp.bfloat16
F32 = jnp.float32
ANY = pl.BlockSpec(memory_space=pl.ANY)
VMEM = pl.BlockSpec(memory_space=pltpu.VMEM)

Z_STEP = 4
FRONT_COPIES = 74
FRONT_LOCAL = 27
BACK_COPIES = 143
BACK_LOCAL = 26


def here():
    return lax.axis_index("dp"), lax.axis_index("row"), lax.axis_index("col")


def flip_near(dp):
    return dp + 2 - 4 * ((dp // 2) % 2)


def pair_of(place, row=None):
    dp, own, col = place
    return flip_near(dp), own if row is None else row, 1 - col


def near_of(place, row=None):
    dp, own, col = place
    return flip_near(dp), own if row is None else row, col


def twin_of(place):
    dp, row, col = place
    return dp + 1 - 2 * (dp % 2), row, col


def along_z(place, step):
    dp, row, col = place
    return (dp + Z_STEP * step) % (4 * Z_STEP), row, col


def along_y(place, step):
    dp, row, col = place
    return dp, (row + step) % 4, col


def meet(peers):
    barrier = pltpu.get_barrier_semaphore()
    for peer in peers:
        pl.semaphore_signal(barrier, inc=1, device_id=peer, device_id_type=MESH)
    pl.semaphore_wait(barrier, len(peers))


class Mail:
    def __init__(self, send, recv):
        self.send, self.recv, self.count, self.sent = send, recv, 0, []

    def post(self, source, target, device):
        index = self.count
        self.count += 1
        copy = pltpu.make_async_remote_copy(
            src_ref=source,
            dst_ref=target,
            send_sem=self.send.at[index],
            recv_sem=self.recv.at[index],
            device_id=device,
            device_id_type=MESH,
        )
        copy.start()
        self.sent.append(copy)
        return copy

    def finish(self):
        assert self.count == self.send.shape[0], (self.count, self.send.shape)
        for copy in self.sent:
            copy.wait_send()


def talk(body, ident, copies, local, outs, in_specs, out_specs, scratch=(), limit=32):
    return pl.pallas_call(
        body,
        out_shape=[jax.ShapeDtypeStruct(*out) for out in outs],
        in_specs=in_specs,
        out_specs=out_specs,
        scratch_shapes=[
            *scratch,
            pltpu.SemaphoreType.DMA((copies,)),
            pltpu.SemaphoreType.DMA((copies,)),
            pltpu.SemaphoreType.DMA((max(local, 1),)),
        ],
        compiler_params=pltpu.CompilerParams(
            collective_id=ident, has_side_effects=True, vmem_limit_bytes=limit << 20
        ),
    )


def front_kernel(
    tok,
    cot,
    lens,
    gains,
    bias,
    wq,
    wk,
    wv,
    wo,
    wg,
    wu,
    wd,
    tok_out,
    cot_full,
    gains_out,
    normed,
    query,
    kva_out,
    kvb_out,
    logs,
    attended,
    tables,
    middle,
    turned_a,
    turned_b,
    normed_ffn,
    w_in_out,
    w_out_out,
    wgu_full,
    wd_full,
    tok_v,
    lens_v,
    gains_v,
    w_in,
    w_out,
    gu_own,
    wd_own,
    blank_gu,
    blank_wd,
    kv,
    kva,
    kvb,
    bias_a,
    bias_b,
    branch,
    branch_in,
    send,
    recv,
    local,
):
    place = here()
    dp, row, col = place
    z, core = dp // Z_STEP, dp % 2
    twin, pair, up, down = twin_of(place), pair_of(place), along_z(place, 1), along_z(place, 3)
    right, left = along_y(place, 1), along_y(place, 3)
    meet(
        [along_y(place, s) for s in (1, 2, 3)]
        + [near_of(place, (row + s) % 4) for s in range(4)]
        + [pair, twin, up, down]
    )
    mail = Mail(send, recv)
    kept = []

    def keep(source, target):
        kept.append(pltpu.make_async_copy(source, target, local.at[len(kept)]))
        kept[-1].start()
        return len(kept) - 1

    def kept_wait(index):
        kept[index].wait()
        kept[index] = None

    def even(start, size):
        return pl.ds(pl.multiple_of(start, 16), size)

    rows, piece = tok.shape[0] // 4, tok.shape[1]
    width = 4 * piece
    own_rows = even(col * rows, rows)
    spot = even(row * rows, rows)

    def spread(source, target):
        got = []
        for step in range(4):
            part = source.at[even(((row + step) % 4) * rows, rows), :]
            lanes = pl.ds(((4 - step) % 4) * piece, piece)
            if step:
                got.append(mail.post(part, target.at[own_rows, lanes], along_y(place, step)))
            else:
                mine = keep(part, target.at[own_rows, lanes])
        return got, mine

    tokens = spread(tok, tok_v)
    lens_got = mail.post(lens, lens_v.at[col], pair)
    lens_kept = keep(lens, lens_v.at[col])
    gains_kept = keep(gains, gains_v.at[0])
    gains_got = [mail.post(gains, gains_v.at[4 - s], along_y(place, s)) for s in (1, 2, 3)]

    q_width, kv_width = wq.shape[1], wk.shape[1]
    stages = [
        keep(wq, w_in.at[0, :, pl.ds(0, q_width)]),
        keep(wk, w_in.at[0, :, pl.ds(q_width, kv_width)]),
        keep(wv, w_in.at[0, :, pl.ds(q_width + kv_width, kv_width)]),
        keep(wo, w_out.at[:, pl.ds(0, piece)]),
    ]
    share = wd_own.shape[0]
    thin = piece // 2
    sure = share - LANES
    take = pl.multiple_of(z * share, LANES)
    big = []
    for k in range(2):
        for i, source in enumerate((wg, wu)):
            from_rows = pl.ds(k * thin, thin)
            big.append(keep(source.at[from_rows, pl.ds(take, sure)], gu_own.at[k, :, pl.ds(i * share, sure)]))
    big.append(keep(wd.at[pl.ds(take, sure), :], wd_own.at[pl.ds(0, sure), :]))
    blank_gu[...] = jnp.zeros_like(blank_gu)
    blank_wd[...] = jnp.zeros_like(blank_wd)
    first_edge = len(kept)
    edges = []
    for k in range(2):
        for i, source in enumerate((wg, wu)):
            target = gu_own.at[k, :, pl.ds(i * share + sure, LANES)]
            edges.append((source, pl.ds(k * thin, thin), None, target, blank_gu))
    edges.append((wd, None, slice(None), wd_own.at[pl.ds(sure, LANES), :], blank_wd))

    def edge(index, last):
        source, from_rows, _, target, blank = edges[index]
        if last:
            origin = blank
        elif from_rows is None:
            origin = source.at[pl.ds(pl.multiple_of(take + sure, LANES), LANES), :]
        else:
            origin = source.at[from_rows, pl.ds(pl.multiple_of(take + sure, LANES), LANES)]
        return pltpu.make_async_copy(origin, target, local.at[first_edge + index])

    @pl.when(z < 3)
    def _():
        for index in range(len(edges)):
            edge(index, False).start()

    @pl.when(z == 3)
    def _():
        for index in range(len(edges)):
            edge(index, True).start()

    for index in range(len(edges)):
        kept.append(edge(index, True))
        big.append(first_edge + index)

    q_rows, o_rows = thin // 4, w_out.shape[0] // 8

    def in_part(j, owner_z):
        return w_in.at[j, even(core * thin + owner_z * q_rows, q_rows), :]

    def in_parts(owner_z):
        return w_in.at[pl.ds(1, 3), even(core * thin + owner_z * q_rows, q_rows), :]

    def in_side(owner_z, side):
        lanes = pl.ds(side * (w_in.shape[2] // 2), w_in.shape[2] // 2)
        return w_in.at[pl.ds(1, 3), even(core * thin + owner_z * q_rows, q_rows), lanes]

    def out_part(j, owner_z):
        return w_out.at[even(core * 4 * o_rows + owner_z * o_rows, o_rows), pl.ds(j * piece, piece)]

    def out_parts(owner_z):
        return w_out.at[even(core * 4 * o_rows + owner_z * o_rows, o_rows), pl.ds(piece, 3 * piece)]

    def out_side(owner_z, side):
        start = core * 4 * o_rows + owner_z * o_rows + side * (o_rows // 2)
        return w_out.at[even(start, o_rows // 2), pl.ds(piece, 3 * piece)]

    for index in stages:
        kept_wait(index)
    in_got = [mail.post(in_part(0, z), in_part(4 - step, z), along_y(place, step)) for step in (1, 3, 2)]
    out_got = [mail.post(out_part(0, z), out_part(4 - step, z), along_y(place, step)) for step in (1, 3, 2)]
    cotangents = spread(cot, cot_full.at[0])

    def to_pair(spreading, target):
        got, mine = spreading
        kept_wait(mine)
        for copy in got:
            copy.wait_recv()
        return mail.post(target.at[own_rows, :], target.at[own_rows, :], pair)

    tokens_pair = to_pair(tokens, tok_v)
    shares = []

    def give(part):
        shares.append(mail.post(part, part, twin))

    def z_first(side):
        copies = {}
        for turn in range(2):
            copies["u", turn] = mail.post(side(z, turn), side(z, turn), up)
            copies["d", 1 - turn] = mail.post(side(z, 1 - turn), side(z, 1 - turn), down)
        return copies

    below, above, across = (z + 3) % 4, (z + 1) % 4, (z + 2) % 4

    def z_second(side, whole, copies):
        copies["u", 0].wait_recv()
        far_up = mail.post(side(below, 0), side(below, 0), up)
        copies["d", 1].wait_recv()
        far_down = mail.post(side(above, 1), side(above, 1), down)
        copies["u", 1].wait_recv()
        give(whole(below))
        copies["d", 0].wait_recv()
        give(whole(above))
        return far_up, far_down

    def z_third(whole, copies):
        for copy in copies:
            copy.wait_recv()
        give(whole(across))

    for copy in in_got:
        copy.wait_recv()
    in_z = z_first(in_side)
    give(in_parts(z))
    for copy in out_got:
        copy.wait_recv()
    give(out_parts(z))

    for index in big:
        kept_wait(index)
    gu_half, wd_half = thin // 2, share // 4

    def gu_part(j, which=None):
        start, size = (0, thin) if which is None else (which * gu_half, gu_half)
        return wgu_full.at[j, core, pl.ds(start, size), :]

    def wd_part(j, which=None):
        start, size = (0, 2 * wd_half) if which is None else (which * wd_half, wd_half)
        return wd_full.at[even(core * 2 * wd_half + start, size), pl.ds(j * piece, piece)]

    def gu_source(which):
        return gu_own.at[core, pl.ds(which * gu_half, gu_half), :]

    def wd_source(which):
        return wd_own.at[even((core * 2 + which) * wd_half, wd_half), :]

    y_ring = {}
    for name, source, part in (("gu", gu_source, gu_part), ("wd", wd_source, wd_part)):
        for turn in range(2):
            y_ring[name, "r", turn] = mail.post(source(turn), part(3, turn), right)
            y_ring[name, "l", 1 - turn] = mail.post(source(1 - turn), part(1, 1 - turn), left)
    keep(gu_own, wgu_full.at[0])
    keep(wd_own, wd_full.at[:, pl.ds(0, piece)])
    twins = []

    def y_forward(name, part):
        y_ring[name, "r", 0].wait_recv()
        y_ring[name, "fr"] = mail.post(part(3, 0), part(2, 0), right)
        y_ring[name, "l", 1].wait_recv()
        y_ring[name, "fl"] = mail.post(part(1, 1), part(2, 1), left)

    def y_share(name, part):
        y_ring[name, "r", 1].wait_recv()
        twins.append(mail.post(part(3), part(3), twin))
        y_ring[name, "l", 0].wait_recv()
        twins.append(mail.post(part(1), part(1), twin))

    def y_end(name, part):
        y_ring[name, "fr"].wait_recv()
        y_ring[name, "fl"].wait_recv()
        twins.append(mail.post(part(2), part(2), twin))

    kept_wait(lens_kept)
    lens_got.wait_recv()
    half_rows = 4 * rows

    def segment_of(which, index):
        end_0 = lens_v[which, 0:1, 0:1]
        end_1 = end_0 + lens_v[which, 0:1, 1:2]
        past_0 = (index >= end_0).astype(jnp.int32)
        past_1 = (index >= end_1).astype(jnp.int32)
        start = jnp.where(past_1 > 0, end_1, jnp.where(past_0 > 0, end_0, 0))
        return past_0 + past_1, start

    lane = lax.broadcasted_iota(jnp.int32, (rows, HEAD_SIZE), 1)
    half_lane = jnp.where(lane >= HEAD_SIZE // 2, lane - HEAD_SIZE // 2, lane).astype(F32)
    inverse = jnp.exp(half_lane * (-2.0 * math.log(THETA) / HEAD_SIZE))
    for which, mask, mask_t, key_count in ((0, bias_a, turned_a, half_rows), (1, bias_b, turned_b, 2 * half_rows)):
        index = lax.broadcasted_iota(jnp.int32, (rows, HEAD_SIZE), 0) + (row * rows + which * half_rows)
        _, start = segment_of(which, index)
        turn = (index - start).astype(F32) * inverse
        tables[0, which * rows : (which + 1) * rows, :] = jnp.cos(turn)
        sine = jnp.sin(turn)
        tables[1, which * rows : (which + 1) * rows, :] = jnp.where(lane >= HEAD_SIZE // 2, sine, -sine)
        at = lax.broadcasted_iota(jnp.int32, (rows, key_count), 0) + (row * rows + which * half_rows)
        keys = lax.broadcasted_iota(jnp.int32, (rows, key_count), 1)
        allowed = jnp.logical_and(segment_of(which, at)[0] == segment_of(which, keys)[0], keys <= at)
        mask[...] = jnp.where(allowed, 0.0, -1e30)
        at = lax.broadcasted_iota(jnp.int32, (key_count, rows), 1) + (row * rows + which * half_rows)
        keys = lax.broadcasted_iota(jnp.int32, (key_count, rows), 0)
        allowed = jnp.logical_and(segment_of(which, at)[0] == segment_of(which, keys)[0], keys <= at)
        mask_t[...] = jnp.where(allowed, 0.0, -1e30)

    kept_wait(gains_kept)
    for copy in gains_got:
        copy.wait_recv()
    keep(gains_v, gains_out)

    def normalise(value, which):
        scale = lax.rsqrt(jnp.sum(value * value, -1, keepdims=True) * (1.0 / width) + EPS)
        return [
            (value[:, j * piece : (j + 1) * piece] * scale * gains_v[j, which : which + 1, :]).astype(BF16)
            for j in range(4)
        ]

    def norm_rows(which):
        part = pl.ds(pl.multiple_of(which * rows, rows), rows)
        for j, block in enumerate(normalise(tok_v[part, :].astype(F32), 0)):
            normed[part, pl.ds(j * piece, piece)] = block

    norm_rows(col)
    in_far = z_second(in_side, in_parts, in_z)
    out_z = z_first(out_side)
    tokens_pair.wait_recv()
    keep(tok_v, tok_out)
    norm_rows(1 - col)
    cot_pair = to_pair(cotangents, cot_full.at[0])
    z_third(in_parts, in_far)
    for copy in shares:
        copy.wait_recv()
    shares.clear()
    keep(w_in, w_in_out)

    in_width = w_in.shape[2]

    def project(lanes):
        value = jnp.dot(normed[:, 0:piece], w_in[0, :, lanes], preferred_element_type=F32)
        for j in range(1, 4):
            value = value + jnp.dot(
                normed[:, j * piece : (j + 1) * piece], w_in[j, :, lanes], preferred_element_type=F32
            )
        return value + bias[0:1, lanes]

    def rotate(value):
        return value * tables[0] + pltpu.roll(value, HEAD_SIZE // 2, 1) * tables[1]

    key_value = project(slice(q_width, in_width))
    kv[:, 0:kv_width] = rotate(key_value[:, 0:kv_width]).astype(BF16)
    kv[:, kv_width : 2 * kv_width] = key_value[:, kv_width : 2 * kv_width].astype(BF16)
    a_rows, b_rows = pl.ds(0, rows), pl.ds(rows, rows)
    high_spot = even(half_rows + row * rows, rows)
    a_got, b_got = [], []
    for step in (1, 2, 3):
        a_got.append(mail.post(kv.at[a_rows, :], kva.at[spot, :], along_y(place, step)))
    for step in range(4):
        b_got.append(mail.post(kv.at[a_rows, :], kvb.at[spot, :], near_of(place, (row + step) % 4)))
        if step:
            b_got.append(mail.post(kv.at[b_rows, :], kvb.at[high_spot, :], along_y(place, step)))
    kva[spot, :] = kv[a_rows, :]
    kvb[high_spot, :] = kv[b_rows, :]
    for first in range(0, q_width, 2 * HEAD_SIZE):
        value = project(slice(first, first + 2 * HEAD_SIZE))
        for i in range(2):
            lanes = slice(first + i * HEAD_SIZE, first + (i + 1) * HEAD_SIZE)
            query[:, lanes] = rotate(value[:, i * HEAD_SIZE : (i + 1) * HEAD_SIZE]).astype(BF16)

    out_far = z_second(out_side, out_parts, out_z)
    heads = q_width // HEAD_SIZE
    factor = HEAD_SIZE ** (-0.5)

    def attend(half, keys, mask):
        part = slice(half * rows, (half + 1) * rows)

        @pl.loop(0, heads)
        def _(h):
            lanes = pl.ds(pl.multiple_of(h * HEAD_SIZE, LANES), HEAD_SIZE)
            raw = lax.dot_general(
                query[part, lanes], keys[:, 0:HEAD_SIZE], (((1,), (1,)), ((), ())), preferred_element_type=F32
            )
            scores = raw * factor + mask[...]
            peak = jnp.max(scores, -1, keepdims=True)
            raised = jnp.exp(scores - peak)
            total = jnp.sum(raised, -1, keepdims=True)
            probs = (raised * (1.0 / total)).astype(BF16)
            out = jnp.dot(probs, keys[:, HEAD_SIZE : 2 * HEAD_SIZE], preferred_element_type=F32)
            attended[part, lanes] = out.astype(BF16)
            logs[half * heads + h] = jnp.broadcast_to(peak + jnp.log(total), (rows, LANES)).T[0:8, :]

        for first in range(0, width, piece):
            lanes = slice(first, first + piece)
            branch[part, lanes] = jnp.dot(
                attended[part, :], w_out[:, lanes], preferred_element_type=F32
            ).astype(BF16)
        return mail.post(branch.at[part, :], branch_in.at[part, :], pair)

    def finish_half(half, copy):
        part = slice(half * rows, (half + 1) * rows)
        copy.wait_recv()
        value = tok_v[part, :].astype(F32) + (branch[part, :].astype(F32) + branch_in[part, :].astype(F32))
        middle[part, :] = value
        for j, block in enumerate(normalise(value, 1)):
            normed_ffn[part, j * piece : (j + 1) * piece] = block

    def z_send(source, target, half):
        part = pl.ds(half * rows, rows)
        return (
            mail.post(source.at[part, :], target.at[1, part, :], up),
            mail.post(source.at[part, :], target.at[3, part, :], down),
        )

    def z_forward(target, half, copies):
        part = pl.ds(half * rows, rows)
        if half == 0:
            copies[0].wait_recv()
            return copies[1], mail.post(target.at[1, part, :], target.at[2, part, :], up)
        copies[1].wait_recv()
        return copies[0], mail.post(target.at[3, part, :], target.at[2, part, :], down)

    for copy in a_got:
        copy.wait_recv()
    keep(kva, kva_out)
    z_third(out_parts, out_far)
    for copy in shares:
        copy.wait_recv()
    keep(w_out, w_out_out)
    cot_pair.wait_recv()
    cot_z = [z_send(cot_full.at[0], cot_full, half) for half in range(2)]
    swap_a = attend(0, kva, bias_a)
    y_forward("gu", gu_part)
    for copy in b_got:
        copy.wait_recv()
    keep(kvb, kvb_out)
    swap_b = attend(1, kvb, bias_b)
    cot_last = [z_forward(cot_full, half, cot_z[half]) for half in range(2)]
    y_forward("wd", wd_part)
    finish_half(0, swap_a)
    y_share("gu", gu_part)
    finish_half(1, swap_b)
    y_share("wd", wd_part)
    y_end("gu", gu_part)
    y_end("wd", wd_part)
    for copies in cot_last:
        for copy in copies:
            copy.wait_recv()
    for copy in twins:
        copy.wait_recv()
    for copy in kept:
        if copy is not None:
            copy.wait()
    mail.finish()


def ffn_kernel(
    normed,
    cot,
    wgu,
    wd,
    total,
    gu_half,
    dn_half,
    down_out,
    x,
    cot_v,
    wgu_v,
    wd_v,
    gb,
    act,
    parts,
    turned,
    down_v,
    gu_in,
    dn_in,
    up1,
    down1,
    up2,
    down2,
    other,
    stage_up,
    stage_down,
    stage,
    send,
    recv,
    local,
):
    place = here()
    dp, row, col = place
    core = dp % 2
    up, down, pair, twin = along_z(place, 1), along_z(place, 3), pair_of(place), twin_of(place)
    meet([up, down, pair, twin])
    mail = Mail(send, recv)
    order = ((0, 0), (0, 1), (1, 0), (3, 1), (1, 1), (3, 0), (2, 0), (2, 1))
    spots = {half: i for i, half in enumerate(order)}
    rows = normed.shape[0] // 2
    size = rows // 2

    def block(ref, slot, half):
        return ref.at[pl.ds(spots[slot, half] * rows, rows), :]

    def halves(ref, half):
        return ref.at[pl.ds(half * rows, rows), :]

    kept = []

    def keep(source, target):
        kept.append(pltpu.make_async_copy(source, target, local.at[len(kept)]))
        kept[-1].start()
        return len(kept) - 1

    def kept_wait(index):
        kept[index].wait()
        kept[index] = None

    got = {}
    for turn in range(2):
        got["u", turn] = mail.post(halves(normed, turn), block(x, 1, turn), up)
        got["d", 1 - turn] = mail.post(halves(normed, 1 - turn), block(x, 3, 1 - turn), down)
    share = wd.shape[0]
    early = [keep(normed, x.at[pl.ds(0, 2 * rows), :]), keep(wgu, wgu_v)]
    early.append(keep(cot.at[0], cot_v.at[pl.ds(0, 2 * rows), :]))
    early.append(keep(wd, wd_v))
    later = [keep(cot.at[slot, pl.ds(half * rows, rows), :], block(cot_v, slot, half)) for slot, half in order[2:]]
    width = normed.shape[1]
    piece = width // 4

    def dot_nt(left, right):
        return lax.dot_general(left, right, (((1,), (1,)), ((), ())), preferred_element_type=F32)

    def compute(c):
        part = slice(2 * rows * c, 2 * rows * (c + 1))
        for start, size in ((0, 512), (512, share - 512)):
            lanes, above = slice(start, start + size), slice(share + start, share + start + size)
            gate = jnp.dot(x[part, :], wgu_v[:, lanes], preferred_element_type=F32)
            value = jnp.dot(x[part, :], wgu_v[:, above], preferred_element_type=F32)
            grad = dot_nt(cot_v[part, :], wd_v[lanes, :])
            spread = 1.0 / (1.0 + jnp.exp(-gate))
            smooth = gate * spread
            act[part, lanes] = (smooth * value).astype(BF16)
            gb[part, lanes] = (grad * value * (spread * (1.0 + gate * (1.0 - spread)))).astype(BF16)
            gb[part, above] = (grad * smooth).astype(BF16)
        for m in range(3):
            lanes = slice(512 * m, 512 * (m + 1))
            parts[part, lanes] = dot_nt(gb[part, :], wgu_v[lanes, :]).astype(BF16)

    for index in early:
        kept_wait(index)
    compute(0)
    got["u", 0].wait_recv()
    far_up = mail.post(block(x, 1, 0), block(x, 2, 0), up)
    got["d", 1].wait_recv()
    far_down = mail.post(block(x, 3, 1), block(x, 2, 1), down)
    for index in later:
        kept_wait(index)
    compute(1)
    got["u", 1].wait_recv()
    got["d", 0].wait_recv()
    compute(2)
    far_up.wait_recv()
    far_down.wait_recv()
    second = {
        ("d", 0): mail.post(block(parts, 1, 0), down2.at[0], down),
        ("u", 1): mail.post(block(parts, 3, 1), up2.at[1], up),
    }
    compute(3)
    first = {}
    for i in range(2):
        rows_i = pl.ds(i * size, size)
        first["u", i] = mail.post(block(parts, 2, 0).at[rows_i, :], up1.at[i], up)
        first["d", i] = mail.post(block(parts, 2, 1).at[rows_i, :], down1.at[i], down)

    def turn_over(source, target):
        @pl.loop(0, source.shape[1] // LANES)
        def _(t):
            lanes = pl.ds(pl.multiple_of(t * LANES, LANES), LANES)
            target[lanes, :] = source[:, lanes].T

    def forward(i):
        rows_i = pl.ds(i * size, size)
        first["u", i].wait_recv()
        stage_up[i] = (block(parts, 3, 0).at[rows_i, :][...].astype(F32) + up1[i].astype(F32)).astype(BF16)
        second["u", 0, i] = mail.post(stage_up.at[i], up2.at[0, rows_i, :], up)
        first["d", i].wait_recv()
        stage_down[i] = (block(parts, 1, 1).at[rows_i, :][...].astype(F32) + down1[i].astype(F32)).astype(BF16)
        second["d", 1, i] = mail.post(stage_down.at[i], down2.at[1, rows_i, :], down)

    turn_over(x, turned)
    forward(0)
    for m in range(3):
        lanes = slice(512 * m, 512 * (m + 1))

        @pl.loop(0, 4)
        def _(c):
            part = pl.ds(pl.multiple_of(c * 2 * rows, 2 * rows), 2 * rows)
            down_v[part, lanes] = jnp.dot(act[part, :], wd_v[:, lanes], preferred_element_type=F32).astype(BF16)

    forward(1)
    for slot, half in order:
        keep(block(down_v, slot, half), down_out.at[slot, pl.ds(half * rows, rows), :])
    tile = 256
    tiles = 2 * share // tile

    def gu_tiles(first_tile, last_tile):
        @pl.loop(first_tile, last_tile)
        def _(n):
            lanes = pl.ds(pl.multiple_of(((n + (tiles // 2) * (1 - core)) % tiles) * tile, tile), tile)
            wgu_v[:, lanes] = jnp.dot(turned[...], gb[:, lanes], preferred_element_type=F32).astype(BF16)

    swaps = {}

    def settle(i):
        rows_i = pl.ds(i * size, size)
        if i == 0:
            second["d", 0].wait_recv()
            second["u", 1].wait_recv()
        second["u", 0, i].wait_recv()
        second["d", 1, i].wait_recv()
        for half in range(2):
            value = block(parts, 0, half).at[rows_i, :][...].astype(F32)
            value = value + up2[half, rows_i, :].astype(F32) + down2[half, rows_i, :].astype(F32)
            stage[half, rows_i, :] = value.astype(BF16)
            swaps[half, i] = mail.post(stage.at[half, rows_i, :], other.at[half, rows_i, :], pair)

    there = pl.ds(pl.multiple_of((1 - core) * share, LANES), share)
    mine = pl.ds(pl.multiple_of(core * share, LANES), share)
    gu_tiles(0, tiles // 2 + 1)
    shared = [
        mail.post(wgu_v.at[pl.ds(j * piece, piece), there], gu_in.at[j], twin) for j in range(4)
    ]
    settle(0)
    gu_tiles(tiles // 2 + 1, tiles)
    settle(1)
    turn_over(act, turned)

    @pl.loop(0, width // tile)
    def _(n):
        lanes = pl.ds(pl.multiple_of(n * tile, tile), tile)
        wd_v[:, lanes] = jnp.dot(
            turned[0:share, :], cot_v[:, lanes], preferred_element_type=F32
        ).astype(BF16)

    half_share = share // 2
    rows_there = pl.ds(pl.multiple_of((1 - core) * half_share, 16), half_share)
    rows_mine = pl.ds(pl.multiple_of(core * half_share, 16), half_share)
    shared += [
        mail.post(wd_v.at[rows_there, pl.ds(j * piece, piece)], dn_in.at[j], twin) for j in range(4)
    ]
    for j in range(4):
        shared[j].wait_recv()
        gu_in[j] = (wgu_v[pl.ds(j * piece, piece), mine].astype(F32) + gu_in[j].astype(F32)).astype(BF16)
        keep(gu_in.at[j], gu_half.at[j])
    for j in range(4):
        shared[4 + j].wait_recv()
        dn_in[j] = (wd_v[rows_mine, pl.ds(j * piece, piece)].astype(F32) + dn_in[j].astype(F32)).astype(BF16)
        keep(dn_in.at[j], dn_half.at[j])
    for half, i in ((0, 0), (1, 0), (0, 1), (1, 1)):
        rows_i = pl.ds(i * size, size)
        swaps[half, i].wait_recv()
        total[pl.ds(half * rows + i * size, size), :] = stage[half, rows_i, :].astype(F32) + other[
            half, rows_i, :
        ].astype(F32)
    for copy in kept:
        if copy is not None:
            copy.wait()
    mail.finish()


def back_kernel(
    total,
    middle,
    cot,
    gains,
    tok,
    normed,
    query,
    kv_a,
    kv_b,
    logs,
    attended,
    tables,
    turned_a,
    turned_b,
    w_in,
    w_out,
    gu,
    dn,
    down_parts,
    gu_out,
    dn_out,
    in_out,
    wo_out,
    grad_out,
    result_out,
    small_out,
    middle_v,
    cot_v,
    tok_v,
    normed_v,
    query_v,
    kva,
    kvb,
    attended_v,
    turned_a_v,
    turned_b_v,
    w_in_v,
    w_out_v,
    gu_v,
    dn_v,
    down_v,
    gain_rows,
    grad_middle,
    grad_low,
    grad_att,
    flat,
    keys_t,
    dkv_a,
    dkv_b,
    low_kv,
    own_kv,
    from_own,
    from_near,
    grad_pre,
    grad_part,
    grad_in,
    part_in,
    rows_out,
    result_rows,
    gu_up1,
    gu_down1,
    gu_up2,
    gu_down2,
    gu_y,
    gu_n,
    gu_s,
    dn_up1,
    dn_down1,
    dn_up2,
    dn_down2,
    dn_y,
    dn_n,
    dn_s,
    in_p,
    in_t,
    in_up1,
    in_down1,
    in_up2,
    in_down2,
    in_s,
    in_n,
    in_z,
    wo_p,
    wo_t,
    wo_up1,
    wo_down1,
    wo_up2,
    wo_down2,
    wo_s,
    wo_n,
    wo_z,
    res_up1,
    res_down1,
    res_up2,
    res_down2,
    res_stage_up,
    res_stage_down,
    bias_own,
    gains_own,
    bias_in,
    gains_in,
    small_a,
    small_b,
    small_t,
    small_n,
    send,
    recv,
    local,
):
    place = here()
    dp, row, col = place
    core = dp % 2
    z = dp // Z_STEP
    twin, near, pair = twin_of(place), near_of(place), pair_of(place)
    up, down, far_z = along_z(place, 1), along_z(place, 3), along_z(place, 2)
    right, left = along_y(place, 1), along_y(place, 3)
    meet(
        [along_y(place, s) for s in (1, 2, 3)]
        + [near_of(place, (row + s) % 4) for s in range(4)]
        + [pair_of(place, (row + s) % 4) for s in range(4)]
        + [twin, up, down, far_z]
    )
    mail = Mail(send, recv)
    kept, arrivals = [], []

    def keep(source, target):
        kept.append(pltpu.make_async_copy(source, target, local.at[len(kept)]))
        kept[-1].start()
        return len(kept) - 1

    def kept_wait(index):
        kept[index].wait()
        kept[index] = None

    def even(start, size):
        return pl.ds(pl.multiple_of(start, 16), size)

    def plus(*values):
        result = values[0].astype(F32)
        for value in values[1:]:
            result = result + value.astype(F32)
        return result

    def dot_nt(left, right):
        return lax.dot_general(left, right, (((1,), (1,)), ((), ())), preferred_element_type=F32)

    rows = tok.shape[0] // 2
    width = tok.shape[1]
    piece = width // 4
    spot = even(row * rows, rows)
    own_rows, other_rows = even(col * rows, rows), even((1 - col) * rows, rows)

    def ffn_flow(i):
        if i < 3:
            height = gu.shape[1] // 3
            start, source, held, out = i * height, gu, gu_v, gu_out
            up1, down1, up2, down2 = gu_up1.at[i], gu_down1.at[i], gu_up2.at[i], gu_down2.at[i]
            mine, theirs, done = gu_y.at[i], gu_n.at[i], gu_s.at[i]
        else:
            height = dn.shape[1]
            start, source, held, out = 0, dn, dn_v, dn_out
            up1, down1, up2, down2 = dn_up1, dn_down1, dn_up2, dn_down2
            mine, theirs, done = dn_y, dn_n, dn_s
        half = height // 2
        low, high = pl.ds(start, half), pl.ds(start + half, half)
        first = (mail.post(source.at[2, low, :], up1, right), mail.post(source.at[2, high, :], down1, left))
        straight = (
            mail.post(source.at[1, high, :], up2.at[pl.ds(half, half), :], right),
            mail.post(source.at[3, low, :], down2.at[pl.ds(0, half), :], left),
        )
        yield
        if i in (0, 3):
            kept_wait(loads["gu" if i == 0 else "dn"])
        first[0].wait_recv()
        up1[...] = plus(held[1, low, :], up1[...]).astype(BF16)
        last = [mail.post(up1, up2.at[pl.ds(0, half), :], right)]
        first[1].wait_recv()
        down1[...] = plus(held[3, high, :], down1[...]).astype(BF16)
        last.append(mail.post(down1, down2.at[pl.ds(half, half), :], left))
        yield
        for copy in straight + tuple(last):
            copy.wait_recv()
        mine[...] = plus(held[0, pl.ds(start, height), :], up2[...], down2[...]).astype(BF16)
        swap = mail.post(mine, theirs, near)
        yield
        swap.wait_recv()
        done[...] = plus(mine[...], theirs[...]).astype(BF16)

        def room(slot, which=None):
            begin, size = (start, height) if which is None else (start + which * half, half)
            return out.at[slot, core, pl.ds(begin, size), :]

        posts = {}
        for turn in range(2):
            for name, device, which in (("u", up, turn), ("d", down, 1 - turn)):
                posts[name, which] = mail.post(done.at[pl.ds(which * half, half), :], room(z, which), device)
        keep(done, room(z))
        arrivals.append(mail.post(done, room(z), twin))
        yield
        posts["u", 0].wait_recv()
        block = room((z + 3) % 4, 0)
        one_more = mail.post(block, block, up)
        posts["d", 1].wait_recv()
        block = room((z + 1) % 4, 1)
        two_more = mail.post(block, block, down)
        yield
        posts["u", 1].wait_recv()
        block = room((z + 3) % 4)
        arrivals.append(mail.post(block, block, twin))
        posts["d", 0].wait_recv()
        block = room((z + 1) % 4)
        arrivals.append(mail.post(block, block, twin))
        one_more.wait_recv()
        two_more.wait_recv()
        block = room((z + 2) % 4)
        arrivals.append(mail.post(block, block, twin))
        yield

    def weight_flow(part, t, up1, down1, up2, down2, total_h, theirs, quarter, out):
        height = t.shape[1]
        half = height // 2
        low, high = pl.ds(0, half), pl.ds(half, half)
        copy = mail.post(part.at[:, even((1 - core) * height, height), :], t, twin)
        yield
        copy.wait_recv()
        for j in range(4):
            t[j] = plus(part[j, even(core * height, height), :], t[j]).astype(BF16)
        first = (mail.post(t.at[2, low, :], up1, right), mail.post(t.at[2, high, :], down1, left))
        straight = (
            mail.post(t.at[1, high, :], up2.at[high, :], right),
            mail.post(t.at[3, low, :], down2.at[low, :], left),
        )
        yield
        first[0].wait_recv()
        up1[...] = plus(t[1, low, :], up1[...]).astype(BF16)
        last = [mail.post(up1, up2.at[low, :], right)]
        first[1].wait_recv()
        down1[...] = plus(t[3, high, :], down1[...]).astype(BF16)
        last.append(mail.post(down1, down2.at[high, :], left))
        yield
        for copy in straight + tuple(last):
            copy.wait_recv()
        total_h[...] = plus(t[0], up2[...], down2[...]).astype(BF16)
        swap = mail.post(total_h, theirs, near)
        yield
        swap.wait_recv()
        t[0] = plus(total_h[...], theirs[...]).astype(BF16)
        size = height // 4
        copies = []
        for step, device in ((1, up), (3, down), (2, far_z)):
            source = t.at[0, even(((z + step) % 4) * size, size), :]
            copies.append(mail.post(source, quarter.at[step - 1], device))
        yield
        for copy in copies:
            copy.wait_recv()
        mine = even(z * size, size)
        theirs[0:size, :] = plus(t[0, mine, :], quarter[0], quarter[1], quarter[2]).astype(BF16)
        place_of = lambda owner: out.at[even(core * height + owner * size, size), :]
        copies = [mail.post(theirs.at[0:size, :], place_of(z), device) for device in (up, down, far_z)]
        arrivals.append(mail.post(theirs.at[0:size, :], place_of(z), twin))
        keep(theirs.at[0:size, :], place_of(z))
        yield
        for copy in copies:
            copy.wait_recv()
        for step in (1, 2, 3):
            block = place_of((z + step) % 4)
            arrivals.append(mail.post(block, block, twin))
        yield

    def result_flow():
        low, high = pl.ds(0, rows), pl.ds(rows, rows)
        first = (mail.post(down_parts.at[2, low, :], res_up1, up), mail.post(down_parts.at[2, high, :], res_down1, down))
        straight = (
            mail.post(down_parts.at[3, high, :], res_up2.at[high, :], up),
            mail.post(down_parts.at[1, low, :], res_down2.at[low, :], down),
        )
        yield
        kept_wait(loads["down"])
        first[0].wait_recv()
        res_stage_up[...] = plus(down_v[3, low, :], res_up1[...]).astype(BF16)
        last = [mail.post(res_stage_up, res_up2.at[low, :], up)]
        first[1].wait_recv()
        res_stage_down[...] = plus(down_v[1, high, :], res_down1[...]).astype(BF16)
        last.append(mail.post(res_stage_down, res_down2.at[high, :], down))
        yield
        for copy in straight + tuple(last):
            copy.wait_recv()
        sums = plus(down_v[0, other_rows, :], res_up2[other_rows, :], res_down2[other_rows, :])
        result_rows[1] = sums.astype(BF16)
        swap = mail.post(result_rows.at[1], part_in, pair)
        yield
        swap.wait_recv()
        sums = plus(down_v[0, own_rows, :], res_up2[own_rows, :], res_down2[own_rows, :])
        result_rows[0] = (middle_v[own_rows, :] + plus(sums, part_in[...])).astype(BF16)
        spread(result_rows.at[0], result_out)
        yield

    def spread(source, target):
        for step in range(4):
            lanes = pl.ds(step * piece, piece)
            if step:
                arrivals.append(mail.post(source.at[:, lanes], target.at[spot, :], along_y(place, step)))
            else:
                keep(source.at[:, lanes], target.at[spot, :])

    flows = [ffn_flow(i) for i in range(4)]
    next(flows[0])
    next(flows[1])
    loads = {}
    for name, source, target in (
        ("middle", middle, middle_v),
        ("cot", cot.at[0], cot_v),
        ("w_out", w_out, w_out_v),
        ("attended", attended, attended_v),
        ("query", query, query_v),
        ("kva", kv_a, kva),
        ("kvb", kv_b, kvb),
        ("ta", turned_a, turned_a_v),
        ("tb", turned_b, turned_b_v),
        ("gu", gu, gu_v),
        ("w_in", w_in, w_in_v),
        ("normed", normed, normed_v),
        ("tok", tok, tok_v),
        ("dn", dn, dn_v),
        ("down", down_parts, down_v),
    ):
        loads[name] = keep(source, target)
    result_steps = result_flow()
    next(result_steps)
    for j in range(4):
        gain_rows[:, j * piece : (j + 1) * piece] = gains[j]

    def norm_back(stream, gain, incoming):
        scale = lax.rsqrt(jnp.sum(stream * stream, -1, keepdims=True) * (1.0 / width) + EPS)
        scaled = incoming * gain
        inner = jnp.sum(scaled * stream, -1, keepdims=True) * (1.0 / width)
        back = scale * scaled - stream * (scale * scale * scale * inner)
        return back, jnp.sum(incoming * stream * scale, 0, keepdims=True)

    kept_wait(loads["middle"])
    kept_wait(loads["cot"])
    gain_ffn_part = jnp.zeros((1, width), F32)
    for half in range(2):
        part = slice(half * rows, (half + 1) * rows)
        back, gain_part = norm_back(middle_v[part, :], gain_rows[1:2, :], total[part, :])
        value = cot_v[part, :].astype(F32) + back
        grad_middle[part, :] = value
        grad_low[part, :] = value.astype(BF16)
        gain_ffn_part = gain_ffn_part + gain_part
    gains_own[...] = jnp.zeros_like(gains_own)
    for j in range(4):
        gains_own[j, 1:2, :] = 0.5 * gain_ffn_part[:, j * piece : (j + 1) * piece]
    kept_wait(loads["w_out"])
    q_width = w_out.shape[0]
    for first in range(0, q_width, 256):
        lanes = slice(first, first + 256)
        grad_att[:, lanes] = dot_nt(grad_low[...], w_out_v[lanes, :]).astype(BF16)
    next(flows[0])
    next(flows[2])

    def turn_over(source, target, count):
        for t in range(count):
            lanes = slice(t * LANES, (t + 1) * LANES)
            target[lanes, 0 : source.shape[0]] = source[:, lanes].T

    kept_wait(loads["attended"])
    turn_over(attended_v, flat, q_width // LANES)
    for j in range(4):
        wo_p[j] = jnp.dot(
            flat[0:q_width, :], grad_low[:, j * piece : (j + 1) * piece], preferred_element_type=F32
        ).astype(BF16)
    wo_steps = weight_flow(wo_p, wo_t, wo_up1, wo_down1, wo_up2, wo_down2, wo_s, wo_n, wo_z, wo_out)
    next(wo_steps)
    next(flows[1])
    next(flows[3])

    for name in ("query", "kva", "kvb", "ta", "tb"):
        kept_wait(loads[name])
    heads = q_width // HEAD_SIZE
    factor = HEAD_SIZE ** (-0.5)

    def unrotate(value, half):
        part = slice(half * rows, (half + 1) * rows)
        return value * tables[0, part, :] + pltpu.roll(value * tables[1, part, :], HEAD_SIZE // 2, 1)

    def attend_back(half, keys, mask, sums):
        part = slice(half * rows, (half + 1) * rows)
        count = keys.shape[0]
        for t in range(count // LANES):
            lanes = slice(t * LANES, (t + 1) * LANES)
            keys_t[:, lanes] = keys[lanes, 0:HEAD_SIZE].T
        sums[...] = jnp.zeros_like(sums)

        @pl.loop(0, heads)
        def _(h):
            lanes = pl.ds(pl.multiple_of(h * HEAD_SIZE, LANES), HEAD_SIZE)
            one, grad = query_v[part, lanes], grad_att[part, lanes]
            raw = dot_nt(keys[:, 0:HEAD_SIZE], one)
            probs = jnp.exp(raw * factor + mask[...] - logs[half * heads + h, 0:1, :])
            grad_probs = dot_nt(keys[:, HEAD_SIZE : 2 * HEAD_SIZE], grad)
            inner = jnp.sum(grad_probs * probs, 0, keepdims=True)
            grad_scores = (probs * (grad_probs - inner)).astype(BF16)
            sums[:, 0:HEAD_SIZE] += jnp.dot(grad_scores, one, preferred_element_type=F32)
            sums[:, HEAD_SIZE : 2 * HEAD_SIZE] += jnp.dot(probs.astype(BF16), grad, preferred_element_type=F32)
            grad_query = jnp.dot(keys_t[:, 0:count], grad_scores, preferred_element_type=F32).T * factor
            grad_pre[part, lanes] = unrotate(grad_query, half).astype(BF16)

    def low_sums(sums, part):
        return (sums[part, 0:HEAD_SIZE] * factor).astype(BF16), sums[part, HEAD_SIZE : 2 * HEAD_SIZE].astype(BF16)

    attend_back(1, kvb, turned_b_v, dkv_b)
    half_rows = kva.shape[0]
    low_part, high_part = slice(0, half_rows), slice(half_rows, 2 * half_rows)
    for target, sums, part in ((low_kv, dkv_b, low_part), (own_kv.at[1], dkv_b, high_part)):
        target[:, 0:HEAD_SIZE], target[:, HEAD_SIZE : 2 * HEAD_SIZE] = low_sums(sums, part)
    kv_got = []
    for step in range(4):
        other = (row + step) % 4
        part = even(other * rows, rows)
        kv_got.append(mail.post(low_kv.at[part, :], from_near.at[step], near_of(place, other)))
        if step:
            kv_got.append(mail.post(own_kv.at[1, part, :], from_own.at[step - 1, 1], along_y(place, step)))
    next(flows[0])
    attend_back(0, kva, turned_a_v, dkv_a)
    target = own_kv.at[0]
    target[:, 0:HEAD_SIZE], target[:, HEAD_SIZE : 2 * HEAD_SIZE] = low_sums(dkv_a, low_part)
    for step in (1, 2, 3):
        part = even(((row + step) % 4) * rows, rows)
        kv_got.append(mail.post(own_kv.at[0, part, :], from_own.at[step - 1, 0], along_y(place, step)))
    next(result_steps)
    next(flows[2])
    next(wo_steps)
    kept_wait(loads["normed"])
    turn_over(normed_v, flat, width // LANES)
    for copy in kv_got:
        copy.wait_recv()
    for half in range(2):
        part = slice(half * rows, (half + 1) * rows)
        value = own_kv[half, spot, :].astype(F32)
        for step in range(3):
            value = value + from_own[step, half].astype(F32)
        if half == 0:
            for step in range(4):
                value = value + from_near[step].astype(F32)
        grad_pre[part, q_width : q_width + HEAD_SIZE] = unrotate(value[:, 0:HEAD_SIZE], half).astype(BF16)
        grad_pre[part, q_width + HEAD_SIZE : q_width + 2 * HEAD_SIZE] = value[:, HEAD_SIZE : 2 * HEAD_SIZE].astype(
            BF16
        )
    kept_wait(loads["w_in"])
    for j in range(4):
        grad_part[:, j * piece : (j + 1) * piece] = dot_nt(grad_pre[...], w_in_v[j]).astype(BF16)
    swap = mail.post(grad_part.at[other_rows, :], grad_in, pair)
    next(flows[1])
    for j in range(4):
        in_p[j] = jnp.dot(flat[j * piece : (j + 1) * piece, :], grad_pre[...], preferred_element_type=F32).astype(BF16)
    in_steps = weight_flow(in_p, in_t, in_up1, in_down1, in_up2, in_down2, in_s, in_n, in_z, in_out)
    next(in_steps)
    bias_own[...] = jnp.zeros_like(bias_own)
    bias_own[0:1, :] = jnp.sum(grad_pre[...].astype(F32), 0, keepdims=True)
    next(flows[3])
    next(flows[0])
    next(wo_steps)
    next(flows[2])
    next(in_steps)
    kept_wait(loads["tok"])
    swap.wait_recv()
    back, gain_part = norm_back(
        tok_v[own_rows, :].astype(F32), gain_rows[0:1, :], plus(grad_part[own_rows, :], grad_in[...])
    )
    rows_out[...] = (grad_middle[own_rows, :] + back).astype(BF16)
    for j in range(4):
        gains_own[j, 0:1, :] = gain_part[:, j * piece : (j + 1) * piece]
    small_copies, small_kept = [], []
    for step in range(4):
        device = along_y(place, step)
        mine = gains_in.at[col * 4 + row]
        if step:
            small_copies.append(mail.post(bias_own, bias_in.at[row], device))
            small_copies.append(mail.post(gains_own.at[step], mine, device))
        else:
            small_kept.append(keep(bias_own, bias_in.at[row]))
            small_kept.append(keep(gains_own.at[step], mine))
        small_copies.append(mail.post(gains_own.at[step], mine, pair_of(place, (row + step) % 4)))
    next(flows[1])
    next(wo_steps)
    next(flows[3])
    next(in_steps)
    next(flows[2])
    next(result_steps)
    spread(rows_out, grad_out)
    for copy in small_copies:
        copy.wait_recv()
    for index in small_kept:
        kept_wait(index)
    small_a[...] = jnp.zeros_like(small_a)
    small_a[0:8, :] = bias_in[0] + bias_in[1] + bias_in[2] + bias_in[3]
    small_a[8:16, 0:piece] = (
        gains_in[0] + gains_in[1] + gains_in[2] + gains_in[3] + gains_in[4] + gains_in[5] + gains_in[6] + gains_in[7]
    )
    small_first = mail.post(small_a, small_t, twin)
    next(flows[0])
    next(flows[1])
    next(flows[3])
    next(wo_steps)
    next(in_steps)
    small_first.wait_recv()
    small_b[...] = small_a[...] + small_t[...]
    small_second = mail.post(small_b, small_n, near)
    next(result_steps)
    next(flows[2])
    next(wo_steps)
    next(in_steps)
    small_second.wait_recv()
    small_t[...] = small_b[...] + small_n[...]
    for device in (up, down, far_z):
        arrivals.append(mail.post(small_t, small_out.at[z], device))
    keep(small_t, small_out.at[z])
    next(flows[3])
    next(wo_steps)
    next(in_steps)
    for steps in [*flows, wo_steps, in_steps, result_steps]:
        for _ in steps:
            pass
    for copy in arrivals:
        copy.wait_recv()
    for copy in kept:
        if copy is not None:
            copy.wait()
    mail.finish()


def on_device(
    tokens,
    cotangent,
    lengths,
    gain_attn,
    w_query,
    key_projection,
    value_projection,
    bias_query,
    key_bias_vector,
    value_bias_vector,
    w_out,
    gain_ffn,
    w_gate,
    w_up,
    w_down,
):
    half_rows, piece = tokens.shape
    width = 4 * piece
    rows = half_rows // 4
    q_width = w_query.shape[1]
    kv_width = key_projection.shape[1]
    heads = q_width // HEAD_SIZE
    hidden = w_gate.shape[1]
    share = -(-hidden // (4 * LANES)) * LANES

    in_width = q_width + 2 * kv_width
    thin = piece // 2
    lens = jnp.pad(lengths, ((0, 7), (0, LANES - lengths.shape[1])))
    gains = jnp.pad(jnp.stack([gain_attn, gain_ffn]), ((0, 6), (0, 0)))
    bias = jnp.concatenate([bias_query, key_bias_vector, value_bias_vector])
    bias = jnp.broadcast_to(bias[None], (8, in_width))
    (
        tok_rows,
        cot_full,
        gains4,
        normed,
        query,
        kv_a,
        kv_b,
        logs,
        attended,
        tables,
        middle,
        mask_a,
        mask_b,
        normed_ffn,
        w_in_full,
        w_out_full,
        w_gu_full,
        w_down_full,
    ) = talk(
        front_kernel,
        0,
        FRONT_COPIES,
        FRONT_LOCAL,
        [
            ((2 * rows, width), BF16),
            ((4, 2 * rows, width), BF16),
            ((4, 8, piece), F32),
            ((2 * rows, width), BF16),
            ((2 * rows, q_width), BF16),
            ((half_rows, 2 * kv_width), BF16),
            ((2 * half_rows, 2 * kv_width), BF16),
            ((2 * heads, 8, rows), F32),
            ((2 * rows, q_width), BF16),
            ((2, 2 * rows, HEAD_SIZE), F32),
            ((2 * rows, width), F32),
            ((half_rows, rows), F32),
            ((2 * half_rows, rows), F32),
            ((2 * rows, width), BF16),
            ((4, piece, in_width), BF16),
            ((q_width, width), BF16),
            ((4, 2, thin, 2 * share), BF16),
            ((share, width), BF16),
        ],
        [ANY] * 4 + [VMEM] + [ANY] * 7,
        [ANY] * 3 + [VMEM] * 2 + [ANY] * 2 + [VMEM] * 7 + [ANY] * 4,
        [
            pltpu.VMEM((2 * rows, width), BF16),
            pltpu.VMEM((2, 8, LANES), jnp.int32),
            pltpu.VMEM((4, 8, piece), F32),
            pltpu.VMEM((4, piece, in_width), BF16),
            pltpu.VMEM((q_width, width), BF16),
            pltpu.VMEM((2, thin, 2 * share), BF16),
            pltpu.VMEM((share, piece), BF16),
            pltpu.VMEM((thin, LANES), BF16),
            pltpu.VMEM((LANES, piece), BF16),
            pltpu.VMEM((2 * rows, 2 * kv_width), BF16),
            pltpu.VMEM((half_rows, 2 * kv_width), BF16),
            pltpu.VMEM((2 * half_rows, 2 * kv_width), BF16),
            pltpu.VMEM((rows, half_rows), F32),
            pltpu.VMEM((rows, 2 * half_rows), F32),
            pltpu.VMEM((2 * rows, width), BF16),
            pltpu.VMEM((2 * rows, width), BF16),
        ],
        limit=56,
    )(
        tokens,
        cotangent,
        lens,
        gains,
        bias,
        w_query,
        key_projection,
        value_projection,
        w_out,
        w_gate,
        w_up,
        w_down,
    )

    w_both_full = w_gu_full.reshape(width, 2 * share)
    half_block = (2, rows, width)
    grad_normed_ffn, both_half, down_half, down_parts = talk(
        ffn_kernel,
        4,
        28,
        26,
        [
            ((2 * rows, width), F32),
            ((4, piece, share), BF16),
            ((4, share // 2, piece), BF16),
            ((4, 2 * rows, width), BF16),
        ],
        [ANY] * 4,
        [VMEM, ANY, ANY, ANY],
        [
            pltpu.VMEM(shape, BF16)
            for shape in (
                (8 * rows, width),
                (8 * rows, width),
                (width, 2 * share),
                (share, width),
                (8 * rows, 2 * share),
                (8 * rows, share),
                (8 * rows, width),
                (width, 8 * rows),
                (8 * rows, width),
                (4, piece, share),
                (4, share // 2, piece),
                (2, rows // 2, width),
                (2, rows // 2, width),
                half_block,
                half_block,
                half_block,
                (2, rows // 2, width),
                (2, rows // 2, width),
                half_block,
            )
        ],
        limit=60,
    )(normed_ffn, cot_full, w_both_full, w_down_full)
    thirds = piece // 3
    q_half, w_half = (thin, in_width), (q_width // 2, piece)
    gu_chunk, dn_chunk = (3, thirds, share), (share // 2, piece)

    def halved(shape):
        return (*shape[:-2], shape[-2] // 2, shape[-1])

    def weight_scratch(shape):
        return [
            (4, 2 * shape[0], shape[1]),
            (4, *shape),
            halved(shape),
            halved(shape),
            shape,
            shape,
            shape,
            shape,
            (3, shape[0] // 4, shape[1]),
        ]

    def scratch(kind, *shapes):
        return [pltpu.VMEM(shape, kind) for shape in shapes]

    gate_up, down_all, in_total, out_total, grad_tokens, result, small_all = talk(
        back_kernel,
        8,
        BACK_COPIES,
        BACK_LOCAL,
        [
            ((4, 2, piece, share), BF16),
            ((4, 2, share // 2, piece), BF16),
            ((piece, in_width), BF16),
            ((q_width, piece), BF16),
            ((half_rows, piece), BF16),
            ((half_rows, piece), BF16),
            ((4, 16, in_width), F32),
        ],
        [VMEM, ANY, ANY, VMEM] + [ANY] * 5 + [VMEM, ANY, VMEM] + [ANY] * 7,
        [ANY] * 7,
        scratch(F32, (2 * rows, width))
        + scratch(
            BF16,
            (2 * rows, width),
            (2 * rows, width),
            (2 * rows, width),
            (2 * rows, q_width),
            (half_rows, 2 * kv_width),
            (2 * half_rows, 2 * kv_width),
            (2 * rows, q_width),
        )
        + scratch(F32, (half_rows, rows), (2 * half_rows, rows))
        + scratch(
            BF16,
            (4, piece, in_width),
            (q_width, width),
            (4, piece, share),
            (4, share // 2, piece),
            (4, 2 * rows, width),
        )
        + scratch(F32, (8, width), (2 * rows, width))
        + scratch(BF16, (2 * rows, width), (2 * rows, q_width), (width, 2 * rows), (HEAD_SIZE, 2 * half_rows))
        + scratch(F32, (half_rows, 2 * kv_width), (2 * half_rows, 2 * kv_width))
        + scratch(
            BF16,
            (half_rows, 2 * kv_width),
            (2, half_rows, 2 * kv_width),
            (3, 2, rows, 2 * kv_width),
            (4, rows, 2 * kv_width),
            (2 * rows, in_width),
            (2 * rows, width),
            (rows, width),
            (rows, width),
            (rows, width),
            (2, rows, width),
            halved(gu_chunk),
            halved(gu_chunk),
            gu_chunk,
            gu_chunk,
            gu_chunk,
            gu_chunk,
            gu_chunk,
            halved(dn_chunk),
            halved(dn_chunk),
            dn_chunk,
            dn_chunk,
            dn_chunk,
            dn_chunk,
            dn_chunk,
            *weight_scratch(q_half),
            *weight_scratch(w_half),
            (rows, width),
            (rows, width),
            (2 * rows, width),
            (2 * rows, width),
            (rows, width),
            (rows, width),
        )
        + scratch(F32, (8, in_width), (4, 8, piece), (4, 8, in_width), (8, 8, piece))
        + scratch(F32, *[(16, in_width)] * 4),
        limit=60,
    )(
        grad_normed_ffn,
        middle,
        cot_full,
        gains4,
        tok_rows,
        normed,
        query,
        kv_a,
        kv_b,
        logs,
        attended,
        tables,
        mask_a,
        mask_b,
        w_in_full,
        w_out_full,
        both_half,
        down_half,
        down_parts,
    )
    small_total = small_all[0] + small_all[1] + small_all[2] + small_all[3]
    bias_total = small_total[0]
    in_total = in_total.astype(F32)
    gate_total = jnp.concatenate([gate_up[i, 0] for i in range(4)], 1)[:, :hidden].astype(F32)
    up_total = jnp.concatenate([gate_up[i, 1] for i in range(4)], 1)[:, :hidden].astype(F32)
    down_total = down_all.reshape(4 * share, piece)[:hidden].astype(F32)
    upper = q_width + kv_width
    return (
        result.astype(F32),
        grad_tokens.astype(F32),
        small_total[8, :piece],
        in_total[:, :q_width],
        in_total[:, q_width:upper],
        in_total[:, upper:],
        bias_total[:q_width],
        bias_total[q_width:upper],
        bias_total[upper:],
        out_total.astype(F32),
        small_total[9, :piece],
        gate_total,
        up_total,
        down_total,
    )


def solution(mesh):
    placed = (
        P(("dp", "col"), "row"),
        P(("dp", "col"), "row"),
        P("dp", None),
        P("row"),
        P("row", "col"),
        P("row", "col"),
        P("row", "col"),
        P("col"),
        P("col"),
        P("col"),
        P("col", "row"),
        P("row"),
        P("row", "col"),
        P("row", "col"),
        P("col", "row"),
    )
    return jax.shard_map(
        on_device,
        mesh=mesh,
        in_specs=placed,
        out_specs=(
            P(("dp", "col"), "row"),
            P(("dp", "col"), "row"),
            P("row"),
            P("row", "col"),
            P("row", "col"),
            P("row", "col"),
            P("col"),
            P("col"),
            P("col"),
            P("col", "row"),
            P("row"),
            P("row", "col"),
            P("row", "col"),
            P("col", "row"),
        ),
        check_vma=False,
    )
```

```python
import math

import jax
import jax.numpy as jnp
from jax import lax
from jax.experimental import pallas as pl
from jax.experimental.pallas import tpu as pltpu
from jax.sharding import PartitionSpec as P

HEAD_SIZE = 128
EPS = 1e-06
THETA = 1000000.0
LANES = 128
MESH = pl.DeviceIdType.MESH
BF16 = jnp.bfloat16
F32 = jnp.float32
ANY = pl.BlockSpec(memory_space=pl.ANY)
VMEM = pl.BlockSpec(memory_space=pltpu.VMEM)

Z_STEP = 4
FRONT_COPIES = 74
FRONT_LOCAL = 27
BACK_COPIES = 137
BACK_LOCAL = 26


def here():
    return lax.axis_index("dp"), lax.axis_index("row"), lax.axis_index("col")


def flip_near(dp):
    return dp + 2 - 4 * ((dp // 2) % 2)


def pair_of(place, row=None):
    dp, own, col = place
    return flip_near(dp), own if row is None else row, 1 - col


def near_of(place, row=None):
    dp, own, col = place
    return flip_near(dp), own if row is None else row, col


def twin_of(place):
    dp, row, col = place
    return dp + 1 - 2 * (dp % 2), row, col


def along_z(place, step):
    dp, row, col = place
    return (dp + Z_STEP * step) % (4 * Z_STEP), row, col


def along_y(place, step):
    dp, row, col = place
    return dp, (row + step) % 4, col


def meet(peers):
    barrier = pltpu.get_barrier_semaphore()
    for peer in peers:
        pl.semaphore_signal(barrier, inc=1, device_id=peer, device_id_type=MESH)
    pl.semaphore_wait(barrier, len(peers))


class Mail:
    def __init__(self, send, recv):
        self.send, self.recv, self.count, self.sent = send, recv, 0, []

    def post(self, source, target, device):
        index = self.count
        self.count += 1
        copy = pltpu.make_async_remote_copy(
            src_ref=source,
            dst_ref=target,
            send_sem=self.send.at[index],
            recv_sem=self.recv.at[index],
            device_id=device,
            device_id_type=MESH,
        )
        copy.start()
        self.sent.append(copy)
        return copy

    def finish(self):
        assert self.count == self.send.shape[0], (self.count, self.send.shape)
        for copy in self.sent:
            copy.wait_send()


def talk(body, ident, copies, local, outs, in_specs, out_specs, scratch=(), limit=32):
    return pl.pallas_call(
        body,
        out_shape=[jax.ShapeDtypeStruct(*out) for out in outs],
        in_specs=in_specs,
        out_specs=out_specs,
        scratch_shapes=[
            *scratch,
            pltpu.SemaphoreType.DMA((copies,)),
            pltpu.SemaphoreType.DMA((copies,)),
            pltpu.SemaphoreType.DMA((max(local, 1),)),
        ],
        compiler_params=pltpu.CompilerParams(
            collective_id=ident, has_side_effects=True, vmem_limit_bytes=limit << 20
        ),
    )


def front_kernel(
    tok,
    cot,
    lens_in,
    gain_attn,
    gain_ffn,
    bias_q,
    bias_k,
    bias_v,
    wq,
    wk,
    wv,
    wo,
    wg,
    wu,
    wd,
    tok_out,
    cot_full,
    gains_out,
    normed,
    query,
    kva_out,
    kvb_out,
    logs,
    attended,
    tables,
    middle,
    turned_a,
    turned_b,
    normed_ffn,
    w_in_out,
    w_out_out,
    wgu_full,
    wd_full,
    lens,
    gains,
    tok_v,
    lens_v,
    gains_v,
    w_in,
    w_out,
    gu_own,
    wd_own,
    blank_gu,
    blank_wd,
    kv,
    kva,
    kvb,
    bias_a,
    bias_b,
    branch,
    branch_in,
    send,
    recv,
    local,
):
    place = here()
    dp, row, col = place
    z, core = dp // Z_STEP, dp % 2
    twin, pair, up, down = twin_of(place), pair_of(place), along_z(place, 1), along_z(place, 3)
    right, left = along_y(place, 1), along_y(place, 3)
    meet(
        [along_y(place, s) for s in (1, 2, 3)]
        + [near_of(place, (row + s) % 4) for s in range(4)]
        + [pair, twin, up, down]
    )
    mail = Mail(send, recv)
    kept = []

    def keep(source, target):
        kept.append(pltpu.make_async_copy(source, target, local.at[len(kept)]))
        kept[-1].start()
        return len(kept) - 1

    def kept_wait(index):
        kept[index].wait()
        kept[index] = None

    def even(start, size):
        return pl.ds(pl.multiple_of(start, 16), size)

    rows, piece = tok.shape[0] // 4, tok.shape[1]
    width = 4 * piece
    own_rows = even(col * rows, rows)
    spot = even(row * rows, rows)

    def spread(source, target):
        got = []
        for step in range(4):
            part = source.at[even(((row + step) % 4) * rows, rows), :]
            lanes = pl.ds(((4 - step) % 4) * piece, piece)
            if step:
                got.append(mail.post(part, target.at[own_rows, lanes], along_y(place, step)))
            else:
                mine = keep(part, target.at[own_rows, lanes])
        return got, mine

    tokens = spread(tok, tok_v)
    lens[...] = jnp.zeros_like(lens)
    lens[0:1, 0 : lens_in.shape[1]] = lens_in[...]
    gains[...] = jnp.zeros_like(gains)
    gains[0:1, :] = gain_attn[...]
    gains[1:2, :] = gain_ffn[...]
    lens_got = mail.post(lens, lens_v.at[col], pair)
    lens_kept = keep(lens, lens_v.at[col])
    gains_kept = keep(gains, gains_v.at[0])
    gains_got = [mail.post(gains, gains_v.at[4 - s], along_y(place, s)) for s in (1, 2, 3)]

    q_width, kv_width = wq.shape[1], wk.shape[1]
    stages = [
        keep(wq, w_in.at[0, :, pl.ds(0, q_width)]),
        keep(wk, w_in.at[0, :, pl.ds(q_width, kv_width)]),
        keep(wv, w_in.at[0, :, pl.ds(q_width + kv_width, kv_width)]),
        keep(wo, w_out.at[:, pl.ds(0, piece)]),
    ]
    share = wd_own.shape[0]
    thin = piece // 2
    sure = share - LANES
    take = pl.multiple_of(z * share, LANES)
    big = []
    for k in range(2):
        for i, source in enumerate((wg, wu)):
            from_rows = pl.ds(k * thin, thin)
            big.append(keep(source.at[from_rows, pl.ds(take, sure)], gu_own.at[k, :, pl.ds(i * share, sure)]))
    big.append(keep(wd.at[pl.ds(take, sure), :], wd_own.at[pl.ds(0, sure), :]))
    blank_gu[...] = jnp.zeros_like(blank_gu)
    blank_wd[...] = jnp.zeros_like(blank_wd)
    first_edge = len(kept)
    edges = []
    for k in range(2):
        for i, source in enumerate((wg, wu)):
            target = gu_own.at[k, :, pl.ds(i * share + sure, LANES)]
            edges.append((source, pl.ds(k * thin, thin), None, target, blank_gu))
    edges.append((wd, None, slice(None), wd_own.at[pl.ds(sure, LANES), :], blank_wd))

    def edge(index, last):
        source, from_rows, _, target, blank = edges[index]
        if last:
            origin = blank
        elif from_rows is None:
            origin = source.at[pl.ds(pl.multiple_of(take + sure, LANES), LANES), :]
        else:
            origin = source.at[from_rows, pl.ds(pl.multiple_of(take + sure, LANES), LANES)]
        return pltpu.make_async_copy(origin, target, local.at[first_edge + index])

    @pl.when(z < 3)
    def _():
        for index in range(len(edges)):
            edge(index, False).start()

    @pl.when(z == 3)
    def _():
        for index in range(len(edges)):
            edge(index, True).start()

    for index in range(len(edges)):
        kept.append(edge(index, True))
        big.append(first_edge + index)

    q_rows, o_rows = thin // 4, w_out.shape[0] // 8

    def in_part(j, owner_z):
        return w_in.at[j, even(core * thin + owner_z * q_rows, q_rows), :]

    def in_parts(owner_z):
        return w_in.at[pl.ds(1, 3), even(core * thin + owner_z * q_rows, q_rows), :]

    def in_side(owner_z, side):
        lanes = pl.ds(side * (w_in.shape[2] // 2), w_in.shape[2] // 2)
        return w_in.at[pl.ds(1, 3), even(core * thin + owner_z * q_rows, q_rows), lanes]

    def out_part(j, owner_z):
        return w_out.at[even(core * 4 * o_rows + owner_z * o_rows, o_rows), pl.ds(j * piece, piece)]

    def out_parts(owner_z):
        return w_out.at[even(core * 4 * o_rows + owner_z * o_rows, o_rows), pl.ds(piece, 3 * piece)]

    def out_side(owner_z, side):
        start = core * 4 * o_rows + owner_z * o_rows + side * (o_rows // 2)
        return w_out.at[even(start, o_rows // 2), pl.ds(piece, 3 * piece)]

    for index in stages:
        kept_wait(index)
    in_got = [mail.post(in_part(0, z), in_part(4 - step, z), along_y(place, step)) for step in (1, 3, 2)]
    out_got = [mail.post(out_part(0, z), out_part(4 - step, z), along_y(place, step)) for step in (1, 3, 2)]
    cotangents = spread(cot, cot_full.at[0])

    def to_pair(spreading, target):
        got, mine = spreading
        kept_wait(mine)
        for copy in got:
            copy.wait_recv()
        return mail.post(target.at[own_rows, :], target.at[own_rows, :], pair)

    tokens_pair = to_pair(tokens, tok_v)
    shares = []

    def give(part):
        shares.append(mail.post(part, part, twin))

    def z_first(side):
        copies = {}
        for turn in range(2):
            copies["u", turn] = mail.post(side(z, turn), side(z, turn), up)
            copies["d", 1 - turn] = mail.post(side(z, 1 - turn), side(z, 1 - turn), down)
        return copies

    below, above, across = (z + 3) % 4, (z + 1) % 4, (z + 2) % 4

    def z_second(side, whole, copies):
        copies["u", 0].wait_recv()
        far_up = mail.post(side(below, 0), side(below, 0), up)
        copies["d", 1].wait_recv()
        far_down = mail.post(side(above, 1), side(above, 1), down)
        copies["u", 1].wait_recv()
        give(whole(below))
        copies["d", 0].wait_recv()
        give(whole(above))
        return far_up, far_down

    def z_third(whole, copies):
        for copy in copies:
            copy.wait_recv()
        give(whole(across))

    for copy in in_got:
        copy.wait_recv()
    in_z = z_first(in_side)
    give(in_parts(z))
    for index in big:
        kept_wait(index)
    gu_half, wd_half = thin // 2, share // 4

    def gu_part(j, which=None):
        start, size = (0, thin) if which is None else (which * gu_half, gu_half)
        return wgu_full.at[j, core, pl.ds(start, size), :]

    def wd_part(j, which=None):
        start, size = (0, 2 * wd_half) if which is None else (which * wd_half, wd_half)
        return wd_full.at[even(core * 2 * wd_half + start, size), pl.ds(j * piece, piece)]

    def gu_source(which):
        return gu_own.at[core, pl.ds(which * gu_half, gu_half), :]

    def wd_source(which):
        return wd_own.at[even((core * 2 + which) * wd_half, wd_half), :]

    y_ring = {}
    for name, source, part in (("gu", gu_source, gu_part), ("wd", wd_source, wd_part)):
        for turn in range(2):
            y_ring[name, "r", turn] = mail.post(source(turn), part(3, turn), right)
            y_ring[name, "l", 1 - turn] = mail.post(source(1 - turn), part(1, 1 - turn), left)
    keep(gu_own, wgu_full.at[0])
    keep(wd_own, wd_full.at[:, pl.ds(0, piece)])
    twins = []

    def y_forward(name, part):
        y_ring[name, "r", 0].wait_recv()
        y_ring[name, "fr"] = mail.post(part(3, 0), part(2, 0), right)
        y_ring[name, "l", 1].wait_recv()
        y_ring[name, "fl"] = mail.post(part(1, 1), part(2, 1), left)

    def y_share(name, part):
        y_ring[name, "r", 1].wait_recv()
        twins.append(mail.post(part(3), part(3), twin))
        y_ring[name, "l", 0].wait_recv()
        twins.append(mail.post(part(1), part(1), twin))

    def y_end(name, part):
        y_ring[name, "fr"].wait_recv()
        y_ring[name, "fl"].wait_recv()
        twins.append(mail.post(part(2), part(2), twin))

    for copy in out_got:
        copy.wait_recv()
    give(out_parts(z))

    kept_wait(lens_kept)
    lens_got.wait_recv()
    half_rows = 4 * rows

    def segment_of(which, index):
        end_0 = lens_v[which, 0:1, 0:1]
        end_1 = end_0 + lens_v[which, 0:1, 1:2]
        past_0 = (index >= end_0).astype(jnp.int32)
        past_1 = (index >= end_1).astype(jnp.int32)
        start = jnp.where(past_1 > 0, end_1, jnp.where(past_0 > 0, end_0, 0))
        return past_0 + past_1, start

    lane = lax.broadcasted_iota(jnp.int32, (rows, HEAD_SIZE), 1)
    half_lane = jnp.where(lane >= HEAD_SIZE // 2, lane - HEAD_SIZE // 2, lane).astype(F32)
    inverse = jnp.exp(half_lane * (-2.0 * math.log(THETA) / HEAD_SIZE))
    for which, mask, mask_t, key_count in ((0, bias_a, turned_a, half_rows), (1, bias_b, turned_b, 2 * half_rows)):
        index = lax.broadcasted_iota(jnp.int32, (rows, HEAD_SIZE), 0) + (row * rows + which * half_rows)
        _, start = segment_of(which, index)
        turn = (index - start).astype(F32) * inverse
        tables[0, which * rows : (which + 1) * rows, :] = jnp.cos(turn)
        sine = jnp.sin(turn)
        tables[1, which * rows : (which + 1) * rows, :] = jnp.where(lane >= HEAD_SIZE // 2, sine, -sine)
        at = lax.broadcasted_iota(jnp.int32, (rows, key_count), 0) + (row * rows + which * half_rows)
        keys = lax.broadcasted_iota(jnp.int32, (rows, key_count), 1)
        allowed = jnp.logical_and(segment_of(which, at)[0] == segment_of(which, keys)[0], keys <= at)
        mask[...] = jnp.where(allowed, 0.0, -1e30)
        at = lax.broadcasted_iota(jnp.int32, (key_count, rows), 1) + (row * rows + which * half_rows)
        keys = lax.broadcasted_iota(jnp.int32, (key_count, rows), 0)
        allowed = jnp.logical_and(segment_of(which, at)[0] == segment_of(which, keys)[0], keys <= at)
        mask_t[...] = jnp.where(allowed, 0.0, -1e30)

    kept_wait(gains_kept)
    for copy in gains_got:
        copy.wait_recv()
    keep(gains_v, gains_out)

    def normalise(value, which):
        scale = lax.rsqrt(jnp.sum(value * value, -1, keepdims=True) * (1.0 / width) + EPS)
        return [
            (value[:, j * piece : (j + 1) * piece] * scale * gains_v[j, which : which + 1, :]).astype(BF16)
            for j in range(4)
        ]

    def norm_rows(which):
        part = pl.ds(pl.multiple_of(which * rows, rows), rows)
        for j, block in enumerate(normalise(tok_v[part, :].astype(F32), 0)):
            normed[part, pl.ds(j * piece, piece)] = block

    norm_rows(col)
    in_far = z_second(in_side, in_parts, in_z)
    out_z = z_first(out_side)
    tokens_pair.wait_recv()
    keep(tok_v, tok_out)
    norm_rows(1 - col)
    cot_pair = to_pair(cotangents, cot_full.at[0])
    z_third(in_parts, in_far)
    for copy in shares:
        copy.wait_recv()
    shares.clear()
    keep(w_in, w_in_out)

    in_width = w_in.shape[2]

    def project(lanes, bias):
        value = jnp.dot(normed[:, 0:piece], w_in[0, :, lanes], preferred_element_type=F32)
        for j in range(1, 4):
            value = value + jnp.dot(
                normed[:, j * piece : (j + 1) * piece], w_in[j, :, lanes], preferred_element_type=F32
            )
        return value + bias

    def rotate(value):
        return value * tables[0] + pltpu.roll(value, HEAD_SIZE // 2, 1) * tables[1]

    key_value = project(slice(q_width, in_width), jnp.concatenate([bias_k[...], bias_v[...]], 1))
    kv[:, 0:kv_width] = rotate(key_value[:, 0:kv_width]).astype(BF16)
    kv[:, kv_width : 2 * kv_width] = key_value[:, kv_width : 2 * kv_width].astype(BF16)
    a_rows, b_rows = pl.ds(0, rows), pl.ds(rows, rows)
    high_spot = even(half_rows + row * rows, rows)
    a_got, b_got = [], []
    for step in (1, 2, 3):
        a_got.append(mail.post(kv.at[a_rows, :], kva.at[spot, :], along_y(place, step)))
    for step in range(4):
        b_got.append(mail.post(kv.at[a_rows, :], kvb.at[spot, :], near_of(place, (row + step) % 4)))
        if step:
            b_got.append(mail.post(kv.at[b_rows, :], kvb.at[high_spot, :], along_y(place, step)))
    kva[spot, :] = kv[a_rows, :]
    kvb[high_spot, :] = kv[b_rows, :]
    for first in range(0, q_width, 2 * HEAD_SIZE):
        value = project(slice(first, first + 2 * HEAD_SIZE), bias_q[:, first : first + 2 * HEAD_SIZE])
        for i in range(2):
            lanes = slice(first + i * HEAD_SIZE, first + (i + 1) * HEAD_SIZE)
            query[:, lanes] = rotate(value[:, i * HEAD_SIZE : (i + 1) * HEAD_SIZE]).astype(BF16)

    y_forward("gu", gu_part)
    out_far = z_second(out_side, out_parts, out_z)
    heads = q_width // HEAD_SIZE
    factor = HEAD_SIZE ** (-0.5)

    def attend(half, keys, mask):
        part = slice(half * rows, (half + 1) * rows)

        @pl.loop(0, heads)
        def _(h):
            lanes = pl.ds(pl.multiple_of(h * HEAD_SIZE, LANES), HEAD_SIZE)
            raw = lax.dot_general(
                query[part, lanes], keys[:, 0:HEAD_SIZE], (((1,), (1,)), ((), ())), preferred_element_type=F32
            )
            scores = raw * factor + mask[...]
            peak = jnp.max(scores, -1, keepdims=True)
            raised = jnp.exp(scores - peak)
            total = jnp.sum(raised, -1, keepdims=True)
            probs = (raised * (1.0 / total)).astype(BF16)
            out = jnp.dot(probs, keys[:, HEAD_SIZE : 2 * HEAD_SIZE], preferred_element_type=F32)
            attended[part, lanes] = out.astype(BF16)
            logs[half * heads + h] = jnp.broadcast_to(peak + jnp.log(total), (rows, LANES)).T[0:8, :]

        for first in range(0, width, piece):
            lanes = slice(first, first + piece)
            branch[part, lanes] = jnp.dot(
                attended[part, :], w_out[:, lanes], preferred_element_type=F32
            ).astype(BF16)
        return mail.post(branch.at[part, :], branch_in.at[part, :], pair)

    def finish_half(half, copy):
        part = slice(half * rows, (half + 1) * rows)
        copy.wait_recv()
        value = tok_v[part, :].astype(F32) + (branch[part, :].astype(F32) + branch_in[part, :].astype(F32))
        middle[part, :] = value
        for j, block in enumerate(normalise(value, 1)):
            normed_ffn[part, j * piece : (j + 1) * piece] = block

    def z_send(source, target, half):
        part = pl.ds(half * rows, rows)
        return (
            mail.post(source.at[part, :], target.at[1, part, :], up),
            mail.post(source.at[part, :], target.at[3, part, :], down),
        )

    def z_forward(target, half, copies):
        part = pl.ds(half * rows, rows)
        if half == 0:
            copies[0].wait_recv()
            return copies[1], mail.post(target.at[1, part, :], target.at[2, part, :], up)
        copies[1].wait_recv()
        return copies[0], mail.post(target.at[3, part, :], target.at[2, part, :], down)

    for copy in a_got:
        copy.wait_recv()
    keep(kva, kva_out)
    z_third(out_parts, out_far)
    for copy in shares:
        copy.wait_recv()
    keep(w_out, w_out_out)
    cot_pair.wait_recv()
    cot_z = [z_send(cot_full.at[0], cot_full, half) for half in range(2)]
    swap_a = attend(0, kva, bias_a)
    y_forward("wd", wd_part)
    y_share("gu", gu_part)
    for copy in b_got:
        copy.wait_recv()
    keep(kvb, kvb_out)
    swap_b = attend(1, kvb, bias_b)
    cot_last = [z_forward(cot_full, half, cot_z[half]) for half in range(2)]
    finish_half(0, swap_a)
    y_share("wd", wd_part)
    y_end("gu", gu_part)
    finish_half(1, swap_b)
    y_end("wd", wd_part)
    for copies in cot_last:
        for copy in copies:
            copy.wait_recv()
    for copy in twins:
        copy.wait_recv()
    for copy in kept:
        if copy is not None:
            copy.wait()
    mail.finish()


def ffn_kernel(
    normed,
    cot,
    wgu,
    wd,
    total,
    gu_half,
    dn_half,
    result_sum,
    x,
    cot_v,
    wgu_v,
    wd_v,
    gb,
    act,
    parts,
    turned,
    down_v,
    gu_in,
    dn_in,
    up1,
    down1,
    up2,
    down2,
    other,
    stage_up,
    stage_down,
    stage,
    res_up1,
    res_down1,
    res_up2,
    res_down2,
    send,
    recv,
    local,
):
    place = here()
    dp, row, col = place
    core = dp % 2
    up, down, pair, twin = along_z(place, 1), along_z(place, 3), pair_of(place), twin_of(place)
    meet([up, down, pair, twin])
    mail = Mail(send, recv)
    order = ((0, 0), (0, 1), (1, 0), (3, 1), (1, 1), (3, 0), (2, 0), (2, 1))
    spots = {half: i for i, half in enumerate(order)}
    rows = normed.shape[0] // 2
    size = rows // 2

    def block(ref, slot, half):
        return ref.at[pl.ds(spots[slot, half] * rows, rows), :]

    def halves(ref, half):
        return ref.at[pl.ds(half * rows, rows), :]

    kept = []

    def keep(source, target):
        kept.append(pltpu.make_async_copy(source, target, local.at[len(kept)]))
        kept[-1].start()
        return len(kept) - 1

    def kept_wait(index):
        kept[index].wait()
        kept[index] = None

    got = {}
    for turn in range(2):
        got["u", turn] = mail.post(halves(normed, turn), block(x, 1, turn), up)
        got["d", 1 - turn] = mail.post(halves(normed, 1 - turn), block(x, 3, 1 - turn), down)
    share = wd.shape[0]
    early = [keep(normed, x.at[pl.ds(0, 2 * rows), :]), keep(wgu, wgu_v)]
    early.append(keep(cot.at[0], cot_v.at[pl.ds(0, 2 * rows), :]))
    early.append(keep(wd, wd_v))
    later = [keep(cot.at[slot, pl.ds(half * rows, rows), :], block(cot_v, slot, half)) for slot, half in order[2:]]
    width = normed.shape[1]
    piece = width // 4

    def dot_nt(left, right):
        return lax.dot_general(left, right, (((1,), (1,)), ((), ())), preferred_element_type=F32)

    def compute(c):
        part = slice(2 * rows * c, 2 * rows * (c + 1))
        for start, size in ((0, 512), (512, share - 512)):
            lanes, above = slice(start, start + size), slice(share + start, share + start + size)
            gate = jnp.dot(x[part, :], wgu_v[:, lanes], preferred_element_type=F32)
            value = jnp.dot(x[part, :], wgu_v[:, above], preferred_element_type=F32)
            grad = dot_nt(cot_v[part, :], wd_v[lanes, :])
            spread = 1.0 / (1.0 + jnp.exp(-gate))
            smooth = gate * spread
            act[part, lanes] = (smooth * value).astype(BF16)
            gb[part, lanes] = (grad * value * (spread * (1.0 + gate * (1.0 - spread)))).astype(BF16)
            gb[part, above] = (grad * smooth).astype(BF16)
        for m in range(3):
            lanes = slice(512 * m, 512 * (m + 1))
            parts[part, lanes] = dot_nt(gb[part, :], wgu_v[lanes, :]).astype(BF16)

    for index in early:
        kept_wait(index)
    compute(0)
    got["u", 0].wait_recv()
    far_up = mail.post(block(x, 1, 0), block(x, 2, 0), up)
    got["d", 1].wait_recv()
    far_down = mail.post(block(x, 3, 1), block(x, 2, 1), down)
    for index in later:
        kept_wait(index)
    compute(1)
    got["u", 1].wait_recv()
    got["d", 0].wait_recv()
    compute(2)
    far_up.wait_recv()
    far_down.wait_recv()
    second = {
        ("d", 0): mail.post(block(parts, 1, 0), down2.at[0], down),
        ("u", 1): mail.post(block(parts, 3, 1), up2.at[1], up),
    }
    compute(3)
    first = {}
    for i in range(2):
        rows_i = pl.ds(i * size, size)
        first["u", i] = mail.post(block(parts, 2, 0).at[rows_i, :], up1.at[i], up)
        first["d", i] = mail.post(block(parts, 2, 1).at[rows_i, :], down1.at[i], down)

    def turn_over(source, target):
        @pl.loop(0, source.shape[1] // LANES)
        def _(t):
            lanes = pl.ds(pl.multiple_of(t * LANES, LANES), LANES)
            target[lanes, :] = source[:, lanes].T

    def forward(i):
        rows_i = pl.ds(i * size, size)
        first["u", i].wait_recv()
        stage_up[i] = (block(parts, 3, 0).at[rows_i, :][...].astype(F32) + up1[i].astype(F32)).astype(BF16)
        second["u", 0, i] = mail.post(stage_up.at[i], up2.at[0, rows_i, :], up)
        first["d", i].wait_recv()
        stage_down[i] = (block(parts, 1, 1).at[rows_i, :][...].astype(F32) + down1[i].astype(F32)).astype(BF16)
        second["d", 1, i] = mail.post(stage_down.at[i], down2.at[1, rows_i, :], down)

    turn_over(x, turned)
    forward(0)
    for m in range(3):
        lanes = slice(512 * m, 512 * (m + 1))

        @pl.loop(0, 4)
        def _(c):
            part = pl.ds(pl.multiple_of(c * 2 * rows, 2 * rows), 2 * rows)
            down_v[part, lanes] = jnp.dot(act[part, :], wd_v[:, lanes], preferred_element_type=F32).astype(BF16)

    forward(1)
    tile = 256
    tiles = 2 * share // tile

    def gu_tiles(first_tile, last_tile):
        @pl.loop(first_tile, last_tile)
        def _(n):
            lanes = pl.ds(pl.multiple_of(((n + (tiles // 2) * (1 - core)) % tiles) * tile, tile), tile)
            wgu_v[:, lanes] = jnp.dot(turned[...], gb[:, lanes], preferred_element_type=F32).astype(BF16)

    swaps = {}

    def settle(i):
        rows_i = pl.ds(i * size, size)
        if i == 0:
            second["d", 0].wait_recv()
            second["u", 1].wait_recv()
        second["u", 0, i].wait_recv()
        second["d", 1, i].wait_recv()
        for half in range(2):
            value = block(parts, 0, half).at[rows_i, :][...].astype(F32)
            value = value + up2[half, rows_i, :].astype(F32) + down2[half, rows_i, :].astype(F32)
            stage[half, rows_i, :] = value.astype(BF16)
            swaps[half, i] = mail.post(stage.at[half, rows_i, :], other.at[half, rows_i, :], pair)

    there = pl.ds(pl.multiple_of((1 - core) * share, LANES), share)
    mine = pl.ds(pl.multiple_of(core * share, LANES), share)
    gu_tiles(0, tiles // 2 + 1)
    shared = [
        mail.post(wgu_v.at[pl.ds(j * piece, piece), there], gu_in.at[j], twin) for j in range(4)
    ]
    settle(0)
    gu_tiles(tiles // 2 + 1, tiles)
    settle(1)
    result = {
        "u1": mail.post(block(down_v, 2, 0), res_up1, up),
        "d1": mail.post(block(down_v, 2, 1), res_down1, down),
        "u2": mail.post(block(down_v, 3, 1), res_up2.at[1], up),
        "d2": mail.post(block(down_v, 1, 0), res_down2.at[0], down),
    }
    turn_over(act, turned)

    @pl.loop(0, width // tile)
    def _(n):
        lanes = pl.ds(pl.multiple_of(n * tile, tile), tile)
        wd_v[:, lanes] = jnp.dot(
            turned[0:share, :], cot_v[:, lanes], preferred_element_type=F32
        ).astype(BF16)

    half_share = share // 2
    rows_there = pl.ds(pl.multiple_of((1 - core) * half_share, 16), half_share)
    rows_mine = pl.ds(pl.multiple_of(core * half_share, 16), half_share)
    shared += [
        mail.post(wd_v.at[rows_there, pl.ds(j * piece, piece)], dn_in.at[j], twin) for j in range(4)
    ]
    result["u1"].wait_recv()
    res_up1[...] = (block(down_v, 3, 0)[...].astype(F32) + res_up1[...].astype(F32)).astype(BF16)
    result["u3"] = mail.post(res_up1, res_up2.at[0], up)
    result["d1"].wait_recv()
    res_down1[...] = (block(down_v, 1, 1)[...].astype(F32) + res_down1[...].astype(F32)).astype(BF16)
    result["d3"] = mail.post(res_down1, res_down2.at[1], down)
    for j in range(4):
        shared[j].wait_recv()
        gu_in[j] = (wgu_v[pl.ds(j * piece, piece), mine].astype(F32) + gu_in[j].astype(F32)).astype(BF16)
        keep(gu_in.at[j], gu_half.at[j])
    for j in range(4):
        shared[4 + j].wait_recv()
        dn_in[j] = (wd_v[rows_mine, pl.ds(j * piece, piece)].astype(F32) + dn_in[j].astype(F32)).astype(BF16)
        keep(dn_in.at[j], dn_half.at[j])
    for half, i in ((0, 0), (1, 0), (0, 1), (1, 1)):
        rows_i = pl.ds(i * size, size)
        swaps[half, i].wait_recv()
        total[pl.ds(half * rows + i * size, size), :] = stage[half, rows_i, :].astype(F32) + other[
            half, rows_i, :
        ].astype(F32)
    for name in ("u2", "d2", "u3", "d3"):
        result[name].wait_recv()
    for half in range(2):
        value = block(down_v, 0, half)[...].astype(F32) + res_up2[half].astype(F32) + res_down2[half].astype(F32)
        result_sum[pl.ds(half * rows, rows), :] = value.astype(BF16)
    for copy in kept:
        if copy is not None:
            copy.wait()
    mail.finish()


def back_kernel(
    total,
    middle,
    cot,
    gains,
    tok,
    normed,
    query,
    kv_a,
    kv_b,
    logs,
    attended,
    tables,
    turned_a,
    turned_b,
    w_in,
    w_out,
    gu,
    dn,
    result_sum,
    gu_out,
    dn_out,
    in_out,
    wo_out,
    grad_out,
    result_out,
    small_out,
    middle_v,
    cot_v,
    tok_v,
    normed_v,
    query_v,
    kva,
    kvb,
    attended_v,
    turned_a_v,
    turned_b_v,
    w_in_v,
    w_out_v,
    gu_v,
    dn_v,
    down_v,
    gain_rows,
    grad_middle,
    grad_low,
    grad_att,
    flat,
    keys_t,
    dkv_a,
    dkv_b,
    low_kv,
    own_kv,
    from_own,
    from_near,
    grad_pre,
    grad_part,
    grad_in,
    part_in,
    rows_out,
    result_rows,
    gu_up1,
    gu_down1,
    gu_up2,
    gu_down2,
    gu_y,
    gu_n,
    gu_s,
    dn_up1,
    dn_down1,
    dn_up2,
    dn_down2,
    dn_y,
    dn_n,
    dn_s,
    in_p,
    in_t,
    in_up1,
    in_down1,
    in_up2,
    in_down2,
    in_s,
    in_n,
    in_z,
    wo_p,
    wo_t,
    wo_up1,
    wo_down1,
    wo_up2,
    wo_down2,
    wo_s,
    wo_n,
    wo_z,
    bias_own,
    gains_own,
    bias_in,
    gains_in,
    small_a,
    small_b,
    small_t,
    small_n,
    send,
    recv,
    local,
):
    place = here()
    dp, row, col = place
    core = dp % 2
    z = dp // Z_STEP
    twin, near, pair = twin_of(place), near_of(place), pair_of(place)
    up, down, far_z = along_z(place, 1), along_z(place, 3), along_z(place, 2)
    right, left = along_y(place, 1), along_y(place, 3)
    meet(
        [along_y(place, s) for s in (1, 2, 3)]
        + [near_of(place, (row + s) % 4) for s in range(4)]
        + [pair_of(place, (row + s) % 4) for s in range(4)]
        + [twin, up, down, far_z]
    )
    mail = Mail(send, recv)
    kept, arrivals = [], []

    def keep(source, target):
        kept.append(pltpu.make_async_copy(source, target, local.at[len(kept)]))
        kept[-1].start()
        return len(kept) - 1

    def kept_wait(index):
        kept[index].wait()
        kept[index] = None

    def even(start, size):
        return pl.ds(pl.multiple_of(start, 16), size)

    def plus(*values):
        result = values[0].astype(F32)
        for value in values[1:]:
            result = result + value.astype(F32)
        return result

    def dot_nt(left, right):
        return lax.dot_general(left, right, (((1,), (1,)), ((), ())), preferred_element_type=F32)

    rows = tok.shape[0] // 2
    width = tok.shape[1]
    piece = width // 4
    spot = even(row * rows, rows)
    own_rows, other_rows = even(col * rows, rows), even((1 - col) * rows, rows)

    def ffn_flow(i):
        if i < 3:
            height = gu.shape[1] // 3
            start, source, held, out = i * height, gu, gu_v, gu_out
            up1, down1, up2, down2 = gu_up1.at[i], gu_down1.at[i], gu_up2.at[i], gu_down2.at[i]
            mine, theirs, done = gu_y.at[i], gu_n.at[i], gu_s.at[i]
        else:
            height = dn.shape[1]
            start, source, held, out = 0, dn, dn_v, dn_out
            up1, down1, up2, down2 = dn_up1, dn_down1, dn_up2, dn_down2
            mine, theirs, done = dn_y, dn_n, dn_s
        half = height // 2
        low, high = pl.ds(start, half), pl.ds(start + half, half)
        first = (mail.post(source.at[2, low, :], up1, right), mail.post(source.at[2, high, :], down1, left))
        straight = (
            mail.post(source.at[1, high, :], up2.at[pl.ds(half, half), :], right),
            mail.post(source.at[3, low, :], down2.at[pl.ds(0, half), :], left),
        )
        yield
        if i in (0, 3):
            kept_wait(loads["gu" if i == 0 else "dn"])
        first[0].wait_recv()
        up1[...] = plus(held[1, low, :], up1[...]).astype(BF16)
        last = [mail.post(up1, up2.at[pl.ds(0, half), :], right)]
        first[1].wait_recv()
        down1[...] = plus(held[3, high, :], down1[...]).astype(BF16)
        last.append(mail.post(down1, down2.at[pl.ds(half, half), :], left))
        yield
        for copy in straight + tuple(last):
            copy.wait_recv()
        mine[...] = plus(held[0, pl.ds(start, height), :], up2[...], down2[...]).astype(BF16)
        swap = mail.post(mine, theirs, near)
        yield
        swap.wait_recv()
        done[...] = plus(mine[...], theirs[...]).astype(BF16)

        def room(slot, which=None):
            begin, size = (start, height) if which is None else (start + which * half, half)
            if i < 3:
                lanes = pl.ds(pl.multiple_of(slot * out.shape[2] // 4, LANES), out.shape[2] // 4)
                return out.at[core, pl.ds(begin, size), lanes]
            return out.at[slot, core, pl.ds(begin, size), :]

        posts = {}
        for turn in range(2):
            for name, device, which in (("u", up, turn), ("d", down, 1 - turn)):
                posts[name, which] = mail.post(done.at[pl.ds(which * half, half), :], room(z, which), device)
        keep(done, room(z))
        arrivals.append(mail.post(done, room(z), twin))
        yield
        posts["u", 0].wait_recv()
        block = room((z + 3) % 4, 0)
        one_more = mail.post(block, block, up)
        posts["d", 1].wait_recv()
        block = room((z + 1) % 4, 1)
        two_more = mail.post(block, block, down)
        yield
        posts["u", 1].wait_recv()
        block = room((z + 3) % 4)
        arrivals.append(mail.post(block, block, twin))
        posts["d", 0].wait_recv()
        block = room((z + 1) % 4)
        arrivals.append(mail.post(block, block, twin))
        one_more.wait_recv()
        two_more.wait_recv()
        block = room((z + 2) % 4)
        arrivals.append(mail.post(block, block, twin))
        yield

    def weight_flow(part, t, up1, down1, up2, down2, total_h, theirs, quarter, out):
        height = t.shape[1]
        half = height // 2
        low, high = pl.ds(0, half), pl.ds(half, half)
        copy = mail.post(part.at[:, even((1 - core) * height, height), :], t, twin)
        yield
        copy.wait_recv()
        for j in range(4):
            t[j] = plus(part[j, even(core * height, height), :], t[j]).astype(BF16)
        first = (mail.post(t.at[2, low, :], up1, right), mail.post(t.at[2, high, :], down1, left))
        straight = (
            mail.post(t.at[1, high, :], up2.at[high, :], right),
            mail.post(t.at[3, low, :], down2.at[low, :], left),
        )
        yield
        first[0].wait_recv()
        up1[...] = plus(t[1, low, :], up1[...]).astype(BF16)
        last = [mail.post(up1, up2.at[low, :], right)]
        first[1].wait_recv()
        down1[...] = plus(t[3, high, :], down1[...]).astype(BF16)
        last.append(mail.post(down1, down2.at[high, :], left))
        yield
        for copy in straight + tuple(last):
            copy.wait_recv()
        total_h[...] = plus(t[0], up2[...], down2[...]).astype(BF16)
        swap = mail.post(total_h, theirs, near)
        yield
        swap.wait_recv()
        t[0] = plus(total_h[...], theirs[...]).astype(BF16)
        size = height // 4
        copies = []
        for step, device in ((1, up), (3, down), (2, far_z)):
            source = t.at[0, even(((z + step) % 4) * size, size), :]
            copies.append(mail.post(source, quarter.at[step - 1], device))
        yield
        for copy in copies:
            copy.wait_recv()
        mine = even(z * size, size)
        theirs[0:size, :] = plus(t[0, mine, :], quarter[0], quarter[1], quarter[2]).astype(BF16)
        place_of = lambda owner: out.at[even(core * height + owner * size, size), :]
        copies = [mail.post(theirs.at[0:size, :], place_of(z), device) for device in (up, down, far_z)]
        arrivals.append(mail.post(theirs.at[0:size, :], place_of(z), twin))
        keep(theirs.at[0:size, :], place_of(z))
        yield
        for copy in copies:
            copy.wait_recv()
        for step in (1, 2, 3):
            block = place_of((z + step) % 4)
            arrivals.append(mail.post(block, block, twin))
        yield

    def result_flow():
        swap = mail.post(result_sum.at[other_rows, :], part_in, pair)
        yield
        kept_wait(loads["down"])
        swap.wait_recv()
        result_rows[...] = (middle_v[own_rows, :] + plus(down_v[own_rows, :], part_in[...])).astype(BF16)
        yield
        spread(result_rows, result_out)
        yield

    def spread(source, target):
        for step in range(4):
            lanes = pl.ds(step * piece, piece)
            if step:
                arrivals.append(mail.post(source.at[:, lanes], target.at[spot, :], along_y(place, step)))
            else:
                keep(source.at[:, lanes], target.at[spot, :])

    flows = [ffn_flow(i) for i in range(4)]
    next(flows[0])
    next(flows[1])
    loads = {}
    for name, source, target in (
        ("middle", middle, middle_v),
        ("cot", cot.at[0], cot_v),
        ("w_out", w_out, w_out_v),
        ("attended", attended, attended_v),
        ("query", query, query_v),
        ("kva", kv_a, kva),
        ("kvb", kv_b, kvb),
        ("ta", turned_a, turned_a_v),
        ("tb", turned_b, turned_b_v),
        ("gu", gu, gu_v),
        ("w_in", w_in, w_in_v),
        ("normed", normed, normed_v),
        ("tok", tok, tok_v),
        ("dn", dn, dn_v),
        ("down", result_sum, down_v),
    ):
        loads[name] = keep(source, target)
    result_steps = result_flow()
    next(result_steps)
    for j in range(4):
        gain_rows[:, j * piece : (j + 1) * piece] = gains[j]

    def norm_back(stream, gain, incoming):
        scale = lax.rsqrt(jnp.sum(stream * stream, -1, keepdims=True) * (1.0 / width) + EPS)
        scaled = incoming * gain
        inner = jnp.sum(scaled * stream, -1, keepdims=True) * (1.0 / width)
        back = scale * scaled - stream * (scale * scale * scale * inner)
        return back, jnp.sum(incoming * stream * scale, 0, keepdims=True)

    kept_wait(loads["middle"])
    kept_wait(loads["cot"])
    gain_ffn_part = jnp.zeros((1, width), F32)
    for half in range(2):
        part = slice(half * rows, (half + 1) * rows)
        back, gain_part = norm_back(middle_v[part, :], gain_rows[1:2, :], total[part, :])
        value = cot_v[part, :].astype(F32) + back
        grad_middle[part, :] = value
        grad_low[part, :] = value.astype(BF16)
        gain_ffn_part = gain_ffn_part + gain_part
    gains_own[...] = jnp.zeros_like(gains_own)
    for j in range(4):
        gains_own[j, 1:2, :] = 0.5 * gain_ffn_part[:, j * piece : (j + 1) * piece]
    kept_wait(loads["w_out"])
    q_width = w_out.shape[0]
    for first in range(0, q_width, 256):
        lanes = slice(first, first + 256)
        grad_att[:, lanes] = dot_nt(grad_low[...], w_out_v[lanes, :]).astype(BF16)

    def turn_over(source, target, count):
        for t in range(count):
            lanes = slice(t * LANES, (t + 1) * LANES)
            target[lanes, 0 : source.shape[0]] = source[:, lanes].T

    kept_wait(loads["attended"])
    turn_over(attended_v, flat, q_width // LANES)
    for j in range(4):
        wo_p[j] = jnp.dot(
            flat[0:q_width, :], grad_low[:, j * piece : (j + 1) * piece], preferred_element_type=F32
        ).astype(BF16)
    wo_steps = weight_flow(wo_p, wo_t, wo_up1, wo_down1, wo_up2, wo_down2, wo_s, wo_n, wo_z, wo_out)
    next(wo_steps)
    next(flows[0])
    next(flows[2])

    for name in ("query", "kva", "kvb", "ta", "tb"):
        kept_wait(loads[name])
    heads = q_width // HEAD_SIZE
    factor = HEAD_SIZE ** (-0.5)

    def unrotate(value, half):
        part = slice(half * rows, (half + 1) * rows)
        return value * tables[0, part, :] + pltpu.roll(value * tables[1, part, :], HEAD_SIZE // 2, 1)

    def attend_back(half, keys, mask, sums):
        part = slice(half * rows, (half + 1) * rows)
        count = keys.shape[0]
        for t in range(count // LANES):
            lanes = slice(t * LANES, (t + 1) * LANES)
            keys_t[:, lanes] = keys[lanes, 0:HEAD_SIZE].T
        sums[...] = jnp.zeros_like(sums)

        @pl.loop(0, heads)
        def _(h):
            lanes = pl.ds(pl.multiple_of(h * HEAD_SIZE, LANES), HEAD_SIZE)
            one, grad = query_v[part, lanes], grad_att[part, lanes]
            raw = dot_nt(keys[:, 0:HEAD_SIZE], one)
            probs = jnp.exp(raw * factor + mask[...] - logs[half * heads + h, 0:1, :])
            grad_probs = dot_nt(keys[:, HEAD_SIZE : 2 * HEAD_SIZE], grad)
            inner = jnp.sum(grad_probs * probs, 0, keepdims=True)
            grad_scores = (probs * (grad_probs - inner)).astype(BF16)
            sums[:, 0:HEAD_SIZE] += jnp.dot(grad_scores, one, preferred_element_type=F32)
            sums[:, HEAD_SIZE : 2 * HEAD_SIZE] += jnp.dot(probs.astype(BF16), grad, preferred_element_type=F32)
            grad_query = jnp.dot(keys_t[:, 0:count], grad_scores, preferred_element_type=F32).T * factor
            grad_pre[part, lanes] = unrotate(grad_query, half).astype(BF16)

    def low_sums(sums, part):
        return (sums[part, 0:HEAD_SIZE] * factor).astype(BF16), sums[part, HEAD_SIZE : 2 * HEAD_SIZE].astype(BF16)

    attend_back(1, kvb, turned_b_v, dkv_b)
    half_rows = kva.shape[0]
    low_part, high_part = slice(0, half_rows), slice(half_rows, 2 * half_rows)
    for target, sums, part in ((low_kv, dkv_b, low_part), (own_kv.at[1], dkv_b, high_part)):
        target[:, 0:HEAD_SIZE], target[:, HEAD_SIZE : 2 * HEAD_SIZE] = low_sums(sums, part)
    kv_got = []
    for step in range(4):
        other = (row + step) % 4
        part = even(other * rows, rows)
        kv_got.append(mail.post(low_kv.at[part, :], from_near.at[step], near_of(place, other)))
        if step:
            kv_got.append(mail.post(own_kv.at[1, part, :], from_own.at[step - 1, 1], along_y(place, step)))
    next(flows[1])
    next(flows[3])
    next(flows[0])
    attend_back(0, kva, turned_a_v, dkv_a)
    target = own_kv.at[0]
    target[:, 0:HEAD_SIZE], target[:, HEAD_SIZE : 2 * HEAD_SIZE] = low_sums(dkv_a, low_part)
    for step in (1, 2, 3):
        part = even(((row + step) % 4) * rows, rows)
        kv_got.append(mail.post(own_kv.at[0, part, :], from_own.at[step - 1, 0], along_y(place, step)))
    next(flows[1])
    next(flows[2])
    next(wo_steps)
    kept_wait(loads["normed"])
    turn_over(normed_v, flat, width // LANES)
    next(result_steps)
    for copy in kv_got:
        copy.wait_recv()
    for half in range(2):
        part = slice(half * rows, (half + 1) * rows)
        value = own_kv[half, spot, :].astype(F32)
        for step in range(3):
            value = value + from_own[step, half].astype(F32)
        if half == 0:
            for step in range(4):
                value = value + from_near[step].astype(F32)
        grad_pre[part, q_width : q_width + HEAD_SIZE] = unrotate(value[:, 0:HEAD_SIZE], half).astype(BF16)
        grad_pre[part, q_width + HEAD_SIZE : q_width + 2 * HEAD_SIZE] = value[:, HEAD_SIZE : 2 * HEAD_SIZE].astype(
            BF16
        )
    kept_wait(loads["w_in"])
    for j in range(4):
        grad_part[:, j * piece : (j + 1) * piece] = dot_nt(grad_pre[...], w_in_v[j]).astype(BF16)
    swap = mail.post(grad_part.at[other_rows, :], grad_in, pair)
    next(flows[0])
    for j in range(4):
        in_p[j] = jnp.dot(flat[j * piece : (j + 1) * piece, :], grad_pre[...], preferred_element_type=F32).astype(BF16)
    in_steps = weight_flow(in_p, in_t, in_up1, in_down1, in_up2, in_down2, in_s, in_n, in_z, in_out)
    next(in_steps)
    bias_own[...] = jnp.zeros_like(bias_own)
    bias_own[0:1, :] = jnp.sum(grad_pre[...].astype(F32), 0, keepdims=True)
    next(flows[1])
    next(flows[2])
    next(flows[3])
    next(in_steps)
    next(wo_steps)
    next(flows[0])
    kept_wait(loads["tok"])
    swap.wait_recv()
    back, gain_part = norm_back(
        tok_v[own_rows, :].astype(F32), gain_rows[0:1, :], plus(grad_part[own_rows, :], grad_in[...])
    )
    rows_out[...] = (grad_middle[own_rows, :] + back).astype(BF16)
    for j in range(4):
        gains_own[j, 0:1, :] = gain_part[:, j * piece : (j + 1) * piece]
    small_copies, small_kept = [], []
    for step in range(4):
        device = along_y(place, step)
        mine = gains_in.at[col * 4 + row]
        if step:
            small_copies.append(mail.post(bias_own, bias_in.at[row], device))
            small_copies.append(mail.post(gains_own.at[step], mine, device))
        else:
            small_kept.append(keep(bias_own, bias_in.at[row]))
            small_kept.append(keep(gains_own.at[step], mine))
        small_copies.append(mail.post(gains_own.at[step], mine, pair_of(place, (row + step) % 4)))
    next(flows[2])
    next(flows[1])
    next(flows[3])
    next(wo_steps)
    next(in_steps)
    spread(rows_out, grad_out)
    next(result_steps)
    next(flows[0])
    for copy in small_copies:
        copy.wait_recv()
    for index in small_kept:
        kept_wait(index)
    small_a[...] = jnp.zeros_like(small_a)
    small_a[0:8, :] = bias_in[0] + bias_in[1] + bias_in[2] + bias_in[3]
    small_a[8:16, 0:piece] = (
        gains_in[0] + gains_in[1] + gains_in[2] + gains_in[3] + gains_in[4] + gains_in[5] + gains_in[6] + gains_in[7]
    )
    small_first = mail.post(small_a, small_t, twin)
    next(in_steps)
    next(wo_steps)
    next(flows[2])
    next(flows[3])
    small_first.wait_recv()
    small_b[...] = small_a[...] + small_t[...]
    small_second = mail.post(small_b, small_n, near)
    next(flows[1])
    next(in_steps)
    next(wo_steps)
    next(flows[2])
    small_second.wait_recv()
    small_t[...] = small_b[...] + small_n[...]
    for device in (up, down, far_z):
        arrivals.append(mail.post(small_t, small_out.at[z], device))
    keep(small_t, small_out.at[z])
    next(flows[3])
    next(in_steps)
    next(wo_steps)
    for steps in [*flows, wo_steps, in_steps, result_steps]:
        for _ in steps:
            pass
    for copy in arrivals:
        copy.wait_recv()
    for copy in kept:
        if copy is not None:
            copy.wait()
    mail.finish()


def on_device(
    tokens,
    cotangent,
    lengths,
    gain_attn,
    w_query,
    key_projection,
    value_projection,
    bias_query,
    key_bias_vector,
    value_bias_vector,
    w_out,
    gain_ffn,
    w_gate,
    w_up,
    w_down,
):
    half_rows, piece = tokens.shape
    width = 4 * piece
    rows = half_rows // 4
    q_width = w_query.shape[1]
    kv_width = key_projection.shape[1]
    heads = q_width // HEAD_SIZE
    hidden = w_gate.shape[1]
    share = -(-hidden // (4 * LANES)) * LANES

    in_width = q_width + 2 * kv_width
    thin = piece // 2
    (
        tok_rows,
        cot_full,
        gains4,
        normed,
        query,
        kv_a,
        kv_b,
        logs,
        attended,
        tables,
        middle,
        mask_a,
        mask_b,
        normed_ffn,
        w_in_full,
        w_out_full,
        w_gu_full,
        w_down_full,
    ) = talk(
        front_kernel,
        0,
        FRONT_COPIES,
        FRONT_LOCAL,
        [
            ((2 * rows, width), BF16),
            ((4, 2 * rows, width), BF16),
            ((4, 8, piece), F32),
            ((2 * rows, width), BF16),
            ((2 * rows, q_width), BF16),
            ((half_rows, 2 * kv_width), BF16),
            ((2 * half_rows, 2 * kv_width), BF16),
            ((2 * heads, 8, rows), F32),
            ((2 * rows, q_width), BF16),
            ((2, 2 * rows, HEAD_SIZE), F32),
            ((2 * rows, width), F32),
            ((half_rows, rows), F32),
            ((2 * half_rows, rows), F32),
            ((2 * rows, width), BF16),
            ((4, piece, in_width), BF16),
            ((q_width, width), BF16),
            ((4, 2, thin, 2 * share), BF16),
            ((share, width), BF16),
        ],
        [ANY] * 2 + [VMEM] * 6 + [ANY] * 7,
        [ANY] * 3 + [VMEM] * 2 + [ANY] * 2 + [VMEM] * 7 + [ANY] * 4,
        [
            pltpu.VMEM((8, LANES), jnp.int32),
            pltpu.VMEM((8, piece), F32),
            pltpu.VMEM((2 * rows, width), BF16),
            pltpu.VMEM((2, 8, LANES), jnp.int32),
            pltpu.VMEM((4, 8, piece), F32),
            pltpu.VMEM((4, piece, in_width), BF16),
            pltpu.VMEM((q_width, width), BF16),
            pltpu.VMEM((2, thin, 2 * share), BF16),
            pltpu.VMEM((share, piece), BF16),
            pltpu.VMEM((thin, LANES), BF16),
            pltpu.VMEM((LANES, piece), BF16),
            pltpu.VMEM((2 * rows, 2 * kv_width), BF16),
            pltpu.VMEM((half_rows, 2 * kv_width), BF16),
            pltpu.VMEM((2 * half_rows, 2 * kv_width), BF16),
            pltpu.VMEM((rows, half_rows), F32),
            pltpu.VMEM((rows, 2 * half_rows), F32),
            pltpu.VMEM((2 * rows, width), BF16),
            pltpu.VMEM((2 * rows, width), BF16),
        ],
        limit=56,
    )(
        tokens,
        cotangent,
        lengths,
        gain_attn[None],
        gain_ffn[None],
        bias_query[None],
        key_bias_vector[None],
        value_bias_vector[None],
        w_query,
        key_projection,
        value_projection,
        w_out,
        w_gate,
        w_up,
        w_down,
    )

    w_both_full = w_gu_full.reshape(width, 2 * share)
    half_block = (2, rows, width)
    grad_normed_ffn, both_half, down_half, result_sum = talk(
        ffn_kernel,
        4,
        34,
        18,
        [
            ((2 * rows, width), F32),
            ((4, piece, share), BF16),
            ((4, share // 2, piece), BF16),
            ((2 * rows, width), BF16),
        ],
        [ANY] * 4,
        [VMEM, ANY, ANY, VMEM],
        [
            pltpu.VMEM(shape, BF16)
            for shape in (
                (8 * rows, width),
                (8 * rows, width),
                (width, 2 * share),
                (share, width),
                (8 * rows, 2 * share),
                (8 * rows, share),
                (8 * rows, width),
                (width, 8 * rows),
                (8 * rows, width),
                (4, piece, share),
                (4, share // 2, piece),
                (2, rows // 2, width),
                (2, rows // 2, width),
                half_block,
                half_block,
                half_block,
                (2, rows // 2, width),
                (2, rows // 2, width),
                half_block,
                (rows, width),
                (rows, width),
                half_block,
                half_block,
            )
        ],
        limit=60,
    )(normed_ffn, cot_full, w_both_full, w_down_full)
    thirds = piece // 3
    q_half, w_half = (thin, in_width), (q_width // 2, piece)
    gu_chunk, dn_chunk = (3, thirds, share), (share // 2, piece)

    def halved(shape):
        return (*shape[:-2], shape[-2] // 2, shape[-1])

    def weight_scratch(shape):
        return [
            (4, 2 * shape[0], shape[1]),
            (4, *shape),
            halved(shape),
            halved(shape),
            shape,
            shape,
            shape,
            shape,
            (3, shape[0] // 4, shape[1]),
        ]

    def scratch(kind, *shapes):
        return [pltpu.VMEM(shape, kind) for shape in shapes]

    gate_up, down_all, in_total, out_total, grad_tokens, result, small_all = talk(
        back_kernel,
        8,
        BACK_COPIES,
        BACK_LOCAL,
        [
            ((2, piece, 4 * share), BF16),
            ((4, 2, share // 2, piece), BF16),
            ((piece, in_width), BF16),
            ((q_width, piece), BF16),
            ((half_rows, piece), BF16),
            ((half_rows, piece), BF16),
            ((4, 16, in_width), F32),
        ],
        [VMEM, ANY, ANY, VMEM] + [ANY] * 5 + [VMEM, ANY, VMEM] + [ANY] * 7,
        [ANY] * 7,
        scratch(F32, (2 * rows, width))
        + scratch(
            BF16,
            (2 * rows, width),
            (2 * rows, width),
            (2 * rows, width),
            (2 * rows, q_width),
            (half_rows, 2 * kv_width),
            (2 * half_rows, 2 * kv_width),
            (2 * rows, q_width),
        )
        + scratch(F32, (half_rows, rows), (2 * half_rows, rows))
        + scratch(
            BF16,
            (4, piece, in_width),
            (q_width, width),
            (4, piece, share),
            (4, share // 2, piece),
            (2 * rows, width),
        )
        + scratch(F32, (8, width), (2 * rows, width))
        + scratch(BF16, (2 * rows, width), (2 * rows, q_width), (width, 2 * rows), (HEAD_SIZE, 2 * half_rows))
        + scratch(F32, (half_rows, 2 * kv_width), (2 * half_rows, 2 * kv_width))
        + scratch(
            BF16,
            (half_rows, 2 * kv_width),
            (2, half_rows, 2 * kv_width),
            (3, 2, rows, 2 * kv_width),
            (4, rows, 2 * kv_width),
            (2 * rows, in_width),
            (2 * rows, width),
            (rows, width),
            (rows, width),
            (rows, width),
            (rows, width),
            halved(gu_chunk),
            halved(gu_chunk),
            gu_chunk,
            gu_chunk,
            gu_chunk,
            gu_chunk,
            gu_chunk,
            halved(dn_chunk),
            halved(dn_chunk),
            dn_chunk,
            dn_chunk,
            dn_chunk,
            dn_chunk,
            dn_chunk,
            *weight_scratch(q_half),
            *weight_scratch(w_half),
        )
        + scratch(F32, (8, in_width), (4, 8, piece), (4, 8, in_width), (8, 8, piece))
        + scratch(F32, *[(16, in_width)] * 4),
        limit=60,
    )(
        grad_normed_ffn,
        middle,
        cot_full,
        gains4,
        tok_rows,
        normed,
        query,
        kv_a,
        kv_b,
        logs,
        attended,
        tables,
        mask_a,
        mask_b,
        w_in_full,
        w_out_full,
        both_half,
        down_half,
        result_sum,
    )
    small_total = small_all[0] + small_all[1] + small_all[2] + small_all[3]
    bias_total = small_total[0]
    gate_total = gate_up[0, :, :hidden].astype(F32)
    up_total = gate_up[1, :, :hidden].astype(F32)
    down_total = down_all.reshape(4 * share, piece)[:hidden].astype(F32)
    upper = q_width + kv_width
    return (
        result.astype(F32),
        grad_tokens.astype(F32),
        small_total[8, :piece],
        in_total[:, :q_width].astype(F32),
        in_total[:, q_width:upper].astype(F32),
        in_total[:, upper:].astype(F32),
        bias_total[:q_width],
        bias_total[q_width:upper],
        bias_total[upper:],
        out_total.astype(F32),
        small_total[9, :piece],
        gate_total,
        up_total,
        down_total,
    )


def solution(mesh):
    placed = (
        P(("dp", "col"), "row"),
        P(("dp", "col"), "row"),
        P("dp", None),
        P("row"),
        P("row", "col"),
        P("row", "col"),
        P("row", "col"),
        P("col"),
        P("col"),
        P("col"),
        P("col", "row"),
        P("row"),
        P("row", "col"),
        P("row", "col"),
        P("col", "row"),
    )
    return jax.shard_map(
        on_device,
        mesh=mesh,
        in_specs=placed,
        out_specs=(
            P(("dp", "col"), "row"),
            P(("dp", "col"), "row"),
            P("row"),
            P("row", "col"),
            P("row", "col"),
            P("row", "col"),
            P("col"),
            P("col"),
            P("col"),
            P("col", "row"),
            P("row"),
            P("row", "col"),
            P("row", "col"),
            P("col", "row"),
        ),
        check_vma=False,
    )
```

```python
import math

import jax
import jax.numpy as jnp
from jax import lax
from jax.experimental import pallas as pl
from jax.experimental.pallas import tpu as pltpu
from jax.sharding import PartitionSpec as P

HEAD_SIZE = 128
EPS = 1e-06
THETA = 1000000.0
LANES = 128
MESH = pl.DeviceIdType.MESH
BF16 = jnp.bfloat16
F32 = jnp.float32
ANY = pl.BlockSpec(memory_space=pl.ANY)
VMEM = pl.BlockSpec(memory_space=pltpu.VMEM)

Z_STEP = 4
FRONT_COPIES = 77
FRONT_LOCAL = 27
BACK_COPIES = 119
BACK_LOCAL = 26


def here():
    return lax.axis_index("dp"), lax.axis_index("row"), lax.axis_index("col")


def flip_near(dp):
    return dp + 2 - 4 * ((dp // 2) % 2)


def pair_of(place, row=None):
    dp, own, col = place
    return flip_near(dp), own if row is None else row, 1 - col


def near_of(place, row=None):
    dp, own, col = place
    return flip_near(dp), own if row is None else row, col


def twin_of(place):
    dp, row, col = place
    return dp + 1 - 2 * (dp % 2), row, col


def along_z(place, step):
    dp, row, col = place
    return (dp + Z_STEP * step) % (4 * Z_STEP), row, col


def along_y(place, step):
    dp, row, col = place
    return dp, (row + step) % 4, col


def meet(peers):
    barrier = pltpu.get_barrier_semaphore()
    for peer in peers:
        pl.semaphore_signal(barrier, inc=1, device_id=peer, device_id_type=MESH)
    pl.semaphore_wait(barrier, len(peers))


class Mail:
    def __init__(self, send, recv):
        self.send, self.recv, self.count, self.sent = send, recv, 0, []

    def post(self, source, target, device):
        index = self.count
        self.count += 1
        copy = pltpu.make_async_remote_copy(
            src_ref=source,
            dst_ref=target,
            send_sem=self.send.at[index],
            recv_sem=self.recv.at[index],
            device_id=device,
            device_id_type=MESH,
        )
        copy.start()
        self.sent.append(copy)
        return copy

    def finish(self):
        assert self.count == self.send.shape[0], (self.count, self.send.shape)
        for copy in self.sent:
            copy.wait_send()


def talk(body, ident, copies, local, outs, in_specs, out_specs, scratch=(), limit=32):
    return pl.pallas_call(
        body,
        out_shape=[jax.ShapeDtypeStruct(*out) for out in outs],
        in_specs=in_specs,
        out_specs=out_specs,
        scratch_shapes=[
            *scratch,
            pltpu.SemaphoreType.DMA((copies,)),
            pltpu.SemaphoreType.DMA((copies,)),
            pltpu.SemaphoreType.DMA((max(local, 1),)),
        ],
        compiler_params=pltpu.CompilerParams(
            collective_id=ident, has_side_effects=True, vmem_limit_bytes=limit << 20
        ),
    )


def front_kernel(
    tok,
    cot,
    lens_in,
    gain_attn,
    gain_ffn,
    bias_q,
    bias_k,
    bias_v,
    wq,
    wk,
    wv,
    wo,
    wg,
    wu,
    wd,
    tok_out,
    cot_full,
    gains_out,
    normed,
    query,
    kva_out,
    kvb_out,
    logs,
    attended,
    tables,
    middle,
    turned_a,
    turned_b,
    normed_ffn,
    w_in_out,
    w_out_out,
    wgu_full,
    wd_full,
    lens,
    gains,
    tok_v,
    lens_v,
    gains_v,
    w_in,
    w_out,
    gu_own,
    wd_own,
    blank_gu,
    blank_wd,
    kv,
    kva,
    kvb,
    bias_a,
    bias_b,
    branch,
    branch_in,
    send,
    recv,
    local,
):
    place = here()
    dp, row, col = place
    z, core = dp // Z_STEP, dp % 2
    twin, pair, up, down = twin_of(place), pair_of(place), along_z(place, 1), along_z(place, 3)
    right, left, near = along_y(place, 1), along_y(place, 3), near_of(place)
    meet(
        [along_y(place, s) for s in (1, 2, 3)]
        + [near_of(place, (row + s) % 4) for s in range(4)]
        + [pair, twin, up, down]
    )
    mail = Mail(send, recv)
    kept = []

    def keep(source, target):
        kept.append(pltpu.make_async_copy(source, target, local.at[len(kept)]))
        kept[-1].start()
        return len(kept) - 1

    def kept_wait(index):
        kept[index].wait()
        kept[index] = None

    def even(start, size):
        return pl.ds(pl.multiple_of(start, 16), size)

    rows, piece = tok.shape[0] // 4, tok.shape[1]
    width = 4 * piece
    own_rows = even(col * rows, rows)
    spot = even(row * rows, rows)

    def spread(source, target):
        got = []
        for step in range(4):
            part = source.at[even(((row + step) % 4) * rows, rows), :]
            lanes = pl.ds(((4 - step) % 4) * piece, piece)
            if step:
                got.append(mail.post(part, target.at[own_rows, lanes], along_y(place, step)))
            else:
                mine = keep(part, target.at[own_rows, lanes])
        return got, mine

    tokens = spread(tok, tok_v)
    lens[...] = jnp.zeros_like(lens)
    lens[0:1, 0 : lens_in.shape[1]] = lens_in[...]
    gains[...] = jnp.zeros_like(gains)
    gains[0:1, :] = gain_attn[...]
    gains[1:2, :] = gain_ffn[...]
    lens_got = mail.post(lens, lens_v.at[col], pair)
    lens_kept = keep(lens, lens_v.at[col])
    gains_kept = keep(gains, gains_v.at[0])
    gains_got = [mail.post(gains, gains_v.at[4 - s], along_y(place, s)) for s in (1, 2, 3)]

    q_width, kv_width = wq.shape[1], wk.shape[1]
    stages = [
        keep(wq, w_in.at[0, :, pl.ds(0, q_width)]),
        keep(wk, w_in.at[0, :, pl.ds(q_width, kv_width)]),
        keep(wv, w_in.at[0, :, pl.ds(q_width + kv_width, kv_width)]),
        keep(wo, w_out.at[:, pl.ds(0, piece)]),
    ]
    share = wd_own.shape[0]
    thin = piece // 2
    sure = share - LANES
    take = pl.multiple_of(z * share, LANES)
    big = []
    for k in range(2):
        for i, source in enumerate((wg, wu)):
            from_rows = pl.ds(k * thin, thin)
            big.append(keep(source.at[from_rows, pl.ds(take, sure)], gu_own.at[k, :, pl.ds(i * share, sure)]))
    big.append(keep(wd.at[pl.ds(take, sure), :], wd_own.at[pl.ds(0, sure), :]))
    blank_gu[...] = jnp.zeros_like(blank_gu)
    blank_wd[...] = jnp.zeros_like(blank_wd)
    first_edge = len(kept)
    edges = []
    for k in range(2):
        for i, source in enumerate((wg, wu)):
            target = gu_own.at[k, :, pl.ds(i * share + sure, LANES)]
            edges.append((source, pl.ds(k * thin, thin), None, target, blank_gu))
    edges.append((wd, None, slice(None), wd_own.at[pl.ds(sure, LANES), :], blank_wd))

    def edge(index, last):
        source, from_rows, _, target, blank = edges[index]
        if last:
            origin = blank
        elif from_rows is None:
            origin = source.at[pl.ds(pl.multiple_of(take + sure, LANES), LANES), :]
        else:
            origin = source.at[from_rows, pl.ds(pl.multiple_of(take + sure, LANES), LANES)]
        return pltpu.make_async_copy(origin, target, local.at[first_edge + index])

    @pl.when(z < 3)
    def _():
        for index in range(len(edges)):
            edge(index, False).start()

    @pl.when(z == 3)
    def _():
        for index in range(len(edges)):
            edge(index, True).start()

    for index in range(len(edges)):
        kept.append(edge(index, True))
        big.append(first_edge + index)

    q_rows, o_rows = thin // 4, w_out.shape[0] // 8

    def in_part(j, owner_z):
        return w_in.at[j, even(core * thin + owner_z * q_rows, q_rows), :]

    def in_parts(owner_z):
        return w_in.at[pl.ds(1, 3), even(core * thin + owner_z * q_rows, q_rows), :]

    def in_side(owner_z, side):
        lanes = pl.ds(side * (w_in.shape[2] // 2), w_in.shape[2] // 2)
        return w_in.at[pl.ds(1, 3), even(core * thin + owner_z * q_rows, q_rows), lanes]

    def out_part(j, owner_z):
        return w_out.at[even(core * 4 * o_rows + owner_z * o_rows, o_rows), pl.ds(j * piece, piece)]

    def out_parts(owner_z):
        return w_out.at[even(core * 4 * o_rows + owner_z * o_rows, o_rows), pl.ds(piece, 3 * piece)]

    def out_side(owner_z, side):
        start = core * 4 * o_rows + owner_z * o_rows + side * (o_rows // 2)
        return w_out.at[even(start, o_rows // 2), pl.ds(piece, 3 * piece)]

    for index in stages:
        kept_wait(index)
    in_got = [mail.post(in_part(0, z), in_part(4 - step, z), along_y(place, step)) for step in (1, 3, 2)]
    out_got = [mail.post(out_part(0, z), out_part(4 - step, z), along_y(place, step)) for step in (1, 3, 2)]
    cotangents = spread(cot, cot_full.at[0])

    def to_pair(spreading, target):
        got, mine = spreading
        kept_wait(mine)
        for copy in got:
            copy.wait_recv()
        return mail.post(target.at[own_rows, :], target.at[own_rows, :], pair)

    tokens_pair = to_pair(tokens, tok_v)
    shares = []

    def give(part):
        shares.append(mail.post(part, part, twin))

    def z_first(side):
        copies = {}
        for turn in range(2):
            copies["u", turn] = mail.post(side(z, turn), side(z, turn), up)
            copies["d", 1 - turn] = mail.post(side(z, 1 - turn), side(z, 1 - turn), down)
        return copies

    below, above, across = (z + 3) % 4, (z + 1) % 4, (z + 2) % 4

    def z_second(side, whole, copies):
        copies["u", 0].wait_recv()
        far_up = mail.post(side(below, 0), side(below, 0), up)
        copies["d", 1].wait_recv()
        far_down = mail.post(side(above, 1), side(above, 1), down)
        copies["u", 1].wait_recv()
        give(whole(below))
        copies["d", 0].wait_recv()
        give(whole(above))
        return far_up, far_down

    def z_third(whole, copies):
        for copy in copies:
            copy.wait_recv()
        give(whole(across))

    for copy in in_got:
        copy.wait_recv()
    in_z = z_first(in_side)
    give(in_parts(z))
    for index in big:
        kept_wait(index)
    x_lo = (dp // 2) % 2
    gu_half, wd_half = thin // 4, share // 4

    def gu_part(j, which=None, owner=x_lo):
        start, size = (0, 2 * gu_half) if which is None else (which * gu_half, gu_half)
        return wgu_full.at[j, core, even(owner * 2 * gu_half + start, size), :]

    def gu_whole(j):
        return wgu_full.at[j, core]

    def wd_part(j, which=None):
        start, size = (0, 2 * wd_half) if which is None else (which * wd_half, wd_half)
        return wd_full.at[even(core * 2 * wd_half + start, size), pl.ds(j * piece, piece)]

    def gu_source(which):
        return gu_own.at[core, even((x_lo * 2 + which) * gu_half, gu_half), :]

    def wd_source(which):
        return wd_own.at[even((core * 2 + which) * wd_half, wd_half), :]

    y_ring, near_gu, twins = {}, [], []

    def y_start(name, source, part):
        for turn in range(2):
            y_ring[name, "r", turn] = mail.post(source(turn), part(3, turn), right)
            y_ring[name, "l", 1 - turn] = mail.post(source(1 - turn), part(1, 1 - turn), left)

    def y_forward(name, part):
        y_ring[name, "r", 0].wait_recv()
        y_ring[name, "fr"] = mail.post(part(3, 0), part(2, 0), right)
        y_ring[name, "l", 1].wait_recv()
        y_ring[name, "fl"] = mail.post(part(1, 1), part(2, 1), left)

    def y_share(name, part, queue, device):
        y_ring[name, "r", 1].wait_recv()
        queue.append(mail.post(part(3), part(3), device))
        y_ring[name, "l", 0].wait_recv()
        queue.append(mail.post(part(1), part(1), device))

    def y_end(name, part, queue, device):
        y_ring[name, "fr"].wait_recv()
        y_ring[name, "fl"].wait_recv()
        queue.append(mail.post(part(2), part(2), device))

    y_start("gu", gu_source, gu_part)
    keep(gu_own, wgu_full.at[0])
    keep(wd_own, wd_full.at[:, pl.ds(0, piece)])
    for copy in out_got:
        copy.wait_recv()
    give(out_parts(z))

    kept_wait(lens_kept)
    lens_got.wait_recv()
    half_rows = 4 * rows

    def segment_of(which, index):
        end_0 = lens_v[which, 0:1, 0:1]
        end_1 = end_0 + lens_v[which, 0:1, 1:2]
        past_0 = (index >= end_0).astype(jnp.int32)
        past_1 = (index >= end_1).astype(jnp.int32)
        start = jnp.where(past_1 > 0, end_1, jnp.where(past_0 > 0, end_0, 0))
        return past_0 + past_1, start

    lane = lax.broadcasted_iota(jnp.int32, (rows, HEAD_SIZE), 1)
    half_lane = jnp.where(lane >= HEAD_SIZE // 2, lane - HEAD_SIZE // 2, lane).astype(F32)
    inverse = jnp.exp(half_lane * (-2.0 * math.log(THETA) / HEAD_SIZE))
    for which, mask, mask_t, key_count in ((0, bias_a, turned_a, half_rows), (1, bias_b, turned_b, 2 * half_rows)):
        index = lax.broadcasted_iota(jnp.int32, (rows, HEAD_SIZE), 0) + (row * rows + which * half_rows)
        _, start = segment_of(which, index)
        turn = (index - start).astype(F32) * inverse
        tables[0, which * rows : (which + 1) * rows, :] = jnp.cos(turn)
        sine = jnp.sin(turn)
        tables[1, which * rows : (which + 1) * rows, :] = jnp.where(lane >= HEAD_SIZE // 2, sine, -sine)
        at = lax.broadcasted_iota(jnp.int32, (rows, key_count), 0) + (row * rows + which * half_rows)
        keys = lax.broadcasted_iota(jnp.int32, (rows, key_count), 1)
        allowed = jnp.logical_and(segment_of(which, at)[0] == segment_of(which, keys)[0], keys <= at)
        mask[...] = jnp.where(allowed, 0.0, -1e30)
        at = lax.broadcasted_iota(jnp.int32, (key_count, rows), 1) + (row * rows + which * half_rows)
        keys = lax.broadcasted_iota(jnp.int32, (key_count, rows), 0)
        allowed = jnp.logical_and(segment_of(which, at)[0] == segment_of(which, keys)[0], keys <= at)
        mask_t[...] = jnp.where(allowed, 0.0, -1e30)

    kept_wait(gains_kept)
    for copy in gains_got:
        copy.wait_recv()
    keep(gains_v, gains_out)

    def normalise(value, which):
        scale = lax.rsqrt(jnp.sum(value * value, -1, keepdims=True) * (1.0 / width) + EPS)
        return [
            (value[:, j * piece : (j + 1) * piece] * scale * gains_v[j, which : which + 1, :]).astype(BF16)
            for j in range(4)
        ]

    def norm_rows(which):
        part = pl.ds(pl.multiple_of(which * rows, rows), rows)
        for j, block in enumerate(normalise(tok_v[part, :].astype(F32), 0)):
            normed[part, pl.ds(j * piece, piece)] = block

    norm_rows(col)
    in_far = z_second(in_side, in_parts, in_z)
    out_z = z_first(out_side)
    tokens_pair.wait_recv()
    keep(tok_v, tok_out)
    norm_rows(1 - col)
    cot_pair = to_pair(cotangents, cot_full.at[0])
    z_third(in_parts, in_far)
    for copy in shares:
        copy.wait_recv()
    shares.clear()
    keep(w_in, w_in_out)

    in_width = w_in.shape[2]

    def project(lanes, bias):
        weights = w_in[:, :, lanes]
        weights = weights.reshape(4 * weights.shape[1], weights.shape[2])
        return jnp.dot(normed[...], weights, preferred_element_type=F32) + bias

    def rotate(value):
        return value * tables[0] + pltpu.roll(value, HEAD_SIZE // 2, 1) * tables[1]

    key_value = project(slice(q_width, in_width), jnp.concatenate([bias_k[...], bias_v[...]], 1))
    kv[:, 0:kv_width] = rotate(key_value[:, 0:kv_width]).astype(BF16)
    kv[:, kv_width : 2 * kv_width] = key_value[:, kv_width : 2 * kv_width].astype(BF16)
    a_rows, b_rows = pl.ds(0, rows), pl.ds(rows, rows)
    high_spot = even(half_rows + row * rows, rows)
    a_got, b_got = [], []
    for step in (1, 2, 3):
        a_got.append(mail.post(kv.at[a_rows, :], kva.at[spot, :], along_y(place, step)))
    for step in range(4):
        b_got.append(mail.post(kv.at[a_rows, :], kvb.at[spot, :], near_of(place, (row + step) % 4)))
        if step:
            b_got.append(mail.post(kv.at[b_rows, :], kvb.at[high_spot, :], along_y(place, step)))
    kva[spot, :] = kv[a_rows, :]
    kvb[high_spot, :] = kv[b_rows, :]
    for first in range(0, q_width, 2 * HEAD_SIZE):
        value = project(slice(first, first + 2 * HEAD_SIZE), bias_q[:, first : first + 2 * HEAD_SIZE])
        for i in range(2):
            lanes = slice(first + i * HEAD_SIZE, first + (i + 1) * HEAD_SIZE)
            query[:, lanes] = rotate(value[:, i * HEAD_SIZE : (i + 1) * HEAD_SIZE]).astype(BF16)

    y_forward("gu", gu_part)
    y_start("wd", wd_source, wd_part)
    out_far = z_second(out_side, out_parts, out_z)
    heads = q_width // HEAD_SIZE
    factor = HEAD_SIZE ** (-0.5)

    def attend(half, keys, mask):
        part = slice(half * rows, (half + 1) * rows)

        @pl.loop(0, heads)
        def _(h):
            lanes = pl.ds(pl.multiple_of(h * HEAD_SIZE, LANES), HEAD_SIZE)
            raw = lax.dot_general(
                query[part, lanes], keys[:, 0:HEAD_SIZE], (((1,), (1,)), ((), ())), preferred_element_type=F32
            )
            scores = raw * factor + mask[...]
            peak = jnp.max(scores, -1, keepdims=True)
            raised = jnp.exp(scores - peak)
            total = jnp.sum(raised, -1, keepdims=True)
            probs = (raised * (1.0 / total)).astype(BF16)
            out = jnp.dot(probs, keys[:, HEAD_SIZE : 2 * HEAD_SIZE], preferred_element_type=F32)
            attended[part, lanes] = out.astype(BF16)
            logs[half * heads + h] = jnp.broadcast_to(peak + jnp.log(total), (rows, LANES)).T[0:8, :]

        for first in range(0, width, piece):
            lanes = slice(first, first + piece)
            branch[part, lanes] = jnp.dot(
                attended[part, :], w_out[:, lanes], preferred_element_type=F32
            ).astype(BF16)
        return mail.post(branch.at[part, :], branch_in.at[part, :], pair)

    def finish_half(half, copy):
        part = slice(half * rows, (half + 1) * rows)
        copy.wait_recv()
        value = tok_v[part, :].astype(F32) + (branch[part, :].astype(F32) + branch_in[part, :].astype(F32))
        middle[part, :] = value
        for j, block in enumerate(normalise(value, 1)):
            normed_ffn[part, j * piece : (j + 1) * piece] = block

    def z_send(source, target, half):
        part = pl.ds(half * rows, rows)
        return (
            mail.post(source.at[part, :], target.at[1, part, :], up),
            mail.post(source.at[part, :], target.at[3, part, :], down),
        )

    def z_forward(target, half, copies):
        part = pl.ds(half * rows, rows)
        if half == 0:
            copies[0].wait_recv()
            return copies[1], mail.post(target.at[1, part, :], target.at[2, part, :], up)
        copies[1].wait_recv()
        return copies[0], mail.post(target.at[3, part, :], target.at[2, part, :], down)

    cot_pair.wait_recv()
    cot_z = [z_send(cot_full.at[0], cot_full, half) for half in range(2)]
    for copy in a_got:
        copy.wait_recv()
    keep(kva, kva_out)
    z_third(out_parts, out_far)
    for copy in shares:
        copy.wait_recv()
    keep(w_out, w_out_out)
    swap_a = attend(0, kva, bias_a)
    y_share("gu", gu_part, near_gu, near)
    for copy in b_got:
        copy.wait_recv()
    keep(kvb, kvb_out)
    swap_b = attend(1, kvb, bias_b)
    y_end("gu", gu_part, near_gu, near)
    y_forward("wd", wd_part)
    finish_half(0, swap_a)
    cot_last = [z_forward(cot_full, half, cot_z[half]) for half in range(2)]
    y_share("wd", wd_part, twins, twin)
    finish_half(1, swap_b)
    for j, copy in zip((3, 1, 2), near_gu):
        copy.wait_recv()
        twins.append(mail.post(gu_whole(j), gu_whole(j), twin))
    y_end("wd", wd_part, twins, twin)
    for copies in cot_last:
        for copy in copies:
            copy.wait_recv()
    for copy in twins:
        copy.wait_recv()
    for copy in kept:
        if copy is not None:
            copy.wait()
    mail.finish()


def ffn_kernel(
    normed,
    cot,
    wgu,
    wd,
    total,
    gu_sum,
    dn_half,
    result_sum,
    x,
    cot_v,
    wgu_v,
    wd_v,
    gb,
    act,
    parts,
    turned,
    down_v,
    gu_in,
    dn_in,
    up1,
    down1,
    up2,
    down2,
    other,
    stage_up,
    stage_down,
    stage,
    res_up1,
    res_down1,
    res_up2,
    res_down2,
    gu_up1,
    gu_down1,
    gu_up2,
    gu_down2,
    send,
    recv,
    local,
):
    place = here()
    dp, row, col = place
    core = dp % 2
    up, down, pair, twin = along_z(place, 1), along_z(place, 3), pair_of(place), twin_of(place)
    right, left = along_y(place, 1), along_y(place, 3)
    meet([up, down, pair, twin, right, left])
    mail = Mail(send, recv)
    order = ((0, 0), (0, 1), (1, 0), (3, 1), (1, 1), (3, 0), (2, 0), (2, 1))
    spots = {half: i for i, half in enumerate(order)}
    rows = normed.shape[0] // 2
    size = rows // 2

    def block(ref, slot, half):
        return ref.at[pl.ds(spots[slot, half] * rows, rows), :]

    def halves(ref, half):
        return ref.at[pl.ds(half * rows, rows), :]

    kept = []

    def keep(source, target):
        kept.append(pltpu.make_async_copy(source, target, local.at[len(kept)]))
        kept[-1].start()
        return len(kept) - 1

    def kept_wait(index):
        kept[index].wait()
        kept[index] = None

    got = {}
    for turn in range(2):
        got["u", turn] = mail.post(halves(normed, turn), block(x, 1, turn), up)
        got["d", 1 - turn] = mail.post(halves(normed, 1 - turn), block(x, 3, 1 - turn), down)
    share = wd.shape[0]
    early = [keep(normed, x.at[pl.ds(0, 2 * rows), :]), keep(wgu, wgu_v)]
    early.append(keep(cot.at[0], cot_v.at[pl.ds(0, 2 * rows), :]))
    early.append(keep(wd, wd_v))
    later = [keep(cot.at[slot, pl.ds(half * rows, rows), :], block(cot_v, slot, half)) for slot, half in order[2:]]
    width = normed.shape[1]
    piece = width // 4

    def dot_nt(left, right):
        return lax.dot_general(left, right, (((1,), (1,)), ((), ())), preferred_element_type=F32)

    def compute(c):
        part = slice(2 * rows * c, 2 * rows * (c + 1))
        for start, size in ((0, 512), (512, share - 512)):
            lanes, above = slice(start, start + size), slice(share + start, share + start + size)
            gate = jnp.dot(x[part, :], wgu_v[:, lanes], preferred_element_type=F32)
            value = jnp.dot(x[part, :], wgu_v[:, above], preferred_element_type=F32)
            grad = dot_nt(cot_v[part, :], wd_v[lanes, :])
            spread = 1.0 / (1.0 + jnp.exp(-gate))
            smooth = gate * spread
            act[part, lanes] = (smooth * value).astype(BF16)
            gb[part, lanes] = (grad * value * (spread * (1.0 + gate * (1.0 - spread)))).astype(BF16)
            gb[part, above] = (grad * smooth).astype(BF16)
        for m in range(3):
            lanes = slice(512 * m, 512 * (m + 1))
            parts[part, lanes] = dot_nt(gb[part, :], wgu_v[lanes, :]).astype(BF16)

    for index in early:
        kept_wait(index)
    compute(0)
    got["u", 0].wait_recv()
    far_up = mail.post(block(x, 1, 0), block(x, 2, 0), up)
    got["d", 1].wait_recv()
    far_down = mail.post(block(x, 3, 1), block(x, 2, 1), down)
    for index in later:
        kept_wait(index)
    compute(1)
    got["u", 1].wait_recv()
    got["d", 0].wait_recv()
    compute(2)
    far_up.wait_recv()
    far_down.wait_recv()
    second = {
        ("d", 0): mail.post(block(parts, 1, 0), down2.at[0], down),
        ("u", 1): mail.post(block(parts, 3, 1), up2.at[1], up),
    }
    compute(3)
    first = {}
    for i in range(2):
        rows_i = pl.ds(i * size, size)
        first["u", i] = mail.post(block(parts, 2, 0).at[rows_i, :], up1.at[i], up)
        first["d", i] = mail.post(block(parts, 2, 1).at[rows_i, :], down1.at[i], down)

    def turn_over(source, target):
        @pl.loop(0, source.shape[1] // LANES)
        def _(t):
            lanes = pl.ds(pl.multiple_of(t * LANES, LANES), LANES)
            target[lanes, :] = source[:, lanes].T

    def forward(i):
        rows_i = pl.ds(i * size, size)
        first["u", i].wait_recv()
        stage_up[i] = (block(parts, 3, 0).at[rows_i, :][...].astype(F32) + up1[i].astype(F32)).astype(BF16)
        second["u", 0, i] = mail.post(stage_up.at[i], up2.at[0, rows_i, :], up)
        first["d", i].wait_recv()
        stage_down[i] = (block(parts, 1, 1).at[rows_i, :][...].astype(F32) + down1[i].astype(F32)).astype(BF16)
        second["d", 1, i] = mail.post(stage_down.at[i], down2.at[1, rows_i, :], down)

    turn_over(x, turned)
    forward(0)
    for m in range(3):
        lanes = slice(512 * m, 512 * (m + 1))

        @pl.loop(0, 4)
        def _(c):
            part = pl.ds(pl.multiple_of(c * 2 * rows, 2 * rows), 2 * rows)
            down_v[part, lanes] = jnp.dot(act[part, :], wd_v[:, lanes], preferred_element_type=F32).astype(BF16)

    forward(1)
    tile = 256
    tiles = 2 * share // tile

    def gu_tiles(first_tile, last_tile):
        @pl.loop(first_tile, last_tile)
        def _(n):
            lanes = pl.ds(pl.multiple_of(((n + (tiles // 2) * (1 - core)) % tiles) * tile, tile), tile)
            wgu_v[:, lanes] = jnp.dot(turned[...], gb[:, lanes], preferred_element_type=F32).astype(BF16)

    swaps = {}

    def settle(i):
        rows_i = pl.ds(i * size, size)
        if i == 0:
            second["d", 0].wait_recv()
            second["u", 1].wait_recv()
        second["u", 0, i].wait_recv()
        second["d", 1, i].wait_recv()
        for half in range(2):
            value = block(parts, 0, half).at[rows_i, :][...].astype(F32)
            value = value + up2[half, rows_i, :].astype(F32) + down2[half, rows_i, :].astype(F32)
            stage[half, rows_i, :] = value.astype(BF16)
            swaps[half, i] = mail.post(stage.at[half, rows_i, :], other.at[half, rows_i, :], pair)

    there = pl.ds(pl.multiple_of((1 - core) * share, LANES), share)
    mine = pl.ds(pl.multiple_of(core * share, LANES), share)
    gu_tiles(0, tiles // 2 + 1)
    shared = [
        mail.post(wgu_v.at[pl.ds(j * piece, piece), there], gu_in.at[j], twin) for j in range(4)
    ]
    settle(0)
    gu_tiles(tiles // 2 + 1, tiles)
    settle(1)
    result = {
        "u1": mail.post(block(down_v, 2, 0), res_up1, up),
        "d1": mail.post(block(down_v, 2, 1), res_down1, down),
        "u2": mail.post(block(down_v, 3, 1), res_up2.at[1], up),
        "d2": mail.post(block(down_v, 1, 0), res_down2.at[0], down),
    }
    for j in range(4):
        shared[j].wait_recv()
        gu_in[j] = (wgu_v[pl.ds(j * piece, piece), mine].astype(F32) + gu_in[j].astype(F32)).astype(BF16)

    def ring_y(i):
        height = piece // 3
        half = height // 2
        low, high = pl.ds(i * height, half), pl.ds(i * height + half, half)
        one, two, three, four = gu_up1.at[i], gu_down1.at[i], gu_up2.at[i], gu_down2.at[i]
        begin = (mail.post(gu_in.at[2, low, :], one, right), mail.post(gu_in.at[2, high, :], two, left))
        straight = [
            mail.post(gu_in.at[1, high, :], three.at[pl.ds(half, half), :], right),
            mail.post(gu_in.at[3, low, :], four.at[pl.ds(0, half), :], left),
        ]
        yield
        begin[0].wait_recv()
        one[...] = (gu_in[1, low, :].astype(F32) + one[...].astype(F32)).astype(BF16)
        straight.append(mail.post(one, three.at[pl.ds(0, half), :], right))
        begin[1].wait_recv()
        two[...] = (gu_in[3, high, :].astype(F32) + two[...].astype(F32)).astype(BF16)
        straight.append(mail.post(two, four.at[pl.ds(half, half), :], left))
        yield
        for copy in straight:
            copy.wait_recv()
        part = pl.ds(i * height, height)
        value = gu_in[0, part, :].astype(F32) + three[...].astype(F32) + four[...].astype(F32)
        gu_sum[part, :] = value.astype(BF16)
        yield

    rings = [ring_y(i) for i in range(3)]
    next(rings[0])
    next(rings[1])
    turn_over(act, turned)

    @pl.loop(0, width // tile)
    def _(n):
        lanes = pl.ds(pl.multiple_of(n * tile, tile), tile)
        wd_v[:, lanes] = jnp.dot(
            turned[0:share, :], cot_v[:, lanes], preferred_element_type=F32
        ).astype(BF16)

    half_share = share // 2
    rows_there = pl.ds(pl.multiple_of((1 - core) * half_share, 16), half_share)
    rows_mine = pl.ds(pl.multiple_of(core * half_share, 16), half_share)
    shared += [
        mail.post(wd_v.at[rows_there, pl.ds(j * piece, piece)], dn_in.at[j], twin) for j in range(4)
    ]
    next(rings[0])
    next(rings[2])
    for j in range(4):
        shared[4 + j].wait_recv()
        dn_in[j] = (wd_v[rows_mine, pl.ds(j * piece, piece)].astype(F32) + dn_in[j].astype(F32)).astype(BF16)
        keep(dn_in.at[j], dn_half.at[j])
    next(rings[1])
    result["u1"].wait_recv()
    res_up1[...] = (block(down_v, 3, 0)[...].astype(F32) + res_up1[...].astype(F32)).astype(BF16)
    result["u3"] = mail.post(res_up1, res_up2.at[0], up)
    result["d1"].wait_recv()
    res_down1[...] = (block(down_v, 1, 1)[...].astype(F32) + res_down1[...].astype(F32)).astype(BF16)
    result["d3"] = mail.post(res_down1, res_down2.at[1], down)
    next(rings[0])
    next(rings[2])
    for half, i in ((0, 0), (1, 0), (0, 1), (1, 1)):
        rows_i = pl.ds(i * size, size)
        swaps[half, i].wait_recv()
        total[pl.ds(half * rows + i * size, size), :] = stage[half, rows_i, :].astype(F32) + other[
            half, rows_i, :
        ].astype(F32)
    next(rings[1])
    next(rings[2])
    for name in ("u2", "d2", "u3", "d3"):
        result[name].wait_recv()
    for half in range(2):
        value = block(down_v, 0, half)[...].astype(F32) + res_up2[half].astype(F32) + res_down2[half].astype(F32)
        result_sum[pl.ds(half * rows, rows), :] = value.astype(BF16)
    for copy in kept:
        if copy is not None:
            copy.wait()
    mail.finish()


def back_kernel(
    total,
    middle,
    cot,
    gains,
    tok,
    normed,
    query,
    kv_a,
    kv_b,
    logs,
    attended,
    tables,
    turned_a,
    turned_b,
    w_in,
    w_out,
    gu,
    dn,
    result_sum,
    gu_out,
    dn_out,
    in_out,
    wo_out,
    grad_out,
    result_out,
    small_out,
    middle_v,
    cot_v,
    tok_v,
    normed_v,
    query_v,
    kva,
    kvb,
    attended_v,
    turned_a_v,
    turned_b_v,
    w_in_v,
    w_out_v,
    gu_v,
    dn_v,
    down_v,
    gain_rows,
    grad_middle,
    grad_low,
    grad_att,
    flat,
    keys_t,
    dkv_a,
    dkv_b,
    low_kv,
    own_kv,
    from_own,
    from_near,
    grad_pre,
    grad_part,
    grad_in,
    part_in,
    rows_out,
    result_rows,
    gu_n,
    gu_s,
    dn_up1,
    dn_down1,
    dn_up2,
    dn_down2,
    dn_y,
    dn_n,
    dn_s,
    in_p,
    in_t,
    in_up1,
    in_down1,
    in_up2,
    in_down2,
    in_s,
    in_n,
    in_z,
    wo_p,
    wo_t,
    wo_up1,
    wo_down1,
    wo_up2,
    wo_down2,
    wo_s,
    wo_n,
    wo_z,
    bias_own,
    gains_own,
    bias_in,
    gains_in,
    small_a,
    small_b,
    small_t,
    small_n,
    send,
    recv,
    local,
):
    place = here()
    dp, row, col = place
    core = dp % 2
    z = dp // Z_STEP
    twin, near, pair = twin_of(place), near_of(place), pair_of(place)
    up, down, far_z = along_z(place, 1), along_z(place, 3), along_z(place, 2)
    right, left = along_y(place, 1), along_y(place, 3)
    meet(
        [along_y(place, s) for s in (1, 2, 3)]
        + [near_of(place, (row + s) % 4) for s in range(4)]
        + [pair_of(place, (row + s) % 4) for s in range(4)]
        + [twin, up, down, far_z]
    )
    mail = Mail(send, recv)
    kept, arrivals = [], []

    def keep(source, target):
        kept.append(pltpu.make_async_copy(source, target, local.at[len(kept)]))
        kept[-1].start()
        return len(kept) - 1

    def kept_wait(index):
        kept[index].wait()
        kept[index] = None

    def even(start, size):
        return pl.ds(pl.multiple_of(start, 16), size)

    def plus(*values):
        result = values[0].astype(F32)
        for value in values[1:]:
            result = result + value.astype(F32)
        return result

    def dot_nt(left, right):
        return lax.dot_general(left, right, (((1,), (1,)), ((), ())), preferred_element_type=F32)

    rows = tok.shape[0] // 2
    width = tok.shape[1]
    piece = width // 4
    spot = even(row * rows, rows)
    own_rows, other_rows = even(col * rows, rows), even((1 - col) * rows, rows)

    def ffn_flow(i):
        if i < 3:
            height = gu.shape[0] // 3
            start = i * height
            theirs, done = gu_n.at[i], gu_s.at[i]
            mine = gu_v.at[pl.ds(start, height), :]
            swap = mail.post(gu.at[pl.ds(start, height), :], theirs, near)
            half = height // 2
            yield
            if i == 0:
                kept_wait(loads["gu"])
        else:
            height = dn.shape[1]
            start, mine, theirs, done = 0, dn_y, dn_n, dn_s
            half = height // 2
            low, high = pl.ds(start, half), pl.ds(start + half, half)
            first = (mail.post(dn.at[2, low, :], dn_up1, right), mail.post(dn.at[2, high, :], dn_down1, left))
            straight = (
                mail.post(dn.at[1, high, :], dn_up2.at[pl.ds(half, half), :], right),
                mail.post(dn.at[3, low, :], dn_down2.at[pl.ds(0, half), :], left),
            )
            yield
            kept_wait(loads["dn"])
            first[0].wait_recv()
            dn_up1[...] = plus(dn_v[1, low, :], dn_up1[...]).astype(BF16)
            last = [mail.post(dn_up1, dn_up2.at[pl.ds(0, half), :], right)]
            first[1].wait_recv()
            dn_down1[...] = plus(dn_v[3, high, :], dn_down1[...]).astype(BF16)
            last.append(mail.post(dn_down1, dn_down2.at[pl.ds(half, half), :], left))
            yield
            for copy in straight + tuple(last):
                copy.wait_recv()
            mine[...] = plus(dn_v[0], dn_up2[...], dn_down2[...]).astype(BF16)
            swap = mail.post(mine, theirs, near)
            yield
        swap.wait_recv()
        done[...] = plus(mine[...], theirs[...]).astype(BF16)

        def room(slot, which=None):
            begin, size = (start, height) if which is None else (start + which * half, half)
            if i < 3:
                share = gu_out.shape[2] // 4
                lanes = pl.ds(pl.multiple_of(slot * share, LANES), share)
                return gu_out.at[core, pl.ds(begin, size), lanes]
            return dn_out.at[even((slot * 2 + core) * height + begin, size), :]

        posts = {}
        for turn in range(2):
            for name, device, which in (("u", up, turn), ("d", down, 1 - turn)):
                posts[name, which] = mail.post(done.at[pl.ds(which * half, half), :], room(z, which), device)
        keep(done, room(z))
        arrivals.append(mail.post(done, room(z), twin))
        yield
        posts["u", 0].wait_recv()
        block = room((z + 3) % 4, 0)
        one_more = mail.post(block, block, up)
        posts["d", 1].wait_recv()
        block = room((z + 1) % 4, 1)
        two_more = mail.post(block, block, down)
        yield
        posts["u", 1].wait_recv()
        block = room((z + 3) % 4)
        arrivals.append(mail.post(block, block, twin))
        posts["d", 0].wait_recv()
        block = room((z + 1) % 4)
        arrivals.append(mail.post(block, block, twin))
        one_more.wait_recv()
        two_more.wait_recv()
        block = room((z + 2) % 4)
        arrivals.append(mail.post(block, block, twin))
        yield

    def weight_flow(part, t, up1, down1, up2, down2, total_h, theirs, quarter, out):
        height = t.shape[1]
        half = height // 2
        low, high = pl.ds(0, half), pl.ds(half, half)
        copy = mail.post(part.at[:, even((1 - core) * height, height), :], t, twin)
        yield
        copy.wait_recv()
        for j in range(4):
            t[j] = plus(part[j, even(core * height, height), :], t[j]).astype(BF16)
        first = (mail.post(t.at[2, low, :], up1, right), mail.post(t.at[2, high, :], down1, left))
        straight = (
            mail.post(t.at[1, high, :], up2.at[high, :], right),
            mail.post(t.at[3, low, :], down2.at[low, :], left),
        )
        yield
        first[0].wait_recv()
        up1[...] = plus(t[1, low, :], up1[...]).astype(BF16)
        last = [mail.post(up1, up2.at[low, :], right)]
        first[1].wait_recv()
        down1[...] = plus(t[3, high, :], down1[...]).astype(BF16)
        last.append(mail.post(down1, down2.at[high, :], left))
        yield
        for copy in straight + tuple(last):
            copy.wait_recv()
        total_h[...] = plus(t[0], up2[...], down2[...]).astype(BF16)
        swap = mail.post(total_h, theirs, near)
        yield
        swap.wait_recv()
        t[0] = plus(total_h[...], theirs[...]).astype(BF16)
        size = height // 4
        copies = []
        for step, device in ((1, up), (3, down), (2, far_z)):
            source = t.at[0, even(((z + step) % 4) * size, size), :]
            copies.append(mail.post(source, quarter.at[step - 1], device))
        yield
        for copy in copies:
            copy.wait_recv()
        mine = even(z * size, size)
        theirs[0:size, :] = plus(t[0, mine, :], quarter[0], quarter[1], quarter[2]).astype(BF16)
        place_of = lambda owner: out.at[even(core * height + owner * size, size), :]
        copies = [mail.post(theirs.at[0:size, :], place_of(z), device) for device in (up, down, far_z)]
        arrivals.append(mail.post(theirs.at[0:size, :], place_of(z), twin))
        keep(theirs.at[0:size, :], place_of(z))
        yield
        for copy in copies:
            copy.wait_recv()
        for step in (1, 2, 3):
            block = place_of((z + step) % 4)
            arrivals.append(mail.post(block, block, twin))
        yield

    def result_flow():
        swap = mail.post(result_sum.at[other_rows, :], part_in, pair)
        yield
        kept_wait(loads["down"])
        swap.wait_recv()
        result_rows[...] = (middle_v[own_rows, :] + plus(down_v[own_rows, :], part_in[...])).astype(BF16)
        yield
        spread(result_rows, result_out)
        yield

    def spread(source, target):
        for step in range(4):
            lanes = pl.ds(step * piece, piece)
            if step:
                arrivals.append(mail.post(source.at[:, lanes], target.at[spot, :], along_y(place, step)))
            else:
                keep(source.at[:, lanes], target.at[spot, :])

    flows = [ffn_flow(i) for i in range(4)]
    next(flows[0])
    next(flows[1])
    next(flows[3])
    loads = {}
    for name, source, target in (
        ("middle", middle, middle_v),
        ("cot", cot.at[0], cot_v),
        ("w_out", w_out, w_out_v),
        ("attended", attended, attended_v),
        ("query", query, query_v),
        ("kva", kv_a, kva),
        ("kvb", kv_b, kvb),
        ("ta", turned_a, turned_a_v),
        ("tb", turned_b, turned_b_v),
        ("gu", gu, gu_v),
        ("w_in", w_in, w_in_v),
        ("normed", normed, normed_v),
        ("tok", tok, tok_v),
        ("dn", dn, dn_v),
        ("down", result_sum, down_v),
    ):
        loads[name] = keep(source, target)
    result_steps = result_flow()
    next(result_steps)
    for j in range(4):
        gain_rows[:, j * piece : (j + 1) * piece] = gains[j]

    def norm_back(stream, gain, incoming):
        scale = lax.rsqrt(jnp.sum(stream * stream, -1, keepdims=True) * (1.0 / width) + EPS)
        scaled = incoming * gain
        inner = jnp.sum(scaled * stream, -1, keepdims=True) * (1.0 / width)
        back = scale * scaled - stream * (scale * scale * scale * inner)
        return back, jnp.sum(incoming * stream * scale, 0, keepdims=True)

    kept_wait(loads["middle"])
    kept_wait(loads["cot"])
    gain_ffn_part = jnp.zeros((1, width), F32)
    for half in range(2):
        part = slice(half * rows, (half + 1) * rows)
        back, gain_part = norm_back(middle_v[part, :], gain_rows[1:2, :], total[part, :])
        value = cot_v[part, :].astype(F32) + back
        grad_middle[part, :] = value
        grad_low[part, :] = value.astype(BF16)
        gain_ffn_part = gain_ffn_part + gain_part
    gains_own[...] = jnp.zeros_like(gains_own)
    for j in range(4):
        gains_own[j, 1:2, :] = 0.5 * gain_ffn_part[:, j * piece : (j + 1) * piece]
    kept_wait(loads["w_out"])
    q_width = w_out.shape[0]
    for first in range(0, q_width, 256):
        lanes = slice(first, first + 256)
        grad_att[:, lanes] = dot_nt(grad_low[...], w_out_v[lanes, :]).astype(BF16)

    def turn_over(source, target, count):
        for t in range(count):
            lanes = slice(t * LANES, (t + 1) * LANES)
            target[lanes, 0 : source.shape[0]] = source[:, lanes].T

    kept_wait(loads["attended"])
    turn_over(attended_v, flat, q_width // LANES)
    for j in range(4):
        wo_p[j] = jnp.dot(
            flat[0:q_width, :], grad_low[:, j * piece : (j + 1) * piece], preferred_element_type=F32
        ).astype(BF16)
    wo_steps = weight_flow(wo_p, wo_t, wo_up1, wo_down1, wo_up2, wo_down2, wo_s, wo_n, wo_z, wo_out)
    next(wo_steps)
    next(flows[0])
    next(flows[2])
    next(flows[3])

    for name in ("query", "kva", "kvb", "ta", "tb"):
        kept_wait(loads[name])
    heads = q_width // HEAD_SIZE
    factor = HEAD_SIZE ** (-0.5)

    def unrotate(value, half):
        part = slice(half * rows, (half + 1) * rows)
        return value * tables[0, part, :] + pltpu.roll(value * tables[1, part, :], HEAD_SIZE // 2, 1)

    def attend_back(half, keys, mask, sums):
        part = slice(half * rows, (half + 1) * rows)
        count = keys.shape[0]
        for t in range(count // LANES):
            lanes = slice(t * LANES, (t + 1) * LANES)
            keys_t[:, lanes] = keys[lanes, 0:HEAD_SIZE].T
        sums[...] = jnp.zeros_like(sums)

        @pl.loop(0, heads)
        def _(h):
            lanes = pl.ds(pl.multiple_of(h * HEAD_SIZE, LANES), HEAD_SIZE)
            one, grad = query_v[part, lanes], grad_att[part, lanes]
            raw = dot_nt(keys[:, 0:HEAD_SIZE], one)
            probs = jnp.exp(raw * factor + mask[...] - logs[half * heads + h, 0:1, :])
            grad_probs = dot_nt(keys[:, HEAD_SIZE : 2 * HEAD_SIZE], grad)
            inner = jnp.sum(grad_probs * probs, 0, keepdims=True)
            grad_scores = (probs * (grad_probs - inner)).astype(BF16)
            sums[:, 0:HEAD_SIZE] += jnp.dot(grad_scores, one, preferred_element_type=F32)
            sums[:, HEAD_SIZE : 2 * HEAD_SIZE] += jnp.dot(probs.astype(BF16), grad, preferred_element_type=F32)
            grad_query = jnp.dot(keys_t[:, 0:count], grad_scores, preferred_element_type=F32).T * factor
            grad_pre[part, lanes] = unrotate(grad_query, half).astype(BF16)

    def low_sums(sums, part):
        return (sums[part, 0:HEAD_SIZE] * factor).astype(BF16), sums[part, HEAD_SIZE : 2 * HEAD_SIZE].astype(BF16)

    attend_back(1, kvb, turned_b_v, dkv_b)
    half_rows = kva.shape[0]
    low_part, high_part = slice(0, half_rows), slice(half_rows, 2 * half_rows)
    for target, sums, part in ((low_kv, dkv_b, low_part), (own_kv.at[1], dkv_b, high_part)):
        target[:, 0:HEAD_SIZE], target[:, HEAD_SIZE : 2 * HEAD_SIZE] = low_sums(sums, part)
    kv_got = []
    for step in range(4):
        other = (row + step) % 4
        part = even(other * rows, rows)
        kv_got.append(mail.post(low_kv.at[part, :], from_near.at[step], near_of(place, other)))
        if step:
            kv_got.append(mail.post(own_kv.at[1, part, :], from_own.at[step - 1, 1], along_y(place, step)))
    next(flows[1])
    next(wo_steps)
    attend_back(0, kva, turned_a_v, dkv_a)
    target = own_kv.at[0]
    target[:, 0:HEAD_SIZE], target[:, HEAD_SIZE : 2 * HEAD_SIZE] = low_sums(dkv_a, low_part)
    for step in (1, 2, 3):
        part = even(((row + step) % 4) * rows, rows)
        kv_got.append(mail.post(own_kv.at[0, part, :], from_own.at[step - 1, 0], along_y(place, step)))
    next(flows[3])
    next(flows[0])
    kept_wait(loads["normed"])
    turn_over(normed_v, flat, width // LANES)
    next(result_steps)
    next(result_steps)
    for copy in kv_got:
        copy.wait_recv()
    for half in range(2):
        part = slice(half * rows, (half + 1) * rows)
        value = own_kv[half, spot, :].astype(F32)
        for step in range(3):
            value = value + from_own[step, half].astype(F32)
        if half == 0:
            for step in range(4):
                value = value + from_near[step].astype(F32)
        grad_pre[part, q_width : q_width + HEAD_SIZE] = unrotate(value[:, 0:HEAD_SIZE], half).astype(BF16)
        grad_pre[part, q_width + HEAD_SIZE : q_width + 2 * HEAD_SIZE] = value[:, HEAD_SIZE : 2 * HEAD_SIZE].astype(
            BF16
        )
    kept_wait(loads["w_in"])
    for j in range(4):
        grad_part[:, j * piece : (j + 1) * piece] = dot_nt(grad_pre[...], w_in_v[j]).astype(BF16)
    swap = mail.post(grad_part.at[other_rows, :], grad_in, pair)
    for j in range(4):
        in_p[j] = jnp.dot(flat[j * piece : (j + 1) * piece, :], grad_pre[...], preferred_element_type=F32).astype(BF16)
    in_steps = weight_flow(in_p, in_t, in_up1, in_down1, in_up2, in_down2, in_s, in_n, in_z, in_out)
    next(in_steps)
    bias_own[...] = jnp.zeros_like(bias_own)
    bias_own[0:1, :] = jnp.sum(grad_pre[...].astype(F32), 0, keepdims=True)
    next(flows[2])
    next(wo_steps)
    next(in_steps)
    next(flows[0])
    next(flows[1])
    next(flows[3])
    kept_wait(loads["tok"])
    swap.wait_recv()
    back, gain_part = norm_back(
        tok_v[own_rows, :].astype(F32), gain_rows[0:1, :], plus(grad_part[own_rows, :], grad_in[...])
    )
    rows_out[...] = (grad_middle[own_rows, :] + back).astype(BF16)
    for j in range(4):
        gains_own[j, 0:1, :] = gain_part[:, j * piece : (j + 1) * piece]
    small_copies, small_kept = [], []
    for step in range(4):
        device = along_y(place, step)
        mine = gains_in.at[col * 4 + row]
        if step:
            small_copies.append(mail.post(bias_own, bias_in.at[row], device))
            small_copies.append(mail.post(gains_own.at[step], mine, device))
        else:
            small_kept.append(keep(bias_own, bias_in.at[row]))
            small_kept.append(keep(gains_own.at[step], mine))
        small_copies.append(mail.post(gains_own.at[step], mine, pair_of(place, (row + step) % 4)))
    next(wo_steps)
    next(in_steps)
    spread(rows_out, grad_out)
    next(flows[1])
    next(flows[2])
    for copy in small_copies:
        copy.wait_recv()
    for index in small_kept:
        kept_wait(index)
    small_a[...] = jnp.zeros_like(small_a)
    small_a[0:8, :] = bias_in[0] + bias_in[1] + bias_in[2] + bias_in[3]
    small_a[8:16, 0:piece] = (
        gains_in[0] + gains_in[1] + gains_in[2] + gains_in[3] + gains_in[4] + gains_in[5] + gains_in[6] + gains_in[7]
    )
    small_first = mail.post(small_a, small_t, twin)
    next(wo_steps)
    next(in_steps)
    next(flows[3])
    small_first.wait_recv()
    small_b[...] = small_a[...] + small_t[...]
    small_second = mail.post(small_b, small_n, near)
    next(wo_steps)
    next(flows[2])
    next(in_steps)
    small_second.wait_recv()
    small_t[...] = small_b[...] + small_n[...]
    for device in (up, down, far_z):
        arrivals.append(mail.post(small_t, small_out.at[z], device))
    keep(small_t, small_out.at[z])
    next(flows[3])
    next(wo_steps)
    next(in_steps)
    for steps in [*flows, wo_steps, in_steps, result_steps]:
        for _ in steps:
            pass
    for copy in arrivals:
        copy.wait_recv()
    for copy in kept:
        if copy is not None:
            copy.wait()
    mail.finish()


def widen_kernel(gate_up, down, w_in, w_out, result, tokens, *outs):
    result_w, tokens_w, query_w, key_w, value_w, out_w, gate_w, up_w, down_w = outs
    result_w[...] = result[...].astype(F32)
    tokens_w[...] = tokens[...].astype(F32)
    first, second = query_w.shape[1], query_w.shape[1] + key_w.shape[1]
    query_w[...] = w_in[:, :first].astype(F32)
    key_w[...] = w_in[:, first:second].astype(F32)
    value_w[...] = w_in[:, second:].astype(F32)
    out_w[...] = w_out[...].astype(F32)
    gate_w[...] = gate_up[0, :, : gate_w.shape[1]].astype(F32)
    up_w[...] = gate_up[1, :, : up_w.shape[1]].astype(F32)
    down_w[...] = down[...].astype(F32)


def on_device(
    tokens,
    cotangent,
    lengths,
    gain_attn,
    w_query,
    key_projection,
    value_projection,
    bias_query,
    key_bias_vector,
    value_bias_vector,
    w_out,
    gain_ffn,
    w_gate,
    w_up,
    w_down,
):
    half_rows, piece = tokens.shape
    width = 4 * piece
    rows = half_rows // 4
    q_width = w_query.shape[1]
    kv_width = key_projection.shape[1]
    heads = q_width // HEAD_SIZE
    hidden = w_gate.shape[1]
    share = -(-hidden // (4 * LANES)) * LANES

    in_width = q_width + 2 * kv_width
    thin = piece // 2
    (
        tok_rows,
        cot_full,
        gains4,
        normed,
        query,
        kv_a,
        kv_b,
        logs,
        attended,
        tables,
        middle,
        mask_a,
        mask_b,
        normed_ffn,
        w_in_full,
        w_out_full,
        w_gu_full,
        w_down_full,
    ) = talk(
        front_kernel,
        0,
        FRONT_COPIES,
        FRONT_LOCAL,
        [
            ((2 * rows, width), BF16),
            ((4, 2 * rows, width), BF16),
            ((4, 8, piece), F32),
            ((2 * rows, width), BF16),
            ((2 * rows, q_width), BF16),
            ((half_rows, 2 * kv_width), BF16),
            ((2 * half_rows, 2 * kv_width), BF16),
            ((2 * heads, 8, rows), F32),
            ((2 * rows, q_width), BF16),
            ((2, 2 * rows, HEAD_SIZE), F32),
            ((2 * rows, width), F32),
            ((half_rows, rows), F32),
            ((2 * half_rows, rows), F32),
            ((2 * rows, width), BF16),
            ((4, piece, in_width), BF16),
            ((q_width, width), BF16),
            ((4, 2, thin, 2 * share), BF16),
            ((share, width), BF16),
        ],
        [ANY] * 2 + [VMEM] * 6 + [ANY] * 7,
        [ANY] * 3 + [VMEM] * 2 + [ANY] * 2 + [VMEM] * 7 + [ANY] * 4,
        [
            pltpu.VMEM((8, LANES), jnp.int32),
            pltpu.VMEM((8, piece), F32),
            pltpu.VMEM((2 * rows, width), BF16),
            pltpu.VMEM((2, 8, LANES), jnp.int32),
            pltpu.VMEM((4, 8, piece), F32),
            pltpu.VMEM((4, piece, in_width), BF16),
            pltpu.VMEM((q_width, width), BF16),
            pltpu.VMEM((2, thin, 2 * share), BF16),
            pltpu.VMEM((share, piece), BF16),
            pltpu.VMEM((thin, LANES), BF16),
            pltpu.VMEM((LANES, piece), BF16),
            pltpu.VMEM((2 * rows, 2 * kv_width), BF16),
            pltpu.VMEM((half_rows, 2 * kv_width), BF16),
            pltpu.VMEM((2 * half_rows, 2 * kv_width), BF16),
            pltpu.VMEM((rows, half_rows), F32),
            pltpu.VMEM((rows, 2 * half_rows), F32),
            pltpu.VMEM((2 * rows, width), BF16),
            pltpu.VMEM((2 * rows, width), BF16),
        ],
        limit=56,
    )(
        tokens,
        cotangent,
        lengths,
        gain_attn[None],
        gain_ffn[None],
        bias_query[None],
        key_bias_vector[None],
        value_bias_vector[None],
        w_query,
        key_projection,
        value_projection,
        w_out,
        w_gate,
        w_up,
        w_down,
    )

    w_both_full = w_gu_full.reshape(width, 2 * share)
    half_block = (2, rows, width)
    grad_normed_ffn, both_sum, down_half, result_sum = talk(
        ffn_kernel,
        4,
        52,
        14,
        [
            ((2 * rows, width), F32),
            ((piece, share), BF16),
            ((4, share // 2, piece), BF16),
            ((2 * rows, width), BF16),
        ],
        [ANY] * 4,
        [VMEM, VMEM, ANY, VMEM],
        [
            pltpu.VMEM(shape, BF16)
            for shape in (
                (8 * rows, width),
                (8 * rows, width),
                (width, 2 * share),
                (share, width),
                (8 * rows, 2 * share),
                (8 * rows, share),
                (8 * rows, width),
                (width, 8 * rows),
                (8 * rows, width),
                (4, piece, share),
                (4, share // 2, piece),
                (2, rows // 2, width),
                (2, rows // 2, width),
                half_block,
                half_block,
                half_block,
                (2, rows // 2, width),
                (2, rows // 2, width),
                half_block,
                (rows, width),
                (rows, width),
                half_block,
                half_block,
                (3, piece // 6, share),
                (3, piece // 6, share),
                (3, piece // 3, share),
                (3, piece // 3, share),
            )
        ],
        limit=60,
    )(normed_ffn, cot_full, w_both_full, w_down_full)
    thirds = piece // 3
    q_half, w_half = (thin, in_width), (q_width // 2, piece)
    gu_chunk, dn_chunk = (3, thirds, share), (share // 2, piece)

    def halved(shape):
        return (*shape[:-2], shape[-2] // 2, shape[-1])

    def weight_scratch(shape):
        return [
            (4, 2 * shape[0], shape[1]),
            (4, *shape),
            halved(shape),
            halved(shape),
            shape,
            shape,
            shape,
            shape,
            (3, shape[0] // 4, shape[1]),
        ]

    def scratch(kind, *shapes):
        return [pltpu.VMEM(shape, kind) for shape in shapes]

    gate_up, down_all, in_total, out_total, grad_tokens, result, small_all = talk(
        back_kernel,
        8,
        BACK_COPIES,
        BACK_LOCAL,
        [
            ((2, piece, 4 * share), BF16),
            ((4 * share, piece), BF16),
            ((piece, in_width), BF16),
            ((q_width, piece), BF16),
            ((half_rows, piece), BF16),
            ((half_rows, piece), BF16),
            ((4, 16, in_width), F32),
        ],
        [VMEM, ANY, ANY, VMEM] + [ANY] * 5 + [VMEM, ANY, VMEM] + [ANY] * 7,
        [ANY] * 7,
        scratch(F32, (2 * rows, width))
        + scratch(
            BF16,
            (2 * rows, width),
            (2 * rows, width),
            (2 * rows, width),
            (2 * rows, q_width),
            (half_rows, 2 * kv_width),
            (2 * half_rows, 2 * kv_width),
            (2 * rows, q_width),
        )
        + scratch(F32, (half_rows, rows), (2 * half_rows, rows))
        + scratch(
            BF16,
            (4, piece, in_width),
            (q_width, width),
            (piece, share),
            (4, share // 2, piece),
            (2 * rows, width),
        )
        + scratch(F32, (8, width), (2 * rows, width))
        + scratch(BF16, (2 * rows, width), (2 * rows, q_width), (width, 2 * rows), (HEAD_SIZE, 2 * half_rows))
        + scratch(F32, (half_rows, 2 * kv_width), (2 * half_rows, 2 * kv_width))
        + scratch(
            BF16,
            (half_rows, 2 * kv_width),
            (2, half_rows, 2 * kv_width),
            (3, 2, rows, 2 * kv_width),
            (4, rows, 2 * kv_width),
            (2 * rows, in_width),
            (2 * rows, width),
            (rows, width),
            (rows, width),
            (rows, width),
            (rows, width),
            gu_chunk,
            gu_chunk,
            halved(dn_chunk),
            halved(dn_chunk),
            dn_chunk,
            dn_chunk,
            dn_chunk,
            dn_chunk,
            dn_chunk,
            *weight_scratch(q_half),
            *weight_scratch(w_half),
        )
        + scratch(F32, (8, in_width), (4, 8, piece), (4, 8, in_width), (8, 8, piece))
        + scratch(F32, *[(16, in_width)] * 4),
        limit=60,
    )(
        grad_normed_ffn,
        middle,
        cot_full,
        gains4,
        tok_rows,
        normed,
        query,
        kv_a,
        kv_b,
        logs,
        attended,
        tables,
        mask_a,
        mask_b,
        w_in_full,
        w_out_full,
        both_sum,
        down_half,
        result_sum,
    )
    small_total = small_all[0] + small_all[1] + small_all[2] + small_all[3]
    bias_total = small_total[0]
    upper = q_width + kv_width
    steps = 8
    narrow = [gate_up, down_all, in_total, out_total, result, grad_tokens]
    wide = [
        (half_rows, piece),
        (half_rows, piece),
        (piece, q_width),
        (piece, kv_width),
        (piece, kv_width),
        (q_width, piece),
        (piece, hidden),
        (piece, hidden),
        (hidden, piece),
    ]

    def in_block(array):
        if array.ndim == 3:
            return pl.BlockSpec((2, array.shape[1] // steps, array.shape[2]), lambda i: (0, i, 0))
        if array is down_all:
            return pl.BlockSpec((hidden // steps, piece), lambda i: (i, 0))
        return pl.BlockSpec((array.shape[0] // steps, array.shape[1]), lambda i: (i, 0))

    wide_out = pl.pallas_call(
        widen_kernel,
        grid=(steps,),
        out_shape=[jax.ShapeDtypeStruct(shape, F32) for shape in wide],
        in_specs=[in_block(array) for array in narrow],
        out_specs=[pl.BlockSpec((shape[0] // steps, shape[1]), lambda i: (i, 0)) for shape in wide],
        compiler_params=pltpu.CompilerParams(vmem_limit_bytes=48 << 20),
    )(*narrow)
    return (
        *wide_out[:2],
        small_total[8, :piece],
        *wide_out[2:5],
        bias_total[:q_width],
        bias_total[q_width:upper],
        bias_total[upper:],
        wide_out[5],
        small_total[9, :piece],
        *wide_out[6:],
    )


def solution(mesh):
    placed = (
        P(("dp", "col"), "row"),
        P(("dp", "col"), "row"),
        P("dp", None),
        P("row"),
        P("row", "col"),
        P("row", "col"),
        P("row", "col"),
        P("col"),
        P("col"),
        P("col"),
        P("col", "row"),
        P("row"),
        P("row", "col"),
        P("row", "col"),
        P("col", "row"),
    )
    return jax.shard_map(
        on_device,
        mesh=mesh,
        in_specs=placed,
        out_specs=(
            P(("dp", "col"), "row"),
            P(("dp", "col"), "row"),
            P("row"),
            P("row", "col"),
            P("row", "col"),
            P("row", "col"),
            P("col"),
            P("col"),
            P("col"),
            P("col", "row"),
            P("row"),
            P("row", "col"),
            P("row", "col"),
            P("col", "row"),
        ),
        check_vma=False,
    )
```

```python
import math

import jax
import jax.numpy as jnp
from jax import lax
from jax.experimental import pallas as pl
from jax.experimental.pallas import tpu as pltpu
from jax.sharding import PartitionSpec as P

HEAD_SIZE = 128
EPS = 1e-06
THETA = 1000000.0
LANES = 128
MESH = pl.DeviceIdType.MESH
BF16 = jnp.bfloat16
F32 = jnp.float32
ANY = pl.BlockSpec(memory_space=pl.ANY)
VMEM = pl.BlockSpec(memory_space=pltpu.VMEM)

Z_STEP = 4
FRONT_COPIES = 77
FRONT_LOCAL = 27
BACK_COPIES = 119
BACK_LOCAL = 26


def here():
    return lax.axis_index("dp"), lax.axis_index("row"), lax.axis_index("col")


def flip_near(dp):
    return dp + 2 - 4 * ((dp // 2) % 2)


def pair_of(place, row=None):
    dp, own, col = place
    return flip_near(dp), own if row is None else row, 1 - col


def near_of(place, row=None):
    dp, own, col = place
    return flip_near(dp), own if row is None else row, col


def twin_of(place):
    dp, row, col = place
    return dp + 1 - 2 * (dp % 2), row, col


def along_z(place, step):
    dp, row, col = place
    return (dp + Z_STEP * step) % (4 * Z_STEP), row, col


def along_y(place, step):
    dp, row, col = place
    return dp, (row + step) % 4, col


def meet(peers):
    barrier = pltpu.get_barrier_semaphore()
    for peer in peers:
        pl.semaphore_signal(barrier, inc=1, device_id=peer, device_id_type=MESH)
    pl.semaphore_wait(barrier, len(peers))


class Mail:
    def __init__(self, send, recv):
        self.send, self.recv, self.count, self.sent = send, recv, 0, []

    def post(self, source, target, device):
        index = self.count
        self.count += 1
        copy = pltpu.make_async_remote_copy(
            src_ref=source,
            dst_ref=target,
            send_sem=self.send.at[index],
            recv_sem=self.recv.at[index],
            device_id=device,
            device_id_type=MESH,
        )
        copy.start()
        self.sent.append(copy)
        return copy

    def finish(self):
        assert self.count == self.send.shape[0], (self.count, self.send.shape)
        for copy in self.sent:
            copy.wait_send()


def talk(body, ident, copies, local, outs, in_specs, out_specs, scratch=(), limit=32):
    return pl.pallas_call(
        body,
        out_shape=[jax.ShapeDtypeStruct(*out) for out in outs],
        in_specs=in_specs,
        out_specs=out_specs,
        scratch_shapes=[
            *scratch,
            pltpu.SemaphoreType.DMA((copies,)),
            pltpu.SemaphoreType.DMA((copies,)),
            pltpu.SemaphoreType.DMA((max(local, 1),)),
        ],
        compiler_params=pltpu.CompilerParams(
            collective_id=ident, has_side_effects=True, vmem_limit_bytes=limit << 20
        ),
    )


def front_kernel(
    tok,
    cot,
    lens_in,
    gain_attn,
    gain_ffn,
    bias_q,
    bias_k,
    bias_v,
    wq,
    wk,
    wv,
    wo,
    wg,
    wu,
    wd,
    tok_out,
    cot_full,
    gains_out,
    normed,
    query,
    kva_out,
    kvb_out,
    logs,
    attended,
    tables,
    middle,
    turned_a,
    turned_b,
    normed_ffn,
    w_in_out,
    w_out_out,
    wgu_full,
    wd_full,
    lens,
    gains,
    tok_v,
    lens_v,
    gains_v,
    w_in,
    w_out,
    gu_own,
    wd_own,
    blank_gu,
    blank_wd,
    kv,
    kva,
    kvb,
    bias_a,
    bias_b,
    branch,
    branch_in,
    send,
    recv,
    local,
):
    place = here()
    dp, row, col = place
    z, core = dp // Z_STEP, dp % 2
    twin, pair, up, down = twin_of(place), pair_of(place), along_z(place, 1), along_z(place, 3)
    right, left, near = along_y(place, 1), along_y(place, 3), near_of(place)
    meet(
        [along_y(place, s) for s in (1, 2, 3)]
        + [near_of(place, (row + s) % 4) for s in range(4)]
        + [pair, twin, up, down]
    )
    mail = Mail(send, recv)
    kept = []

    def keep(source, target):
        kept.append(pltpu.make_async_copy(source, target, local.at[len(kept)]))
        kept[-1].start()
        return len(kept) - 1

    def kept_wait(index):
        kept[index].wait()
        kept[index] = None

    def even(start, size):
        return pl.ds(pl.multiple_of(start, 16), size)

    rows, piece = tok.shape[0] // 4, tok.shape[1]
    width = 4 * piece
    own_rows = even(col * rows, rows)
    spot = even(row * rows, rows)

    def spread(source, target):
        got = []
        for step in range(4):
            part = source.at[even(((row + step) % 4) * rows, rows), :]
            lanes = pl.ds(((4 - step) % 4) * piece, piece)
            if step:
                got.append(mail.post(part, target.at[own_rows, lanes], along_y(place, step)))
            else:
                mine = keep(part, target.at[own_rows, lanes])
        return got, mine

    tokens = spread(tok, tok_v)
    lens[...] = jnp.zeros_like(lens)
    lens[0:1, 0 : lens_in.shape[1]] = lens_in[...]
    gains[...] = jnp.zeros_like(gains)
    gains[0:1, :] = gain_attn[...].reshape(1, piece)
    gains[1:2, :] = gain_ffn[...].reshape(1, piece)
    lens_got = mail.post(lens, lens_v.at[col], pair)
    lens_kept = keep(lens, lens_v.at[col])
    gains_kept = keep(gains, gains_v.at[0])
    gains_got = [mail.post(gains, gains_v.at[4 - s], along_y(place, s)) for s in (1, 2, 3)]

    q_width, kv_width = wq.shape[1], wk.shape[1]
    stages = [
        keep(wq, w_in.at[0, :, pl.ds(0, q_width)]),
        keep(wk, w_in.at[0, :, pl.ds(q_width, kv_width)]),
        keep(wv, w_in.at[0, :, pl.ds(q_width + kv_width, kv_width)]),
        keep(wo, w_out.at[:, pl.ds(0, piece)]),
    ]
    share = wd_own.shape[0]
    thin = piece // 2
    sure = share - LANES
    take = pl.multiple_of(z * share, LANES)
    big = []
    for k in range(2):
        for i, source in enumerate((wg, wu)):
            from_rows = pl.ds(k * thin, thin)
            big.append(keep(source.at[from_rows, pl.ds(take, sure)], gu_own.at[k, :, pl.ds(i * share, sure)]))
    big.append(keep(wd.at[pl.ds(take, sure), :], wd_own.at[pl.ds(0, sure), :]))
    blank_gu[...] = jnp.zeros_like(blank_gu)
    blank_wd[...] = jnp.zeros_like(blank_wd)
    first_edge = len(kept)
    edges = []
    for k in range(2):
        for i, source in enumerate((wg, wu)):
            target = gu_own.at[k, :, pl.ds(i * share + sure, LANES)]
            edges.append((source, pl.ds(k * thin, thin), None, target, blank_gu))
    edges.append((wd, None, slice(None), wd_own.at[pl.ds(sure, LANES), :], blank_wd))

    def edge(index, last):
        source, from_rows, _, target, blank = edges[index]
        if last:
            origin = blank
        elif from_rows is None:
            origin = source.at[pl.ds(pl.multiple_of(take + sure, LANES), LANES), :]
        else:
            origin = source.at[from_rows, pl.ds(pl.multiple_of(take + sure, LANES), LANES)]
        return pltpu.make_async_copy(origin, target, local.at[first_edge + index])

    @pl.when(z < 3)
    def _():
        for index in range(len(edges)):
            edge(index, False).start()

    @pl.when(z == 3)
    def _():
        for index in range(len(edges)):
            edge(index, True).start()

    for index in range(len(edges)):
        kept.append(edge(index, True))
        big.append(first_edge + index)

    q_rows, o_rows = thin // 4, w_out.shape[0] // 8

    def in_part(j, owner_z):
        return w_in.at[j, even(core * thin + owner_z * q_rows, q_rows), :]

    def in_parts(owner_z):
        return w_in.at[pl.ds(1, 3), even(core * thin + owner_z * q_rows, q_rows), :]

    def in_side(owner_z, side):
        lanes = pl.ds(side * (w_in.shape[2] // 2), w_in.shape[2] // 2)
        return w_in.at[pl.ds(1, 3), even(core * thin + owner_z * q_rows, q_rows), lanes]

    def out_part(j, owner_z):
        return w_out.at[even(core * 4 * o_rows + owner_z * o_rows, o_rows), pl.ds(j * piece, piece)]

    def out_parts(owner_z):
        return w_out.at[even(core * 4 * o_rows + owner_z * o_rows, o_rows), pl.ds(piece, 3 * piece)]

    def out_side(owner_z, side):
        start = core * 4 * o_rows + owner_z * o_rows + side * (o_rows // 2)
        return w_out.at[even(start, o_rows // 2), pl.ds(piece, 3 * piece)]

    for index in stages:
        kept_wait(index)
    in_got = [mail.post(in_part(0, z), in_part(4 - step, z), along_y(place, step)) for step in (1, 3, 2)]

    def to_pair(spreading, target):
        got, mine = spreading
        kept_wait(mine)
        for copy in got:
            copy.wait_recv()
        return mail.post(target.at[own_rows, :], target.at[own_rows, :], pair)

    tokens_pair = to_pair(tokens, tok_v)
    shares = []

    def give(part):
        shares.append(mail.post(part, part, twin))

    def z_first(side):
        copies = {}
        for turn in range(2):
            copies["u", turn] = mail.post(side(z, turn), side(z, turn), up)
            copies["d", 1 - turn] = mail.post(side(z, 1 - turn), side(z, 1 - turn), down)
        return copies

    below, above, across = (z + 3) % 4, (z + 1) % 4, (z + 2) % 4

    def z_second(side, whole, copies):
        copies["u", 0].wait_recv()
        far_up = mail.post(side(below, 0), side(below, 0), up)
        copies["d", 1].wait_recv()
        far_down = mail.post(side(above, 1), side(above, 1), down)
        copies["u", 1].wait_recv()
        give(whole(below))
        copies["d", 0].wait_recv()
        give(whole(above))
        return far_up, far_down

    def z_third(whole, copies):
        for copy in copies:
            copy.wait_recv()
        give(whole(across))

    for copy in in_got:
        copy.wait_recv()
    in_z = z_first(in_side)
    give(in_parts(z))
    out_got = [mail.post(out_part(0, z), out_part(4 - step, z), along_y(place, step)) for step in (1, 3, 2)]
    cotangents = spread(cot, cot_full.at[0])
    for index in big:
        kept_wait(index)
    x_lo = (dp // 2) % 2
    gu_half, wd_half = thin // 4, share // 4

    def gu_part(j, which=None, owner=x_lo):
        start, size = (0, 2 * gu_half) if which is None else (which * gu_half, gu_half)
        return wgu_full.at[j, core, even(owner * 2 * gu_half + start, size), :]

    def gu_whole(j):
        return wgu_full.at[j, core]

    def wd_part(j, which=None):
        start, size = (0, 2 * wd_half) if which is None else (which * wd_half, wd_half)
        return wd_full.at[even(core * 2 * wd_half + start, size), pl.ds(j * piece, piece)]

    def gu_source(which):
        return gu_own.at[core, even((x_lo * 2 + which) * gu_half, gu_half), :]

    def wd_source(which):
        return wd_own.at[even((core * 2 + which) * wd_half, wd_half), :]

    y_ring, near_gu, twins = {}, [], []

    def y_start(name, source, part):
        for turn in range(2):
            y_ring[name, "r", turn] = mail.post(source(turn), part(3, turn), right)
            y_ring[name, "l", 1 - turn] = mail.post(source(1 - turn), part(1, 1 - turn), left)

    def y_forward(name, part):
        y_ring[name, "r", 0].wait_recv()
        y_ring[name, "fr"] = mail.post(part(3, 0), part(2, 0), right)
        y_ring[name, "l", 1].wait_recv()
        y_ring[name, "fl"] = mail.post(part(1, 1), part(2, 1), left)

    def y_share(name, part, queue, device):
        y_ring[name, "r", 1].wait_recv()
        queue.append(mail.post(part(3), part(3), device))
        y_ring[name, "l", 0].wait_recv()
        queue.append(mail.post(part(1), part(1), device))

    def y_end(name, part, queue, device):
        y_ring[name, "fr"].wait_recv()
        y_ring[name, "fl"].wait_recv()
        queue.append(mail.post(part(2), part(2), device))


    kept_wait(lens_kept)
    lens_got.wait_recv()
    half_rows = 4 * rows

    def segment_of(which, index):
        end_0 = lens_v[which, 0:1, 0:1]
        end_1 = end_0 + lens_v[which, 0:1, 1:2]
        past_0 = (index >= end_0).astype(jnp.int32)
        past_1 = (index >= end_1).astype(jnp.int32)
        start = jnp.where(past_1 > 0, end_1, jnp.where(past_0 > 0, end_0, 0))
        return past_0 + past_1, start

    lane = lax.broadcasted_iota(jnp.int32, (rows, HEAD_SIZE), 1)
    half_lane = jnp.where(lane >= HEAD_SIZE // 2, lane - HEAD_SIZE // 2, lane).astype(F32)
    inverse = jnp.exp(half_lane * (-2.0 * math.log(THETA) / HEAD_SIZE))
    for which, mask, mask_t, key_count in ((0, bias_a, turned_a, half_rows), (1, bias_b, turned_b, 2 * half_rows)):
        index = lax.broadcasted_iota(jnp.int32, (rows, HEAD_SIZE), 0) + (row * rows + which * half_rows)
        _, start = segment_of(which, index)
        turn = (index - start).astype(F32) * inverse
        tables[0, which * rows : (which + 1) * rows, :] = jnp.cos(turn)
        sine = jnp.sin(turn)
        tables[1, which * rows : (which + 1) * rows, :] = jnp.where(lane >= HEAD_SIZE // 2, sine, -sine)
        at = lax.broadcasted_iota(jnp.int32, (rows, key_count), 0) + (row * rows + which * half_rows)
        keys = lax.broadcasted_iota(jnp.int32, (rows, key_count), 1)
        allowed = jnp.logical_and(segment_of(which, at)[0] == segment_of(which, keys)[0], keys <= at)
        mask[...] = jnp.where(allowed, 0.0, -1e30)
        at = lax.broadcasted_iota(jnp.int32, (key_count, rows), 1) + (row * rows + which * half_rows)
        keys = lax.broadcasted_iota(jnp.int32, (key_count, rows), 0)
        allowed = jnp.logical_and(segment_of(which, at)[0] == segment_of(which, keys)[0], keys <= at)
        mask_t[...] = jnp.where(allowed, 0.0, -1e30)

    kept_wait(gains_kept)
    for copy in gains_got:
        copy.wait_recv()
    keep(gains_v, gains_out)

    def normalise(value, which):
        scale = lax.rsqrt(jnp.sum(value * value, -1, keepdims=True) * (1.0 / width) + EPS)
        return [
            (value[:, j * piece : (j + 1) * piece] * scale * gains_v[j, which : which + 1, :]).astype(BF16)
            for j in range(4)
        ]

    def norm_rows(which):
        part = pl.ds(pl.multiple_of(which * rows, rows), rows)
        for j, block in enumerate(normalise(tok_v[part, :].astype(F32), 0)):
            normed[part, pl.ds(j * piece, piece)] = block

    norm_rows(col)
    for copy in out_got:
        copy.wait_recv()
    give(out_parts(z))
    y_start("gu", gu_source, gu_part)
    keep(gu_own, wgu_full.at[0])
    keep(wd_own, wd_full.at[:, pl.ds(0, piece)])
    in_far = z_second(in_side, in_parts, in_z)
    out_z = z_first(out_side)
    tokens_pair.wait_recv()
    keep(tok_v, tok_out)
    norm_rows(1 - col)
    cot_pair = to_pair(cotangents, cot_full.at[0])
    z_third(in_parts, in_far)
    for copy in shares:
        copy.wait_recv()
    shares.clear()
    keep(w_in, w_in_out)

    in_width = w_in.shape[2]

    def project(lanes, bias):
        weights = w_in[:, :, lanes]
        weights = weights.reshape(4 * weights.shape[1], weights.shape[2])
        return jnp.dot(normed[...], weights, preferred_element_type=F32) + bias

    def rotate(value):
        return value * tables[0] + pltpu.roll(value, HEAD_SIZE // 2, 1) * tables[1]

    key_value = project(slice(q_width, in_width), jnp.concatenate([bias_k[...].reshape(1, kv_width), bias_v[...].reshape(1, kv_width)], 1))
    kv[:, 0:kv_width] = rotate(key_value[:, 0:kv_width]).astype(BF16)
    kv[:, kv_width : 2 * kv_width] = key_value[:, kv_width : 2 * kv_width].astype(BF16)
    a_rows, b_rows = pl.ds(0, rows), pl.ds(rows, rows)
    high_spot = even(half_rows + row * rows, rows)
    a_got, b_got = [], []
    for step in (1, 2, 3):
        a_got.append(mail.post(kv.at[a_rows, :], kva.at[spot, :], along_y(place, step)))
    for step in range(4):
        b_got.append(mail.post(kv.at[a_rows, :], kvb.at[spot, :], near_of(place, (row + step) % 4)))
        if step:
            b_got.append(mail.post(kv.at[b_rows, :], kvb.at[high_spot, :], along_y(place, step)))
    kva[spot, :] = kv[a_rows, :]
    kvb[high_spot, :] = kv[b_rows, :]
    for first in range(0, q_width, 2 * HEAD_SIZE):
        value = project(slice(first, first + 2 * HEAD_SIZE), bias_q[first : first + 2 * HEAD_SIZE].reshape(1, 2 * HEAD_SIZE))
        for i in range(2):
            lanes = slice(first + i * HEAD_SIZE, first + (i + 1) * HEAD_SIZE)
            query[:, lanes] = rotate(value[:, i * HEAD_SIZE : (i + 1) * HEAD_SIZE]).astype(BF16)

    y_forward("gu", gu_part)
    y_share("gu", gu_part, near_gu, near)
    out_far = z_second(out_side, out_parts, out_z)
    heads = q_width // HEAD_SIZE
    factor = HEAD_SIZE ** (-0.5)

    def attend(half, keys, mask):
        part = slice(half * rows, (half + 1) * rows)

        @pl.loop(0, heads)
        def _(h):
            lanes = pl.ds(pl.multiple_of(h * HEAD_SIZE, LANES), HEAD_SIZE)
            raw = lax.dot_general(
                query[part, lanes], keys[:, 0:HEAD_SIZE], (((1,), (1,)), ((), ())), preferred_element_type=F32
            )
            scores = raw * factor + mask[...]
            peak = jnp.max(scores, -1, keepdims=True)
            raised = jnp.exp(scores - peak)
            total = jnp.sum(raised, -1, keepdims=True)
            probs = (raised * (1.0 / total)).astype(BF16)
            out = jnp.dot(probs, keys[:, HEAD_SIZE : 2 * HEAD_SIZE], preferred_element_type=F32)
            attended[part, lanes] = out.astype(BF16)
            logs[half * heads + h] = jnp.broadcast_to(peak + jnp.log(total), (rows, LANES)).T[0:8, :]

        for first in range(0, width, piece):
            lanes = slice(first, first + piece)
            branch[part, lanes] = jnp.dot(
                attended[part, :], w_out[:, lanes], preferred_element_type=F32
            ).astype(BF16)
        return mail.post(branch.at[part, :], branch_in.at[part, :], pair)

    def finish_half(half, copy):
        part = slice(half * rows, (half + 1) * rows)
        copy.wait_recv()
        value = tok_v[part, :].astype(F32) + (branch[part, :].astype(F32) + branch_in[part, :].astype(F32))
        middle[part, :] = value
        for j, block in enumerate(normalise(value, 1)):
            normed_ffn[part, j * piece : (j + 1) * piece] = block

    def z_send(source, target, half):
        part = pl.ds(half * rows, rows)
        return (
            mail.post(source.at[part, :], target.at[1, part, :], up),
            mail.post(source.at[part, :], target.at[3, part, :], down),
        )

    def z_forward(target, half, copies):
        part = pl.ds(half * rows, rows)
        if half == 0:
            copies[0].wait_recv()
            return copies[1], mail.post(target.at[1, part, :], target.at[2, part, :], up)
        copies[1].wait_recv()
        return copies[0], mail.post(target.at[3, part, :], target.at[2, part, :], down)

    cot_pair.wait_recv()
    cot_z = [z_send(cot_full.at[0], cot_full, half) for half in range(2)]
    for copy in a_got:
        copy.wait_recv()
    keep(kva, kva_out)
    z_third(out_parts, out_far)
    for copy in shares:
        copy.wait_recv()
    keep(w_out, w_out_out)
    swap_a = attend(0, kva, bias_a)
    for copy in b_got:
        copy.wait_recv()
    keep(kvb, kvb_out)
    y_start("wd", wd_source, wd_part)
    swap_b = attend(1, kvb, bias_b)
    y_end("gu", gu_part, near_gu, near)
    finish_half(0, swap_a)
    y_forward("wd", wd_part)
    cot_last = [z_forward(cot_full, half, cot_z[half]) for half in range(2)]
    y_share("wd", wd_part, twins, twin)
    finish_half(1, swap_b)
    for j, copy in zip((3, 1, 2), near_gu):
        copy.wait_recv()
        twins.append(mail.post(gu_whole(j), gu_whole(j), twin))
    y_end("wd", wd_part, twins, twin)
    for copies in cot_last:
        for copy in copies:
            copy.wait_recv()
    for copy in twins:
        copy.wait_recv()
    for copy in kept:
        if copy is not None:
            copy.wait()
    mail.finish()


def ffn_kernel(
    normed,
    cot,
    wgu,
    wd,
    total,
    gu_sum,
    dn_half,
    result_sum,
    x,
    cot_v,
    wgu_v,
    wd_v,
    gb,
    act,
    parts,
    turned,
    down_v,
    gu_in,
    dn_in,
    up1,
    down1,
    up2,
    down2,
    other,
    stage_up,
    stage_down,
    stage,
    res_up1,
    res_down1,
    res_up2,
    res_down2,
    gu_up1,
    gu_down1,
    gu_up2,
    gu_down2,
    send,
    recv,
    local,
):
    place = here()
    dp, row, col = place
    core = dp % 2
    up, down, pair, twin = along_z(place, 1), along_z(place, 3), pair_of(place), twin_of(place)
    right, left = along_y(place, 1), along_y(place, 3)
    meet([up, down, pair, twin, right, left])
    mail = Mail(send, recv)
    order = ((0, 0), (0, 1), (1, 0), (3, 1), (2, 0), (2, 1), (1, 1), (3, 0))
    spots = {half: i for i, half in enumerate(order)}
    rows = normed.shape[0] // 2
    size = rows // 2

    def block(ref, slot, half):
        return ref.at[pl.ds(spots[slot, half] * rows, rows), :]

    def halves(ref, half):
        return ref.at[pl.ds(half * rows, rows), :]

    kept = []

    def keep(source, target):
        kept.append(pltpu.make_async_copy(source, target, local.at[len(kept)]))
        kept[-1].start()
        return len(kept) - 1

    def kept_wait(index):
        kept[index].wait()
        kept[index] = None

    got = {}

    def z_start(which):
        got["u", which] = mail.post(halves(normed, which), block(x, 1, which), up)
        got["d", 1 - which] = mail.post(halves(normed, 1 - which), block(x, 3, 1 - which), down)

    z_start(0)
    share = wd.shape[0]
    early = [keep(normed, x.at[pl.ds(0, 2 * rows), :]), keep(wgu, wgu_v)]
    early.append(keep(cot.at[0], cot_v.at[pl.ds(0, 2 * rows), :]))
    early.append(keep(wd, wd_v))
    later = [keep(cot.at[slot, pl.ds(half * rows, rows), :], block(cot_v, slot, half)) for slot, half in order[2:]]
    width = normed.shape[1]
    piece = width // 4

    def dot_nt(left, right):
        return lax.dot_general(left, right, (((1,), (1,)), ((), ())), preferred_element_type=F32)

    def compute(c):
        part = slice(2 * rows * c, 2 * rows * (c + 1))
        for start, size in ((0, 512), (512, share - 512)):
            lanes, above = slice(start, start + size), slice(share + start, share + start + size)
            gate = jnp.dot(x[part, :], wgu_v[:, lanes], preferred_element_type=F32)
            value = jnp.dot(x[part, :], wgu_v[:, above], preferred_element_type=F32)
            grad = dot_nt(cot_v[part, :], wd_v[lanes, :])
            spread = 1.0 / (1.0 + jnp.exp(-gate))
            smooth = gate * spread
            act[part, lanes] = (smooth * value).astype(BF16)
            gb[part, lanes] = (grad * value * (spread * (1.0 + gate * (1.0 - spread)))).astype(BF16)
            gb[part, above] = (grad * smooth).astype(BF16)
        for m in range(3):
            lanes = slice(512 * m, 512 * (m + 1))
            parts[part, lanes] = dot_nt(gb[part, :], wgu_v[lanes, :]).astype(BF16)

    for index in early:
        kept_wait(index)
    compute(0)
    got["u", 0].wait_recv()
    far_up = mail.post(block(x, 1, 0), block(x, 2, 0), up)
    got["d", 1].wait_recv()
    far_down = mail.post(block(x, 3, 1), block(x, 2, 1), down)
    for index in later:
        kept_wait(index)
    compute(1)
    z_start(1)
    far_up.wait_recv()
    far_down.wait_recv()
    compute(2)
    first = {}
    for i in range(2):
        rows_i = pl.ds(i * size, size)
        first["u", i] = mail.post(block(parts, 2, 0).at[rows_i, :], up1.at[i], up)
        first["d", i] = mail.post(block(parts, 2, 1).at[rows_i, :], down1.at[i], down)
    got["u", 1].wait_recv()
    got["d", 0].wait_recv()
    compute(3)
    second = {
        ("d", 0): mail.post(block(parts, 1, 0), down2.at[0], down),
        ("u", 1): mail.post(block(parts, 3, 1), up2.at[1], up),
    }

    def turn_over(source, target):
        @pl.loop(0, source.shape[1] // LANES)
        def _(t):
            lanes = pl.ds(pl.multiple_of(t * LANES, LANES), LANES)
            target[lanes, :] = source[:, lanes].T

    def forward(i):
        rows_i = pl.ds(i * size, size)
        first["u", i].wait_recv()
        stage_up[i] = (block(parts, 3, 0).at[rows_i, :][...].astype(F32) + up1[i].astype(F32)).astype(BF16)
        second["u", 0, i] = mail.post(stage_up.at[i], up2.at[0, rows_i, :], up)
        first["d", i].wait_recv()
        stage_down[i] = (block(parts, 1, 1).at[rows_i, :][...].astype(F32) + down1[i].astype(F32)).astype(BF16)
        second["d", 1, i] = mail.post(stage_down.at[i], down2.at[1, rows_i, :], down)

    turn_over(x, turned)
    tile = 256
    tiles = 2 * share // tile

    def gu_tiles(first_tile, last_tile):
        @pl.loop(first_tile, last_tile)
        def _(n):
            lanes = pl.ds(pl.multiple_of(((n + (tiles // 2) * (1 - core)) % tiles) * tile, tile), tile)
            wgu_v[:, lanes] = jnp.dot(turned[...], gb[:, lanes], preferred_element_type=F32).astype(BF16)

    swaps = {}

    def settle(i):
        rows_i = pl.ds(i * size, size)
        if i == 0:
            second["d", 0].wait_recv()
            second["u", 1].wait_recv()
        second["u", 0, i].wait_recv()
        second["d", 1, i].wait_recv()
        for half in range(2):
            value = block(parts, 0, half).at[rows_i, :][...].astype(F32)
            value = value + up2[half, rows_i, :].astype(F32) + down2[half, rows_i, :].astype(F32)
            stage[half, rows_i, :] = value.astype(BF16)
            swaps[half, i] = mail.post(stage.at[half, rows_i, :], other.at[half, rows_i, :], pair)

    there = pl.ds(pl.multiple_of((1 - core) * share, LANES), share)
    mine = pl.ds(pl.multiple_of(core * share, LANES), share)
    gu_tiles(0, tiles // 2 + 1)
    shared = [
        mail.post(wgu_v.at[pl.ds(j * piece, piece), there], gu_in.at[j], twin) for j in range(4)
    ]
    forward(0)
    forward(1)
    gu_tiles(tiles // 2 + 1, tiles)
    for j in range(4):
        shared[j].wait_recv()
        gu_in[j] = (wgu_v[pl.ds(j * piece, piece), mine].astype(F32) + gu_in[j].astype(F32)).astype(BF16)

    def ring_y(i):
        height = piece // 3
        half = height // 2
        low, high = pl.ds(i * height, half), pl.ds(i * height + half, half)
        one, two, three, four = gu_up1.at[i], gu_down1.at[i], gu_up2.at[i], gu_down2.at[i]
        begin = (mail.post(gu_in.at[2, low, :], one, right), mail.post(gu_in.at[2, high, :], two, left))
        straight = [
            mail.post(gu_in.at[1, high, :], three.at[pl.ds(half, half), :], right),
            mail.post(gu_in.at[3, low, :], four.at[pl.ds(0, half), :], left),
        ]
        yield
        begin[0].wait_recv()
        one[...] = (gu_in[1, low, :].astype(F32) + one[...].astype(F32)).astype(BF16)
        straight.append(mail.post(one, three.at[pl.ds(0, half), :], right))
        begin[1].wait_recv()
        two[...] = (gu_in[3, high, :].astype(F32) + two[...].astype(F32)).astype(BF16)
        straight.append(mail.post(two, four.at[pl.ds(half, half), :], left))
        yield
        for copy in straight:
            copy.wait_recv()
        part = pl.ds(i * height, height)
        value = gu_in[0, part, :].astype(F32) + three[...].astype(F32) + four[...].astype(F32)
        gu_sum[part, :] = value.astype(BF16)
        yield

    rings = [ring_y(i) for i in range(3)]
    for ring in rings:
        next(ring)
    for m in range(3):
        lanes = slice(512 * m, 512 * (m + 1))

        @pl.loop(0, 4)
        def _(c):
            part = pl.ds(pl.multiple_of(c * 2 * rows, 2 * rows), 2 * rows)
            down_v[part, lanes] = jnp.dot(act[part, :], wd_v[:, lanes], preferred_element_type=F32).astype(BF16)

    result = {
        "u1": mail.post(block(down_v, 2, 0), res_up1, up),
        "d1": mail.post(block(down_v, 2, 1), res_down1, down),
        "u2": mail.post(block(down_v, 3, 1), res_up2.at[1], up),
        "d2": mail.post(block(down_v, 1, 0), res_down2.at[0], down),
    }
    settle(0)
    settle(1)
    turn_over(act, turned)

    @pl.loop(0, width // tile)
    def _(n):
        lanes = pl.ds(pl.multiple_of(n * tile, tile), tile)
        wd_v[:, lanes] = jnp.dot(
            turned[0:share, :], cot_v[:, lanes], preferred_element_type=F32
        ).astype(BF16)

    half_share = share // 2
    rows_there = pl.ds(pl.multiple_of((1 - core) * half_share, 16), half_share)
    rows_mine = pl.ds(pl.multiple_of(core * half_share, 16), half_share)
    shared += [
        mail.post(wd_v.at[rows_there, pl.ds(j * piece, piece)], dn_in.at[j], twin) for j in range(4)
    ]
    for ring in rings:
        next(ring)
    for j in range(4):
        shared[4 + j].wait_recv()
        dn_in[j] = (wd_v[rows_mine, pl.ds(j * piece, piece)].astype(F32) + dn_in[j].astype(F32)).astype(BF16)
        keep(dn_in.at[j], dn_half.at[j])
    result["u1"].wait_recv()
    res_up1[...] = (block(down_v, 3, 0)[...].astype(F32) + res_up1[...].astype(F32)).astype(BF16)
    result["u3"] = mail.post(res_up1, res_up2.at[0], up)
    result["d1"].wait_recv()
    res_down1[...] = (block(down_v, 1, 1)[...].astype(F32) + res_down1[...].astype(F32)).astype(BF16)
    result["d3"] = mail.post(res_down1, res_down2.at[1], down)
    for half, i in ((0, 0), (1, 0), (0, 1), (1, 1)):
        rows_i = pl.ds(i * size, size)
        swaps[half, i].wait_recv()
        total[pl.ds(half * rows + i * size, size), :] = stage[half, rows_i, :].astype(F32) + other[
            half, rows_i, :
        ].astype(F32)
    next(rings[0])
    next(rings[1])
    next(rings[2])
    for name in ("u2", "d2", "u3", "d3"):
        result[name].wait_recv()
    for half in range(2):
        value = block(down_v, 0, half)[...].astype(F32) + res_up2[half].astype(F32) + res_down2[half].astype(F32)
        result_sum[pl.ds(half * rows, rows), :] = value.astype(BF16)
    for copy in kept:
        if copy is not None:
            copy.wait()
    mail.finish()


def back_kernel(
    total,
    middle,
    cot,
    gains,
    tok,
    normed,
    query,
    kv_a,
    kv_b,
    logs,
    attended,
    tables,
    turned_a,
    turned_b,
    w_in,
    w_out,
    gu,
    dn,
    result_sum,
    gu_out,
    dn_out,
    in_out,
    wo_out,
    grad_out,
    result_out,
    small_out,
    middle_v,
    cot_v,
    tok_v,
    normed_v,
    query_v,
    kva,
    kvb,
    attended_v,
    turned_a_v,
    turned_b_v,
    w_in_v,
    w_out_v,
    gu_v,
    dn_v,
    down_v,
    gain_rows,
    grad_middle,
    grad_low,
    grad_att,
    flat,
    keys_t,
    dkv_a,
    dkv_b,
    low_kv,
    own_kv,
    from_own,
    from_near,
    grad_pre,
    grad_part,
    grad_in,
    part_in,
    rows_out,
    result_rows,
    gu_n,
    gu_s,
    dn_up1,
    dn_down1,
    dn_up2,
    dn_down2,
    dn_y,
    dn_n,
    dn_s,
    in_p,
    in_t,
    in_up1,
    in_down1,
    in_up2,
    in_down2,
    in_s,
    in_n,
    in_z,
    wo_p,
    wo_t,
    wo_up1,
    wo_down1,
    wo_up2,
    wo_down2,
    wo_s,
    wo_n,
    wo_z,
    bias_own,
    gains_own,
    bias_in,
    gains_in,
    small_a,
    small_b,
    small_t,
    small_n,
    send,
    recv,
    local,
):
    place = here()
    dp, row, col = place
    core = dp % 2
    z = dp // Z_STEP
    twin, near, pair = twin_of(place), near_of(place), pair_of(place)
    up, down, far_z = along_z(place, 1), along_z(place, 3), along_z(place, 2)
    right, left = along_y(place, 1), along_y(place, 3)
    meet(
        [along_y(place, s) for s in (1, 2, 3)]
        + [near_of(place, (row + s) % 4) for s in range(4)]
        + [pair_of(place, (row + s) % 4) for s in range(4)]
        + [twin, up, down, far_z]
    )
    mail = Mail(send, recv)
    kept, arrivals = [], []

    def keep(source, target):
        kept.append(pltpu.make_async_copy(source, target, local.at[len(kept)]))
        kept[-1].start()
        return len(kept) - 1

    def kept_wait(index):
        kept[index].wait()
        kept[index] = None

    def even(start, size):
        return pl.ds(pl.multiple_of(start, 16), size)

    def plus(*values):
        result = values[0].astype(F32)
        for value in values[1:]:
            result = result + value.astype(F32)
        return result

    def dot_nt(left, right):
        return lax.dot_general(left, right, (((1,), (1,)), ((), ())), preferred_element_type=F32)

    rows = tok.shape[0] // 2
    width = tok.shape[1]
    piece = width // 4
    spot = even(row * rows, rows)
    own_rows, other_rows = even(col * rows, rows), even((1 - col) * rows, rows)

    def ffn_flow(i):
        if i < 3:
            height = gu.shape[0] // 3
            start = i * height
            theirs, done = gu_n.at[i], gu_s.at[i]
            mine = gu_v.at[pl.ds(start, height), :]
            swap = mail.post(gu.at[pl.ds(start, height), :], theirs, near)
            half = height // 2
            yield
            if i == 0:
                kept_wait(loads["gu"])
        else:
            height = dn.shape[1]
            start, mine, theirs, done = 0, dn_y, dn_n, dn_s
            half = height // 2
            low, high = pl.ds(start, half), pl.ds(start + half, half)
            first = (mail.post(dn.at[2, low, :], dn_up1, right), mail.post(dn.at[2, high, :], dn_down1, left))
            straight = (
                mail.post(dn.at[1, high, :], dn_up2.at[pl.ds(half, half), :], right),
                mail.post(dn.at[3, low, :], dn_down2.at[pl.ds(0, half), :], left),
            )
            yield
            kept_wait(loads["dn"])
            first[0].wait_recv()
            dn_up1[...] = plus(dn_v[1, low, :], dn_up1[...]).astype(BF16)
            last = [mail.post(dn_up1, dn_up2.at[pl.ds(0, half), :], right)]
            first[1].wait_recv()
            dn_down1[...] = plus(dn_v[3, high, :], dn_down1[...]).astype(BF16)
            last.append(mail.post(dn_down1, dn_down2.at[pl.ds(half, half), :], left))
            yield
            for copy in straight + tuple(last):
                copy.wait_recv()
            mine[...] = plus(dn_v[0], dn_up2[...], dn_down2[...]).astype(BF16)
            swap = mail.post(mine, theirs, near)
            yield
        swap.wait_recv()
        done[...] = plus(mine[...], theirs[...]).astype(BF16)

        def room(slot, which=None):
            begin, size = (start, height) if which is None else (start + which * half, half)
            if i < 3:
                share = gu_out.shape[2] // 4
                lanes = pl.ds(pl.multiple_of(slot * share, LANES), share)
                return gu_out.at[core, pl.ds(begin, size), lanes]
            return dn_out.at[even((slot * 2 + core) * height + begin, size), :]

        posts = {}
        for turn in range(2):
            for name, device, which in (("u", up, turn), ("d", down, 1 - turn)):
                posts[name, which] = mail.post(done.at[pl.ds(which * half, half), :], room(z, which), device)
        keep(done, room(z))
        arrivals.append(mail.post(done, room(z), twin))
        yield
        posts["u", 0].wait_recv()
        block = room((z + 3) % 4, 0)
        one_more = mail.post(block, block, up)
        posts["d", 1].wait_recv()
        block = room((z + 1) % 4, 1)
        two_more = mail.post(block, block, down)
        yield
        posts["u", 1].wait_recv()
        block = room((z + 3) % 4)
        arrivals.append(mail.post(block, block, twin))
        posts["d", 0].wait_recv()
        block = room((z + 1) % 4)
        arrivals.append(mail.post(block, block, twin))
        one_more.wait_recv()
        two_more.wait_recv()
        block = room((z + 2) % 4)
        arrivals.append(mail.post(block, block, twin))
        yield

    def weight_flow(part, t, up1, down1, up2, down2, total_h, theirs, quarter, out):
        height = t.shape[1]
        half = height // 2
        low, high = pl.ds(0, half), pl.ds(half, half)
        copy = mail.post(part.at[:, even((1 - core) * height, height), :], t, twin)
        yield
        copy.wait_recv()
        for j in range(4):
            t[j] = plus(part[j, even(core * height, height), :], t[j]).astype(BF16)
        first = (mail.post(t.at[2, low, :], up1, right), mail.post(t.at[2, high, :], down1, left))
        straight = (
            mail.post(t.at[1, high, :], up2.at[high, :], right),
            mail.post(t.at[3, low, :], down2.at[low, :], left),
        )
        yield
        first[0].wait_recv()
        up1[...] = plus(t[1, low, :], up1[...]).astype(BF16)
        last = [mail.post(up1, up2.at[low, :], right)]
        first[1].wait_recv()
        down1[...] = plus(t[3, high, :], down1[...]).astype(BF16)
        last.append(mail.post(down1, down2.at[high, :], left))
        yield
        for copy in straight + tuple(last):
            copy.wait_recv()
        total_h[...] = plus(t[0], up2[...], down2[...]).astype(BF16)
        swap = mail.post(total_h, theirs, near)
        yield
        swap.wait_recv()
        t[0] = plus(total_h[...], theirs[...]).astype(BF16)
        size = height // 4
        copies = []
        for step, device in ((1, up), (3, down), (2, far_z)):
            source = t.at[0, even(((z + step) % 4) * size, size), :]
            copies.append(mail.post(source, quarter.at[step - 1], device))
        yield
        for copy in copies:
            copy.wait_recv()
        mine = even(z * size, size)
        theirs[0:size, :] = plus(t[0, mine, :], quarter[0], quarter[1], quarter[2]).astype(BF16)
        place_of = lambda owner: out.at[even(core * height + owner * size, size), :]
        copies = [mail.post(theirs.at[0:size, :], place_of(z), device) for device in (up, down, far_z)]
        arrivals.append(mail.post(theirs.at[0:size, :], place_of(z), twin))
        keep(theirs.at[0:size, :], place_of(z))
        yield
        for copy in copies:
            copy.wait_recv()
        for step in (1, 2, 3):
            block = place_of((z + step) % 4)
            arrivals.append(mail.post(block, block, twin))
        yield

    def result_flow():
        swap = mail.post(result_sum.at[other_rows, :], part_in, pair)
        yield
        kept_wait(loads["down"])
        swap.wait_recv()
        result_rows[...] = (middle_v[own_rows, :] + plus(down_v[own_rows, :], part_in[...])).astype(BF16)
        yield
        spread(result_rows, result_out)
        yield

    def spread(source, target):
        for step in range(4):
            lanes = pl.ds(step * piece, piece)
            if step:
                arrivals.append(mail.post(source.at[:, lanes], target.at[spot, :], along_y(place, step)))
            else:
                keep(source.at[:, lanes], target.at[spot, :])

    flows = [ffn_flow(i) for i in range(4)]
    loads = {}
    for name, source, target in (
        ("middle", middle, middle_v),
        ("cot", cot.at[0], cot_v),
        ("w_out", w_out, w_out_v),
        ("attended", attended, attended_v),
        ("query", query, query_v),
        ("kva", kv_a, kva),
        ("kvb", kv_b, kvb),
        ("ta", turned_a, turned_a_v),
        ("tb", turned_b, turned_b_v),
        ("gu", gu, gu_v),
        ("w_in", w_in, w_in_v),
        ("normed", normed, normed_v),
        ("tok", tok, tok_v),
        ("dn", dn, dn_v),
        ("down", result_sum, down_v),
    ):
        loads[name] = keep(source, target)
    result_steps = result_flow()
    for j in range(4):
        gain_rows[:, j * piece : (j + 1) * piece] = gains[j]

    def norm_back(stream, gain, incoming):
        scale = lax.rsqrt(jnp.sum(stream * stream, -1, keepdims=True) * (1.0 / width) + EPS)
        scaled = incoming * gain
        inner = jnp.sum(scaled * stream, -1, keepdims=True) * (1.0 / width)
        back = scale * scaled - stream * (scale * scale * scale * inner)
        return back, jnp.sum(incoming * stream * scale, 0, keepdims=True)

    kept_wait(loads["middle"])
    kept_wait(loads["cot"])
    gain_ffn_part = jnp.zeros((1, width), F32)
    for half in range(2):
        part = slice(half * rows, (half + 1) * rows)
        back, gain_part = norm_back(middle_v[part, :], gain_rows[1:2, :], total[part, :])
        value = cot_v[part, :].astype(F32) + back
        grad_middle[part, :] = value
        grad_low[part, :] = value.astype(BF16)
        gain_ffn_part = gain_ffn_part + gain_part
    gains_own[...] = jnp.zeros_like(gains_own)
    for j in range(4):
        gains_own[j, 1:2, :] = 0.5 * gain_ffn_part[:, j * piece : (j + 1) * piece]
    next(flows[0])
    next(flows[3])
    kept_wait(loads["w_out"])
    q_width = w_out.shape[0]
    for first in range(0, q_width, 256):
        lanes = slice(first, first + 256)
        grad_att[:, lanes] = dot_nt(grad_low[...], w_out_v[lanes, :]).astype(BF16)

    def turn_over(source, target, count):
        for t in range(count):
            lanes = slice(t * LANES, (t + 1) * LANES)
            target[lanes, 0 : source.shape[0]] = source[:, lanes].T

    kept_wait(loads["attended"])
    turn_over(attended_v, flat, q_width // LANES)
    for j in range(4):
        wo_p[j] = jnp.dot(
            flat[0:q_width, :], grad_low[:, j * piece : (j + 1) * piece], preferred_element_type=F32
        ).astype(BF16)
    wo_steps = weight_flow(wo_p, wo_t, wo_up1, wo_down1, wo_up2, wo_down2, wo_s, wo_n, wo_z, wo_out)

    for name in ("query", "kva", "kvb", "ta", "tb"):
        kept_wait(loads[name])
    heads = q_width // HEAD_SIZE
    factor = HEAD_SIZE ** (-0.5)

    def unrotate(value, half):
        part = slice(half * rows, (half + 1) * rows)
        return value * tables[0, part, :] + pltpu.roll(value * tables[1, part, :], HEAD_SIZE // 2, 1)

    def attend_back(half, keys, mask, sums):
        part = slice(half * rows, (half + 1) * rows)
        count = keys.shape[0]
        for t in range(count // LANES):
            lanes = slice(t * LANES, (t + 1) * LANES)
            keys_t[:, lanes] = keys[lanes, 0:HEAD_SIZE].T
        sums[...] = jnp.zeros_like(sums)

        @pl.loop(0, heads)
        def _(h):
            lanes = pl.ds(pl.multiple_of(h * HEAD_SIZE, LANES), HEAD_SIZE)
            one, grad = query_v[part, lanes], grad_att[part, lanes]
            raw = dot_nt(keys[:, 0:HEAD_SIZE], one)
            probs = jnp.exp(raw * factor + mask[...] - logs[half * heads + h, 0:1, :])
            grad_probs = dot_nt(keys[:, HEAD_SIZE : 2 * HEAD_SIZE], grad)
            inner = jnp.sum(grad_probs * probs, 0, keepdims=True)
            grad_scores = (probs * (grad_probs - inner)).astype(BF16)
            sums[:, 0:HEAD_SIZE] += jnp.dot(grad_scores, one, preferred_element_type=F32)
            sums[:, HEAD_SIZE : 2 * HEAD_SIZE] += jnp.dot(probs.astype(BF16), grad, preferred_element_type=F32)
            grad_query = jnp.dot(keys_t[:, 0:count], grad_scores, preferred_element_type=F32).T * factor
            grad_pre[part, lanes] = unrotate(grad_query, half).astype(BF16)

    def low_sums(sums, part):
        return (sums[part, 0:HEAD_SIZE] * factor).astype(BF16), sums[part, HEAD_SIZE : 2 * HEAD_SIZE].astype(BF16)

    next(flows[1])
    attend_back(1, kvb, turned_b_v, dkv_b)
    half_rows = kva.shape[0]
    low_part, high_part = slice(0, half_rows), slice(half_rows, 2 * half_rows)
    for target, sums, part in ((low_kv, dkv_b, low_part), (own_kv.at[1], dkv_b, high_part)):
        target[:, 0:HEAD_SIZE], target[:, HEAD_SIZE : 2 * HEAD_SIZE] = low_sums(sums, part)
    kv_got = []
    for step in range(4):
        other = (row + step) % 4
        part = even(other * rows, rows)
        kv_got.append(mail.post(low_kv.at[part, :], from_near.at[step], near_of(place, other)))
        if step:
            kv_got.append(mail.post(own_kv.at[1, part, :], from_own.at[step - 1, 1], along_y(place, step)))
    next(flows[0])
    attend_back(0, kva, turned_a_v, dkv_a)
    target = own_kv.at[0]
    target[:, 0:HEAD_SIZE], target[:, HEAD_SIZE : 2 * HEAD_SIZE] = low_sums(dkv_a, low_part)
    for step in (1, 2, 3):
        part = even(((row + step) % 4) * rows, rows)
        kv_got.append(mail.post(own_kv.at[0, part, :], from_own.at[step - 1, 0], along_y(place, step)))
    next(result_steps)
    next(flows[3])
    next(flows[0])
    next(wo_steps)
    next(flows[2])
    kept_wait(loads["normed"])
    turn_over(normed_v, flat, width // LANES)
    next(flows[1])
    for copy in kv_got:
        copy.wait_recv()
    for half in range(2):
        part = slice(half * rows, (half + 1) * rows)
        value = own_kv[half, spot, :].astype(F32)
        for step in range(3):
            value = value + from_own[step, half].astype(F32)
        if half == 0:
            for step in range(4):
                value = value + from_near[step].astype(F32)
        grad_pre[part, q_width : q_width + HEAD_SIZE] = unrotate(value[:, 0:HEAD_SIZE], half).astype(BF16)
        grad_pre[part, q_width + HEAD_SIZE : q_width + 2 * HEAD_SIZE] = value[:, HEAD_SIZE : 2 * HEAD_SIZE].astype(
            BF16
        )
    next(wo_steps)
    kept_wait(loads["w_in"])
    for j in range(4):
        grad_part[:, j * piece : (j + 1) * piece] = dot_nt(grad_pre[...], w_in_v[j]).astype(BF16)
    swap = mail.post(grad_part.at[other_rows, :], grad_in, pair)
    for j in range(4):
        in_p[j] = jnp.dot(flat[j * piece : (j + 1) * piece, :], grad_pre[...], preferred_element_type=F32).astype(BF16)
    in_steps = weight_flow(in_p, in_t, in_up1, in_down1, in_up2, in_down2, in_s, in_n, in_z, in_out)
    next(flows[3])
    next(flows[2])
    next(flows[1])
    next(wo_steps)
    next(in_steps)
    next(in_steps)
    next(flows[3])
    next(wo_steps)
    bias_own[...] = jnp.zeros_like(bias_own)
    bias_own[0:1, :] = jnp.sum(grad_pre[...].astype(F32), 0, keepdims=True)
    next(in_steps)
    kept_wait(loads["tok"])
    swap.wait_recv()
    back, gain_part = norm_back(
        tok_v[own_rows, :].astype(F32), gain_rows[0:1, :], plus(grad_part[own_rows, :], grad_in[...])
    )
    rows_out[...] = (grad_middle[own_rows, :] + back).astype(BF16)
    for j in range(4):
        gains_own[j, 0:1, :] = gain_part[:, j * piece : (j + 1) * piece]
    next(result_steps)
    next(wo_steps)
    next(in_steps)
    next(flows[0])
    next(flows[2])
    next(wo_steps)
    next(result_steps)
    small_copies, small_kept = [], []
    for step in range(4):
        device = along_y(place, step)
        mine = gains_in.at[col * 4 + row]
        if step:
            small_copies.append(mail.post(bias_own, bias_in.at[row], device))
            small_copies.append(mail.post(gains_own.at[step], mine, device))
        else:
            small_kept.append(keep(bias_own, bias_in.at[row]))
            small_kept.append(keep(gains_own.at[step], mine))
        small_copies.append(mail.post(gains_own.at[step], mine, pair_of(place, (row + step) % 4)))
    spread(rows_out, grad_out)
    next(flows[3])
    next(in_steps)
    for copy in small_copies:
        copy.wait_recv()
    for index in small_kept:
        kept_wait(index)
    small_a[...] = jnp.zeros_like(small_a)
    small_a[0:8, :] = bias_in[0] + bias_in[1] + bias_in[2] + bias_in[3]
    small_a[8:16, 0:piece] = (
        gains_in[0] + gains_in[1] + gains_in[2] + gains_in[3] + gains_in[4] + gains_in[5] + gains_in[6] + gains_in[7]
    )
    small_first = mail.post(small_a, small_t, twin)
    next(flows[1])
    next(wo_steps)
    next(in_steps)
    small_first.wait_recv()
    small_b[...] = small_a[...] + small_t[...]
    small_second = mail.post(small_b, small_n, near)
    small_second.wait_recv()
    small_t[...] = small_b[...] + small_n[...]
    for device in (up, down, far_z):
        arrivals.append(mail.post(small_t, small_out.at[z], device))
    keep(small_t, small_out.at[z])
    for steps in [*flows, wo_steps, in_steps, result_steps]:
        for _ in steps:
            pass
    for copy in arrivals:
        copy.wait_recv()
    for copy in kept:
        if copy is not None:
            copy.wait()
    mail.finish()


def widen_kernel(gate_up, down, w_in, w_out, result, tokens, small, *outs):
    result_w, tokens_w, query_w, key_w, value_w, out_w, gate_w, up_w, down_w, *flat = outs
    total = small[0] + small[1] + small[2] + small[3]
    start = 0
    for line, out in zip((0, 0, 0, 8, 9), flat):
        start = 0 if line else start
        out[...] = total[line, start : start + out.shape[0]]
        start += out.shape[0]
    result_w[...] = result[...].astype(F32)
    tokens_w[...] = tokens[...].astype(F32)
    first, second = query_w.shape[1], query_w.shape[1] + key_w.shape[1]
    query_w[...] = w_in[:, :first].astype(F32)
    key_w[...] = w_in[:, first:second].astype(F32)
    value_w[...] = w_in[:, second:].astype(F32)
    out_w[...] = w_out[...].astype(F32)
    gate_w[...] = gate_up[0, :, : gate_w.shape[1]].astype(F32)
    up_w[...] = gate_up[1, :, : up_w.shape[1]].astype(F32)
    down_w[...] = down[...].astype(F32)


def on_device(
    tokens,
    cotangent,
    lengths,
    gain_attn,
    w_query,
    key_projection,
    value_projection,
    bias_query,
    key_bias_vector,
    value_bias_vector,
    w_out,
    gain_ffn,
    w_gate,
    w_up,
    w_down,
):
    half_rows, piece = tokens.shape
    width = 4 * piece
    rows = half_rows // 4
    q_width = w_query.shape[1]
    kv_width = key_projection.shape[1]
    heads = q_width // HEAD_SIZE
    hidden = w_gate.shape[1]
    share = -(-hidden // (4 * LANES)) * LANES

    in_width = q_width + 2 * kv_width
    thin = piece // 2
    (
        tok_rows,
        cot_full,
        gains4,
        normed,
        query,
        kv_a,
        kv_b,
        logs,
        attended,
        tables,
        middle,
        mask_a,
        mask_b,
        normed_ffn,
        w_in_full,
        w_out_full,
        w_gu_full,
        w_down_full,
    ) = talk(
        front_kernel,
        0,
        FRONT_COPIES,
        FRONT_LOCAL,
        [
            ((2 * rows, width), BF16),
            ((4, 2 * rows, width), BF16),
            ((4, 8, piece), F32),
            ((2 * rows, width), BF16),
            ((2 * rows, q_width), BF16),
            ((half_rows, 2 * kv_width), BF16),
            ((2 * half_rows, 2 * kv_width), BF16),
            ((2 * heads, 8, rows), F32),
            ((2 * rows, q_width), BF16),
            ((2, 2 * rows, HEAD_SIZE), F32),
            ((2 * rows, width), F32),
            ((half_rows, rows), F32),
            ((2 * half_rows, rows), F32),
            ((2 * rows, width), BF16),
            ((4, piece, in_width), BF16),
            ((q_width, width), BF16),
            ((4, 2, thin, 2 * share), BF16),
            ((share, width), BF16),
        ],
        [ANY] * 2 + [VMEM] * 6 + [ANY] * 7,
        [ANY] * 3 + [VMEM] * 2 + [ANY] * 2 + [VMEM] * 7 + [ANY] * 4,
        [
            pltpu.VMEM((8, LANES), jnp.int32),
            pltpu.VMEM((8, piece), F32),
            pltpu.VMEM((2 * rows, width), BF16),
            pltpu.VMEM((2, 8, LANES), jnp.int32),
            pltpu.VMEM((4, 8, piece), F32),
            pltpu.VMEM((4, piece, in_width), BF16),
            pltpu.VMEM((q_width, width), BF16),
            pltpu.VMEM((2, thin, 2 * share), BF16),
            pltpu.VMEM((share, piece), BF16),
            pltpu.VMEM((thin, LANES), BF16),
            pltpu.VMEM((LANES, piece), BF16),
            pltpu.VMEM((2 * rows, 2 * kv_width), BF16),
            pltpu.VMEM((half_rows, 2 * kv_width), BF16),
            pltpu.VMEM((2 * half_rows, 2 * kv_width), BF16),
            pltpu.VMEM((rows, half_rows), F32),
            pltpu.VMEM((rows, 2 * half_rows), F32),
            pltpu.VMEM((2 * rows, width), BF16),
            pltpu.VMEM((2 * rows, width), BF16),
        ],
        limit=56,
    )(
        tokens,
        cotangent,
        lengths,
        gain_attn,
        gain_ffn,
        bias_query,
        key_bias_vector,
        value_bias_vector,
        w_query,
        key_projection,
        value_projection,
        w_out,
        w_gate,
        w_up,
        w_down,
    )

    w_both_full = w_gu_full.reshape(width, 2 * share)
    half_block = (2, rows, width)
    grad_normed_ffn, both_sum, down_half, result_sum = talk(
        ffn_kernel,
        4,
        52,
        14,
        [
            ((2 * rows, width), F32),
            ((piece, share), BF16),
            ((4, share // 2, piece), BF16),
            ((2 * rows, width), BF16),
        ],
        [ANY] * 4,
        [VMEM, VMEM, ANY, VMEM],
        [
            pltpu.VMEM(shape, BF16)
            for shape in (
                (8 * rows, width),
                (8 * rows, width),
                (width, 2 * share),
                (share, width),
                (8 * rows, 2 * share),
                (8 * rows, share),
                (8 * rows, width),
                (width, 8 * rows),
                (8 * rows, width),
                (4, piece, share),
                (4, share // 2, piece),
                (2, rows // 2, width),
                (2, rows // 2, width),
                half_block,
                half_block,
                half_block,
                (2, rows // 2, width),
                (2, rows // 2, width),
                half_block,
                (rows, width),
                (rows, width),
                half_block,
                half_block,
                (3, piece // 6, share),
                (3, piece // 6, share),
                (3, piece // 3, share),
                (3, piece // 3, share),
            )
        ],
        limit=60,
    )(normed_ffn, cot_full, w_both_full, w_down_full)
    thirds = piece // 3
    q_half, w_half = (thin, in_width), (q_width // 2, piece)
    gu_chunk, dn_chunk = (3, thirds, share), (share // 2, piece)

    def halved(shape):
        return (*shape[:-2], shape[-2] // 2, shape[-1])

    def weight_scratch(shape):
        return [
            (4, 2 * shape[0], shape[1]),
            (4, *shape),
            halved(shape),
            halved(shape),
            shape,
            shape,
            shape,
            shape,
            (3, shape[0] // 4, shape[1]),
        ]

    def scratch(kind, *shapes):
        return [pltpu.VMEM(shape, kind) for shape in shapes]

    gate_up, down_all, in_total, out_total, grad_tokens, result, small_all = talk(
        back_kernel,
        8,
        BACK_COPIES,
        BACK_LOCAL,
        [
            ((2, piece, 4 * share), BF16),
            ((4 * share, piece), BF16),
            ((piece, in_width), BF16),
            ((q_width, piece), BF16),
            ((half_rows, piece), BF16),
            ((half_rows, piece), BF16),
            ((4, 16, in_width), F32),
        ],
        [VMEM, ANY, ANY, VMEM] + [ANY] * 5 + [VMEM, ANY, VMEM] + [ANY] * 7,
        [ANY] * 7,
        scratch(F32, (2 * rows, width))
        + scratch(
            BF16,
            (2 * rows, width),
            (2 * rows, width),
            (2 * rows, width),
            (2 * rows, q_width),
            (half_rows, 2 * kv_width),
            (2 * half_rows, 2 * kv_width),
            (2 * rows, q_width),
        )
        + scratch(F32, (half_rows, rows), (2 * half_rows, rows))
        + scratch(
            BF16,
            (4, piece, in_width),
            (q_width, width),
            (piece, share),
            (4, share // 2, piece),
            (2 * rows, width),
        )
        + scratch(F32, (8, width), (2 * rows, width))
        + scratch(BF16, (2 * rows, width), (2 * rows, q_width), (width, 2 * rows), (HEAD_SIZE, 2 * half_rows))
        + scratch(F32, (half_rows, 2 * kv_width), (2 * half_rows, 2 * kv_width))
        + scratch(
            BF16,
            (half_rows, 2 * kv_width),
            (2, half_rows, 2 * kv_width),
            (3, 2, rows, 2 * kv_width),
            (4, rows, 2 * kv_width),
            (2 * rows, in_width),
            (2 * rows, width),
            (rows, width),
            (rows, width),
            (rows, width),
            (rows, width),
            gu_chunk,
            gu_chunk,
            halved(dn_chunk),
            halved(dn_chunk),
            dn_chunk,
            dn_chunk,
            dn_chunk,
            dn_chunk,
            dn_chunk,
            *weight_scratch(q_half),
            *weight_scratch(w_half),
        )
        + scratch(F32, (8, in_width), (4, 8, piece), (4, 8, in_width), (8, 8, piece))
        + scratch(F32, *[(16, in_width)] * 4),
        limit=60,
    )(
        grad_normed_ffn,
        middle,
        cot_full,
        gains4,
        tok_rows,
        normed,
        query,
        kv_a,
        kv_b,
        logs,
        attended,
        tables,
        mask_a,
        mask_b,
        w_in_full,
        w_out_full,
        both_sum,
        down_half,
        result_sum,
    )
    steps = 8
    narrow = [gate_up, down_all, in_total, out_total, result, grad_tokens, small_all]
    lines = [(q_width,), (kv_width,), (kv_width,), (piece,), (piece,)]
    wide = [
        (half_rows, piece),
        (half_rows, piece),
        (piece, q_width),
        (piece, kv_width),
        (piece, kv_width),
        (q_width, piece),
        (piece, hidden),
        (piece, hidden),
        (hidden, piece),
    ]

    def in_block(array):
        if array is small_all:
            return pl.BlockSpec(array.shape, lambda i: (0, 0, 0))
        if array.ndim == 3:
            return pl.BlockSpec((2, array.shape[1] // steps, array.shape[2]), lambda i: (0, i, 0))
        if array is down_all:
            return pl.BlockSpec((hidden // steps, piece), lambda i: (i, 0))
        return pl.BlockSpec((array.shape[0] // steps, array.shape[1]), lambda i: (i, 0))

    wide_out = pl.pallas_call(
        widen_kernel,
        grid=(steps,),
        out_shape=[jax.ShapeDtypeStruct(shape, F32) for shape in wide + lines],
        in_specs=[in_block(array) for array in narrow],
        out_specs=[pl.BlockSpec((shape[0] // steps, shape[1]), lambda i: (i, 0)) for shape in wide]
        + [pl.BlockSpec(shape, lambda i: (0,)) for shape in lines],
        compiler_params=pltpu.CompilerParams(vmem_limit_bytes=60 << 20),
    )(*narrow)
    result_w, tokens_w, query_w, key_w, value_w, out_w, gate_w, up_w, down_w, *flat = wide_out
    bias_q, bias_k, bias_v, gain_one, gain_two = flat
    return (
        result_w,
        tokens_w,
        gain_one,
        query_w,
        key_w,
        value_w,
        bias_q,
        bias_k,
        bias_v,
        out_w,
        gain_two,
        gate_w,
        up_w,
        down_w,
    )


def solution(mesh):
    placed = (
        P(("dp", "col"), "row"),
        P(("dp", "col"), "row"),
        P("dp", None),
        P("row"),
        P("row", "col"),
        P("row", "col"),
        P("row", "col"),
        P("col"),
        P("col"),
        P("col"),
        P("col", "row"),
        P("row"),
        P("row", "col"),
        P("row", "col"),
        P("col", "row"),
    )
    return jax.shard_map(
        on_device,
        mesh=mesh,
        in_specs=placed,
        out_specs=(
            P(("dp", "col"), "row"),
            P(("dp", "col"), "row"),
            P("row"),
            P("row", "col"),
            P("row", "col"),
            P("row", "col"),
            P("col"),
            P("col"),
            P("col"),
            P("col", "row"),
            P("row"),
            P("row", "col"),
            P("row", "col"),
            P("col", "row"),
        ),
        check_vma=False,
    )
```

```python
import math

import jax
import jax.numpy as jnp
from jax import lax
from jax.experimental import pallas as pl
from jax.experimental.pallas import tpu as pltpu
from jax.sharding import PartitionSpec as P

HEAD_SIZE = 128
EPS = 1e-06
THETA = 1000000.0
LANES = 128
MESH = pl.DeviceIdType.MESH
BF16 = jnp.bfloat16
F32 = jnp.float32
ANY = pl.BlockSpec(memory_space=pl.ANY)
VMEM = pl.BlockSpec(memory_space=pltpu.VMEM)

Z_STEP = 4
FRONT_COPIES = 77
FRONT_LOCAL = 27
BACK_COPIES = 139
BACK_LOCAL = 27


def here():
    return lax.axis_index("dp"), lax.axis_index("row"), lax.axis_index("col")


def flip_near(dp):
    return dp + 2 - 4 * ((dp // 2) % 2)


def pair_of(place, row=None):
    dp, own, col = place
    return flip_near(dp), own if row is None else row, 1 - col


def near_of(place, row=None):
    dp, own, col = place
    return flip_near(dp), own if row is None else row, col


def twin_of(place):
    dp, row, col = place
    return dp + 1 - 2 * (dp % 2), row, col


def along_z(place, step):
    dp, row, col = place
    return (dp + Z_STEP * step) % (4 * Z_STEP), row, col


def along_y(place, step):
    dp, row, col = place
    return dp, (row + step) % 4, col


def meet(peers):
    barrier = pltpu.get_barrier_semaphore()
    for peer in peers:
        pl.semaphore_signal(barrier, inc=1, device_id=peer, device_id_type=MESH)
    pl.semaphore_wait(barrier, len(peers))


class Mail:
    def __init__(self, send, recv):
        self.send, self.recv, self.count, self.sent = send, recv, 0, []

    def post(self, source, target, device):
        index = self.count
        self.count += 1
        copy = pltpu.make_async_remote_copy(
            src_ref=source,
            dst_ref=target,
            send_sem=self.send.at[index],
            recv_sem=self.recv.at[index],
            device_id=device,
            device_id_type=MESH,
        )
        copy.start()
        self.sent.append(copy)
        return copy

    def finish(self):
        assert self.count == self.send.shape[0], (self.count, self.send.shape)
        for copy in self.sent:
            copy.wait_send()


def talk(body, ident, copies, local, outs, in_specs, out_specs, scratch=(), limit=32):
    return pl.pallas_call(
        body,
        out_shape=[jax.ShapeDtypeStruct(*out) for out in outs],
        in_specs=in_specs,
        out_specs=out_specs,
        scratch_shapes=[
            *scratch,
            pltpu.SemaphoreType.DMA((copies,)),
            pltpu.SemaphoreType.DMA((copies,)),
            pltpu.SemaphoreType.DMA((max(local, 1),)),
        ],
        compiler_params=pltpu.CompilerParams(
            collective_id=ident, has_side_effects=True, vmem_limit_bytes=limit << 20
        ),
    )


def front_kernel(
    tok,
    cot,
    lens_in,
    gain_attn,
    gain_ffn,
    bias_q,
    bias_k,
    bias_v,
    wq,
    wk,
    wv,
    wo,
    wg,
    wu,
    wd,
    tok_out,
    cot_full,
    gains_out,
    normed,
    query,
    kva_out,
    kvb_out,
    logs,
    attended,
    tables,
    middle,
    turned_a,
    turned_b,
    normed_ffn,
    w_in_out,
    w_out_out,
    wgu_full,
    wd_full,
    lens,
    gains,
    tok_v,
    lens_v,
    gains_v,
    w_in,
    w_out,
    gu_own,
    wd_own,
    blank_gu,
    blank_wd,
    kv,
    kva,
    kvb,
    bias_a,
    bias_b,
    branch,
    branch_in,
    send,
    recv,
    local,
):
    place = here()
    dp, row, col = place
    z, core = dp // Z_STEP, dp % 2
    twin, pair, up, down = twin_of(place), pair_of(place), along_z(place, 1), along_z(place, 3)
    right, left, near = along_y(place, 1), along_y(place, 3), near_of(place)
    meet(
        [along_y(place, s) for s in (1, 2, 3)]
        + [near_of(place, (row + s) % 4) for s in range(4)]
        + [pair, twin, up, down]
    )
    mail = Mail(send, recv)
    kept = []

    def keep(source, target):
        kept.append(pltpu.make_async_copy(source, target, local.at[len(kept)]))
        kept[-1].start()
        return len(kept) - 1

    def kept_wait(index):
        kept[index].wait()
        kept[index] = None

    def even(start, size):
        return pl.ds(pl.multiple_of(start, 16), size)

    rows, piece = tok.shape[0] // 4, tok.shape[1]
    width = 4 * piece
    own_rows = even(col * rows, rows)
    spot = even(row * rows, rows)

    def spread(source, target):
        got = []
        for step in range(4):
            part = source.at[even(((row + step) % 4) * rows, rows), :]
            lanes = pl.ds(((4 - step) % 4) * piece, piece)
            if step:
                got.append(mail.post(part, target.at[own_rows, lanes], along_y(place, step)))
            else:
                mine = keep(part, target.at[own_rows, lanes])
        return got, mine

    tokens = spread(tok, tok_v)
    lens[...] = jnp.zeros_like(lens)
    lens[0:1, 0 : lens_in.shape[1]] = lens_in[...]
    gains[...] = jnp.zeros_like(gains)
    gains[0:1, :] = gain_attn[...].reshape(1, piece)
    gains[1:2, :] = gain_ffn[...].reshape(1, piece)
    lens_got = mail.post(lens, lens_v.at[col], pair)
    lens_kept = keep(lens, lens_v.at[col])
    gains_kept = keep(gains, gains_v.at[0])
    gains_got = [mail.post(gains, gains_v.at[4 - s], along_y(place, s)) for s in (1, 2, 3)]

    q_width, kv_width = wq.shape[1], wk.shape[1]
    stages = [
        keep(wq, w_in.at[0, :, pl.ds(0, q_width)]),
        keep(wk, w_in.at[0, :, pl.ds(q_width, kv_width)]),
        keep(wv, w_in.at[0, :, pl.ds(q_width + kv_width, kv_width)]),
        keep(wo, w_out.at[:, pl.ds(0, piece)]),
    ]
    share = wd_own.shape[0]
    thin = piece // 2
    sure = share - LANES
    take = pl.multiple_of(z * share, LANES)
    big = []
    for k in range(2):
        for i, source in enumerate((wg, wu)):
            from_rows = pl.ds(k * thin, thin)
            big.append(keep(source.at[from_rows, pl.ds(take, sure)], gu_own.at[k, :, pl.ds(i * share, sure)]))
    big.append(keep(wd.at[pl.ds(take, sure), :], wd_own.at[pl.ds(0, sure), :]))
    blank_gu[...] = jnp.zeros_like(blank_gu)
    blank_wd[...] = jnp.zeros_like(blank_wd)
    first_edge = len(kept)
    edges = []
    for k in range(2):
        for i, source in enumerate((wg, wu)):
            target = gu_own.at[k, :, pl.ds(i * share + sure, LANES)]
            edges.append((source, pl.ds(k * thin, thin), None, target, blank_gu))
    edges.append((wd, None, slice(None), wd_own.at[pl.ds(sure, LANES), :], blank_wd))

    def edge(index, last):
        source, from_rows, _, target, blank = edges[index]
        if last:
            origin = blank
        elif from_rows is None:
            origin = source.at[pl.ds(pl.multiple_of(take + sure, LANES), LANES), :]
        else:
            origin = source.at[from_rows, pl.ds(pl.multiple_of(take + sure, LANES), LANES)]
        return pltpu.make_async_copy(origin, target, local.at[first_edge + index])

    @pl.when(z < 3)
    def _():
        for index in range(len(edges)):
            edge(index, False).start()

    @pl.when(z == 3)
    def _():
        for index in range(len(edges)):
            edge(index, True).start()

    for index in range(len(edges)):
        kept.append(edge(index, True))
        big.append(first_edge + index)

    q_rows, o_rows = thin // 4, w_out.shape[0] // 8

    def in_part(j, owner_z):
        return w_in.at[j, even(core * thin + owner_z * q_rows, q_rows), :]

    def in_parts(owner_z):
        return w_in.at[pl.ds(1, 3), even(core * thin + owner_z * q_rows, q_rows), :]

    def in_side(owner_z, side):
        lanes = pl.ds(side * (w_in.shape[2] // 2), w_in.shape[2] // 2)
        return w_in.at[pl.ds(1, 3), even(core * thin + owner_z * q_rows, q_rows), lanes]

    def out_part(j, owner_z):
        return w_out.at[even(core * 4 * o_rows + owner_z * o_rows, o_rows), pl.ds(j * piece, piece)]

    def out_parts(owner_z):
        return w_out.at[even(core * 4 * o_rows + owner_z * o_rows, o_rows), pl.ds(piece, 3 * piece)]

    def out_side(owner_z, side):
        start = core * 4 * o_rows + owner_z * o_rows + side * (o_rows // 2)
        return w_out.at[even(start, o_rows // 2), pl.ds(piece, 3 * piece)]

    for index in stages:
        kept_wait(index)
    in_got = [mail.post(in_part(0, z), in_part(4 - step, z), along_y(place, step)) for step in (1, 3, 2)]

    def to_pair(spreading, target):
        got, mine = spreading
        kept_wait(mine)
        for copy in got:
            copy.wait_recv()
        return mail.post(target.at[own_rows, :], target.at[own_rows, :], pair)

    tokens_pair = to_pair(tokens, tok_v)
    shares = []

    def give(part):
        shares.append(mail.post(part, part, twin))

    def z_first(side):
        copies = {}
        for turn in range(2):
            copies["u", turn] = mail.post(side(z, turn), side(z, turn), up)
            copies["d", 1 - turn] = mail.post(side(z, 1 - turn), side(z, 1 - turn), down)
        return copies

    below, above, across = (z + 3) % 4, (z + 1) % 4, (z + 2) % 4

    def z_second(side, whole, copies):
        copies["u", 0].wait_recv()
        far_up = mail.post(side(below, 0), side(below, 0), up)
        copies["d", 1].wait_recv()
        far_down = mail.post(side(above, 1), side(above, 1), down)
        copies["u", 1].wait_recv()
        give(whole(below))
        copies["d", 0].wait_recv()
        give(whole(above))
        return far_up, far_down

    def z_third(whole, copies):
        for copy in copies:
            copy.wait_recv()
        give(whole(across))

    for copy in in_got:
        copy.wait_recv()
    in_z = z_first(in_side)
    give(in_parts(z))
    out_got = [mail.post(out_part(0, z), out_part(4 - step, z), along_y(place, step)) for step in (1, 3, 2)]
    cotangents = spread(cot, cot_full.at[0])
    for index in big:
        kept_wait(index)
    x_lo = (dp // 2) % 2
    gu_half, wd_half = thin // 4, share // 4

    def gu_part(j, which=None, owner=x_lo):
        start, size = (0, 2 * gu_half) if which is None else (which * gu_half, gu_half)
        return wgu_full.at[j, core, even(owner * 2 * gu_half + start, size), :]

    def gu_whole(j):
        return wgu_full.at[j, core]

    def wd_part(j, which=None):
        start, size = (0, 2 * wd_half) if which is None else (which * wd_half, wd_half)
        return wd_full.at[even(core * 2 * wd_half + start, size), pl.ds(j * piece, piece)]

    def gu_source(which):
        return gu_own.at[core, even((x_lo * 2 + which) * gu_half, gu_half), :]

    def wd_source(which):
        return wd_own.at[even((core * 2 + which) * wd_half, wd_half), :]

    y_ring, near_gu, twins = {}, [], []

    def y_start(name, source, part):
        for turn in range(2):
            y_ring[name, "r", turn] = mail.post(source(turn), part(3, turn), right)
            y_ring[name, "l", 1 - turn] = mail.post(source(1 - turn), part(1, 1 - turn), left)

    def y_forward(name, part):
        y_ring[name, "r", 0].wait_recv()
        y_ring[name, "fr"] = mail.post(part(3, 0), part(2, 0), right)
        y_ring[name, "l", 1].wait_recv()
        y_ring[name, "fl"] = mail.post(part(1, 1), part(2, 1), left)

    def y_share(name, part, queue, device):
        y_ring[name, "r", 1].wait_recv()
        queue.append(mail.post(part(3), part(3), device))
        y_ring[name, "l", 0].wait_recv()
        queue.append(mail.post(part(1), part(1), device))

    def y_end(name, part, queue, device):
        y_ring[name, "fr"].wait_recv()
        y_ring[name, "fl"].wait_recv()
        queue.append(mail.post(part(2), part(2), device))


    kept_wait(lens_kept)
    lens_got.wait_recv()
    half_rows = 4 * rows

    def segment_of(which, index):
        end_0 = lens_v[which, 0:1, 0:1]
        end_1 = end_0 + lens_v[which, 0:1, 1:2]
        past_0 = (index >= end_0).astype(jnp.int32)
        past_1 = (index >= end_1).astype(jnp.int32)
        start = jnp.where(past_1 > 0, end_1, jnp.where(past_0 > 0, end_0, 0))
        return past_0 + past_1, start

    lane = lax.broadcasted_iota(jnp.int32, (rows, HEAD_SIZE), 1)
    half_lane = jnp.where(lane >= HEAD_SIZE // 2, lane - HEAD_SIZE // 2, lane).astype(F32)
    inverse = jnp.exp(half_lane * (-2.0 * math.log(THETA) / HEAD_SIZE))
    for which, mask, mask_t, key_count in ((0, bias_a, turned_a, half_rows), (1, bias_b, turned_b, 2 * half_rows)):
        index = lax.broadcasted_iota(jnp.int32, (rows, HEAD_SIZE), 0) + (row * rows + which * half_rows)
        _, start = segment_of(which, index)
        turn = (index - start).astype(F32) * inverse
        tables[0, which * rows : (which + 1) * rows, :] = jnp.cos(turn)
        sine = jnp.sin(turn)
        tables[1, which * rows : (which + 1) * rows, :] = jnp.where(lane >= HEAD_SIZE // 2, sine, -sine)
        at = lax.broadcasted_iota(jnp.int32, (rows, key_count), 0) + (row * rows + which * half_rows)
        keys = lax.broadcasted_iota(jnp.int32, (rows, key_count), 1)
        allowed = jnp.logical_and(segment_of(which, at)[0] == segment_of(which, keys)[0], keys <= at)
        mask[...] = jnp.where(allowed, 0.0, -1e30)
        at = lax.broadcasted_iota(jnp.int32, (key_count, rows), 1) + (row * rows + which * half_rows)
        keys = lax.broadcasted_iota(jnp.int32, (key_count, rows), 0)
        allowed = jnp.logical_and(segment_of(which, at)[0] == segment_of(which, keys)[0], keys <= at)
        mask_t[...] = jnp.where(allowed, 0.0, -1e30)

    kept_wait(gains_kept)
    for copy in gains_got:
        copy.wait_recv()
    keep(gains_v, gains_out)

    def normalise(value, which):
        scale = lax.rsqrt(jnp.sum(value * value, -1, keepdims=True) * (1.0 / width) + EPS)
        return [
            (value[:, j * piece : (j + 1) * piece] * scale * gains_v[j, which : which + 1, :]).astype(BF16)
            for j in range(4)
        ]

    def norm_rows(which):
        part = pl.ds(pl.multiple_of(which * rows, rows), rows)
        for j, block in enumerate(normalise(tok_v[part, :].astype(F32), 0)):
            normed[part, pl.ds(j * piece, piece)] = block

    norm_rows(col)
    for copy in out_got:
        copy.wait_recv()
    give(out_parts(z))
    y_start("gu", gu_source, gu_part)
    keep(gu_own, wgu_full.at[0])
    keep(wd_own, wd_full.at[:, pl.ds(0, piece)])
    in_far = z_second(in_side, in_parts, in_z)
    out_z = z_first(out_side)
    tokens_pair.wait_recv()
    keep(tok_v, tok_out)
    norm_rows(1 - col)
    cot_pair = to_pair(cotangents, cot_full.at[0])
    z_third(in_parts, in_far)
    y_forward("gu", gu_part)
    y_share("gu", gu_part, near_gu, near)
    for copy in shares:
        copy.wait_recv()
    shares.clear()
    keep(w_in, w_in_out)

    in_width = w_in.shape[2]

    def project(lanes, bias):
        weights = w_in[:, :, lanes]
        weights = weights.reshape(4 * weights.shape[1], weights.shape[2])
        return jnp.dot(normed[...], weights, preferred_element_type=F32) + bias

    def rotate(value):
        return value * tables[0] + pltpu.roll(value, HEAD_SIZE // 2, 1) * tables[1]

    key_value = project(slice(q_width, in_width), jnp.concatenate([bias_k[...].reshape(1, kv_width), bias_v[...].reshape(1, kv_width)], 1))
    kv[:, 0:kv_width] = rotate(key_value[:, 0:kv_width]).astype(BF16)
    kv[:, kv_width : 2 * kv_width] = key_value[:, kv_width : 2 * kv_width].astype(BF16)
    a_rows, b_rows = pl.ds(0, rows), pl.ds(rows, rows)
    high_spot = even(half_rows + row * rows, rows)
    a_got, b_got = [], []
    for step in (1, 2, 3):
        a_got.append(mail.post(kv.at[a_rows, :], kva.at[spot, :], along_y(place, step)))
    kva[spot, :] = kv[a_rows, :]
    kvb[high_spot, :] = kv[b_rows, :]
    for first in range(0, q_width, 2 * HEAD_SIZE):
        value = project(slice(first, first + 2 * HEAD_SIZE), bias_q[first : first + 2 * HEAD_SIZE].reshape(1, 2 * HEAD_SIZE))
        for i in range(2):
            lanes = slice(first + i * HEAD_SIZE, first + (i + 1) * HEAD_SIZE)
            query[:, lanes] = rotate(value[:, i * HEAD_SIZE : (i + 1) * HEAD_SIZE]).astype(BF16)

    out_far = z_second(out_side, out_parts, out_z)
    heads = q_width // HEAD_SIZE
    factor = HEAD_SIZE ** (-0.5)

    def attend(half, keys, mask):
        part = slice(half * rows, (half + 1) * rows)

        @pl.loop(0, heads)
        def _(h):
            lanes = pl.ds(pl.multiple_of(h * HEAD_SIZE, LANES), HEAD_SIZE)
            raw = lax.dot_general(
                query[part, lanes], keys[:, 0:HEAD_SIZE], (((1,), (1,)), ((), ())), preferred_element_type=F32
            )
            scores = raw * factor + mask[...]
            peak = jnp.max(scores, -1, keepdims=True)
            raised = jnp.exp(scores - peak)
            total = jnp.sum(raised, -1, keepdims=True)
            probs = (raised * (1.0 / total)).astype(BF16)
            out = jnp.dot(probs, keys[:, HEAD_SIZE : 2 * HEAD_SIZE], preferred_element_type=F32)
            attended[part, lanes] = out.astype(BF16)
            logs[half * heads + h] = jnp.broadcast_to(peak + jnp.log(total), (rows, LANES)).T[0:8, :]

        for first in range(0, width, piece):
            lanes = slice(first, first + piece)
            branch[part, lanes] = jnp.dot(
                attended[part, :], w_out[:, lanes], preferred_element_type=F32
            ).astype(BF16)
        return mail.post(branch.at[part, :], branch_in.at[part, :], pair)

    def finish_half(half, copy):
        part = slice(half * rows, (half + 1) * rows)
        copy.wait_recv()
        value = tok_v[part, :].astype(F32) + (branch[part, :].astype(F32) + branch_in[part, :].astype(F32))
        middle[part, :] = value
        for j, block in enumerate(normalise(value, 1)):
            normed_ffn[part, j * piece : (j + 1) * piece] = block

    def z_send(source, target, half):
        part = pl.ds(half * rows, rows)
        return (
            mail.post(source.at[part, :], target.at[1, part, :], up),
            mail.post(source.at[part, :], target.at[3, part, :], down),
        )

    def z_forward(target, half, copies):
        part = pl.ds(half * rows, rows)
        if half == 0:
            copies[0].wait_recv()
            return copies[1], mail.post(target.at[1, part, :], target.at[2, part, :], up)
        copies[1].wait_recv()
        return copies[0], mail.post(target.at[3, part, :], target.at[2, part, :], down)

    for copy in a_got:
        copy.wait_recv()
    for step in range(4):
        b_got.append(mail.post(kv.at[a_rows, :], kvb.at[spot, :], near_of(place, (row + step) % 4)))
        if step:
            b_got.append(mail.post(kv.at[b_rows, :], kvb.at[high_spot, :], along_y(place, step)))
    keep(kva, kva_out)
    z_third(out_parts, out_far)
    for copy in shares:
        copy.wait_recv()
    keep(w_out, w_out_out)
    swap_a = attend(0, kva, bias_a)
    cot_pair.wait_recv()
    cot_z = [z_send(cot_full.at[0], cot_full, half) for half in range(2)]
    for copy in b_got:
        copy.wait_recv()
    keep(kvb, kvb_out)
    swap_b = attend(1, kvb, bias_b)
    y_end("gu", gu_part, near_gu, near)
    y_start("wd", wd_source, wd_part)
    finish_half(0, swap_a)
    cot_last = [z_forward(cot_full, half, cot_z[half]) for half in range(2)]
    y_forward("wd", wd_part)
    finish_half(1, swap_b)
    y_share("wd", wd_part, twins, twin)
    for j, copy in zip((3, 1, 2), near_gu):
        copy.wait_recv()
        twins.append(mail.post(gu_whole(j), gu_whole(j), twin))
    y_end("wd", wd_part, twins, twin)
    for copies in cot_last:
        for copy in copies:
            copy.wait_recv()
    for copy in twins:
        copy.wait_recv()
    for copy in kept:
        if copy is not None:
            copy.wait()
    mail.finish()


def ffn_kernel(
    normed,
    cot,
    wgu,
    wd,
    total,
    gu_sum,
    dn_half,
    result_sum,
    result_ahead,
    x,
    cot_v,
    wgu_v,
    wd_v,
    gb,
    act,
    parts,
    turned,
    down_v,
    gu_in,
    dn_in,
    up1,
    down1,
    up2,
    down2,
    other,
    stage_up,
    stage_down,
    stage,
    res_up1,
    res_down1,
    res_up2,
    res_down2,
    gu_up1,
    gu_down1,
    gu_up2,
    gu_down2,
    send,
    recv,
    local,
):
    place = here()
    dp, row, col = place
    core = dp % 2
    up, down, pair, twin = along_z(place, 1), along_z(place, 3), pair_of(place), twin_of(place)
    right, left = along_y(place, 1), along_y(place, 3)
    meet([up, down, pair, twin, right, left])
    mail = Mail(send, recv)
    order = ((0, 0), (0, 1), (1, 0), (3, 1), (2, 0), (2, 1), (1, 1), (3, 0))
    spots = {half: i for i, half in enumerate(order)}
    rows = normed.shape[0] // 2
    size = rows // 2

    def block(ref, slot, half):
        return ref.at[pl.ds(spots[slot, half] * rows, rows), :]

    def halves(ref, half):
        return ref.at[pl.ds(half * rows, rows), :]

    kept = []

    def keep(source, target):
        kept.append(pltpu.make_async_copy(source, target, local.at[len(kept)]))
        kept[-1].start()
        return len(kept) - 1

    def kept_wait(index):
        kept[index].wait()
        kept[index] = None

    got = {}

    def z_start(which):
        got["u", which] = mail.post(halves(normed, which), block(x, 1, which), up)
        got["d", 1 - which] = mail.post(halves(normed, 1 - which), block(x, 3, 1 - which), down)

    z_start(0)
    share = wd.shape[0]
    early = [keep(normed, x.at[pl.ds(0, 2 * rows), :]), keep(wgu, wgu_v)]
    early.append(keep(cot.at[0], cot_v.at[pl.ds(0, 2 * rows), :]))
    early.append(keep(wd, wd_v))
    later = [keep(cot.at[slot, pl.ds(half * rows, rows), :], block(cot_v, slot, half)) for slot, half in order[2:]]
    width = normed.shape[1]
    piece = width // 4

    def dot_nt(left, right):
        return lax.dot_general(left, right, (((1,), (1,)), ((), ())), preferred_element_type=F32)

    def compute(c):
        part = slice(2 * rows * c, 2 * rows * (c + 1))
        for start, size in ((0, 512), (512, share - 512)):
            lanes, above = slice(start, start + size), slice(share + start, share + start + size)
            gate = jnp.dot(x[part, :], wgu_v[:, lanes], preferred_element_type=F32)
            value = jnp.dot(x[part, :], wgu_v[:, above], preferred_element_type=F32)
            grad = dot_nt(cot_v[part, :], wd_v[lanes, :])
            spread = 1.0 / (1.0 + jnp.exp(-gate))
            smooth = gate * spread
            act[part, lanes] = (smooth * value).astype(BF16)
            gb[part, lanes] = (grad * value * (spread * (1.0 + gate * (1.0 - spread)))).astype(BF16)
            gb[part, above] = (grad * smooth).astype(BF16)
        for m in range(3):
            lanes = slice(512 * m, 512 * (m + 1))
            parts[part, lanes] = dot_nt(gb[part, :], wgu_v[lanes, :]).astype(BF16)

    for index in early:
        kept_wait(index)
    compute(0)
    got["u", 0].wait_recv()
    far_up = mail.post(block(x, 1, 0), block(x, 2, 0), up)
    got["d", 1].wait_recv()
    far_down = mail.post(block(x, 3, 1), block(x, 2, 1), down)
    for index in later:
        kept_wait(index)
    compute(1)
    z_start(1)
    far_up.wait_recv()
    far_down.wait_recv()
    compute(2)
    first = {}
    for i in range(2):
        rows_i = pl.ds(i * size, size)
        first["u", i] = mail.post(block(parts, 2, 0).at[rows_i, :], up1.at[i], up)
        first["d", i] = mail.post(block(parts, 2, 1).at[rows_i, :], down1.at[i], down)
    got["u", 1].wait_recv()
    got["d", 0].wait_recv()
    compute(3)
    second = {
        ("d", 0): mail.post(block(parts, 1, 0), down2.at[0], down),
        ("u", 1): mail.post(block(parts, 3, 1), up2.at[1], up),
    }

    def turn_over(source, target):
        @pl.loop(0, source.shape[1] // LANES)
        def _(t):
            lanes = pl.ds(pl.multiple_of(t * LANES, LANES), LANES)
            target[lanes, :] = source[:, lanes].T

    def forward(i):
        rows_i = pl.ds(i * size, size)
        first["u", i].wait_recv()
        stage_up[i] = (block(parts, 3, 0).at[rows_i, :][...].astype(F32) + up1[i].astype(F32)).astype(BF16)
        second["u", 0, i] = mail.post(stage_up.at[i], up2.at[0, rows_i, :], up)
        first["d", i].wait_recv()
        stage_down[i] = (block(parts, 1, 1).at[rows_i, :][...].astype(F32) + down1[i].astype(F32)).astype(BF16)
        second["d", 1, i] = mail.post(stage_down.at[i], down2.at[1, rows_i, :], down)

    turn_over(x, turned)
    tile = 256
    tiles = 2 * share // tile

    def gu_tiles(first_tile, last_tile):
        @pl.loop(first_tile, last_tile)
        def _(n):
            lanes = pl.ds(pl.multiple_of(((n + (tiles // 2) * (1 - core)) % tiles) * tile, tile), tile)
            wgu_v[:, lanes] = jnp.dot(turned[...], gb[:, lanes], preferred_element_type=F32).astype(BF16)

    swaps = {}

    def settle(i):
        rows_i = pl.ds(i * size, size)
        if i == 0:
            second["d", 0].wait_recv()
            second["u", 1].wait_recv()
        second["u", 0, i].wait_recv()
        second["d", 1, i].wait_recv()
        for half in range(2):
            value = block(parts, 0, half).at[rows_i, :][...].astype(F32)
            value = value + up2[half, rows_i, :].astype(F32) + down2[half, rows_i, :].astype(F32)
            stage[half, rows_i, :] = value.astype(BF16)
            swaps[half, i] = mail.post(stage.at[half, rows_i, :], other.at[half, rows_i, :], pair)

    there = pl.ds(pl.multiple_of((1 - core) * share, LANES), share)
    mine = pl.ds(pl.multiple_of(core * share, LANES), share)
    gu_tiles(0, tiles // 2 + 1)
    shared = [
        mail.post(wgu_v.at[pl.ds(j * piece, piece), there], gu_in.at[j], twin) for j in range(4)
    ]
    forward(0)
    forward(1)
    gu_tiles(tiles // 2 + 1, tiles)
    for j in range(4):
        shared[j].wait_recv()
        gu_in[j] = (wgu_v[pl.ds(j * piece, piece), mine].astype(F32) + gu_in[j].astype(F32)).astype(BF16)

    def ring_y(i):
        height = piece // 3
        half = height // 2
        low, high = pl.ds(i * height, half), pl.ds(i * height + half, half)
        one, two, three, four = gu_up1.at[i], gu_down1.at[i], gu_up2.at[i], gu_down2.at[i]
        begin = (mail.post(gu_in.at[2, low, :], one, right), mail.post(gu_in.at[2, high, :], two, left))
        straight = [
            mail.post(gu_in.at[1, high, :], three.at[pl.ds(half, half), :], right),
            mail.post(gu_in.at[3, low, :], four.at[pl.ds(0, half), :], left),
        ]
        yield
        begin[0].wait_recv()
        one[...] = (gu_in[1, low, :].astype(F32) + one[...].astype(F32)).astype(BF16)
        straight.append(mail.post(one, three.at[pl.ds(0, half), :], right))
        begin[1].wait_recv()
        two[...] = (gu_in[3, high, :].astype(F32) + two[...].astype(F32)).astype(BF16)
        straight.append(mail.post(two, four.at[pl.ds(half, half), :], left))
        yield
        for copy in straight:
            copy.wait_recv()
        part = pl.ds(i * height, height)
        value = gu_in[0, part, :].astype(F32) + three[...].astype(F32) + four[...].astype(F32)
        gu_sum[part, :] = value.astype(BF16)
        yield

    rings = [ring_y(i) for i in range(3)]
    for ring in rings:
        next(ring)
    for m in range(3):
        lanes = slice(512 * m, 512 * (m + 1))

        @pl.loop(0, 4)
        def _(c):
            part = pl.ds(pl.multiple_of(c * 2 * rows, 2 * rows), 2 * rows)
            down_v[part, lanes] = jnp.dot(act[part, :], wd_v[:, lanes], preferred_element_type=F32).astype(BF16)

    settle(0)
    settle(1)
    result = {
        "u1": mail.post(block(down_v, 2, 0), res_up1, up),
        "d1": mail.post(block(down_v, 2, 1), res_down1, down),
        "u2": mail.post(block(down_v, 3, 1), res_up2, up),
        "d2": mail.post(block(down_v, 1, 0), res_down2, down),
    }
    turn_over(act, turned)

    @pl.loop(0, width // tile)
    def _(n):
        lanes = pl.ds(pl.multiple_of(n * tile, tile), tile)
        wd_v[:, lanes] = jnp.dot(
            turned[0:share, :], cot_v[:, lanes], preferred_element_type=F32
        ).astype(BF16)

    half_share = share // 2
    rows_there = pl.ds(pl.multiple_of((1 - core) * half_share, 16), half_share)
    rows_mine = pl.ds(pl.multiple_of(core * half_share, 16), half_share)
    shared += [
        mail.post(wd_v.at[rows_there, pl.ds(j * piece, piece)], dn_in.at[j], twin) for j in range(4)
    ]
    for ring in rings:
        next(ring)
    for j in range(4):
        shared[4 + j].wait_recv()
        dn_in[j] = (wd_v[rows_mine, pl.ds(j * piece, piece)].astype(F32) + dn_in[j].astype(F32)).astype(BF16)
        keep(dn_in.at[j], dn_half.at[j])
    for half, i in ((0, 0), (1, 0), (0, 1), (1, 1)):
        rows_i = pl.ds(i * size, size)
        swaps[half, i].wait_recv()
        total[pl.ds(half * rows + i * size, size), :] = stage[half, rows_i, :].astype(F32) + other[
            half, rows_i, :
        ].astype(F32)
    next(rings[0])
    next(rings[1])
    next(rings[2])
    for copy in result.values():
        copy.wait_recv()
    result_ahead[0] = (block(down_v, 3, 0)[...].astype(F32) + res_up1[...].astype(F32)).astype(BF16)
    result_ahead[1] = (block(down_v, 1, 1)[...].astype(F32) + res_down1[...].astype(F32)).astype(BF16)
    for half, theirs in ((0, res_down2), (1, res_up2)):
        value = block(down_v, 0, half)[...].astype(F32) + theirs[...].astype(F32)
        result_sum[pl.ds(half * rows, rows), :] = value.astype(BF16)
    for copy in kept:
        if copy is not None:
            copy.wait()
    mail.finish()


def back_kernel(
    total,
    middle,
    cot,
    gains,
    tok,
    normed,
    query,
    kv_a,
    kv_b,
    logs,
    attended,
    tables,
    turned_a,
    turned_b,
    w_in,
    w_out,
    gu,
    dn,
    result_sum,
    ahead,
    gu_out,
    dn_out,
    in_out,
    kw_out,
    wo_out,
    grad_out,
    result_out,
    small_out,
    middle_v,
    cot_v,
    tok_v,
    normed_v,
    query_v,
    kva,
    kvb,
    attended_v,
    turned_a_v,
    turned_b_v,
    w_in_v,
    w_out_v,
    gu_v,
    dn_v,
    down_v,
    gain_rows,
    grad_middle,
    grad_low,
    grad_att,
    flat,
    keys_t,
    dkv_a,
    dkv_b,
    low_kv,
    own_kv,
    from_own,
    from_near,
    grad_pre,
    grad_part,
    grad_in,
    part_in,
    rows_out,
    result_rows,
    gu_n,
    gu_s,
    dn_up1,
    dn_down1,
    dn_up2,
    dn_down2,
    dn_y,
    dn_n,
    dn_s,
    in_p,
    in_t,
    in_up1,
    in_down1,
    in_up2,
    in_down2,
    in_s,
    in_n,
    in_z,
    kw_p,
    kw_t,
    kw_up1,
    kw_down1,
    kw_up2,
    kw_down2,
    kw_s,
    kw_n,
    kw_z,
    wo_p,
    wo_t,
    wo_up1,
    wo_down1,
    wo_up2,
    wo_down2,
    wo_s,
    wo_n,
    wo_z,
    res_in,
    res_total,
    bias_own,
    gains_own,
    bias_in,
    gains_in,
    small_a,
    small_b,
    small_t,
    small_n,
    send,
    recv,
    local,
):
    place = here()
    dp, row, col = place
    core = dp % 2
    z = dp // Z_STEP
    twin, near, pair = twin_of(place), near_of(place), pair_of(place)
    up, down, far_z = along_z(place, 1), along_z(place, 3), along_z(place, 2)
    right, left = along_y(place, 1), along_y(place, 3)
    meet(
        [along_y(place, s) for s in (1, 2, 3)]
        + [near_of(place, (row + s) % 4) for s in range(4)]
        + [pair_of(place, (row + s) % 4) for s in range(4)]
        + [twin, up, down, far_z]
    )
    mail = Mail(send, recv)
    kept, arrivals = [], []

    def keep(source, target):
        kept.append(pltpu.make_async_copy(source, target, local.at[len(kept)]))
        kept[-1].start()
        return len(kept) - 1

    def kept_wait(index):
        if kept[index] is not None:
            kept[index].wait()
            kept[index] = None

    def even(start, size):
        return pl.ds(pl.multiple_of(start, 16), size)

    def plus(*values):
        result = values[0].astype(F32)
        for value in values[1:]:
            result = result + value.astype(F32)
        return result

    def dot_nt(left, right):
        return lax.dot_general(left, right, (((1,), (1,)), ((), ())), preferred_element_type=F32)

    rows = tok.shape[0] // 2
    width = tok.shape[1]
    piece = width // 4
    spot = even(row * rows, rows)
    own_rows, other_rows = even(col * rows, rows), even((1 - col) * rows, rows)

    def ffn_flow(i):
        if i < 3:
            height = gu.shape[0] // 3
            start = i * height
            theirs, done = gu_n.at[i], gu_s.at[i]
            mine = gu_v.at[pl.ds(start, height), :]
            swap = mail.post(gu.at[pl.ds(start, height), :], theirs, near)
            half = height // 2
            yield
            kept_wait(loads["gu"])
        else:
            height = dn.shape[1]
            start, mine, theirs, done = 0, dn_y, dn_n, dn_s
            half = height // 2
            low, high = pl.ds(start, half), pl.ds(start + half, half)
            first = (mail.post(dn.at[2, low, :], dn_up1, right), mail.post(dn.at[2, high, :], dn_down1, left))
            straight = (
                mail.post(dn.at[1, high, :], dn_up2.at[pl.ds(half, half), :], right),
                mail.post(dn.at[3, low, :], dn_down2.at[pl.ds(0, half), :], left),
            )
            yield
            kept_wait(loads["dn"])
            first[0].wait_recv()
            dn_up1[...] = plus(dn_v[1, low, :], dn_up1[...]).astype(BF16)
            last = [mail.post(dn_up1, dn_up2.at[pl.ds(0, half), :], right)]
            first[1].wait_recv()
            dn_down1[...] = plus(dn_v[3, high, :], dn_down1[...]).astype(BF16)
            last.append(mail.post(dn_down1, dn_down2.at[pl.ds(half, half), :], left))
            yield
            for copy in straight + tuple(last):
                copy.wait_recv()
            mine[...] = plus(dn_v[0], dn_up2[...], dn_down2[...]).astype(BF16)
            swap = mail.post(mine, theirs, near)
            yield
        swap.wait_recv()
        done[...] = plus(mine[...], theirs[...]).astype(BF16)

        def room(slot, which=None):
            begin, size = (start, height) if which is None else (start + which * half, half)
            if i < 3:
                share = gu_out.shape[2] // 4
                lanes = pl.ds(pl.multiple_of(slot * share, LANES), share)
                return gu_out.at[core, pl.ds(begin, size), lanes]
            return dn_out.at[even((slot * 2 + core) * height + begin, size), :]

        posts = {}
        for turn in range(2):
            for name, device, which in (("u", up, turn), ("d", down, 1 - turn)):
                posts[name, which] = mail.post(done.at[pl.ds(which * half, half), :], room(z, which), device)
        keep(done, room(z))
        arrivals.append(mail.post(done, room(z), twin))
        yield
        posts["u", 0].wait_recv()
        block = room((z + 3) % 4, 0)
        one_more = mail.post(block, block, up)
        posts["d", 1].wait_recv()
        block = room((z + 1) % 4, 1)
        two_more = mail.post(block, block, down)
        yield
        posts["u", 1].wait_recv()
        block = room((z + 3) % 4)
        arrivals.append(mail.post(block, block, twin))
        posts["d", 0].wait_recv()
        block = room((z + 1) % 4)
        arrivals.append(mail.post(block, block, twin))
        one_more.wait_recv()
        two_more.wait_recv()
        block = room((z + 2) % 4)
        arrivals.append(mail.post(block, block, twin))
        yield

    def weight_flow(part, t, up1, down1, up2, down2, total_h, theirs, quarter, out):
        height = t.shape[1]
        half = height // 2
        low, high = pl.ds(0, half), pl.ds(half, half)
        copy = mail.post(part.at[:, even((1 - core) * height, height), :], t, twin)
        yield
        copy.wait_recv()
        for j in range(4):
            t[j] = plus(part[j, even(core * height, height), :], t[j]).astype(BF16)
        first = (mail.post(t.at[2, low, :], up1, right), mail.post(t.at[2, high, :], down1, left))
        straight = (
            mail.post(t.at[1, high, :], up2.at[high, :], right),
            mail.post(t.at[3, low, :], down2.at[low, :], left),
        )
        yield
        first[0].wait_recv()
        up1[...] = plus(t[1, low, :], up1[...]).astype(BF16)
        last = [mail.post(up1, up2.at[low, :], right)]
        first[1].wait_recv()
        down1[...] = plus(t[3, high, :], down1[...]).astype(BF16)
        last.append(mail.post(down1, down2.at[high, :], left))
        yield
        for copy in straight + tuple(last):
            copy.wait_recv()
        total_h[...] = plus(t[0], up2[...], down2[...]).astype(BF16)
        swap = mail.post(total_h, theirs, near)
        yield
        swap.wait_recv()
        t[0] = plus(total_h[...], theirs[...]).astype(BF16)
        size = height // 4
        copies = []
        for step, device in ((1, up), (3, down), (2, far_z)):
            source = t.at[0, even(((z + step) % 4) * size, size), :]
            copies.append(mail.post(source, quarter.at[step - 1], device))
        yield
        for copy in copies:
            copy.wait_recv()
        mine = even(z * size, size)
        theirs[0:size, :] = plus(t[0, mine, :], quarter[0], quarter[1], quarter[2]).astype(BF16)
        place_of = lambda owner: out.at[even(core * height + owner * size, size), :]
        copies = [mail.post(theirs.at[0:size, :], place_of(z), device) for device in (up, down, far_z)]
        arrivals.append(mail.post(theirs.at[0:size, :], place_of(z), twin))
        keep(theirs.at[0:size, :], place_of(z))
        yield
        for copy in copies:
            copy.wait_recv()
        for step in (1, 2, 3):
            block = place_of((z + step) % 4)
            arrivals.append(mail.post(block, block, twin))
        yield

    def result_flow():
        copies = (mail.post(ahead.at[0], res_in.at[0], up), mail.post(ahead.at[1], res_in.at[1], down))
        yield
        kept_wait(loads["down"])
        for half, copy in enumerate(copies):
            copy.wait_recv()
            part = pl.ds(half * rows, rows)
            res_total[part, :] = plus(down_v[part, :], res_in[half]).astype(BF16)
        swap = mail.post(res_total.at[other_rows, :], part_in, pair)
        yield
        swap.wait_recv()
        result_rows[...] = (middle_v[own_rows, :] + plus(res_total[own_rows, :], part_in[...])).astype(BF16)
        yield
        spread(result_rows, result_out)
        yield

    def spread(source, target):
        for step in range(4):
            lanes = pl.ds(step * piece, piece)
            if step:
                arrivals.append(mail.post(source.at[:, lanes], target.at[spot, :], along_y(place, step)))
            else:
                keep(source.at[:, lanes], target.at[spot, :])

    flows = [ffn_flow(i) for i in range(4)]
    loads = {}
    for name, source, target in (
        ("middle", middle, middle_v),
        ("cot", cot.at[0], cot_v),
        ("w_out", w_out, w_out_v),
        ("attended", attended, attended_v),
        ("query", query, query_v),
        ("kva", kv_a, kva),
        ("kvb", kv_b, kvb),
        ("ta", turned_a, turned_a_v),
        ("tb", turned_b, turned_b_v),
        ("gu", gu, gu_v),
        ("w_in", w_in, w_in_v),
        ("normed", normed, normed_v),
        ("tok", tok, tok_v),
        ("dn", dn, dn_v),
        ("down", result_sum, down_v),
    ):
        loads[name] = keep(source, target)
    result_steps = result_flow()
    next(flows[2])
    for j in range(4):
        gain_rows[:, j * piece : (j + 1) * piece] = gains[j]

    def norm_back(stream, gain, incoming):
        scale = lax.rsqrt(jnp.sum(stream * stream, -1, keepdims=True) * (1.0 / width) + EPS)
        scaled = incoming * gain
        inner = jnp.sum(scaled * stream, -1, keepdims=True) * (1.0 / width)
        back = scale * scaled - stream * (scale * scale * scale * inner)
        return back, jnp.sum(incoming * stream * scale, 0, keepdims=True)

    kept_wait(loads["middle"])
    kept_wait(loads["cot"])
    gain_ffn_part = jnp.zeros((1, width), F32)
    for half in range(2):
        part = slice(half * rows, (half + 1) * rows)
        back, gain_part = norm_back(middle_v[part, :], gain_rows[1:2, :], total[part, :])
        value = cot_v[part, :].astype(F32) + back
        grad_middle[part, :] = value
        grad_low[part, :] = value.astype(BF16)
        gain_ffn_part = gain_ffn_part + gain_part
    gains_own[...] = jnp.zeros_like(gains_own)
    for j in range(4):
        gains_own[j, 1:2, :] = 0.5 * gain_ffn_part[:, j * piece : (j + 1) * piece]
    next(flows[3])
    next(result_steps)
    kept_wait(loads["w_out"])
    q_width = w_out.shape[0]
    for first in range(0, q_width, 256):
        lanes = slice(first, first + 256)
        grad_att[:, lanes] = dot_nt(grad_low[...], w_out_v[lanes, :]).astype(BF16)

    def turn_over(source, target, count):
        for t in range(count):
            lanes = slice(t * LANES, (t + 1) * LANES)
            target[lanes, 0 : source.shape[0]] = source[:, lanes].T

    kept_wait(loads["attended"])
    turn_over(attended_v, flat, q_width // LANES)
    for j in range(4):
        wo_p[j] = jnp.dot(
            flat[0:q_width, :], grad_low[:, j * piece : (j + 1) * piece], preferred_element_type=F32
        ).astype(BF16)
    wo_steps = weight_flow(wo_p, wo_t, wo_up1, wo_down1, wo_up2, wo_down2, wo_s, wo_n, wo_z, wo_out)
    next(flows[0])

    for name in ("query", "kva", "kvb", "ta", "tb"):
        kept_wait(loads[name])
    heads = q_width // HEAD_SIZE
    factor = HEAD_SIZE ** (-0.5)

    def unrotate(value, half):
        part = slice(half * rows, (half + 1) * rows)
        return value * tables[0, part, :] + pltpu.roll(value * tables[1, part, :], HEAD_SIZE // 2, 1)

    def attend_back(half, keys, mask, sums):
        part = slice(half * rows, (half + 1) * rows)
        count = keys.shape[0]
        for t in range(count // LANES):
            lanes = slice(t * LANES, (t + 1) * LANES)
            keys_t[:, lanes] = keys[lanes, 0:HEAD_SIZE].T
        sums[...] = jnp.zeros_like(sums)

        @pl.loop(0, heads)
        def _(h):
            lanes = pl.ds(pl.multiple_of(h * HEAD_SIZE, LANES), HEAD_SIZE)
            one, grad = query_v[part, lanes], grad_att[part, lanes]
            raw = dot_nt(keys[:, 0:HEAD_SIZE], one)
            probs = jnp.exp(raw * factor + mask[...] - logs[half * heads + h, 0:1, :])
            grad_probs = dot_nt(keys[:, HEAD_SIZE : 2 * HEAD_SIZE], grad)
            inner = jnp.sum(grad_probs * probs, 0, keepdims=True)
            grad_scores = (probs * (grad_probs - inner)).astype(BF16)
            sums[:, 0:HEAD_SIZE] += jnp.dot(grad_scores, one, preferred_element_type=F32)
            sums[:, HEAD_SIZE : 2 * HEAD_SIZE] += jnp.dot(probs.astype(BF16), grad, preferred_element_type=F32)
            grad_query = jnp.dot(keys_t[:, 0:count], grad_scores, preferred_element_type=F32).T * factor
            grad_pre[part, lanes] = unrotate(grad_query, half).astype(BF16)

    def low_sums(sums, part):
        return (sums[part, 0:HEAD_SIZE] * factor).astype(BF16), sums[part, HEAD_SIZE : 2 * HEAD_SIZE].astype(BF16)

    next(flows[2])
    attend_back(1, kvb, turned_b_v, dkv_b)
    half_rows = kva.shape[0]
    low_part, high_part = slice(0, half_rows), slice(half_rows, 2 * half_rows)
    for target, sums, part in ((low_kv, dkv_b, low_part), (own_kv.at[1], dkv_b, high_part)):
        target[:, 0:HEAD_SIZE], target[:, HEAD_SIZE : 2 * HEAD_SIZE] = low_sums(sums, part)
    kv_got = []
    for step in range(4):
        other = (row + step) % 4
        part = even(other * rows, rows)
        kv_got.append(mail.post(low_kv.at[part, :], from_near.at[step], near_of(place, other)))
        if step:
            kv_got.append(mail.post(own_kv.at[1, part, :], from_own.at[step - 1, 1], along_y(place, step)))
    attend_back(0, kva, turned_a_v, dkv_a)
    target = own_kv.at[0]
    target[:, 0:HEAD_SIZE], target[:, HEAD_SIZE : 2 * HEAD_SIZE] = low_sums(dkv_a, low_part)
    for step in (1, 2, 3):
        part = even(((row + step) % 4) * rows, rows)
        kv_got.append(mail.post(own_kv.at[0, part, :], from_own.at[step - 1, 0], along_y(place, step)))
    next(flows[2])
    next(result_steps)
    next(wo_steps)
    next(flows[3])
    next(flows[1])
    next(flows[0])
    kept_wait(loads["normed"])
    turn_over(normed_v, flat, width // LANES)
    for j in range(4):
        in_p[j] = jnp.dot(
            flat[j * piece : (j + 1) * piece, :], grad_pre[:, 0:q_width], preferred_element_type=F32
        ).astype(BF16)
    in_steps = weight_flow(in_p, in_t, in_up1, in_down1, in_up2, in_down2, in_s, in_n, in_z, in_out)
    next(wo_steps)
    next(flows[3])
    next(flows[1])
    next(flows[0])
    for copy in kv_got:
        copy.wait_recv()
    for half in range(2):
        part = slice(half * rows, (half + 1) * rows)
        value = own_kv[half, spot, :].astype(F32)
        for step in range(3):
            value = value + from_own[step, half].astype(F32)
        if half == 0:
            for step in range(4):
                value = value + from_near[step].astype(F32)
        grad_pre[part, q_width : q_width + HEAD_SIZE] = unrotate(value[:, 0:HEAD_SIZE], half).astype(BF16)
        grad_pre[part, q_width + HEAD_SIZE : q_width + 2 * HEAD_SIZE] = value[:, HEAD_SIZE : 2 * HEAD_SIZE].astype(
            BF16
        )
    next(in_steps)
    next(wo_steps)
    kept_wait(loads["w_in"])
    for j in range(4):
        grad_part[:, j * piece : (j + 1) * piece] = dot_nt(grad_pre[...], w_in_v[j]).astype(BF16)
    swap = mail.post(grad_part.at[other_rows, :], grad_in, pair)
    for j in range(4):
        kw_p[j] = jnp.dot(
            flat[j * piece : (j + 1) * piece, :], grad_pre[:, q_width:], preferred_element_type=F32
        ).astype(BF16)
    kw_steps = weight_flow(kw_p, kw_t, kw_up1, kw_down1, kw_up2, kw_down2, kw_s, kw_n, kw_z, kw_out)
    next(in_steps)
    next(flows[3])
    next(kw_steps)
    next(wo_steps)
    bias_own[...] = jnp.zeros_like(bias_own)
    bias_own[0:1, :] = jnp.sum(grad_pre[...].astype(F32), 0, keepdims=True)
    next(in_steps)
    next(wo_steps)
    next(in_steps)
    next(flows[1])
    next(kw_steps)
    next(wo_steps)
    next(kw_steps)
    kept_wait(loads["tok"])
    swap.wait_recv()
    back, gain_part = norm_back(
        tok_v[own_rows, :].astype(F32), gain_rows[0:1, :], plus(grad_part[own_rows, :], grad_in[...])
    )
    rows_out[...] = (grad_middle[own_rows, :] + back).astype(BF16)
    for j in range(4):
        gains_own[j, 0:1, :] = gain_part[:, j * piece : (j + 1) * piece]
    next(result_steps)
    next(kw_steps)
    next(in_steps)
    small_copies, small_kept = [], []
    for step in range(4):
        device = along_y(place, step)
        mine = gains_in.at[col * 4 + row]
        if step:
            small_copies.append(mail.post(bias_own, bias_in.at[row], device))
            small_copies.append(mail.post(gains_own.at[step], mine, device))
        else:
            small_kept.append(keep(bias_own, bias_in.at[row]))
            small_kept.append(keep(gains_own.at[step], mine))
        small_copies.append(mail.post(gains_own.at[step], mine, pair_of(place, (row + step) % 4)))
    next(wo_steps)
    next(kw_steps)
    next(flows[3])
    next(in_steps)
    spread(rows_out, grad_out)
    next(result_steps)
    for copy in small_copies:
        copy.wait_recv()
    for index in small_kept:
        kept_wait(index)
    small_a[...] = jnp.zeros_like(small_a)
    small_a[0:8, :] = bias_in[0] + bias_in[1] + bias_in[2] + bias_in[3]
    small_a[8:16, 0:piece] = (
        gains_in[0] + gains_in[1] + gains_in[2] + gains_in[3] + gains_in[4] + gains_in[5] + gains_in[6] + gains_in[7]
    )
    small_first = mail.post(small_a, small_t, twin)
    small_first.wait_recv()
    small_b[...] = small_a[...] + small_t[...]
    small_second = mail.post(small_b, small_n, near)
    next(in_steps)
    next(kw_steps)
    small_second.wait_recv()
    small_t[...] = small_b[...] + small_n[...]
    for device in (up, down, far_z):
        arrivals.append(mail.post(small_t, small_out.at[z], device))
    keep(small_t, small_out.at[z])
    for steps in [*flows, wo_steps, in_steps, kw_steps, result_steps]:
        for _ in steps:
            pass
    for copy in arrivals:
        copy.wait_recv()
    for copy in kept:
        if copy is not None:
            copy.wait()
    mail.finish()


def widen_kernel(gate_up, down, w_in, w_kv, w_out, result, tokens, small, *outs):
    result_w, tokens_w, query_w, key_w, value_w, out_w, gate_w, up_w, down_w, *flat = outs
    total = small[0] + small[1] + small[2] + small[3]
    start = 0
    for line, out in zip((0, 0, 0, 8, 9), flat):
        start = 0 if line else start
        out[...] = total[line, start : start + out.shape[0]]
        start += out.shape[0]
    result_w[...] = result[...].astype(F32)
    tokens_w[...] = tokens[...].astype(F32)
    query_w[...] = w_in[...].astype(F32)
    key_w[...] = w_kv[:, : key_w.shape[1]].astype(F32)
    value_w[...] = w_kv[:, key_w.shape[1] :].astype(F32)
    out_w[...] = w_out[...].astype(F32)
    gate_w[...] = gate_up[0, :, : gate_w.shape[1]].astype(F32)
    up_w[...] = gate_up[1, :, : up_w.shape[1]].astype(F32)
    down_w[...] = down[...].astype(F32)


def on_device(
    tokens,
    cotangent,
    lengths,
    gain_attn,
    w_query,
    key_projection,
    value_projection,
    bias_query,
    key_bias_vector,
    value_bias_vector,
    w_out,
    gain_ffn,
    w_gate,
    w_up,
    w_down,
):
    half_rows, piece = tokens.shape
    width = 4 * piece
    rows = half_rows // 4
    q_width = w_query.shape[1]
    kv_width = key_projection.shape[1]
    heads = q_width // HEAD_SIZE
    hidden = w_gate.shape[1]
    share = -(-hidden // (4 * LANES)) * LANES

    in_width = q_width + 2 * kv_width
    thin = piece // 2
    (
        tok_rows,
        cot_full,
        gains4,
        normed,
        query,
        kv_a,
        kv_b,
        logs,
        attended,
        tables,
        middle,
        mask_a,
        mask_b,
        normed_ffn,
        w_in_full,
        w_out_full,
        w_gu_full,
        w_down_full,
    ) = talk(
        front_kernel,
        0,
        FRONT_COPIES,
        FRONT_LOCAL,
        [
            ((2 * rows, width), BF16),
            ((4, 2 * rows, width), BF16),
            ((4, 8, piece), F32),
            ((2 * rows, width), BF16),
            ((2 * rows, q_width), BF16),
            ((half_rows, 2 * kv_width), BF16),
            ((2 * half_rows, 2 * kv_width), BF16),
            ((2 * heads, 8, rows), F32),
            ((2 * rows, q_width), BF16),
            ((2, 2 * rows, HEAD_SIZE), F32),
            ((2 * rows, width), F32),
            ((half_rows, rows), F32),
            ((2 * half_rows, rows), F32),
            ((2 * rows, width), BF16),
            ((4, piece, in_width), BF16),
            ((q_width, width), BF16),
            ((4, 2, thin, 2 * share), BF16),
            ((share, width), BF16),
        ],
        [ANY] * 2 + [VMEM] * 6 + [ANY] * 7,
        [ANY] * 3 + [VMEM] * 2 + [ANY] * 2 + [VMEM] * 7 + [ANY] * 4,
        [
            pltpu.VMEM((8, LANES), jnp.int32),
            pltpu.VMEM((8, piece), F32),
            pltpu.VMEM((2 * rows, width), BF16),
            pltpu.VMEM((2, 8, LANES), jnp.int32),
            pltpu.VMEM((4, 8, piece), F32),
            pltpu.VMEM((4, piece, in_width), BF16),
            pltpu.VMEM((q_width, width), BF16),
            pltpu.VMEM((2, thin, 2 * share), BF16),
            pltpu.VMEM((share, piece), BF16),
            pltpu.VMEM((thin, LANES), BF16),
            pltpu.VMEM((LANES, piece), BF16),
            pltpu.VMEM((2 * rows, 2 * kv_width), BF16),
            pltpu.VMEM((half_rows, 2 * kv_width), BF16),
            pltpu.VMEM((2 * half_rows, 2 * kv_width), BF16),
            pltpu.VMEM((rows, half_rows), F32),
            pltpu.VMEM((rows, 2 * half_rows), F32),
            pltpu.VMEM((2 * rows, width), BF16),
            pltpu.VMEM((2 * rows, width), BF16),
        ],
        limit=56,
    )(
        tokens,
        cotangent,
        lengths,
        gain_attn,
        gain_ffn,
        bias_query,
        key_bias_vector,
        value_bias_vector,
        w_query,
        key_projection,
        value_projection,
        w_out,
        w_gate,
        w_up,
        w_down,
    )

    w_both_full = w_gu_full.reshape(width, 2 * share)
    half_block = (2, rows, width)
    grad_normed_ffn, both_sum, down_half, result_sum, result_ahead = talk(
        ffn_kernel,
        4,
        50,
        14,
        [
            ((2 * rows, width), F32),
            ((piece, share), BF16),
            ((4, share // 2, piece), BF16),
            ((2 * rows, width), BF16),
            ((2, rows, width), BF16),
        ],
        [ANY] * 4,
        [VMEM, VMEM, ANY, VMEM, VMEM],
        [
            pltpu.VMEM(shape, BF16)
            for shape in (
                (8 * rows, width),
                (8 * rows, width),
                (width, 2 * share),
                (share, width),
                (8 * rows, 2 * share),
                (8 * rows, share),
                (8 * rows, width),
                (width, 8 * rows),
                (8 * rows, width),
                (4, piece, share),
                (4, share // 2, piece),
                (2, rows // 2, width),
                (2, rows // 2, width),
                half_block,
                half_block,
                half_block,
                (2, rows // 2, width),
                (2, rows // 2, width),
                half_block,
                (rows, width),
                (rows, width),
                (rows, width),
                (rows, width),
                (3, piece // 6, share),
                (3, piece // 6, share),
                (3, piece // 3, share),
                (3, piece // 3, share),
            )
        ],
        limit=60,
    )(normed_ffn, cot_full, w_both_full, w_down_full)
    thirds = piece // 3
    q_half, w_half = (thin, q_width), (q_width // 2, piece)
    gu_chunk, dn_chunk = (3, thirds, share), (share // 2, piece)

    def halved(shape):
        return (*shape[:-2], shape[-2] // 2, shape[-1])

    def weight_scratch(shape):
        return [
            (4, 2 * shape[0], shape[1]),
            (4, *shape),
            halved(shape),
            halved(shape),
            shape,
            shape,
            shape,
            shape,
            (3, shape[0] // 4, shape[1]),
        ]

    def scratch(kind, *shapes):
        return [pltpu.VMEM(shape, kind) for shape in shapes]

    gate_up, down_all, in_total, kv_total, out_total, grad_tokens, result, small_all = talk(
        back_kernel,
        8,
        BACK_COPIES,
        BACK_LOCAL,
        [
            ((2, piece, 4 * share), BF16),
            ((4 * share, piece), BF16),
            ((piece, q_width), BF16),
            ((piece, 2 * kv_width), BF16),
            ((q_width, piece), BF16),
            ((half_rows, piece), BF16),
            ((half_rows, piece), BF16),
            ((4, 16, in_width), F32),
        ],
        [VMEM, ANY, ANY, VMEM] + [ANY] * 5 + [VMEM, ANY, VMEM] + [ANY] * 8,
        [ANY] * 8,
        scratch(F32, (2 * rows, width))
        + scratch(
            BF16,
            (2 * rows, width),
            (2 * rows, width),
            (2 * rows, width),
            (2 * rows, q_width),
            (half_rows, 2 * kv_width),
            (2 * half_rows, 2 * kv_width),
            (2 * rows, q_width),
        )
        + scratch(F32, (half_rows, rows), (2 * half_rows, rows))
        + scratch(
            BF16,
            (4, piece, in_width),
            (q_width, width),
            (piece, share),
            (4, share // 2, piece),
            (2 * rows, width),
        )
        + scratch(F32, (8, width), (2 * rows, width))
        + scratch(BF16, (2 * rows, width), (2 * rows, q_width), (width, 2 * rows), (HEAD_SIZE, 2 * half_rows))
        + scratch(F32, (half_rows, 2 * kv_width), (2 * half_rows, 2 * kv_width))
        + scratch(
            BF16,
            (half_rows, 2 * kv_width),
            (2, half_rows, 2 * kv_width),
            (3, 2, rows, 2 * kv_width),
            (4, rows, 2 * kv_width),
            (2 * rows, in_width),
            (2 * rows, width),
            (rows, width),
            (rows, width),
            (rows, width),
            (rows, width),
            gu_chunk,
            gu_chunk,
            halved(dn_chunk),
            halved(dn_chunk),
            dn_chunk,
            dn_chunk,
            dn_chunk,
            dn_chunk,
            dn_chunk,
            *weight_scratch(q_half),
            *weight_scratch((thin, 2 * kv_width)),
            *weight_scratch(w_half),
            (2, rows, width),
            (2 * rows, width),
        )
        + scratch(F32, (8, in_width), (4, 8, piece), (4, 8, in_width), (8, 8, piece))
        + scratch(F32, *[(16, in_width)] * 4),
        limit=60,
    )(
        grad_normed_ffn,
        middle,
        cot_full,
        gains4,
        tok_rows,
        normed,
        query,
        kv_a,
        kv_b,
        logs,
        attended,
        tables,
        mask_a,
        mask_b,
        w_in_full,
        w_out_full,
        both_sum,
        down_half,
        result_sum,
        result_ahead,
    )
    steps = 8
    narrow = [gate_up, down_all, in_total, kv_total, out_total, result, grad_tokens, small_all]
    lines = [(q_width,), (kv_width,), (kv_width,), (piece,), (piece,)]
    wide = [
        (half_rows, piece),
        (half_rows, piece),
        (piece, q_width),
        (piece, kv_width),
        (piece, kv_width),
        (q_width, piece),
        (piece, hidden),
        (piece, hidden),
        (hidden, piece),
    ]

    def in_block(array):
        if array is small_all:
            return pl.BlockSpec(array.shape, lambda i: (0, 0, 0))
        if array.ndim == 3:
            return pl.BlockSpec((2, array.shape[1] // steps, array.shape[2]), lambda i: (0, i, 0))
        if array is down_all:
            return pl.BlockSpec((hidden // steps, piece), lambda i: (i, 0))
        return pl.BlockSpec((array.shape[0] // steps, array.shape[1]), lambda i: (i, 0))

    wide_out = pl.pallas_call(
        widen_kernel,
        grid=(steps,),
        out_shape=[jax.ShapeDtypeStruct(shape, F32) for shape in wide + lines],
        in_specs=[in_block(array) for array in narrow],
        out_specs=[pl.BlockSpec((shape[0] // steps, shape[1]), lambda i: (i, 0)) for shape in wide]
        + [pl.BlockSpec(shape, lambda i: (0,)) for shape in lines],
        compiler_params=pltpu.CompilerParams(vmem_limit_bytes=60 << 20),
    )(*narrow)
    result_w, tokens_w, query_w, key_w, value_w, out_w, gate_w, up_w, down_w, *flat = wide_out
    bias_q, bias_k, bias_v, gain_one, gain_two = flat
    return (
        result_w,
        tokens_w,
        gain_one,
        query_w,
        key_w,
        value_w,
        bias_q,
        bias_k,
        bias_v,
        out_w,
        gain_two,
        gate_w,
        up_w,
        down_w,
    )


def solution(mesh):
    placed = (
        P(("dp", "col"), "row"),
        P(("dp", "col"), "row"),
        P("dp", None),
        P("row"),
        P("row", "col"),
        P("row", "col"),
        P("row", "col"),
        P("col"),
        P("col"),
        P("col"),
        P("col", "row"),
        P("row"),
        P("row", "col"),
        P("row", "col"),
        P("col", "row"),
    )
    return jax.shard_map(
        on_device,
        mesh=mesh,
        in_specs=placed,
        out_specs=(
            P(("dp", "col"), "row"),
            P(("dp", "col"), "row"),
            P("row"),
            P("row", "col"),
            P("row", "col"),
            P("row", "col"),
            P("col"),
            P("col"),
            P("col"),
            P("col", "row"),
            P("row"),
            P("row", "col"),
            P("row", "col"),
            P("col", "row"),
        ),
        check_vma=False,
    )
```

```python
import math

import jax
import jax.numpy as jnp
from jax import lax
from jax.experimental import pallas as pl
from jax.experimental.pallas import tpu as pltpu
from jax.sharding import PartitionSpec as P

HEAD_SIZE = 128
EPS = 1e-06
THETA = 1000000.0
LANES = 128
MESH = pl.DeviceIdType.MESH
BF16 = jnp.bfloat16
F32 = jnp.float32
ANY = pl.BlockSpec(memory_space=pl.ANY)
VMEM = pl.BlockSpec(memory_space=pltpu.VMEM)

Z_STEP = 4
FRONT_COPIES = 77
FRONT_LOCAL = 27
BACK_COPIES = 145
BACK_LOCAL = 28


def here():
    return lax.axis_index("dp"), lax.axis_index("row"), lax.axis_index("col")


def flip_near(dp):
    return dp + 2 - 4 * ((dp // 2) % 2)


def pair_of(place, row=None):
    dp, own, col = place
    return flip_near(dp), own if row is None else row, 1 - col


def near_of(place, row=None):
    dp, own, col = place
    return flip_near(dp), own if row is None else row, col


def twin_of(place):
    dp, row, col = place
    return dp + 1 - 2 * (dp % 2), row, col


def along_z(place, step):
    dp, row, col = place
    return (dp + Z_STEP * step) % (4 * Z_STEP), row, col


def along_y(place, step):
    dp, row, col = place
    return dp, (row + step) % 4, col


def meet(peers):
    barrier = pltpu.get_barrier_semaphore()
    for peer in peers:
        pl.semaphore_signal(barrier, inc=1, device_id=peer, device_id_type=MESH)
    pl.semaphore_wait(barrier, len(peers))


class Mail:
    def __init__(self, send, recv):
        self.send, self.recv, self.count, self.sent = send, recv, 0, []

    def post(self, source, target, device):
        index = self.count
        self.count += 1
        copy = pltpu.make_async_remote_copy(
            src_ref=source,
            dst_ref=target,
            send_sem=self.send.at[index],
            recv_sem=self.recv.at[index],
            device_id=device,
            device_id_type=MESH,
        )
        copy.start()
        self.sent.append(copy)
        return copy

    def finish(self):
        assert self.count == self.send.shape[0], (self.count, self.send.shape)
        for copy in self.sent:
            copy.wait_send()


def talk(body, ident, copies, local, outs, in_specs, out_specs, scratch=(), limit=32):
    return pl.pallas_call(
        body,
        out_shape=[jax.ShapeDtypeStruct(*out) for out in outs],
        in_specs=in_specs,
        out_specs=out_specs,
        scratch_shapes=[
            *scratch,
            pltpu.SemaphoreType.DMA((copies,)),
            pltpu.SemaphoreType.DMA((copies,)),
            pltpu.SemaphoreType.DMA((max(local, 1),)),
        ],
        compiler_params=pltpu.CompilerParams(
            collective_id=ident, has_side_effects=True, vmem_limit_bytes=limit << 20
        ),
    )


def front_kernel(
    tok,
    cot,
    lens_in,
    gain_attn,
    gain_ffn,
    bias_q,
    bias_k,
    bias_v,
    wq,
    wk,
    wv,
    wo,
    wg,
    wu,
    wd,
    tok_out,
    cot_full,
    gains_out,
    normed,
    query,
    kva_out,
    kvb_out,
    logs,
    attended,
    tables,
    middle,
    turned_a,
    turned_b,
    normed_ffn,
    w_in_out,
    w_out_out,
    wgu_full,
    wd_full,
    lens,
    gains,
    tok_v,
    lens_v,
    gains_v,
    w_in,
    w_out,
    gu_own,
    wd_own,
    blank_gu,
    blank_wd,
    kv,
    kva,
    kvb,
    bias_a,
    bias_b,
    branch,
    branch_in,
    send,
    recv,
    local,
):
    place = here()
    dp, row, col = place
    z, core = dp // Z_STEP, dp % 2
    twin, pair, up, down = twin_of(place), pair_of(place), along_z(place, 1), along_z(place, 3)
    right, left, near = along_y(place, 1), along_y(place, 3), near_of(place)
    meet(
        [along_y(place, s) for s in (1, 2, 3)]
        + [near_of(place, (row + s) % 4) for s in range(4)]
        + [pair, twin, up, down]
    )
    mail = Mail(send, recv)
    kept = []

    def keep(source, target):
        kept.append(pltpu.make_async_copy(source, target, local.at[len(kept)]))
        kept[-1].start()
        return len(kept) - 1

    def kept_wait(index):
        kept[index].wait()
        kept[index] = None

    def even(start, size):
        return pl.ds(pl.multiple_of(start, 16), size)

    rows, piece = tok.shape[0] // 4, tok.shape[1]
    width = 4 * piece
    own_rows = even(col * rows, rows)
    spot = even(row * rows, rows)

    def spread(source, target):
        got = []
        for step in range(4):
            part = source.at[even(((row + step) % 4) * rows, rows), :]
            lanes = pl.ds(((4 - step) % 4) * piece, piece)
            if step:
                got.append(mail.post(part, target.at[own_rows, lanes], along_y(place, step)))
            else:
                mine = keep(part, target.at[own_rows, lanes])
        return got, mine

    tokens = spread(tok, tok_v)
    lens[...] = jnp.zeros_like(lens)
    lens[0:1, 0 : lens_in.shape[1]] = lens_in[...]
    gains[...] = jnp.zeros_like(gains)
    gains[0:1, :] = gain_attn[...].reshape(1, piece)
    gains[1:2, :] = gain_ffn[...].reshape(1, piece)
    lens_got = mail.post(lens, lens_v.at[col], pair)
    lens_kept = keep(lens, lens_v.at[col])
    gains_kept = keep(gains, gains_v.at[0])
    gains_got = [mail.post(gains, gains_v.at[4 - s], along_y(place, s)) for s in (1, 2, 3)]

    q_width, kv_width = wq.shape[1], wk.shape[1]
    stages = [
        keep(wq, w_in.at[0, :, pl.ds(0, q_width)]),
        keep(wk, w_in.at[0, :, pl.ds(q_width, kv_width)]),
        keep(wv, w_in.at[0, :, pl.ds(q_width + kv_width, kv_width)]),
        keep(wo, w_out.at[:, pl.ds(0, piece)]),
    ]
    share = wd_own.shape[0]
    thin = piece // 2
    sure = share - LANES
    take = pl.multiple_of(z * share, LANES)
    big = []
    for k in range(2):
        for i, source in enumerate((wg, wu)):
            from_rows = pl.ds(k * thin, thin)
            big.append(keep(source.at[from_rows, pl.ds(take, sure)], gu_own.at[k, :, pl.ds(i * share, sure)]))
    big.append(keep(wd.at[pl.ds(take, sure), :], wd_own.at[pl.ds(0, sure), :]))
    blank_gu[...] = jnp.zeros_like(blank_gu)
    blank_wd[...] = jnp.zeros_like(blank_wd)
    first_edge = len(kept)
    edges = []
    for k in range(2):
        for i, source in enumerate((wg, wu)):
            target = gu_own.at[k, :, pl.ds(i * share + sure, LANES)]
            edges.append((source, pl.ds(k * thin, thin), None, target, blank_gu))
    edges.append((wd, None, slice(None), wd_own.at[pl.ds(sure, LANES), :], blank_wd))

    def edge(index, last):
        source, from_rows, _, target, blank = edges[index]
        if last:
            origin = blank
        elif from_rows is None:
            origin = source.at[pl.ds(pl.multiple_of(take + sure, LANES), LANES), :]
        else:
            origin = source.at[from_rows, pl.ds(pl.multiple_of(take + sure, LANES), LANES)]
        return pltpu.make_async_copy(origin, target, local.at[first_edge + index])

    @pl.when(z < 3)
    def _():
        for index in range(len(edges)):
            edge(index, False).start()

    @pl.when(z == 3)
    def _():
        for index in range(len(edges)):
            edge(index, True).start()

    for index in range(len(edges)):
        kept.append(edge(index, True))
        big.append(first_edge + index)

    q_rows, o_rows = thin // 4, w_out.shape[0] // 8

    def in_part(j, owner_z):
        return w_in.at[j, even(core * thin + owner_z * q_rows, q_rows), :]

    def in_parts(owner_z):
        return w_in.at[pl.ds(1, 3), even(core * thin + owner_z * q_rows, q_rows), :]

    def in_side(owner_z, side):
        lanes = pl.ds(side * (w_in.shape[2] // 2), w_in.shape[2] // 2)
        return w_in.at[pl.ds(1, 3), even(core * thin + owner_z * q_rows, q_rows), lanes]

    def out_part(j, owner_z):
        return w_out.at[even(core * 4 * o_rows + owner_z * o_rows, o_rows), pl.ds(j * piece, piece)]

    def out_parts(owner_z):
        return w_out.at[even(core * 4 * o_rows + owner_z * o_rows, o_rows), pl.ds(piece, 3 * piece)]

    def out_side(owner_z, side):
        start = core * 4 * o_rows + owner_z * o_rows + side * (o_rows // 2)
        return w_out.at[even(start, o_rows // 2), pl.ds(piece, 3 * piece)]

    for index in stages:
        kept_wait(index)
    in_got = [mail.post(in_part(0, z), in_part(4 - step, z), along_y(place, step)) for step in (1, 3, 2)]

    def to_pair(spreading, target):
        got, mine = spreading
        kept_wait(mine)
        for copy in got:
            copy.wait_recv()
        return mail.post(target.at[own_rows, :], target.at[own_rows, :], pair)

    tokens_pair = to_pair(tokens, tok_v)
    shares = []

    def give(part):
        shares.append(mail.post(part, part, twin))

    def z_first(side):
        copies = {}
        for turn in range(2):
            copies["u", turn] = mail.post(side(z, turn), side(z, turn), up)
            copies["d", 1 - turn] = mail.post(side(z, 1 - turn), side(z, 1 - turn), down)
        return copies

    below, above, across = (z + 3) % 4, (z + 1) % 4, (z + 2) % 4

    def z_second(side, whole, copies):
        copies["u", 0].wait_recv()
        far_up = mail.post(side(below, 0), side(below, 0), up)
        copies["d", 1].wait_recv()
        far_down = mail.post(side(above, 1), side(above, 1), down)
        copies["u", 1].wait_recv()
        give(whole(below))
        copies["d", 0].wait_recv()
        give(whole(above))
        return far_up, far_down

    def z_third(whole, copies):
        for copy in copies:
            copy.wait_recv()
        give(whole(across))

    for copy in in_got:
        copy.wait_recv()
    in_z = z_first(in_side)
    give(in_parts(z))
    out_got = [mail.post(out_part(0, z), out_part(4 - step, z), along_y(place, step)) for step in (1, 3, 2)]
    cotangents = spread(cot, cot_full.at[0])
    for index in big:
        kept_wait(index)
    x_lo = (dp // 2) % 2
    gu_half, wd_half = thin // 4, share // 4

    def gu_part(j, which=None, owner=x_lo):
        start, size = (0, 2 * gu_half) if which is None else (which * gu_half, gu_half)
        return wgu_full.at[j, core, even(owner * 2 * gu_half + start, size), :]

    def gu_whole(j):
        return wgu_full.at[j, core]

    def wd_part(j, which=None):
        start, size = (0, 2 * wd_half) if which is None else (which * wd_half, wd_half)
        return wd_full.at[even(core * 2 * wd_half + start, size), pl.ds(j * piece, piece)]

    def gu_source(which):
        return gu_own.at[core, even((x_lo * 2 + which) * gu_half, gu_half), :]

    def wd_source(which):
        return wd_own.at[even((core * 2 + which) * wd_half, wd_half), :]

    y_ring, near_gu, twins = {}, [], []

    def y_start(name, source, part):
        for turn in range(2):
            y_ring[name, "r", turn] = mail.post(source(turn), part(3, turn), right)
            y_ring[name, "l", 1 - turn] = mail.post(source(1 - turn), part(1, 1 - turn), left)

    def y_forward(name, part):
        y_ring[name, "r", 0].wait_recv()
        y_ring[name, "fr"] = mail.post(part(3, 0), part(2, 0), right)
        y_ring[name, "l", 1].wait_recv()
        y_ring[name, "fl"] = mail.post(part(1, 1), part(2, 1), left)

    def y_share(name, part, queue, device):
        y_ring[name, "r", 1].wait_recv()
        queue.append(mail.post(part(3), part(3), device))
        y_ring[name, "l", 0].wait_recv()
        queue.append(mail.post(part(1), part(1), device))

    def y_end(name, part, queue, device):
        y_ring[name, "fr"].wait_recv()
        y_ring[name, "fl"].wait_recv()
        queue.append(mail.post(part(2), part(2), device))


    kept_wait(lens_kept)
    lens_got.wait_recv()
    half_rows = 4 * rows

    def segment_of(which, index):
        end_0 = lens_v[which, 0:1, 0:1]
        end_1 = end_0 + lens_v[which, 0:1, 1:2]
        past_0 = (index >= end_0).astype(jnp.int32)
        past_1 = (index >= end_1).astype(jnp.int32)
        start = jnp.where(past_1 > 0, end_1, jnp.where(past_0 > 0, end_0, 0))
        return past_0 + past_1, start

    lane = lax.broadcasted_iota(jnp.int32, (rows, HEAD_SIZE), 1)
    half_lane = jnp.where(lane >= HEAD_SIZE // 2, lane - HEAD_SIZE // 2, lane).astype(F32)
    inverse = jnp.exp(half_lane * (-2.0 * math.log(THETA) / HEAD_SIZE))
    for which, mask, mask_t, key_count in ((0, bias_a, turned_a, half_rows), (1, bias_b, turned_b, 2 * half_rows)):
        index = lax.broadcasted_iota(jnp.int32, (rows, HEAD_SIZE), 0) + (row * rows + which * half_rows)
        _, start = segment_of(which, index)
        turn = (index - start).astype(F32) * inverse
        tables[0, which * rows : (which + 1) * rows, :] = jnp.cos(turn)
        sine = jnp.sin(turn)
        tables[1, which * rows : (which + 1) * rows, :] = jnp.where(lane >= HEAD_SIZE // 2, sine, -sine)
        at = lax.broadcasted_iota(jnp.int32, (rows, key_count), 0) + (row * rows + which * half_rows)
        keys = lax.broadcasted_iota(jnp.int32, (rows, key_count), 1)
        allowed = jnp.logical_and(segment_of(which, at)[0] == segment_of(which, keys)[0], keys <= at)
        mask[...] = jnp.where(allowed, 0.0, -1e30)
        at = lax.broadcasted_iota(jnp.int32, (key_count, rows), 1) + (row * rows + which * half_rows)
        keys = lax.broadcasted_iota(jnp.int32, (key_count, rows), 0)
        allowed = jnp.logical_and(segment_of(which, at)[0] == segment_of(which, keys)[0], keys <= at)
        mask_t[...] = jnp.where(allowed, 0.0, -1e30)

    kept_wait(gains_kept)
    for copy in gains_got:
        copy.wait_recv()
    keep(gains_v, gains_out)

    def normalise(value, which):
        scale = lax.rsqrt(jnp.sum(value * value, -1, keepdims=True) * (1.0 / width) + EPS)
        return [
            (value[:, j * piece : (j + 1) * piece] * scale * gains_v[j, which : which + 1, :]).astype(BF16)
            for j in range(4)
        ]

    def norm_rows(which):
        part = pl.ds(pl.multiple_of(which * rows, rows), rows)
        for j, block in enumerate(normalise(tok_v[part, :].astype(F32), 0)):
            normed[part, pl.ds(j * piece, piece)] = block

    norm_rows(col)
    for copy in out_got:
        copy.wait_recv()
    give(out_parts(z))
    y_start("gu", gu_source, gu_part)
    keep(gu_own, wgu_full.at[0])
    keep(wd_own, wd_full.at[:, pl.ds(0, piece)])
    in_far = z_second(in_side, in_parts, in_z)
    out_z = z_first(out_side)
    tokens_pair.wait_recv()
    keep(tok_v, tok_out)
    norm_rows(1 - col)
    cot_pair = to_pair(cotangents, cot_full.at[0])
    z_third(in_parts, in_far)
    for copy in shares:
        copy.wait_recv()
    shares.clear()
    keep(w_in, w_in_out)

    in_width = w_in.shape[2]

    def project(lanes, bias):
        weights = w_in[:, :, lanes]
        weights = weights.reshape(4 * weights.shape[1], weights.shape[2])
        return jnp.dot(normed[...], weights, preferred_element_type=F32) + bias

    def rotate(value):
        return value * tables[0] + pltpu.roll(value, HEAD_SIZE // 2, 1) * tables[1]

    key_value = project(slice(q_width, in_width), jnp.concatenate([bias_k[...].reshape(1, kv_width), bias_v[...].reshape(1, kv_width)], 1))
    kv[:, 0:kv_width] = rotate(key_value[:, 0:kv_width]).astype(BF16)
    kv[:, kv_width : 2 * kv_width] = key_value[:, kv_width : 2 * kv_width].astype(BF16)
    a_rows, b_rows = pl.ds(0, rows), pl.ds(rows, rows)
    high_spot = even(half_rows + row * rows, rows)
    a_got, b_got = [], []
    for step in (1, 2, 3):
        a_got.append(mail.post(kv.at[a_rows, :], kva.at[spot, :], along_y(place, step)))
    kva[spot, :] = kv[a_rows, :]
    kvb[high_spot, :] = kv[b_rows, :]
    for first in range(0, q_width, 2 * HEAD_SIZE):
        value = project(slice(first, first + 2 * HEAD_SIZE), bias_q[first : first + 2 * HEAD_SIZE].reshape(1, 2 * HEAD_SIZE))
        for i in range(2):
            lanes = slice(first + i * HEAD_SIZE, first + (i + 1) * HEAD_SIZE)
            query[:, lanes] = rotate(value[:, i * HEAD_SIZE : (i + 1) * HEAD_SIZE]).astype(BF16)

    y_forward("gu", gu_part)
    y_share("gu", gu_part, near_gu, near)
    out_far = z_second(out_side, out_parts, out_z)
    heads = q_width // HEAD_SIZE
    factor = HEAD_SIZE ** (-0.5)

    def attend(half, keys, mask):
        part = slice(half * rows, (half + 1) * rows)

        @pl.loop(0, heads)
        def _(h):
            lanes = pl.ds(pl.multiple_of(h * HEAD_SIZE, LANES), HEAD_SIZE)
            raw = lax.dot_general(
                query[part, lanes], keys[:, 0:HEAD_SIZE], (((1,), (1,)), ((), ())), preferred_element_type=F32
            )
            scores = raw * factor + mask[...]
            peak = jnp.max(scores, -1, keepdims=True)
            raised = jnp.exp(scores - peak)
            total = jnp.sum(raised, -1, keepdims=True)
            probs = (raised * (1.0 / total)).astype(BF16)
            out = jnp.dot(probs, keys[:, HEAD_SIZE : 2 * HEAD_SIZE], preferred_element_type=F32)
            attended[part, lanes] = out.astype(BF16)
            logs[half * heads + h] = jnp.broadcast_to(peak + jnp.log(total), (rows, LANES)).T[0:8, :]

        for first in range(0, width, piece):
            lanes = slice(first, first + piece)
            branch[part, lanes] = jnp.dot(
                attended[part, :], w_out[:, lanes], preferred_element_type=F32
            ).astype(BF16)
        return mail.post(branch.at[part, :], branch_in.at[part, :], pair)

    def finish_half(half, copy):
        part = slice(half * rows, (half + 1) * rows)
        copy.wait_recv()
        value = tok_v[part, :].astype(F32) + (branch[part, :].astype(F32) + branch_in[part, :].astype(F32))
        middle[part, :] = value
        for j, block in enumerate(normalise(value, 1)):
            normed_ffn[part, j * piece : (j + 1) * piece] = block

    def z_send(source, target, half):
        part = pl.ds(half * rows, rows)
        return (
            mail.post(source.at[part, :], target.at[1, part, :], up),
            mail.post(source.at[part, :], target.at[3, part, :], down),
        )

    def z_forward(target, half, copies):
        part = pl.ds(half * rows, rows)
        if half == 0:
            copies[0].wait_recv()
            return copies[1], mail.post(target.at[1, part, :], target.at[2, part, :], up)
        copies[1].wait_recv()
        return copies[0], mail.post(target.at[3, part, :], target.at[2, part, :], down)

    for copy in a_got:
        copy.wait_recv()
    for step in range(4):
        b_got.append(mail.post(kv.at[a_rows, :], kvb.at[spot, :], near_of(place, (row + step) % 4)))
        if step:
            b_got.append(mail.post(kv.at[b_rows, :], kvb.at[high_spot, :], along_y(place, step)))
    keep(kva, kva_out)
    z_third(out_parts, out_far)
    for copy in shares:
        copy.wait_recv()
    keep(w_out, w_out_out)
    swap_a = attend(0, kva, bias_a)
    cot_pair.wait_recv()
    cot_z = [z_send(cot_full.at[0], cot_full, half) for half in range(2)]
    for copy in b_got:
        copy.wait_recv()
    keep(kvb, kvb_out)
    swap_b = attend(1, kvb, bias_b)
    y_end("gu", gu_part, near_gu, near)
    y_start("wd", wd_source, wd_part)
    finish_half(0, swap_a)
    cot_last = [z_forward(cot_full, half, cot_z[half]) for half in range(2)]
    y_forward("wd", wd_part)
    finish_half(1, swap_b)
    y_share("wd", wd_part, twins, twin)
    for j, copy in zip((3, 1, 2), near_gu):
        copy.wait_recv()
        twins.append(mail.post(gu_whole(j), gu_whole(j), twin))
    y_end("wd", wd_part, twins, twin)
    for copies in cot_last:
        for copy in copies:
            copy.wait_recv()
    for copy in twins:
        copy.wait_recv()
    for copy in kept:
        if copy is not None:
            copy.wait()
    mail.finish()


def ffn_kernel(
    normed,
    cot,
    wgu,
    wd,
    total,
    gu_sum,
    gu_late,
    dn_half,
    result_sum,
    result_ahead,
    x,
    cot_v,
    wgu_v,
    wd_v,
    gb,
    act,
    parts,
    turned,
    down_v,
    gu_in,
    dn_in,
    up1,
    down1,
    up2,
    down2,
    other,
    stage_up,
    stage_down,
    stage,
    res_up1,
    res_down1,
    res_up2,
    res_down2,
    gu_up1,
    gu_down1,
    gu_up2,
    gu_down2,
    send,
    recv,
    local,
):
    place = here()
    dp, row, col = place
    core = dp % 2
    up, down, pair, twin = along_z(place, 1), along_z(place, 3), pair_of(place), twin_of(place)
    right, left = along_y(place, 1), along_y(place, 3)
    meet([up, down, pair, twin, right, left])
    mail = Mail(send, recv)
    order = ((0, 0), (0, 1), (1, 0), (3, 1), (2, 0), (2, 1), (1, 1), (3, 0))
    spots = {half: i for i, half in enumerate(order)}
    rows = normed.shape[0] // 2
    size = rows // 2

    def block(ref, slot, half):
        return ref.at[pl.ds(spots[slot, half] * rows, rows), :]

    def halves(ref, half):
        return ref.at[pl.ds(half * rows, rows), :]

    kept = []

    def keep(source, target):
        kept.append(pltpu.make_async_copy(source, target, local.at[len(kept)]))
        kept[-1].start()
        return len(kept) - 1

    def kept_wait(index):
        kept[index].wait()
        kept[index] = None

    got = {}

    def z_start(which):
        got["u", which] = mail.post(halves(normed, which), block(x, 1, which), up)
        got["d", 1 - which] = mail.post(halves(normed, 1 - which), block(x, 3, 1 - which), down)

    z_start(0)
    share = wd.shape[0]
    early = [keep(normed, x.at[pl.ds(0, 2 * rows), :]), keep(wgu, wgu_v)]
    early.append(keep(cot.at[0], cot_v.at[pl.ds(0, 2 * rows), :]))
    early.append(keep(wd, wd_v))
    later = [keep(cot.at[slot, pl.ds(half * rows, rows), :], block(cot_v, slot, half)) for slot, half in order[2:]]
    width = normed.shape[1]
    piece = width // 4

    def dot_nt(left, right):
        return lax.dot_general(left, right, (((1,), (1,)), ((), ())), preferred_element_type=F32)

    def compute(c):
        part = slice(2 * rows * c, 2 * rows * (c + 1))
        for start, size in ((0, 512), (512, share - 512)):
            lanes, above = slice(start, start + size), slice(share + start, share + start + size)
            gate = jnp.dot(x[part, :], wgu_v[:, lanes], preferred_element_type=F32)
            value = jnp.dot(x[part, :], wgu_v[:, above], preferred_element_type=F32)
            grad = dot_nt(cot_v[part, :], wd_v[lanes, :])
            spread = 1.0 / (1.0 + jnp.exp(-gate))
            smooth = gate * spread
            act[part, lanes] = (smooth * value).astype(BF16)
            gb[part, lanes] = (grad * value * (spread * (1.0 + gate * (1.0 - spread)))).astype(BF16)
            gb[part, above] = (grad * smooth).astype(BF16)
        for m in range(3):
            lanes = slice(512 * m, 512 * (m + 1))
            parts[part, lanes] = dot_nt(gb[part, :], wgu_v[lanes, :]).astype(BF16)

    for index in early:
        kept_wait(index)
    compute(0)
    got["u", 0].wait_recv()
    far_up = mail.post(block(x, 1, 0), block(x, 2, 0), up)
    got["d", 1].wait_recv()
    far_down = mail.post(block(x, 3, 1), block(x, 2, 1), down)
    for index in later:
        kept_wait(index)
    compute(1)
    z_start(1)
    far_up.wait_recv()
    far_down.wait_recv()
    compute(2)
    first = {}
    for i in range(2):
        rows_i = pl.ds(i * size, size)
        first["u", i] = mail.post(block(parts, 2, 0).at[rows_i, :], up1.at[i], up)
        first["d", i] = mail.post(block(parts, 2, 1).at[rows_i, :], down1.at[i], down)
    got["u", 1].wait_recv()
    got["d", 0].wait_recv()
    compute(3)
    second = {
        ("d", 0): mail.post(block(parts, 1, 0), down2.at[0], down),
        ("u", 1): mail.post(block(parts, 3, 1), up2.at[1], up),
    }

    def turn_over(source, target):
        @pl.loop(0, source.shape[1] // LANES)
        def _(t):
            lanes = pl.ds(pl.multiple_of(t * LANES, LANES), LANES)
            target[lanes, :] = source[:, lanes].T

    def forward(i):
        rows_i = pl.ds(i * size, size)
        first["u", i].wait_recv()
        stage_up[i] = (block(parts, 3, 0).at[rows_i, :][...].astype(F32) + up1[i].astype(F32)).astype(BF16)
        second["u", 0, i] = mail.post(stage_up.at[i], up2.at[0, rows_i, :], up)
        first["d", i].wait_recv()
        stage_down[i] = (block(parts, 1, 1).at[rows_i, :][...].astype(F32) + down1[i].astype(F32)).astype(BF16)
        second["d", 1, i] = mail.post(stage_down.at[i], down2.at[1, rows_i, :], down)

    turn_over(x, turned)
    tile = 256
    tiles = 2 * share // tile

    def gu_tiles(first_tile, last_tile):
        @pl.loop(first_tile, last_tile)
        def _(n):
            lanes = pl.ds(pl.multiple_of(((n + (tiles // 2) * (1 - core)) % tiles) * tile, tile), tile)
            wgu_v[:, lanes] = jnp.dot(turned[...], gb[:, lanes], preferred_element_type=F32).astype(BF16)

    swaps = {}

    def settle(i):
        rows_i = pl.ds(i * size, size)
        if i == 0:
            second["d", 0].wait_recv()
            second["u", 1].wait_recv()
        second["u", 0, i].wait_recv()
        second["d", 1, i].wait_recv()
        for half in range(2):
            value = block(parts, 0, half).at[rows_i, :][...].astype(F32)
            value = value + up2[half, rows_i, :].astype(F32) + down2[half, rows_i, :].astype(F32)
            stage[half, rows_i, :] = value.astype(BF16)
            swaps[half, i] = mail.post(stage.at[half, rows_i, :], other.at[half, rows_i, :], pair)

    there = pl.ds(pl.multiple_of((1 - core) * share, LANES), share)
    mine = pl.ds(pl.multiple_of(core * share, LANES), share)
    gu_tiles(0, tiles // 2 + 1)
    shared = [
        mail.post(wgu_v.at[pl.ds(j * piece, piece), there], gu_in.at[j], twin) for j in range(4)
    ]
    forward(0)
    forward(1)
    gu_tiles(tiles // 2 + 1, tiles)
    for j in range(4):
        shared[j].wait_recv()
        gu_in[j] = (wgu_v[pl.ds(j * piece, piece), mine].astype(F32) + gu_in[j].astype(F32)).astype(BF16)

    def ring_y(i):
        height = piece // 3
        half = height // 2
        low, high = pl.ds(i * height, half), pl.ds(i * height + half, half)
        one, two, three, four = gu_up1.at[i], gu_down1.at[i], gu_up2.at[i], gu_down2.at[i]
        begin = (mail.post(gu_in.at[2, low, :], one, right), mail.post(gu_in.at[2, high, :], two, left))
        straight = [
            mail.post(gu_in.at[1, high, :], three.at[pl.ds(half, half), :], right),
            mail.post(gu_in.at[3, low, :], four.at[pl.ds(0, half), :], left),
        ]
        yield
        begin[0].wait_recv()
        one[...] = (gu_in[1, low, :].astype(F32) + one[...].astype(F32)).astype(BF16)
        straight.append(mail.post(one, three.at[pl.ds(0, half), :], right))
        begin[1].wait_recv()
        two[...] = (gu_in[3, high, :].astype(F32) + two[...].astype(F32)).astype(BF16)
        straight.append(mail.post(two, four.at[pl.ds(half, half), :], left))
        yield
        for copy in straight:
            copy.wait_recv()
        part = pl.ds(i * height, height)
        value = gu_in[0, part, :].astype(F32) + three[...].astype(F32) + four[...].astype(F32)
        gu_sum[part, :] = value.astype(BF16)
        yield

    rings = [ring_y(i) for i in range(2)]
    keep(gu_in.at[:, pl.ds(2 * (piece // 3), piece // 3), :], gu_late)
    for ring in rings:
        next(ring)
    for m in range(3):
        lanes = slice(512 * m, 512 * (m + 1))

        @pl.loop(0, 4)
        def _(c):
            part = pl.ds(pl.multiple_of(c * 2 * rows, 2 * rows), 2 * rows)
            down_v[part, lanes] = jnp.dot(act[part, :], wd_v[:, lanes], preferred_element_type=F32).astype(BF16)

    settle(0)
    settle(1)
    result = {
        "u1": mail.post(block(down_v, 2, 0), res_up1, up),
        "d1": mail.post(block(down_v, 2, 1), res_down1, down),
        "u2": mail.post(block(down_v, 3, 1), res_up2, up),
        "d2": mail.post(block(down_v, 1, 0), res_down2, down),
    }
    turn_over(act, turned)

    @pl.loop(0, width // tile)
    def _(n):
        lanes = pl.ds(pl.multiple_of(n * tile, tile), tile)
        wd_v[:, lanes] = jnp.dot(
            turned[0:share, :], cot_v[:, lanes], preferred_element_type=F32
        ).astype(BF16)

    half_share = share // 2
    rows_there = pl.ds(pl.multiple_of((1 - core) * half_share, 16), half_share)
    rows_mine = pl.ds(pl.multiple_of(core * half_share, 16), half_share)
    shared += [
        mail.post(wd_v.at[rows_there, pl.ds(j * piece, piece)], dn_in.at[j], twin) for j in range(4)
    ]
    for ring in rings:
        next(ring)
    for j in range(4):
        shared[4 + j].wait_recv()
        dn_in[j] = (wd_v[rows_mine, pl.ds(j * piece, piece)].astype(F32) + dn_in[j].astype(F32)).astype(BF16)
        keep(dn_in.at[j], dn_half.at[j])
    for half, i in ((0, 0), (1, 0), (0, 1), (1, 1)):
        rows_i = pl.ds(i * size, size)
        swaps[half, i].wait_recv()
        total[pl.ds(half * rows + i * size, size), :] = stage[half, rows_i, :].astype(F32) + other[
            half, rows_i, :
        ].astype(F32)
    next(rings[0])
    next(rings[1])
    for copy in result.values():
        copy.wait_recv()
    result_ahead[0] = (block(down_v, 3, 0)[...].astype(F32) + res_up1[...].astype(F32)).astype(BF16)
    result_ahead[1] = (block(down_v, 1, 1)[...].astype(F32) + res_down1[...].astype(F32)).astype(BF16)
    for half, theirs in ((0, res_down2), (1, res_up2)):
        value = block(down_v, 0, half)[...].astype(F32) + theirs[...].astype(F32)
        result_sum[pl.ds(half * rows, rows), :] = value.astype(BF16)
    for copy in kept:
        if copy is not None:
            copy.wait()
    mail.finish()


def back_kernel(
    total,
    middle,
    cot,
    gains,
    tok,
    normed,
    query,
    kv_a,
    kv_b,
    logs,
    attended,
    tables,
    turned_a,
    turned_b,
    w_in,
    w_out,
    gu,
    gl,
    dn,
    result_sum,
    ahead,
    gu_out,
    dn_out,
    in_out,
    kw_out,
    wo_out,
    grad_out,
    result_out,
    small_out,
    middle_v,
    cot_v,
    tok_v,
    normed_v,
    query_v,
    kva,
    kvb,
    attended_v,
    turned_a_v,
    turned_b_v,
    w_in_v,
    w_out_v,
    gu_v,
    gl_v,
    dn_v,
    down_v,
    gain_rows,
    grad_middle,
    grad_low,
    grad_att,
    flat,
    keys_t,
    dkv_a,
    dkv_b,
    low_kv,
    own_kv,
    from_own,
    from_near,
    grad_pre,
    grad_part,
    grad_in,
    part_in,
    rows_out,
    result_rows,
    gu_n,
    gu_s,
    gl_up1,
    gl_down1,
    gl_up2,
    gl_down2,
    gl_y,
    dn_up1,
    dn_down1,
    dn_up2,
    dn_down2,
    dn_y,
    dn_n,
    dn_s,
    in_p,
    in_t,
    in_up1,
    in_down1,
    in_up2,
    in_down2,
    in_s,
    in_n,
    in_z,
    kw_p,
    kw_t,
    kw_up1,
    kw_down1,
    kw_up2,
    kw_down2,
    kw_s,
    kw_n,
    kw_z,
    wo_p,
    wo_t,
    wo_up1,
    wo_down1,
    wo_up2,
    wo_down2,
    wo_s,
    wo_n,
    wo_z,
    res_in,
    res_total,
    bias_own,
    gains_own,
    bias_in,
    gains_in,
    small_a,
    small_b,
    small_t,
    small_n,
    send,
    recv,
    local,
):
    place = here()
    dp, row, col = place
    core = dp % 2
    z = dp // Z_STEP
    twin, near, pair = twin_of(place), near_of(place), pair_of(place)
    up, down, far_z = along_z(place, 1), along_z(place, 3), along_z(place, 2)
    right, left = along_y(place, 1), along_y(place, 3)
    meet(
        [along_y(place, s) for s in (1, 2, 3)]
        + [near_of(place, (row + s) % 4) for s in range(4)]
        + [pair_of(place, (row + s) % 4) for s in range(4)]
        + [twin, up, down, far_z]
    )
    mail = Mail(send, recv)
    kept, arrivals = [], []

    def keep(source, target):
        kept.append(pltpu.make_async_copy(source, target, local.at[len(kept)]))
        kept[-1].start()
        return len(kept) - 1

    def kept_wait(index):
        if kept[index] is not None:
            kept[index].wait()
            kept[index] = None

    def even(start, size):
        return pl.ds(pl.multiple_of(start, 16), size)

    def plus(*values):
        result = values[0].astype(F32)
        for value in values[1:]:
            result = result + value.astype(F32)
        return result

    def dot_nt(left, right):
        return lax.dot_general(left, right, (((1,), (1,)), ((), ())), preferred_element_type=F32)

    rows = tok.shape[0] // 2
    width = tok.shape[1]
    piece = width // 4
    spot = even(row * rows, rows)
    own_rows, other_rows = even(col * rows, rows), even((1 - col) * rows, rows)

    def ffn_flow(i):
        if i < 2:
            height = gu.shape[0] // 2
            start = i * height
            theirs, done = gu_n.at[i], gu_s.at[i]
            mine = gu_v.at[pl.ds(start, height), :]
            swap = mail.post(gu.at[pl.ds(start, height), :], theirs, near)
            half = height // 2
            yield
            kept_wait(loads["gu"])
        else:
            if i == 2:
                held, loaded, name, height, start = gl, gl_v, "gl", gl.shape[1], 2 * gl.shape[1]
                mine, theirs, done = gl_y, gu_n.at[2], gu_s.at[2]
                one, two, three, four = gl_up1, gl_down1, gl_up2, gl_down2
            else:
                held, loaded, name, height, start = dn, dn_v, "dn", dn.shape[1], 0
                mine, theirs, done = dn_y, dn_n, dn_s
                one, two, three, four = dn_up1, dn_down1, dn_up2, dn_down2
            half = height // 2
            low, high = pl.ds(0, half), pl.ds(half, half)
            first = (mail.post(held.at[2, low, :], one, right), mail.post(held.at[2, high, :], two, left))
            straight = (
                mail.post(held.at[1, high, :], three.at[high, :], right),
                mail.post(held.at[3, low, :], four.at[low, :], left),
            )
            yield
            kept_wait(loads[name])
            first[0].wait_recv()
            one[...] = plus(loaded[1, low, :], one[...]).astype(BF16)
            last = [mail.post(one, three.at[low, :], right)]
            first[1].wait_recv()
            two[...] = plus(loaded[3, high, :], two[...]).astype(BF16)
            last.append(mail.post(two, four.at[high, :], left))
            yield
            for copy in straight + tuple(last):
                copy.wait_recv()
            mine[...] = plus(loaded[0], three[...], four[...]).astype(BF16)
            swap = mail.post(mine, theirs, near)
            yield
        swap.wait_recv()
        done[...] = plus(mine[...], theirs[...]).astype(BF16)

        def room(slot, which=None):
            begin, size = (start, height) if which is None else (start + which * half, half)
            if i < 3:
                share = gu_out.shape[2] // 4
                lanes = pl.ds(pl.multiple_of(slot * share, LANES), share)
                return gu_out.at[core, pl.ds(begin, size), lanes]
            return dn_out.at[even((slot * 2 + core) * height + begin, size), :]

        posts = {}
        for turn in range(2):
            for name, device, which in (("u", up, turn), ("d", down, 1 - turn)):
                posts[name, which] = mail.post(done.at[pl.ds(which * half, half), :], room(z, which), device)
        keep(done, room(z))
        arrivals.append(mail.post(done, room(z), twin))
        yield
        posts["u", 0].wait_recv()
        block = room((z + 3) % 4, 0)
        one_more = mail.post(block, block, up)
        posts["d", 1].wait_recv()
        block = room((z + 1) % 4, 1)
        two_more = mail.post(block, block, down)
        yield
        posts["u", 1].wait_recv()
        block = room((z + 3) % 4)
        arrivals.append(mail.post(block, block, twin))
        posts["d", 0].wait_recv()
        block = room((z + 1) % 4)
        arrivals.append(mail.post(block, block, twin))
        one_more.wait_recv()
        two_more.wait_recv()
        block = room((z + 2) % 4)
        arrivals.append(mail.post(block, block, twin))
        yield

    def weight_flow(part, t, up1, down1, up2, down2, total_h, theirs, quarter, out):
        height = t.shape[1]
        half = height // 2
        low, high = pl.ds(0, half), pl.ds(half, half)
        copy = mail.post(part.at[:, even((1 - core) * height, height), :], t, twin)
        yield
        copy.wait_recv()
        for j in range(4):
            t[j] = plus(part[j, even(core * height, height), :], t[j]).astype(BF16)
        first = (mail.post(t.at[2, low, :], up1, right), mail.post(t.at[2, high, :], down1, left))
        straight = (
            mail.post(t.at[1, high, :], up2.at[high, :], right),
            mail.post(t.at[3, low, :], down2.at[low, :], left),
        )
        yield
        first[0].wait_recv()
        up1[...] = plus(t[1, low, :], up1[...]).astype(BF16)
        last = [mail.post(up1, up2.at[low, :], right)]
        first[1].wait_recv()
        down1[...] = plus(t[3, high, :], down1[...]).astype(BF16)
        last.append(mail.post(down1, down2.at[high, :], left))
        yield
        for copy in straight + tuple(last):
            copy.wait_recv()
        total_h[...] = plus(t[0], up2[...], down2[...]).astype(BF16)
        swap = mail.post(total_h, theirs, near)
        yield
        swap.wait_recv()
        t[0] = plus(total_h[...], theirs[...]).astype(BF16)
        size = height // 4
        copies = []
        for step, device in ((1, up), (3, down), (2, far_z)):
            source = t.at[0, even(((z + step) % 4) * size, size), :]
            copies.append(mail.post(source, quarter.at[step - 1], device))
        yield
        for copy in copies:
            copy.wait_recv()
        mine = even(z * size, size)
        theirs[0:size, :] = plus(t[0, mine, :], quarter[0], quarter[1], quarter[2]).astype(BF16)
        place_of = lambda owner: out.at[even(core * height + owner * size, size), :]
        copies = [mail.post(theirs.at[0:size, :], place_of(z), device) for device in (up, down, far_z)]
        arrivals.append(mail.post(theirs.at[0:size, :], place_of(z), twin))
        keep(theirs.at[0:size, :], place_of(z))
        yield
        for copy in copies:
            copy.wait_recv()
        for step in (1, 2, 3):
            block = place_of((z + step) % 4)
            arrivals.append(mail.post(block, block, twin))
        yield

    def result_flow():
        copies = (mail.post(ahead.at[0], res_in.at[0], up), mail.post(ahead.at[1], res_in.at[1], down))
        yield
        kept_wait(loads["down"])
        for half, copy in enumerate(copies):
            copy.wait_recv()
            part = pl.ds(half * rows, rows)
            res_total[part, :] = plus(down_v[part, :], res_in[half]).astype(BF16)
        swap = mail.post(res_total.at[other_rows, :], part_in, pair)
        yield
        swap.wait_recv()
        result_rows[...] = (middle_v[own_rows, :] + plus(res_total[own_rows, :], part_in[...])).astype(BF16)
        yield
        spread(result_rows, result_out)
        yield

    def spread(source, target):
        for step in range(4):
            lanes = pl.ds(step * piece, piece)
            if step:
                arrivals.append(mail.post(source.at[:, lanes], target.at[spot, :], along_y(place, step)))
            else:
                keep(source.at[:, lanes], target.at[spot, :])

    flows = [ffn_flow(i) for i in range(4)]
    loads = {}
    for name, source, target in (
        ("middle", middle, middle_v),
        ("cot", cot.at[0], cot_v),
        ("w_out", w_out, w_out_v),
        ("attended", attended, attended_v),
        ("query", query, query_v),
        ("kva", kv_a, kva),
        ("kvb", kv_b, kvb),
        ("ta", turned_a, turned_a_v),
        ("tb", turned_b, turned_b_v),
        ("gu", gu, gu_v),
        ("w_in", w_in, w_in_v),
        ("normed", normed, normed_v),
        ("tok", tok, tok_v),
        ("dn", dn, dn_v),
        ("gl", gl, gl_v),
        ("down", result_sum, down_v),
    ):
        loads[name] = keep(source, target)
    result_steps = result_flow()
    next(flows[3])
    next(flows[1])
    for j in range(4):
        gain_rows[:, j * piece : (j + 1) * piece] = gains[j]

    def norm_back(stream, gain, incoming):
        scale = lax.rsqrt(jnp.sum(stream * stream, -1, keepdims=True) * (1.0 / width) + EPS)
        scaled = incoming * gain
        inner = jnp.sum(scaled * stream, -1, keepdims=True) * (1.0 / width)
        back = scale * scaled - stream * (scale * scale * scale * inner)
        return back, jnp.sum(incoming * stream * scale, 0, keepdims=True)

    kept_wait(loads["middle"])
    kept_wait(loads["cot"])
    gain_ffn_part = jnp.zeros((1, width), F32)
    for half in range(2):
        part = slice(half * rows, (half + 1) * rows)
        back, gain_part = norm_back(middle_v[part, :], gain_rows[1:2, :], total[part, :])
        value = cot_v[part, :].astype(F32) + back
        grad_middle[part, :] = value
        grad_low[part, :] = value.astype(BF16)
        gain_ffn_part = gain_ffn_part + gain_part
    gains_own[...] = jnp.zeros_like(gains_own)
    for j in range(4):
        gains_own[j, 1:2, :] = 0.5 * gain_ffn_part[:, j * piece : (j + 1) * piece]
    next(result_steps)
    kept_wait(loads["w_out"])
    q_width = w_out.shape[0]
    for first in range(0, q_width, 256):
        lanes = slice(first, first + 256)
        grad_att[:, lanes] = dot_nt(grad_low[...], w_out_v[lanes, :]).astype(BF16)

    def turn_over(source, target, count):
        for t in range(count):
            lanes = slice(t * LANES, (t + 1) * LANES)
            target[lanes, 0 : source.shape[0]] = source[:, lanes].T

    next(flows[0])
    next(flows[3])
    kept_wait(loads["attended"])
    turn_over(attended_v, flat, q_width // LANES)
    for j in range(4):
        wo_p[j] = jnp.dot(
            flat[0:q_width, :], grad_low[:, j * piece : (j + 1) * piece], preferred_element_type=F32
        ).astype(BF16)
    wo_steps = weight_flow(wo_p, wo_t, wo_up1, wo_down1, wo_up2, wo_down2, wo_s, wo_n, wo_z, wo_out)

    for name in ("query", "kva", "kvb", "ta", "tb"):
        kept_wait(loads[name])
    heads = q_width // HEAD_SIZE
    factor = HEAD_SIZE ** (-0.5)

    def unrotate(value, half):
        part = slice(half * rows, (half + 1) * rows)
        return value * tables[0, part, :] + pltpu.roll(value * tables[1, part, :], HEAD_SIZE // 2, 1)

    def attend_back(half, keys, mask, sums):
        part = slice(half * rows, (half + 1) * rows)
        count = keys.shape[0]
        for t in range(count // LANES):
            lanes = slice(t * LANES, (t + 1) * LANES)
            keys_t[:, lanes] = keys[lanes, 0:HEAD_SIZE].T
        sums[...] = jnp.zeros_like(sums)

        @pl.loop(0, heads)
        def _(h):
            lanes = pl.ds(pl.multiple_of(h * HEAD_SIZE, LANES), HEAD_SIZE)
            one, grad = query_v[part, lanes], grad_att[part, lanes]
            raw = dot_nt(keys[:, 0:HEAD_SIZE], one)
            probs = jnp.exp(raw * factor + mask[...] - logs[half * heads + h, 0:1, :])
            grad_probs = dot_nt(keys[:, HEAD_SIZE : 2 * HEAD_SIZE], grad)
            inner = jnp.sum(grad_probs * probs, 0, keepdims=True)
            grad_scores = (probs * (grad_probs - inner)).astype(BF16)
            sums[:, 0:HEAD_SIZE] += jnp.dot(grad_scores, one, preferred_element_type=F32)
            sums[:, HEAD_SIZE : 2 * HEAD_SIZE] += jnp.dot(probs.astype(BF16), grad, preferred_element_type=F32)
            grad_query = jnp.dot(keys_t[:, 0:count], grad_scores, preferred_element_type=F32).T * factor
            grad_pre[part, lanes] = unrotate(grad_query, half).astype(BF16)

    def low_sums(sums, part):
        return (sums[part, 0:HEAD_SIZE] * factor).astype(BF16), sums[part, HEAD_SIZE : 2 * HEAD_SIZE].astype(BF16)

    next(wo_steps)
    next(flows[1])
    next(flows[2])
    next(result_steps)
    next(flows[1])
    next(flows[3])
    attend_back(1, kvb, turned_b_v, dkv_b)
    half_rows = kva.shape[0]
    low_part, high_part = slice(0, half_rows), slice(half_rows, 2 * half_rows)
    for target, sums, part in ((low_kv, dkv_b, low_part), (own_kv.at[1], dkv_b, high_part)):
        target[:, 0:HEAD_SIZE], target[:, HEAD_SIZE : 2 * HEAD_SIZE] = low_sums(sums, part)
    kv_got = []
    for step in range(4):
        other = (row + step) % 4
        part = even(other * rows, rows)
        kv_got.append(mail.post(low_kv.at[part, :], from_near.at[step], near_of(place, other)))
        if step:
            kv_got.append(mail.post(own_kv.at[1, part, :], from_own.at[step - 1, 1], along_y(place, step)))
    next(flows[0])
    attend_back(0, kva, turned_a_v, dkv_a)
    target = own_kv.at[0]
    target[:, 0:HEAD_SIZE], target[:, HEAD_SIZE : 2 * HEAD_SIZE] = low_sums(dkv_a, low_part)
    for step in (1, 2, 3):
        part = even(((row + step) % 4) * rows, rows)
        kv_got.append(mail.post(own_kv.at[0, part, :], from_own.at[step - 1, 0], along_y(place, step)))
    next(flows[2])
    next(flows[3])
    next(wo_steps)
    kept_wait(loads["normed"])
    turn_over(normed_v, flat, width // LANES)
    for j in range(4):
        in_p[j] = jnp.dot(
            flat[j * piece : (j + 1) * piece, :], grad_pre[:, 0:q_width], preferred_element_type=F32
        ).astype(BF16)
    in_steps = weight_flow(in_p, in_t, in_up1, in_down1, in_up2, in_down2, in_s, in_n, in_z, in_out)
    next(flows[3])
    next(flows[2])
    next(flows[0])
    next(in_steps)
    for copy in kv_got:
        copy.wait_recv()
    for half in range(2):
        part = slice(half * rows, (half + 1) * rows)
        value = own_kv[half, spot, :].astype(F32)
        for step in range(3):
            value = value + from_own[step, half].astype(F32)
        if half == 0:
            for step in range(4):
                value = value + from_near[step].astype(F32)
        grad_pre[part, q_width : q_width + HEAD_SIZE] = unrotate(value[:, 0:HEAD_SIZE], half).astype(BF16)
        grad_pre[part, q_width + HEAD_SIZE : q_width + 2 * HEAD_SIZE] = value[:, HEAD_SIZE : 2 * HEAD_SIZE].astype(
            BF16
        )
    next(wo_steps)
    next(in_steps)
    kept_wait(loads["w_in"])
    for j in range(4):
        grad_part[:, j * piece : (j + 1) * piece] = dot_nt(grad_pre[...], w_in_v[j]).astype(BF16)
    swap = mail.post(grad_part.at[other_rows, :], grad_in, pair)
    for j in range(4):
        kw_p[j] = jnp.dot(
            flat[j * piece : (j + 1) * piece, :], grad_pre[:, q_width:], preferred_element_type=F32
        ).astype(BF16)
    kw_steps = weight_flow(kw_p, kw_t, kw_up1, kw_down1, kw_up2, kw_down2, kw_s, kw_n, kw_z, kw_out)
    next(wo_steps)
    next(flows[2])
    next(kw_steps)
    next(result_steps)
    next(in_steps)
    next(kw_steps)
    bias_own[...] = jnp.zeros_like(bias_own)
    bias_own[0:1, :] = jnp.sum(grad_pre[...].astype(F32), 0, keepdims=True)
    next(wo_steps)
    kept_wait(loads["tok"])
    swap.wait_recv()
    back, gain_part = norm_back(
        tok_v[own_rows, :].astype(F32), gain_rows[0:1, :], plus(grad_part[own_rows, :], grad_in[...])
    )
    rows_out[...] = (grad_middle[own_rows, :] + back).astype(BF16)
    for j in range(4):
        gains_own[j, 0:1, :] = gain_part[:, j * piece : (j + 1) * piece]
    next(in_steps)
    next(flows[2])
    next(kw_steps)
    next(wo_steps)
    small_copies, small_kept = [], []
    for step in range(4):
        device = along_y(place, step)
        mine = gains_in.at[col * 4 + row]
        if step:
            small_copies.append(mail.post(bias_own, bias_in.at[row], device))
            small_copies.append(mail.post(gains_own.at[step], mine, device))
        else:
            small_kept.append(keep(bias_own, bias_in.at[row]))
            small_kept.append(keep(gains_own.at[step], mine))
        small_copies.append(mail.post(gains_own.at[step], mine, pair_of(place, (row + step) % 4)))
    spread(rows_out, grad_out)
    next(kw_steps)
    next(in_steps)
    for copy in small_copies:
        copy.wait_recv()
    for index in small_kept:
        kept_wait(index)
    small_a[...] = jnp.zeros_like(small_a)
    small_a[0:8, :] = bias_in[0] + bias_in[1] + bias_in[2] + bias_in[3]
    small_a[8:16, 0:piece] = (
        gains_in[0] + gains_in[1] + gains_in[2] + gains_in[3] + gains_in[4] + gains_in[5] + gains_in[6] + gains_in[7]
    )
    small_first = mail.post(small_a, small_t, twin)
    next(result_steps)
    next(kw_steps)
    small_first.wait_recv()
    small_b[...] = small_a[...] + small_t[...]
    small_second = mail.post(small_b, small_n, near)
    next(in_steps)
    next(flows[2])
    small_second.wait_recv()
    small_t[...] = small_b[...] + small_n[...]
    for device in (up, down, far_z):
        arrivals.append(mail.post(small_t, small_out.at[z], device))
    keep(small_t, small_out.at[z])
    next(wo_steps)
    next(kw_steps)
    next(in_steps)
    for steps in [*flows, wo_steps, in_steps, kw_steps, result_steps]:
        for _ in steps:
            pass
    for copy in arrivals:
        copy.wait_recv()
    for copy in kept:
        if copy is not None:
            copy.wait()
    mail.finish()


def widen_kernel(gate_up, down, w_in, w_kv, w_out, result, tokens, small, *outs):
    result_w, tokens_w, query_w, key_w, value_w, out_w, gate_w, up_w, down_w, *flat = outs
    total = small[0] + small[1] + small[2] + small[3]
    start = 0
    for line, out in zip((0, 0, 0, 8, 9), flat):
        start = 0 if line else start
        out[...] = total[line, start : start + out.shape[0]]
        start += out.shape[0]
    result_w[...] = result[...].astype(F32)
    tokens_w[...] = tokens[...].astype(F32)
    query_w[...] = w_in[...].astype(F32)
    key_w[...] = w_kv[:, : key_w.shape[1]].astype(F32)
    value_w[...] = w_kv[:, key_w.shape[1] :].astype(F32)
    out_w[...] = w_out[...].astype(F32)
    gate_w[...] = gate_up[0, :, : gate_w.shape[1]].astype(F32)
    up_w[...] = gate_up[1, :, : up_w.shape[1]].astype(F32)
    down_w[...] = down[...].astype(F32)


def on_device(
    tokens,
    cotangent,
    lengths,
    gain_attn,
    w_query,
    key_projection,
    value_projection,
    bias_query,
    key_bias_vector,
    value_bias_vector,
    w_out,
    gain_ffn,
    w_gate,
    w_up,
    w_down,
):
    half_rows, piece = tokens.shape
    width = 4 * piece
    rows = half_rows // 4
    q_width = w_query.shape[1]
    kv_width = key_projection.shape[1]
    heads = q_width // HEAD_SIZE
    hidden = w_gate.shape[1]
    share = -(-hidden // (4 * LANES)) * LANES

    in_width = q_width + 2 * kv_width
    thin = piece // 2
    (
        tok_rows,
        cot_full,
        gains4,
        normed,
        query,
        kv_a,
        kv_b,
        logs,
        attended,
        tables,
        middle,
        mask_a,
        mask_b,
        normed_ffn,
        w_in_full,
        w_out_full,
        w_gu_full,
        w_down_full,
    ) = talk(
        front_kernel,
        0,
        FRONT_COPIES,
        FRONT_LOCAL,
        [
            ((2 * rows, width), BF16),
            ((4, 2 * rows, width), BF16),
            ((4, 8, piece), F32),
            ((2 * rows, width), BF16),
            ((2 * rows, q_width), BF16),
            ((half_rows, 2 * kv_width), BF16),
            ((2 * half_rows, 2 * kv_width), BF16),
            ((2 * heads, 8, rows), F32),
            ((2 * rows, q_width), BF16),
            ((2, 2 * rows, HEAD_SIZE), F32),
            ((2 * rows, width), F32),
            ((half_rows, rows), F32),
            ((2 * half_rows, rows), F32),
            ((2 * rows, width), BF16),
            ((4, piece, in_width), BF16),
            ((q_width, width), BF16),
            ((4, 2, thin, 2 * share), BF16),
            ((share, width), BF16),
        ],
        [ANY] * 2 + [VMEM] * 6 + [ANY] * 7,
        [ANY] * 3 + [VMEM] * 2 + [ANY] * 2 + [VMEM] * 7 + [ANY] * 4,
        [
            pltpu.VMEM((8, LANES), jnp.int32),
            pltpu.VMEM((8, piece), F32),
            pltpu.VMEM((2 * rows, width), BF16),
            pltpu.VMEM((2, 8, LANES), jnp.int32),
            pltpu.VMEM((4, 8, piece), F32),
            pltpu.VMEM((4, piece, in_width), BF16),
            pltpu.VMEM((q_width, width), BF16),
            pltpu.VMEM((2, thin, 2 * share), BF16),
            pltpu.VMEM((share, piece), BF16),
            pltpu.VMEM((thin, LANES), BF16),
            pltpu.VMEM((LANES, piece), BF16),
            pltpu.VMEM((2 * rows, 2 * kv_width), BF16),
            pltpu.VMEM((half_rows, 2 * kv_width), BF16),
            pltpu.VMEM((2 * half_rows, 2 * kv_width), BF16),
            pltpu.VMEM((rows, half_rows), F32),
            pltpu.VMEM((rows, 2 * half_rows), F32),
            pltpu.VMEM((2 * rows, width), BF16),
            pltpu.VMEM((2 * rows, width), BF16),
        ],
        limit=56,
    )(
        tokens,
        cotangent,
        lengths,
        gain_attn,
        gain_ffn,
        bias_query,
        key_bias_vector,
        value_bias_vector,
        w_query,
        key_projection,
        value_projection,
        w_out,
        w_gate,
        w_up,
        w_down,
    )

    w_both_full = w_gu_full.reshape(width, 2 * share)
    half_block = (2, rows, width)
    grad_normed_ffn, both_sum, both_late, down_half, result_sum, result_ahead = talk(
        ffn_kernel,
        4,
        44,
        15,
        [
            ((2 * rows, width), F32),
            ((2 * piece // 3, share), BF16),
            ((4, piece // 3, share), BF16),
            ((4, share // 2, piece), BF16),
            ((2 * rows, width), BF16),
            ((2, rows, width), BF16),
        ],
        [ANY] * 4,
        [VMEM, VMEM, ANY, ANY, VMEM, VMEM],
        [
            pltpu.VMEM(shape, BF16)
            for shape in (
                (8 * rows, width),
                (8 * rows, width),
                (width, 2 * share),
                (share, width),
                (8 * rows, 2 * share),
                (8 * rows, share),
                (8 * rows, width),
                (width, 8 * rows),
                (8 * rows, width),
                (4, piece, share),
                (4, share // 2, piece),
                (2, rows // 2, width),
                (2, rows // 2, width),
                half_block,
                half_block,
                half_block,
                (2, rows // 2, width),
                (2, rows // 2, width),
                half_block,
                (rows, width),
                (rows, width),
                (rows, width),
                (rows, width),
                (2, piece // 6, share),
                (2, piece // 6, share),
                (2, piece // 3, share),
                (2, piece // 3, share),
            )
        ],
        limit=60,
    )(normed_ffn, cot_full, w_both_full, w_down_full)
    thirds = piece // 3
    q_half, w_half = (thin, q_width), (q_width // 2, piece)
    gu_chunk, dn_chunk = (3, thirds, share), (share // 2, piece)

    def halved(shape):
        return (*shape[:-2], shape[-2] // 2, shape[-1])

    def weight_scratch(shape):
        return [
            (4, 2 * shape[0], shape[1]),
            (4, *shape),
            halved(shape),
            halved(shape),
            shape,
            shape,
            shape,
            shape,
            (3, shape[0] // 4, shape[1]),
        ]

    def scratch(kind, *shapes):
        return [pltpu.VMEM(shape, kind) for shape in shapes]

    gate_up, down_all, in_total, kv_total, out_total, grad_tokens, result, small_all = talk(
        back_kernel,
        8,
        BACK_COPIES,
        BACK_LOCAL,
        [
            ((2, piece, 4 * share), BF16),
            ((4 * share, piece), BF16),
            ((piece, q_width), BF16),
            ((piece, 2 * kv_width), BF16),
            ((q_width, piece), BF16),
            ((half_rows, piece), BF16),
            ((half_rows, piece), BF16),
            ((4, 16, in_width), F32),
        ],
        [VMEM, ANY, ANY, VMEM] + [ANY] * 5 + [VMEM, ANY, VMEM] + [ANY] * 9,
        [ANY] * 8,
        scratch(F32, (2 * rows, width))
        + scratch(
            BF16,
            (2 * rows, width),
            (2 * rows, width),
            (2 * rows, width),
            (2 * rows, q_width),
            (half_rows, 2 * kv_width),
            (2 * half_rows, 2 * kv_width),
            (2 * rows, q_width),
        )
        + scratch(F32, (half_rows, rows), (2 * half_rows, rows))
        + scratch(
            BF16,
            (4, piece, in_width),
            (q_width, width),
            (2 * thirds, share),
            (4, thirds, share),
            (4, share // 2, piece),
            (2 * rows, width),
        )
        + scratch(F32, (8, width), (2 * rows, width))
        + scratch(BF16, (2 * rows, width), (2 * rows, q_width), (width, 2 * rows), (HEAD_SIZE, 2 * half_rows))
        + scratch(F32, (half_rows, 2 * kv_width), (2 * half_rows, 2 * kv_width))
        + scratch(
            BF16,
            (half_rows, 2 * kv_width),
            (2, half_rows, 2 * kv_width),
            (3, 2, rows, 2 * kv_width),
            (4, rows, 2 * kv_width),
            (2 * rows, in_width),
            (2 * rows, width),
            (rows, width),
            (rows, width),
            (rows, width),
            (rows, width),
            gu_chunk,
            gu_chunk,
            halved((thirds, share)),
            halved((thirds, share)),
            (thirds, share),
            (thirds, share),
            (thirds, share),
            halved(dn_chunk),
            halved(dn_chunk),
            dn_chunk,
            dn_chunk,
            dn_chunk,
            dn_chunk,
            dn_chunk,
            *weight_scratch(q_half),
            *weight_scratch((thin, 2 * kv_width)),
            *weight_scratch(w_half),
            (2, rows, width),
            (2 * rows, width),
        )
        + scratch(F32, (8, in_width), (4, 8, piece), (4, 8, in_width), (8, 8, piece))
        + scratch(F32, *[(16, in_width)] * 4),
        limit=60,
    )(
        grad_normed_ffn,
        middle,
        cot_full,
        gains4,
        tok_rows,
        normed,
        query,
        kv_a,
        kv_b,
        logs,
        attended,
        tables,
        mask_a,
        mask_b,
        w_in_full,
        w_out_full,
        both_sum,
        both_late,
        down_half,
        result_sum,
        result_ahead,
    )
    steps = 8
    narrow = [gate_up, down_all, in_total, kv_total, out_total, result, grad_tokens, small_all]
    lines = [(q_width,), (kv_width,), (kv_width,), (piece,), (piece,)]
    wide = [
        (half_rows, piece),
        (half_rows, piece),
        (piece, q_width),
        (piece, kv_width),
        (piece, kv_width),
        (q_width, piece),
        (piece, hidden),
        (piece, hidden),
        (hidden, piece),
    ]

    def in_block(array):
        if array is small_all:
            return pl.BlockSpec(array.shape, lambda i: (0, 0, 0))
        if array.ndim == 3:
            return pl.BlockSpec((2, array.shape[1] // steps, array.shape[2]), lambda i: (0, i, 0))
        if array is down_all:
            return pl.BlockSpec((hidden // steps, piece), lambda i: (i, 0))
        return pl.BlockSpec((array.shape[0] // steps, array.shape[1]), lambda i: (i, 0))

    wide_out = pl.pallas_call(
        widen_kernel,
        grid=(steps,),
        out_shape=[jax.ShapeDtypeStruct(shape, F32) for shape in wide + lines],
        in_specs=[in_block(array) for array in narrow],
        out_specs=[pl.BlockSpec((shape[0] // steps, shape[1]), lambda i: (i, 0)) for shape in wide]
        + [pl.BlockSpec(shape, lambda i: (0,)) for shape in lines],
        compiler_params=pltpu.CompilerParams(vmem_limit_bytes=60 << 20),
    )(*narrow)
    result_w, tokens_w, query_w, key_w, value_w, out_w, gate_w, up_w, down_w, *flat = wide_out
    bias_q, bias_k, bias_v, gain_one, gain_two = flat
    return (
        result_w,
        tokens_w,
        gain_one,
        query_w,
        key_w,
        value_w,
        bias_q,
        bias_k,
        bias_v,
        out_w,
        gain_two,
        gate_w,
        up_w,
        down_w,
    )


def solution(mesh):
    placed = (
        P(("dp", "col"), "row"),
        P(("dp", "col"), "row"),
        P("dp", None),
        P("row"),
        P("row", "col"),
        P("row", "col"),
        P("row", "col"),
        P("col"),
        P("col"),
        P("col"),
        P("col", "row"),
        P("row"),
        P("row", "col"),
        P("row", "col"),
        P("col", "row"),
    )
    return jax.shard_map(
        on_device,
        mesh=mesh,
        in_specs=placed,
        out_specs=(
            P(("dp", "col"), "row"),
            P(("dp", "col"), "row"),
            P("row"),
            P("row", "col"),
            P("row", "col"),
            P("row", "col"),
            P("col"),
            P("col"),
            P("col"),
            P("col", "row"),
            P("row"),
            P("row", "col"),
            P("row", "col"),
            P("col", "row"),
        ),
        check_vma=False,
    )
```

```python
import math

import jax
import jax.numpy as jnp
from jax import lax
from jax.experimental import pallas as pl
from jax.experimental.pallas import tpu as pltpu
from jax.sharding import PartitionSpec as P

HEAD_SIZE = 128
EPS = 1e-06
THETA = 1000000.0
LANES = 128
MESH = pl.DeviceIdType.MESH
BF16 = jnp.bfloat16
F32 = jnp.float32
ANY = pl.BlockSpec(memory_space=pl.ANY)
VMEM = pl.BlockSpec(memory_space=pltpu.VMEM)

Z_STEP = 4
FRONT_COPIES = 77
FRONT_LOCAL = 27
BACK_COPIES = 145
BACK_LOCAL = 28


def here():
    return lax.axis_index("dp"), lax.axis_index("row"), lax.axis_index("col")


def flip_near(dp):
    return dp + 2 - 4 * ((dp // 2) % 2)


def pair_of(place, row=None):
    dp, own, col = place
    return flip_near(dp), own if row is None else row, 1 - col


def near_of(place, row=None):
    dp, own, col = place
    return flip_near(dp), own if row is None else row, col


def twin_of(place):
    dp, row, col = place
    return dp + 1 - 2 * (dp % 2), row, col


def along_z(place, step):
    dp, row, col = place
    return (dp + Z_STEP * step) % (4 * Z_STEP), row, col


def along_y(place, step):
    dp, row, col = place
    return dp, (row + step) % 4, col


def meet(peers):
    barrier = pltpu.get_barrier_semaphore()
    for peer in peers:
        pl.semaphore_signal(barrier, inc=1, device_id=peer, device_id_type=MESH)
    pl.semaphore_wait(barrier, len(peers))


class Mail:
    def __init__(self, send, recv):
        self.send, self.recv, self.count, self.sent = send, recv, 0, []

    def post(self, source, target, device):
        index = self.count
        self.count += 1
        copy = pltpu.make_async_remote_copy(
            src_ref=source,
            dst_ref=target,
            send_sem=self.send.at[index],
            recv_sem=self.recv.at[index],
            device_id=device,
            device_id_type=MESH,
        )
        copy.start()
        self.sent.append(copy)
        return copy

    def finish(self):
        assert self.count == self.send.shape[0], (self.count, self.send.shape)
        for copy in self.sent:
            copy.wait_send()


def talk(body, ident, copies, local, outs, in_specs, out_specs, scratch=(), limit=32):
    return pl.pallas_call(
        body,
        out_shape=[jax.ShapeDtypeStruct(*out) for out in outs],
        in_specs=in_specs,
        out_specs=out_specs,
        scratch_shapes=[
            *scratch,
            pltpu.SemaphoreType.DMA((copies,)),
            pltpu.SemaphoreType.DMA((copies,)),
            pltpu.SemaphoreType.DMA((max(local, 1),)),
        ],
        compiler_params=pltpu.CompilerParams(
            collective_id=ident, has_side_effects=True, vmem_limit_bytes=limit << 20
        ),
    )


def front_kernel(
    tok,
    cot,
    lens_in,
    gain_attn,
    gain_ffn,
    bias_q,
    bias_k,
    bias_v,
    wq,
    wk,
    wv,
    wo,
    wg,
    wu,
    wd,
    tok_out,
    cot_full,
    gains_out,
    normed,
    query,
    kva_out,
    kvb_out,
    logs,
    attended,
    tables,
    middle,
    turned_a,
    turned_b,
    normed_ffn,
    w_in_out,
    w_out_out,
    wgu_full,
    wd_full,
    lens,
    gains,
    tok_v,
    lens_v,
    gains_v,
    w_in,
    w_out,
    gu_own,
    wd_own,
    blank_gu,
    blank_wd,
    kv,
    kva,
    kvb,
    bias_a,
    bias_b,
    branch,
    branch_in,
    send,
    recv,
    local,
):
    place = here()
    dp, row, col = place
    z, core = dp // Z_STEP, dp % 2
    twin, pair, up, down = twin_of(place), pair_of(place), along_z(place, 1), along_z(place, 3)
    right, left, near = along_y(place, 1), along_y(place, 3), near_of(place)
    meet(
        [along_y(place, s) for s in (1, 2, 3)]
        + [near_of(place, (row + s) % 4) for s in range(4)]
        + [pair, twin, up, down]
    )
    mail = Mail(send, recv)
    kept = []

    def keep(source, target):
        kept.append(pltpu.make_async_copy(source, target, local.at[len(kept)]))
        kept[-1].start()
        return len(kept) - 1

    def kept_wait(index):
        kept[index].wait()
        kept[index] = None

    def even(start, size):
        return pl.ds(pl.multiple_of(start, 16), size)

    rows, piece = tok.shape[0] // 4, tok.shape[1]
    width = 4 * piece
    own_rows = even(col * rows, rows)
    spot = even(row * rows, rows)

    def spread(source, target):
        got = []
        for step in range(4):
            part = source.at[even(((row + step) % 4) * rows, rows), :]
            lanes = pl.ds(((4 - step) % 4) * piece, piece)
            if step:
                got.append(mail.post(part, target.at[own_rows, lanes], along_y(place, step)))
            else:
                mine = keep(part, target.at[own_rows, lanes])
        return got, mine

    tokens = spread(tok, tok_v)
    lens[...] = jnp.zeros_like(lens)
    lens[0:1, 0 : lens_in.shape[1]] = lens_in[...]
    gains[...] = jnp.zeros_like(gains)
    gains[0:1, :] = gain_attn[...].reshape(1, piece)
    gains[1:2, :] = gain_ffn[...].reshape(1, piece)
    lens_got = mail.post(lens, lens_v.at[col], pair)
    lens_kept = keep(lens, lens_v.at[col])
    gains_kept = keep(gains, gains_v.at[0])
    gains_got = [mail.post(gains, gains_v.at[4 - s], along_y(place, s)) for s in (1, 2, 3)]

    q_width, kv_width = wq.shape[1], wk.shape[1]
    stages = [
        keep(wq, w_in.at[0, :, pl.ds(0, q_width)]),
        keep(wk, w_in.at[0, :, pl.ds(q_width, kv_width)]),
        keep(wv, w_in.at[0, :, pl.ds(q_width + kv_width, kv_width)]),
        keep(wo, w_out.at[:, pl.ds(0, piece)]),
    ]
    share = wd_own.shape[0]
    thin = piece // 2
    sure = share - LANES
    take = pl.multiple_of(z * share, LANES)
    big = []
    for k in range(2):
        for i, source in enumerate((wg, wu)):
            from_rows = pl.ds(k * thin, thin)
            big.append(keep(source.at[from_rows, pl.ds(take, sure)], gu_own.at[k, :, pl.ds(i * share, sure)]))
    big.append(keep(wd.at[pl.ds(take, sure), :], wd_own.at[pl.ds(0, sure), :]))
    blank_gu[...] = jnp.zeros_like(blank_gu)
    blank_wd[...] = jnp.zeros_like(blank_wd)
    first_edge = len(kept)
    edges = []
    for k in range(2):
        for i, source in enumerate((wg, wu)):
            target = gu_own.at[k, :, pl.ds(i * share + sure, LANES)]
            edges.append((source, pl.ds(k * thin, thin), None, target, blank_gu))
    edges.append((wd, None, slice(None), wd_own.at[pl.ds(sure, LANES), :], blank_wd))

    def edge(index, last):
        source, from_rows, _, target, blank = edges[index]
        if last:
            origin = blank
        elif from_rows is None:
            origin = source.at[pl.ds(pl.multiple_of(take + sure, LANES), LANES), :]
        else:
            origin = source.at[from_rows, pl.ds(pl.multiple_of(take + sure, LANES), LANES)]
        return pltpu.make_async_copy(origin, target, local.at[first_edge + index])

    @pl.when(z < 3)
    def _():
        for index in range(len(edges)):
            edge(index, False).start()

    @pl.when(z == 3)
    def _():
        for index in range(len(edges)):
            edge(index, True).start()

    for index in range(len(edges)):
        kept.append(edge(index, True))
        big.append(first_edge + index)

    q_rows, o_rows = thin // 4, w_out.shape[0] // 8

    def in_part(j, owner_z):
        return w_in.at[j, even(core * thin + owner_z * q_rows, q_rows), :]

    def in_parts(owner_z):
        return w_in.at[pl.ds(1, 3), even(core * thin + owner_z * q_rows, q_rows), :]

    def in_side(owner_z, side):
        lanes = pl.ds(side * (w_in.shape[2] // 2), w_in.shape[2] // 2)
        return w_in.at[pl.ds(1, 3), even(core * thin + owner_z * q_rows, q_rows), lanes]

    def out_part(j, owner_z):
        return w_out.at[even(core * 4 * o_rows + owner_z * o_rows, o_rows), pl.ds(j * piece, piece)]

    def out_parts(owner_z):
        return w_out.at[even(core * 4 * o_rows + owner_z * o_rows, o_rows), pl.ds(piece, 3 * piece)]

    def out_side(owner_z, side):
        start = core * 4 * o_rows + owner_z * o_rows + side * (o_rows // 2)
        return w_out.at[even(start, o_rows // 2), pl.ds(piece, 3 * piece)]

    for index in stages:
        kept_wait(index)
    in_got = [mail.post(in_part(0, z), in_part(4 - step, z), along_y(place, step)) for step in (1, 3, 2)]

    def to_pair(spreading, target):
        got, mine = spreading
        kept_wait(mine)
        for copy in got:
            copy.wait_recv()
        return mail.post(target.at[own_rows, :], target.at[own_rows, :], pair)

    tokens_pair = to_pair(tokens, tok_v)
    shares = []

    def give(part):
        shares.append(mail.post(part, part, twin))

    def z_first(side):
        copies = {}
        for turn in range(2):
            copies["u", turn] = mail.post(side(z, turn), side(z, turn), up)
            copies["d", 1 - turn] = mail.post(side(z, 1 - turn), side(z, 1 - turn), down)
        return copies

    below, above, across = (z + 3) % 4, (z + 1) % 4, (z + 2) % 4

    def z_second(side, whole, copies):
        copies["u", 0].wait_recv()
        far_up = mail.post(side(below, 0), side(below, 0), up)
        copies["d", 1].wait_recv()
        far_down = mail.post(side(above, 1), side(above, 1), down)
        copies["u", 1].wait_recv()
        give(whole(below))
        copies["d", 0].wait_recv()
        give(whole(above))
        return far_up, far_down

    def z_third(whole, copies):
        for copy in copies:
            copy.wait_recv()
        give(whole(across))

    for copy in in_got:
        copy.wait_recv()
    in_z = z_first(in_side)
    give(in_parts(z))
    out_got = [mail.post(out_part(0, z), out_part(4 - step, z), along_y(place, step)) for step in (1, 3, 2)]
    cotangents = spread(cot, cot_full.at[0])
    for index in big:
        kept_wait(index)
    x_lo = (dp // 2) % 2
    gu_half, wd_half = thin // 4, share // 4

    def gu_part(j, which=None, owner=x_lo):
        start, size = (0, 2 * gu_half) if which is None else (which * gu_half, gu_half)
        return wgu_full.at[j, core, even(owner * 2 * gu_half + start, size), :]

    def gu_whole(j):
        return wgu_full.at[j, core]

    def wd_part(j, which=None):
        start, size = (0, 2 * wd_half) if which is None else (which * wd_half, wd_half)
        return wd_full.at[even(core * 2 * wd_half + start, size), pl.ds(j * piece, piece)]

    def gu_source(which):
        return gu_own.at[core, even((x_lo * 2 + which) * gu_half, gu_half), :]

    def wd_source(which):
        return wd_own.at[even((core * 2 + which) * wd_half, wd_half), :]

    y_ring, near_gu, twins = {}, [], []

    def y_start(name, source, part):
        for turn in range(2):
            y_ring[name, "r", turn] = mail.post(source(turn), part(3, turn), right)
            y_ring[name, "l", 1 - turn] = mail.post(source(1 - turn), part(1, 1 - turn), left)

    def y_forward(name, part):
        y_ring[name, "r", 0].wait_recv()
        y_ring[name, "fr"] = mail.post(part(3, 0), part(2, 0), right)
        y_ring[name, "l", 1].wait_recv()
        y_ring[name, "fl"] = mail.post(part(1, 1), part(2, 1), left)

    def y_share(name, part, queue, device):
        y_ring[name, "r", 1].wait_recv()
        queue.append(mail.post(part(3), part(3), device))
        y_ring[name, "l", 0].wait_recv()
        queue.append(mail.post(part(1), part(1), device))

    def y_end(name, part, queue, device):
        y_ring[name, "fr"].wait_recv()
        y_ring[name, "fl"].wait_recv()
        queue.append(mail.post(part(2), part(2), device))


    kept_wait(lens_kept)
    lens_got.wait_recv()
    half_rows = 4 * rows

    def segment_of(which, index):
        end_0 = lens_v[which, 0:1, 0:1]
        end_1 = end_0 + lens_v[which, 0:1, 1:2]
        past_0 = (index >= end_0).astype(jnp.int32)
        past_1 = (index >= end_1).astype(jnp.int32)
        start = jnp.where(past_1 > 0, end_1, jnp.where(past_0 > 0, end_0, 0))
        return past_0 + past_1, start

    lane = lax.broadcasted_iota(jnp.int32, (rows, HEAD_SIZE), 1)
    half_lane = jnp.where(lane >= HEAD_SIZE // 2, lane - HEAD_SIZE // 2, lane).astype(F32)
    inverse = jnp.exp(half_lane * (-2.0 * math.log(THETA) / HEAD_SIZE))
    for which, mask, mask_t, key_count in ((0, bias_a, turned_a, half_rows), (1, bias_b, turned_b, 2 * half_rows)):
        index = lax.broadcasted_iota(jnp.int32, (rows, HEAD_SIZE), 0) + (row * rows + which * half_rows)
        _, start = segment_of(which, index)
        turn = (index - start).astype(F32) * inverse
        tables[0, which * rows : (which + 1) * rows, :] = jnp.cos(turn)
        sine = jnp.sin(turn)
        tables[1, which * rows : (which + 1) * rows, :] = jnp.where(lane >= HEAD_SIZE // 2, sine, -sine)
        at = lax.broadcasted_iota(jnp.int32, (rows, key_count), 0) + (row * rows + which * half_rows)
        keys = lax.broadcasted_iota(jnp.int32, (rows, key_count), 1)
        allowed = jnp.logical_and(segment_of(which, at)[0] == segment_of(which, keys)[0], keys <= at)
        mask[...] = jnp.where(allowed, 0.0, -1e30)
        at = lax.broadcasted_iota(jnp.int32, (key_count, rows), 1) + (row * rows + which * half_rows)
        keys = lax.broadcasted_iota(jnp.int32, (key_count, rows), 0)
        allowed = jnp.logical_and(segment_of(which, at)[0] == segment_of(which, keys)[0], keys <= at)
        mask_t[...] = jnp.where(allowed, 0.0, -1e30)

    kept_wait(gains_kept)
    for copy in gains_got:
        copy.wait_recv()
    keep(gains_v, gains_out)

    def normalise(value, which):
        scale = lax.rsqrt(jnp.sum(value * value, -1, keepdims=True) * (1.0 / width) + EPS)
        return [
            (value[:, j * piece : (j + 1) * piece] * scale * gains_v[j, which : which + 1, :]).astype(BF16)
            for j in range(4)
        ]

    def norm_rows(which):
        part = pl.ds(pl.multiple_of(which * rows, rows), rows)
        for j, block in enumerate(normalise(tok_v[part, :].astype(F32), 0)):
            normed[part, pl.ds(j * piece, piece)] = block

    norm_rows(col)
    for copy in out_got:
        copy.wait_recv()
    give(out_parts(z))
    y_start("gu", gu_source, gu_part)
    keep(gu_own, wgu_full.at[0])
    keep(wd_own, wd_full.at[:, pl.ds(0, piece)])
    in_far = z_second(in_side, in_parts, in_z)
    out_z = z_first(out_side)
    tokens_pair.wait_recv()
    keep(tok_v, tok_out)
    norm_rows(1 - col)
    cot_pair = to_pair(cotangents, cot_full.at[0])
    z_third(in_parts, in_far)
    for copy in shares:
        copy.wait_recv()
    shares.clear()
    keep(w_in, w_in_out)

    in_width = w_in.shape[2]

    def project(lanes, bias):
        weights = w_in[:, :, lanes]
        weights = weights.reshape(4 * weights.shape[1], weights.shape[2])
        return jnp.dot(normed[...], weights, preferred_element_type=F32) + bias

    def rotate(value):
        return value * tables[0] + pltpu.roll(value, HEAD_SIZE // 2, 1) * tables[1]

    key_value = project(slice(q_width, in_width), jnp.concatenate([bias_k[...].reshape(1, kv_width), bias_v[...].reshape(1, kv_width)], 1))
    kv[:, 0:kv_width] = rotate(key_value[:, 0:kv_width]).astype(BF16)
    kv[:, kv_width : 2 * kv_width] = key_value[:, kv_width : 2 * kv_width].astype(BF16)
    a_rows, b_rows = pl.ds(0, rows), pl.ds(rows, rows)
    high_spot = even(half_rows + row * rows, rows)
    a_got, b_got = [], []
    for step in (1, 2, 3):
        a_got.append(mail.post(kv.at[a_rows, :], kva.at[spot, :], along_y(place, step)))
    for step in range(4):
        b_got.append(mail.post(kv.at[a_rows, :], kvb.at[spot, :], near_of(place, (row + step) % 4)))
        if step:
            b_got.append(mail.post(kv.at[b_rows, :], kvb.at[high_spot, :], along_y(place, step)))
    kva[spot, :] = kv[a_rows, :]
    kvb[high_spot, :] = kv[b_rows, :]
    for first in range(0, q_width, 2 * HEAD_SIZE):
        value = project(slice(first, first + 2 * HEAD_SIZE), bias_q[first : first + 2 * HEAD_SIZE].reshape(1, 2 * HEAD_SIZE))
        for i in range(2):
            lanes = slice(first + i * HEAD_SIZE, first + (i + 1) * HEAD_SIZE)
            query[:, lanes] = rotate(value[:, i * HEAD_SIZE : (i + 1) * HEAD_SIZE]).astype(BF16)

    y_forward("gu", gu_part)
    y_share("gu", gu_part, near_gu, near)
    out_far = z_second(out_side, out_parts, out_z)
    heads = q_width // HEAD_SIZE
    factor = HEAD_SIZE ** (-0.5)

    def attend(half, keys, mask):
        part = slice(half * rows, (half + 1) * rows)

        @pl.loop(0, heads)
        def _(h):
            lanes = pl.ds(pl.multiple_of(h * HEAD_SIZE, LANES), HEAD_SIZE)
            raw = lax.dot_general(
                query[part, lanes], keys[:, 0:HEAD_SIZE], (((1,), (1,)), ((), ())), preferred_element_type=F32
            )
            scores = raw * factor + mask[...]
            peak = jnp.max(scores, -1, keepdims=True)
            raised = jnp.exp(scores - peak)
            total = jnp.sum(raised, -1, keepdims=True)
            probs = (raised * (1.0 / total)).astype(BF16)
            out = jnp.dot(probs, keys[:, HEAD_SIZE : 2 * HEAD_SIZE], preferred_element_type=F32)
            attended[part, lanes] = out.astype(BF16)
            logs[half * heads + h] = jnp.broadcast_to(peak + jnp.log(total), (rows, LANES)).T[0:8, :]

        for first in range(0, width, piece):
            lanes = slice(first, first + piece)
            branch[part, lanes] = jnp.dot(
                attended[part, :], w_out[:, lanes], preferred_element_type=F32
            ).astype(BF16)
        return mail.post(branch.at[part, :], branch_in.at[part, :], pair)

    def finish_half(half, copy):
        part = slice(half * rows, (half + 1) * rows)
        copy.wait_recv()
        value = tok_v[part, :].astype(F32) + (branch[part, :].astype(F32) + branch_in[part, :].astype(F32))
        middle[part, :] = value
        for j, block in enumerate(normalise(value, 1)):
            normed_ffn[part, j * piece : (j + 1) * piece] = block

    def z_part(slot, half):
        return cot_full.at[slot, pl.ds(half * rows, rows), :]

    def z_send():
        copies = {}
        for turn in range(2):
            copies["u", turn] = mail.post(z_part(0, turn), z_part(1, turn), up)
            copies["d", 1 - turn] = mail.post(z_part(0, 1 - turn), z_part(3, 1 - turn), down)
        return copies

    def z_forward(copies):
        copies["u", 0].wait_recv()
        far_up = mail.post(z_part(1, 0), z_part(2, 0), up)
        copies["d", 1].wait_recv()
        far_down = mail.post(z_part(3, 1), z_part(2, 1), down)
        return [copies["u", 1], copies["d", 0], far_up, far_down]

    cot_pair.wait_recv()
    cot_z = z_send()
    for copy in a_got:
        copy.wait_recv()
    keep(kva, kva_out)
    z_third(out_parts, out_far)
    for copy in shares:
        copy.wait_recv()
    keep(w_out, w_out_out)
    swap_a = attend(0, kva, bias_a)
    for copy in b_got:
        copy.wait_recv()
    keep(kvb, kvb_out)
    y_start("wd", wd_source, wd_part)
    swap_b = attend(1, kvb, bias_b)
    y_end("gu", gu_part, near_gu, near)
    finish_half(0, swap_a)
    y_forward("wd", wd_part)
    cot_last = z_forward(cot_z)
    y_share("wd", wd_part, twins, twin)
    finish_half(1, swap_b)
    for j, copy in zip((3, 1, 2), near_gu):
        copy.wait_recv()
        twins.append(mail.post(gu_whole(j), gu_whole(j), twin))
    y_end("wd", wd_part, twins, twin)
    for copy in cot_last:
        copy.wait_recv()
    for copy in twins:
        copy.wait_recv()
    for copy in kept:
        if copy is not None:
            copy.wait()
    mail.finish()


def ffn_kernel(
    normed,
    cot,
    wgu,
    wd,
    total,
    gu_sum,
    gu_late,
    dn_half,
    result_sum,
    result_ahead,
    x,
    cot_v,
    wgu_v,
    wd_v,
    gb,
    act,
    parts,
    turned,
    down_v,
    gu_in,
    dn_in,
    up1,
    down1,
    up2,
    down2,
    other,
    stage_up,
    stage_down,
    stage,
    res_up1,
    res_down1,
    res_up2,
    res_down2,
    gu_up1,
    gu_down1,
    gu_up2,
    gu_down2,
    send,
    recv,
    local,
):
    place = here()
    dp, row, col = place
    core = dp % 2
    up, down, pair, twin = along_z(place, 1), along_z(place, 3), pair_of(place), twin_of(place)
    right, left = along_y(place, 1), along_y(place, 3)
    meet([up, down, pair, twin, right, left])
    mail = Mail(send, recv)
    order = ((0, 0), (0, 1), (1, 0), (3, 1), (2, 0), (2, 1), (1, 1), (3, 0))
    spots = {half: i for i, half in enumerate(order)}
    rows = normed.shape[0] // 2
    size = rows // 2

    def block(ref, slot, half):
        return ref.at[pl.ds(spots[slot, half] * rows, rows), :]

    def halves(ref, half):
        return ref.at[pl.ds(half * rows, rows), :]

    kept = []

    def keep(source, target):
        kept.append(pltpu.make_async_copy(source, target, local.at[len(kept)]))
        kept[-1].start()
        return len(kept) - 1

    def kept_wait(index):
        kept[index].wait()
        kept[index] = None

    got = {}

    def z_start(which):
        got["u", which] = mail.post(halves(normed, which), block(x, 1, which), up)
        got["d", 1 - which] = mail.post(halves(normed, 1 - which), block(x, 3, 1 - which), down)

    z_start(0)
    share = wd.shape[0]
    early = [keep(normed, x.at[pl.ds(0, 2 * rows), :]), keep(wgu, wgu_v)]
    early.append(keep(cot.at[0], cot_v.at[pl.ds(0, 2 * rows), :]))
    early.append(keep(wd, wd_v))
    later = [keep(cot.at[slot, pl.ds(half * rows, rows), :], block(cot_v, slot, half)) for slot, half in order[2:]]
    width = normed.shape[1]
    piece = width // 4

    def dot_nt(left, right):
        return lax.dot_general(left, right, (((1,), (1,)), ((), ())), preferred_element_type=F32)

    def compute(c):
        part = slice(2 * rows * c, 2 * rows * (c + 1))
        for start, size in ((0, 512), (512, share - 512)):
            lanes, above = slice(start, start + size), slice(share + start, share + start + size)
            gate = jnp.dot(x[part, :], wgu_v[:, lanes], preferred_element_type=F32)
            value = jnp.dot(x[part, :], wgu_v[:, above], preferred_element_type=F32)
            grad = dot_nt(cot_v[part, :], wd_v[lanes, :])
            spread = 1.0 / (1.0 + jnp.exp(-gate))
            smooth = gate * spread
            act[part, lanes] = (smooth * value).astype(BF16)
            gb[part, lanes] = (grad * value * (spread * (1.0 + gate * (1.0 - spread)))).astype(BF16)
            gb[part, above] = (grad * smooth).astype(BF16)
        for m in range(3):
            lanes = slice(512 * m, 512 * (m + 1))
            parts[part, lanes] = dot_nt(gb[part, :], wgu_v[lanes, :]).astype(BF16)

    for index in early:
        kept_wait(index)
    compute(0)
    got["u", 0].wait_recv()
    far_up = mail.post(block(x, 1, 0), block(x, 2, 0), up)
    got["d", 1].wait_recv()
    far_down = mail.post(block(x, 3, 1), block(x, 2, 1), down)
    for index in later:
        kept_wait(index)
    compute(1)
    z_start(1)
    far_up.wait_recv()
    far_down.wait_recv()
    compute(2)
    first = {}
    for i in range(2):
        rows_i = pl.ds(i * size, size)
        first["u", i] = mail.post(block(parts, 2, 0).at[rows_i, :], up1.at[i], up)
        first["d", i] = mail.post(block(parts, 2, 1).at[rows_i, :], down1.at[i], down)
    got["u", 1].wait_recv()
    got["d", 0].wait_recv()
    compute(3)
    second = {
        ("d", 0): mail.post(block(parts, 1, 0), down2.at[0], down),
        ("u", 1): mail.post(block(parts, 3, 1), up2.at[1], up),
    }

    def turn_over(source, target):
        @pl.loop(0, source.shape[1] // LANES)
        def _(t):
            lanes = pl.ds(pl.multiple_of(t * LANES, LANES), LANES)
            target[lanes, :] = source[:, lanes].T

    def forward(i):
        rows_i = pl.ds(i * size, size)
        first["u", i].wait_recv()
        stage_up[i] = (block(parts, 3, 0).at[rows_i, :][...].astype(F32) + up1[i].astype(F32)).astype(BF16)
        second["u", 0, i] = mail.post(stage_up.at[i], up2.at[0, rows_i, :], up)
        first["d", i].wait_recv()
        stage_down[i] = (block(parts, 1, 1).at[rows_i, :][...].astype(F32) + down1[i].astype(F32)).astype(BF16)
        second["d", 1, i] = mail.post(stage_down.at[i], down2.at[1, rows_i, :], down)

    turn_over(x, turned)
    tile = 256
    tiles = 2 * share // tile

    def gu_tiles(first_tile, last_tile):
        @pl.loop(first_tile, last_tile)
        def _(n):
            lanes = pl.ds(pl.multiple_of(((n + (tiles // 2) * (1 - core)) % tiles) * tile, tile), tile)
            wgu_v[:, lanes] = jnp.dot(turned[...], gb[:, lanes], preferred_element_type=F32).astype(BF16)

    swaps = {}

    def settle(i):
        rows_i = pl.ds(i * size, size)
        if i == 0:
            second["d", 0].wait_recv()
            second["u", 1].wait_recv()
        second["u", 0, i].wait_recv()
        second["d", 1, i].wait_recv()
        for half in range(2):
            value = block(parts, 0, half).at[rows_i, :][...].astype(F32)
            value = value + up2[half, rows_i, :].astype(F32) + down2[half, rows_i, :].astype(F32)
            stage[half, rows_i, :] = value.astype(BF16)
            swaps[half, i] = mail.post(stage.at[half, rows_i, :], other.at[half, rows_i, :], pair)

    there = pl.ds(pl.multiple_of((1 - core) * share, LANES), share)
    mine = pl.ds(pl.multiple_of(core * share, LANES), share)
    gu_tiles(0, tiles // 2 + 1)
    shared = [
        mail.post(wgu_v.at[pl.ds(j * piece, piece), there], gu_in.at[j], twin) for j in range(4)
    ]
    forward(0)
    forward(1)
    gu_tiles(tiles // 2 + 1, tiles)
    for j in range(4):
        shared[j].wait_recv()
        gu_in[j] = (wgu_v[pl.ds(j * piece, piece), mine].astype(F32) + gu_in[j].astype(F32)).astype(BF16)

    def ring_y(i):
        height = piece // 3
        half = height // 2
        low, high = pl.ds(i * height, half), pl.ds(i * height + half, half)
        one, two, three, four = gu_up1.at[i], gu_down1.at[i], gu_up2.at[i], gu_down2.at[i]
        begin = (mail.post(gu_in.at[2, low, :], one, right), mail.post(gu_in.at[2, high, :], two, left))
        straight = [
            mail.post(gu_in.at[1, high, :], three.at[pl.ds(half, half), :], right),
            mail.post(gu_in.at[3, low, :], four.at[pl.ds(0, half), :], left),
        ]
        yield
        begin[0].wait_recv()
        one[...] = (gu_in[1, low, :].astype(F32) + one[...].astype(F32)).astype(BF16)
        straight.append(mail.post(one, three.at[pl.ds(0, half), :], right))
        begin[1].wait_recv()
        two[...] = (gu_in[3, high, :].astype(F32) + two[...].astype(F32)).astype(BF16)
        straight.append(mail.post(two, four.at[pl.ds(half, half), :], left))
        yield
        for copy in straight:
            copy.wait_recv()
        part = pl.ds(i * height, height)
        value = gu_in[0, part, :].astype(F32) + three[...].astype(F32) + four[...].astype(F32)
        gu_sum[part, :] = value.astype(BF16)
        yield

    rings = [ring_y(i) for i in range(2)]
    keep(gu_in.at[:, pl.ds(2 * (piece // 3), piece // 3), :], gu_late)
    for ring in rings:
        next(ring)
    for m in range(3):
        lanes = slice(512 * m, 512 * (m + 1))

        @pl.loop(0, 4)
        def _(c):
            part = pl.ds(pl.multiple_of(c * 2 * rows, 2 * rows), 2 * rows)
            down_v[part, lanes] = jnp.dot(act[part, :], wd_v[:, lanes], preferred_element_type=F32).astype(BF16)

    settle(0)
    settle(1)
    result = {
        "u1": mail.post(block(down_v, 2, 0), res_up1, up),
        "d1": mail.post(block(down_v, 2, 1), res_down1, down),
        "u2": mail.post(block(down_v, 3, 1), res_up2, up),
        "d2": mail.post(block(down_v, 1, 0), res_down2, down),
    }
    turn_over(act, turned)

    @pl.loop(0, width // tile)
    def _(n):
        lanes = pl.ds(pl.multiple_of(n * tile, tile), tile)
        wd_v[:, lanes] = jnp.dot(
            turned[0:share, :], cot_v[:, lanes], preferred_element_type=F32
        ).astype(BF16)

    half_share = share // 2
    rows_there = pl.ds(pl.multiple_of((1 - core) * half_share, 16), half_share)
    rows_mine = pl.ds(pl.multiple_of(core * half_share, 16), half_share)
    shared += [
        mail.post(wd_v.at[rows_there, pl.ds(j * piece, piece)], dn_in.at[j], twin) for j in range(4)
    ]
    for ring in rings:
        next(ring)
    for j in range(4):
        shared[4 + j].wait_recv()
        dn_in[j] = (wd_v[rows_mine, pl.ds(j * piece, piece)].astype(F32) + dn_in[j].astype(F32)).astype(BF16)
        keep(dn_in.at[j], dn_half.at[j])
    for half, i in ((0, 0), (1, 0), (0, 1), (1, 1)):
        rows_i = pl.ds(i * size, size)
        swaps[half, i].wait_recv()
        total[pl.ds(half * rows + i * size, size), :] = stage[half, rows_i, :].astype(F32) + other[
            half, rows_i, :
        ].astype(F32)
    next(rings[0])
    next(rings[1])
    for copy in result.values():
        copy.wait_recv()
    result_ahead[0] = (block(down_v, 3, 0)[...].astype(F32) + res_up1[...].astype(F32)).astype(BF16)
    result_ahead[1] = (block(down_v, 1, 1)[...].astype(F32) + res_down1[...].astype(F32)).astype(BF16)
    for half, theirs in ((0, res_down2), (1, res_up2)):
        value = block(down_v, 0, half)[...].astype(F32) + theirs[...].astype(F32)
        result_sum[pl.ds(half * rows, rows), :] = value.astype(BF16)
    for copy in kept:
        if copy is not None:
            copy.wait()
    mail.finish()


def back_kernel(
    total,
    middle,
    cot,
    gains,
    tok,
    normed,
    query,
    kv_a,
    kv_b,
    logs,
    attended,
    tables,
    turned_a,
    turned_b,
    w_in,
    w_out,
    gu,
    gl,
    dn,
    result_sum,
    ahead,
    gu_out,
    dn_out,
    in_out,
    kw_out,
    wo_out,
    grad_out,
    result_out,
    small_out,
    middle_v,
    cot_v,
    tok_v,
    normed_v,
    query_v,
    kva,
    kvb,
    attended_v,
    turned_a_v,
    turned_b_v,
    w_in_v,
    w_out_v,
    gu_v,
    gl_v,
    dn_v,
    down_v,
    gain_rows,
    grad_middle,
    grad_low,
    grad_att,
    flat,
    keys_t,
    dkv_a,
    dkv_b,
    low_kv,
    own_kv,
    from_own,
    from_near,
    grad_pre,
    grad_part,
    grad_in,
    part_in,
    rows_out,
    result_rows,
    gu_n,
    gu_s,
    gl_up1,
    gl_down1,
    gl_up2,
    gl_down2,
    gl_y,
    dn_up1,
    dn_down1,
    dn_up2,
    dn_down2,
    dn_y,
    dn_n,
    dn_s,
    in_p,
    in_t,
    in_up1,
    in_down1,
    in_up2,
    in_down2,
    in_s,
    in_n,
    in_z,
    kw_p,
    kw_t,
    kw_up1,
    kw_down1,
    kw_up2,
    kw_down2,
    kw_s,
    kw_n,
    kw_z,
    wo_p,
    wo_t,
    wo_up1,
    wo_down1,
    wo_up2,
    wo_down2,
    wo_s,
    wo_n,
    wo_z,
    res_in,
    res_total,
    bias_own,
    gains_own,
    bias_in,
    gains_in,
    small_a,
    small_b,
    small_t,
    small_n,
    send,
    recv,
    local,
):
    place = here()
    dp, row, col = place
    core = dp % 2
    z = dp // Z_STEP
    twin, near, pair = twin_of(place), near_of(place), pair_of(place)
    up, down, far_z = along_z(place, 1), along_z(place, 3), along_z(place, 2)
    right, left = along_y(place, 1), along_y(place, 3)
    meet(
        [along_y(place, s) for s in (1, 2, 3)]
        + [near_of(place, (row + s) % 4) for s in range(4)]
        + [pair_of(place, (row + s) % 4) for s in range(4)]
        + [twin, up, down, far_z]
    )
    mail = Mail(send, recv)
    kept, arrivals = [], []

    def keep(source, target):
        kept.append(pltpu.make_async_copy(source, target, local.at[len(kept)]))
        kept[-1].start()
        return len(kept) - 1

    def kept_wait(index):
        if kept[index] is not None:
            kept[index].wait()
            kept[index] = None

    def even(start, size):
        return pl.ds(pl.multiple_of(start, 16), size)

    def plus(*values):
        result = values[0].astype(F32)
        for value in values[1:]:
            result = result + value.astype(F32)
        return result

    def dot_nt(left, right):
        return lax.dot_general(left, right, (((1,), (1,)), ((), ())), preferred_element_type=F32)

    rows = tok.shape[0] // 2
    width = tok.shape[1]
    piece = width // 4
    spot = even(row * rows, rows)
    own_rows, other_rows = even(col * rows, rows), even((1 - col) * rows, rows)

    def ffn_flow(i):
        if i < 2:
            height = gu.shape[0] // 2
            start = i * height
            theirs, done = gu_n.at[i], gu_s.at[i]
            mine = gu_v.at[pl.ds(start, height), :]
            swap = mail.post(gu.at[pl.ds(start, height), :], theirs, near)
            half = height // 2
            yield
            kept_wait(loads["gu"])
        else:
            if i == 2:
                held, loaded, name, height, start = gl, gl_v, "gl", gl.shape[1], 2 * gl.shape[1]
                mine, theirs, done = gl_y, gu_n.at[2], gu_s.at[2]
                one, two, three, four = gl_up1, gl_down1, gl_up2, gl_down2
            else:
                held, loaded, name, height, start = dn, dn_v, "dn", dn.shape[1], 0
                mine, theirs, done = dn_y, dn_n, dn_s
                one, two, three, four = dn_up1, dn_down1, dn_up2, dn_down2
            half = height // 2
            low, high = pl.ds(0, half), pl.ds(half, half)
            first = (mail.post(held.at[2, low, :], one, right), mail.post(held.at[2, high, :], two, left))
            straight = (
                mail.post(held.at[1, high, :], three.at[high, :], right),
                mail.post(held.at[3, low, :], four.at[low, :], left),
            )
            yield
            kept_wait(loads[name])
            first[0].wait_recv()
            one[...] = plus(loaded[1, low, :], one[...]).astype(BF16)
            last = [mail.post(one, three.at[low, :], right)]
            first[1].wait_recv()
            two[...] = plus(loaded[3, high, :], two[...]).astype(BF16)
            last.append(mail.post(two, four.at[high, :], left))
            yield
            for copy in straight + tuple(last):
                copy.wait_recv()
            mine[...] = plus(loaded[0], three[...], four[...]).astype(BF16)
            swap = mail.post(mine, theirs, near)
            yield
        swap.wait_recv()
        done[...] = plus(mine[...], theirs[...]).astype(BF16)

        def room(slot, which=None):
            begin, size = (start, height) if which is None else (start + which * half, half)
            if i < 3:
                share = gu_out.shape[2] // 4
                lanes = pl.ds(pl.multiple_of(slot * share, LANES), share)
                return gu_out.at[core, pl.ds(begin, size), lanes]
            return dn_out.at[even((slot * 2 + core) * height + begin, size), :]

        posts = {}
        for turn in range(2):
            for name, device, which in (("u", up, turn), ("d", down, 1 - turn)):
                posts[name, which] = mail.post(done.at[pl.ds(which * half, half), :], room(z, which), device)
        keep(done, room(z))
        arrivals.append(mail.post(done, room(z), twin))
        yield
        posts["u", 0].wait_recv()
        block = room((z + 3) % 4, 0)
        one_more = mail.post(block, block, up)
        posts["d", 1].wait_recv()
        block = room((z + 1) % 4, 1)
        two_more = mail.post(block, block, down)
        yield
        posts["u", 1].wait_recv()
        block = room((z + 3) % 4)
        arrivals.append(mail.post(block, block, twin))
        posts["d", 0].wait_recv()
        block = room((z + 1) % 4)
        arrivals.append(mail.post(block, block, twin))
        one_more.wait_recv()
        two_more.wait_recv()
        block = room((z + 2) % 4)
        arrivals.append(mail.post(block, block, twin))
        yield

    def weight_flow(part, t, up1, down1, up2, down2, total_h, theirs, quarter, out):
        height = t.shape[1]
        half = height // 2
        low, high = pl.ds(0, half), pl.ds(half, half)
        copy = mail.post(part.at[:, even((1 - core) * height, height), :], t, twin)
        yield
        copy.wait_recv()
        for j in range(4):
            t[j] = plus(part[j, even(core * height, height), :], t[j]).astype(BF16)
        first = (mail.post(t.at[2, low, :], up1, right), mail.post(t.at[2, high, :], down1, left))
        straight = (
            mail.post(t.at[1, high, :], up2.at[high, :], right),
            mail.post(t.at[3, low, :], down2.at[low, :], left),
        )
        yield
        first[0].wait_recv()
        up1[...] = plus(t[1, low, :], up1[...]).astype(BF16)
        last = [mail.post(up1, up2.at[low, :], right)]
        first[1].wait_recv()
        down1[...] = plus(t[3, high, :], down1[...]).astype(BF16)
        last.append(mail.post(down1, down2.at[high, :], left))
        yield
        for copy in straight + tuple(last):
            copy.wait_recv()
        total_h[...] = plus(t[0], up2[...], down2[...]).astype(BF16)
        swap = mail.post(total_h, theirs, near)
        yield
        swap.wait_recv()
        t[0] = plus(total_h[...], theirs[...]).astype(BF16)
        size = height // 4
        copies = []
        for step, device in ((1, up), (3, down), (2, far_z)):
            source = t.at[0, even(((z + step) % 4) * size, size), :]
            copies.append(mail.post(source, quarter.at[step - 1], device))
        yield
        for copy in copies:
            copy.wait_recv()
        mine = even(z * size, size)
        theirs[0:size, :] = plus(t[0, mine, :], quarter[0], quarter[1], quarter[2]).astype(BF16)
        place_of = lambda owner: out.at[even(core * height + owner * size, size), :]
        copies = [mail.post(theirs.at[0:size, :], place_of(z), device) for device in (up, down, far_z)]
        arrivals.append(mail.post(theirs.at[0:size, :], place_of(z), twin))
        keep(theirs.at[0:size, :], place_of(z))
        yield
        for copy in copies:
            copy.wait_recv()
        for step in (1, 2, 3):
            block = place_of((z + step) % 4)
            arrivals.append(mail.post(block, block, twin))
        yield

    def result_flow():
        copies = (mail.post(ahead.at[0], res_in.at[0], up), mail.post(ahead.at[1], res_in.at[1], down))
        yield
        kept_wait(loads["down"])
        for half, copy in enumerate(copies):
            copy.wait_recv()
            part = pl.ds(half * rows, rows)
            res_total[part, :] = plus(down_v[part, :], res_in[half]).astype(BF16)
        swap = mail.post(res_total.at[other_rows, :], part_in, pair)
        yield
        swap.wait_recv()
        result_rows[...] = (middle_v[own_rows, :] + plus(res_total[own_rows, :], part_in[...])).astype(BF16)
        yield
        spread(result_rows, result_out)
        yield

    def spread(source, target):
        for step in range(4):
            lanes = pl.ds(step * piece, piece)
            if step:
                arrivals.append(mail.post(source.at[:, lanes], target.at[spot, :], along_y(place, step)))
            else:
                keep(source.at[:, lanes], target.at[spot, :])

    flows = [ffn_flow(i) for i in range(4)]
    loads = {}
    for name, source, target in (
        ("middle", middle, middle_v),
        ("cot", cot.at[0], cot_v),
        ("w_out", w_out, w_out_v),
        ("attended", attended, attended_v),
        ("query", query, query_v),
        ("kva", kv_a, kva),
        ("kvb", kv_b, kvb),
        ("ta", turned_a, turned_a_v),
        ("tb", turned_b, turned_b_v),
        ("gu", gu, gu_v),
        ("w_in", w_in, w_in_v),
        ("normed", normed, normed_v),
        ("tok", tok, tok_v),
        ("dn", dn, dn_v),
        ("gl", gl, gl_v),
        ("down", result_sum, down_v),
    ):
        loads[name] = keep(source, target)
    result_steps = result_flow()
    next(flows[3])
    next(flows[1])
    for j in range(4):
        gain_rows[:, j * piece : (j + 1) * piece] = gains[j]

    def norm_back(stream, gain, incoming):
        scale = lax.rsqrt(jnp.sum(stream * stream, -1, keepdims=True) * (1.0 / width) + EPS)
        scaled = incoming * gain
        inner = jnp.sum(scaled * stream, -1, keepdims=True) * (1.0 / width)
        back = scale * scaled - stream * (scale * scale * scale * inner)
        return back, jnp.sum(incoming * stream * scale, 0, keepdims=True)

    kept_wait(loads["middle"])
    kept_wait(loads["cot"])
    gain_ffn_part = jnp.zeros((1, width), F32)
    for half in range(2):
        part = slice(half * rows, (half + 1) * rows)
        back, gain_part = norm_back(middle_v[part, :], gain_rows[1:2, :], total[part, :])
        value = cot_v[part, :].astype(F32) + back
        grad_middle[part, :] = value
        grad_low[part, :] = value.astype(BF16)
        gain_ffn_part = gain_ffn_part + gain_part
    gains_own[...] = jnp.zeros_like(gains_own)
    for j in range(4):
        gains_own[j, 1:2, :] = 0.5 * gain_ffn_part[:, j * piece : (j + 1) * piece]
    next(result_steps)
    kept_wait(loads["w_out"])
    q_width = w_out.shape[0]
    for first in range(0, q_width, 256):
        lanes = slice(first, first + 256)
        grad_att[:, lanes] = dot_nt(grad_low[...], w_out_v[lanes, :]).astype(BF16)

    def turn_over(source, target, count):
        for t in range(count):
            lanes = slice(t * LANES, (t + 1) * LANES)
            target[lanes, 0 : source.shape[0]] = source[:, lanes].T

    next(flows[0])
    next(flows[3])
    kept_wait(loads["attended"])
    turn_over(attended_v, flat, q_width // LANES)
    for j in range(4):
        wo_p[j] = jnp.dot(
            flat[0:q_width, :], grad_low[:, j * piece : (j + 1) * piece], preferred_element_type=F32
        ).astype(BF16)
    wo_steps = weight_flow(wo_p, wo_t, wo_up1, wo_down1, wo_up2, wo_down2, wo_s, wo_n, wo_z, wo_out)

    for name in ("query", "kva", "kvb", "ta", "tb"):
        kept_wait(loads[name])
    heads = q_width // HEAD_SIZE
    factor = HEAD_SIZE ** (-0.5)

    def unrotate(value, half):
        part = slice(half * rows, (half + 1) * rows)
        return value * tables[0, part, :] + pltpu.roll(value * tables[1, part, :], HEAD_SIZE // 2, 1)

    def attend_back(half, keys, mask, sums):
        part = slice(half * rows, (half + 1) * rows)
        count = keys.shape[0]
        for t in range(count // LANES):
            lanes = slice(t * LANES, (t + 1) * LANES)
            keys_t[:, lanes] = keys[lanes, 0:HEAD_SIZE].T
        sums[...] = jnp.zeros_like(sums)

        @pl.loop(0, heads)
        def _(h):
            lanes = pl.ds(pl.multiple_of(h * HEAD_SIZE, LANES), HEAD_SIZE)
            one, grad = query_v[part, lanes], grad_att[part, lanes]
            raw = dot_nt(keys[:, 0:HEAD_SIZE], one)
            probs = jnp.exp(raw * factor + mask[...] - logs[half * heads + h, 0:1, :])
            grad_probs = dot_nt(keys[:, HEAD_SIZE : 2 * HEAD_SIZE], grad)
            inner = jnp.sum(grad_probs * probs, 0, keepdims=True)
            grad_scores = (probs * (grad_probs - inner)).astype(BF16)
            sums[:, 0:HEAD_SIZE] += jnp.dot(grad_scores, one, preferred_element_type=F32)
            sums[:, HEAD_SIZE : 2 * HEAD_SIZE] += jnp.dot(probs.astype(BF16), grad, preferred_element_type=F32)
            grad_query = jnp.dot(keys_t[:, 0:count], grad_scores, preferred_element_type=F32).T * factor
            grad_pre[part, lanes] = unrotate(grad_query, half).astype(BF16)

    def low_sums(sums, part):
        return (sums[part, 0:HEAD_SIZE] * factor).astype(BF16), sums[part, HEAD_SIZE : 2 * HEAD_SIZE].astype(BF16)

    next(wo_steps)
    next(flows[1])
    next(flows[2])
    next(result_steps)
    next(flows[1])
    next(flows[3])
    attend_back(1, kvb, turned_b_v, dkv_b)
    half_rows = kva.shape[0]
    low_part, high_part = slice(0, half_rows), slice(half_rows, 2 * half_rows)
    for target, sums, part in ((low_kv, dkv_b, low_part), (own_kv.at[1], dkv_b, high_part)):
        target[:, 0:HEAD_SIZE], target[:, HEAD_SIZE : 2 * HEAD_SIZE] = low_sums(sums, part)
    kv_got = []
    for step in range(4):
        other = (row + step) % 4
        part = even(other * rows, rows)
        kv_got.append(mail.post(low_kv.at[part, :], from_near.at[step], near_of(place, other)))
        if step:
            kv_got.append(mail.post(own_kv.at[1, part, :], from_own.at[step - 1, 1], along_y(place, step)))
    next(flows[0])
    attend_back(0, kva, turned_a_v, dkv_a)
    target = own_kv.at[0]
    target[:, 0:HEAD_SIZE], target[:, HEAD_SIZE : 2 * HEAD_SIZE] = low_sums(dkv_a, low_part)
    for step in (1, 2, 3):
        part = even(((row + step) % 4) * rows, rows)
        kv_got.append(mail.post(own_kv.at[0, part, :], from_own.at[step - 1, 0], along_y(place, step)))
    next(flows[2])
    next(flows[3])
    next(wo_steps)
    kept_wait(loads["normed"])
    turn_over(normed_v, flat, width // LANES)
    for j in range(4):
        in_p[j] = jnp.dot(
            flat[j * piece : (j + 1) * piece, :], grad_pre[:, 0:q_width], preferred_element_type=F32
        ).astype(BF16)
    in_steps = weight_flow(in_p, in_t, in_up1, in_down1, in_up2, in_down2, in_s, in_n, in_z, in_out)
    next(flows[3])
    next(flows[2])
    next(flows[0])
    next(in_steps)
    for copy in kv_got:
        copy.wait_recv()
    for half in range(2):
        part = slice(half * rows, (half + 1) * rows)
        value = own_kv[half, spot, :].astype(F32)
        for step in range(3):
            value = value + from_own[step, half].astype(F32)
        if half == 0:
            for step in range(4):
                value = value + from_near[step].astype(F32)
        grad_pre[part, q_width : q_width + HEAD_SIZE] = unrotate(value[:, 0:HEAD_SIZE], half).astype(BF16)
        grad_pre[part, q_width + HEAD_SIZE : q_width + 2 * HEAD_SIZE] = value[:, HEAD_SIZE : 2 * HEAD_SIZE].astype(
            BF16
        )
    next(wo_steps)
    next(in_steps)
    kept_wait(loads["w_in"])
    for j in range(4):
        grad_part[:, j * piece : (j + 1) * piece] = dot_nt(grad_pre[...], w_in_v[j]).astype(BF16)
    swap = mail.post(grad_part.at[other_rows, :], grad_in, pair)
    for j in range(4):
        kw_p[j] = jnp.dot(
            flat[j * piece : (j + 1) * piece, :], grad_pre[:, q_width:], preferred_element_type=F32
        ).astype(BF16)
    kw_steps = weight_flow(kw_p, kw_t, kw_up1, kw_down1, kw_up2, kw_down2, kw_s, kw_n, kw_z, kw_out)
    next(wo_steps)
    next(flows[2])
    next(kw_steps)
    next(result_steps)
    next(in_steps)
    next(kw_steps)
    bias_own[...] = jnp.zeros_like(bias_own)
    bias_own[0:1, :] = jnp.sum(grad_pre[...].astype(F32), 0, keepdims=True)
    next(wo_steps)
    kept_wait(loads["tok"])
    swap.wait_recv()
    back, gain_part = norm_back(
        tok_v[own_rows, :].astype(F32), gain_rows[0:1, :], plus(grad_part[own_rows, :], grad_in[...])
    )
    rows_out[...] = (grad_middle[own_rows, :] + back).astype(BF16)
    for j in range(4):
        gains_own[j, 0:1, :] = gain_part[:, j * piece : (j + 1) * piece]
    next(in_steps)
    next(flows[2])
    next(kw_steps)
    next(wo_steps)
    small_copies, small_kept = [], []
    for step in range(4):
        device = along_y(place, step)
        mine = gains_in.at[col * 4 + row]
        if step:
            small_copies.append(mail.post(bias_own, bias_in.at[row], device))
            small_copies.append(mail.post(gains_own.at[step], mine, device))
        else:
            small_kept.append(keep(bias_own, bias_in.at[row]))
            small_kept.append(keep(gains_own.at[step], mine))
        small_copies.append(mail.post(gains_own.at[step], mine, pair_of(place, (row + step) % 4)))
    spread(rows_out, grad_out)
    next(kw_steps)
    next(in_steps)
    for copy in small_copies:
        copy.wait_recv()
    for index in small_kept:
        kept_wait(index)
    small_a[...] = jnp.zeros_like(small_a)
    small_a[0:8, :] = bias_in[0] + bias_in[1] + bias_in[2] + bias_in[3]
    small_a[8:16, 0:piece] = (
        gains_in[0] + gains_in[1] + gains_in[2] + gains_in[3] + gains_in[4] + gains_in[5] + gains_in[6] + gains_in[7]
    )
    small_first = mail.post(small_a, small_t, twin)
    next(result_steps)
    next(kw_steps)
    small_first.wait_recv()
    small_b[...] = small_a[...] + small_t[...]
    small_second = mail.post(small_b, small_n, near)
    next(in_steps)
    next(flows[2])
    small_second.wait_recv()
    small_t[...] = small_b[...] + small_n[...]
    for device in (up, down, far_z):
        arrivals.append(mail.post(small_t, small_out.at[z], device))
    keep(small_t, small_out.at[z])
    next(wo_steps)
    next(kw_steps)
    next(in_steps)
    for steps in [*flows, wo_steps, in_steps, kw_steps, result_steps]:
        for _ in steps:
            pass
    for copy in arrivals:
        copy.wait_recv()
    for copy in kept:
        if copy is not None:
            copy.wait()
    mail.finish()


def widen_kernel(gate_up, down, w_in, w_kv, w_out, result, tokens, small, *outs):
    result_w, tokens_w, query_w, key_w, value_w, out_w, gate_w, up_w, down_w, *flat = outs
    total = small[0] + small[1] + small[2] + small[3]
    start = 0
    for line, out in zip((0, 0, 0, 8, 9), flat):
        start = 0 if line else start
        out[...] = total[line, start : start + out.shape[0]]
        start += out.shape[0]
    result_w[...] = result[...].astype(F32)
    tokens_w[...] = tokens[...].astype(F32)
    query_w[...] = w_in[...].astype(F32)
    key_w[...] = w_kv[:, : key_w.shape[1]].astype(F32)
    value_w[...] = w_kv[:, key_w.shape[1] :].astype(F32)
    out_w[...] = w_out[...].astype(F32)
    gate_w[...] = gate_up[0, :, : gate_w.shape[1]].astype(F32)
    up_w[...] = gate_up[1, :, : up_w.shape[1]].astype(F32)
    down_w[...] = down[...].astype(F32)


def on_device(
    tokens,
    cotangent,
    lengths,
    gain_attn,
    w_query,
    key_projection,
    value_projection,
    bias_query,
    key_bias_vector,
    value_bias_vector,
    w_out,
    gain_ffn,
    w_gate,
    w_up,
    w_down,
):
    half_rows, piece = tokens.shape
    width = 4 * piece
    rows = half_rows // 4
    q_width = w_query.shape[1]
    kv_width = key_projection.shape[1]
    heads = q_width // HEAD_SIZE
    hidden = w_gate.shape[1]
    share = -(-hidden // (4 * LANES)) * LANES

    in_width = q_width + 2 * kv_width
    thin = piece // 2
    (
        tok_rows,
        cot_full,
        gains4,
        normed,
        query,
        kv_a,
        kv_b,
        logs,
        attended,
        tables,
        middle,
        mask_a,
        mask_b,
        normed_ffn,
        w_in_full,
        w_out_full,
        w_gu_full,
        w_down_full,
    ) = talk(
        front_kernel,
        0,
        FRONT_COPIES,
        FRONT_LOCAL,
        [
            ((2 * rows, width), BF16),
            ((4, 2 * rows, width), BF16),
            ((4, 8, piece), F32),
            ((2 * rows, width), BF16),
            ((2 * rows, q_width), BF16),
            ((half_rows, 2 * kv_width), BF16),
            ((2 * half_rows, 2 * kv_width), BF16),
            ((2 * heads, 8, rows), F32),
            ((2 * rows, q_width), BF16),
            ((2, 2 * rows, HEAD_SIZE), F32),
            ((2 * rows, width), F32),
            ((half_rows, rows), F32),
            ((2 * half_rows, rows), F32),
            ((2 * rows, width), BF16),
            ((4, piece, in_width), BF16),
            ((q_width, width), BF16),
            ((4, 2, thin, 2 * share), BF16),
            ((share, width), BF16),
        ],
        [ANY] * 2 + [VMEM] * 6 + [ANY] * 7,
        [ANY] * 3 + [VMEM] * 2 + [ANY] * 2 + [VMEM] * 7 + [ANY] * 4,
        [
            pltpu.VMEM((8, LANES), jnp.int32),
            pltpu.VMEM((8, piece), F32),
            pltpu.VMEM((2 * rows, width), BF16),
            pltpu.VMEM((2, 8, LANES), jnp.int32),
            pltpu.VMEM((4, 8, piece), F32),
            pltpu.VMEM((4, piece, in_width), BF16),
            pltpu.VMEM((q_width, width), BF16),
            pltpu.VMEM((2, thin, 2 * share), BF16),
            pltpu.VMEM((share, piece), BF16),
            pltpu.VMEM((thin, LANES), BF16),
            pltpu.VMEM((LANES, piece), BF16),
            pltpu.VMEM((2 * rows, 2 * kv_width), BF16),
            pltpu.VMEM((half_rows, 2 * kv_width), BF16),
            pltpu.VMEM((2 * half_rows, 2 * kv_width), BF16),
            pltpu.VMEM((rows, half_rows), F32),
            pltpu.VMEM((rows, 2 * half_rows), F32),
            pltpu.VMEM((2 * rows, width), BF16),
            pltpu.VMEM((2 * rows, width), BF16),
        ],
        limit=56,
    )(
        tokens,
        cotangent,
        lengths,
        gain_attn,
        gain_ffn,
        bias_query,
        key_bias_vector,
        value_bias_vector,
        w_query,
        key_projection,
        value_projection,
        w_out,
        w_gate,
        w_up,
        w_down,
    )

    w_both_full = w_gu_full.reshape(width, 2 * share)
    half_block = (2, rows, width)
    grad_normed_ffn, both_sum, both_late, down_half, result_sum, result_ahead = talk(
        ffn_kernel,
        4,
        44,
        15,
        [
            ((2 * rows, width), F32),
            ((2 * piece // 3, share), BF16),
            ((4, piece // 3, share), BF16),
            ((4, share // 2, piece), BF16),
            ((2 * rows, width), BF16),
            ((2, rows, width), BF16),
        ],
        [ANY] * 4,
        [VMEM, VMEM, ANY, ANY, VMEM, VMEM],
        [
            pltpu.VMEM(shape, BF16)
            for shape in (
                (8 * rows, width),
                (8 * rows, width),
                (width, 2 * share),
                (share, width),
                (8 * rows, 2 * share),
                (8 * rows, share),
                (8 * rows, width),
                (width, 8 * rows),
                (8 * rows, width),
                (4, piece, share),
                (4, share // 2, piece),
                (2, rows // 2, width),
                (2, rows // 2, width),
                half_block,
                half_block,
                half_block,
                (2, rows // 2, width),
                (2, rows // 2, width),
                half_block,
                (rows, width),
                (rows, width),
                (rows, width),
                (rows, width),
                (2, piece // 6, share),
                (2, piece // 6, share),
                (2, piece // 3, share),
                (2, piece // 3, share),
            )
        ],
        limit=60,
    )(normed_ffn, cot_full, w_both_full, w_down_full)
    thirds = piece // 3
    q_half, w_half = (thin, q_width), (q_width // 2, piece)
    gu_chunk, dn_chunk = (3, thirds, share), (share // 2, piece)

    def halved(shape):
        return (*shape[:-2], shape[-2] // 2, shape[-1])

    def weight_scratch(shape):
        return [
            (4, 2 * shape[0], shape[1]),
            (4, *shape),
            halved(shape),
            halved(shape),
            shape,
            shape,
            shape,
            shape,
            (3, shape[0] // 4, shape[1]),
        ]

    def scratch(kind, *shapes):
        return [pltpu.VMEM(shape, kind) for shape in shapes]

    gate_up, down_all, in_total, kv_total, out_total, grad_tokens, result, small_all = talk(
        back_kernel,
        8,
        BACK_COPIES,
        BACK_LOCAL,
        [
            ((2, piece, 4 * share), BF16),
            ((4 * share, piece), BF16),
            ((piece, q_width), BF16),
            ((piece, 2 * kv_width), BF16),
            ((q_width, piece), BF16),
            ((half_rows, piece), BF16),
            ((half_rows, piece), BF16),
            ((4, 16, in_width), F32),
        ],
        [VMEM, ANY, ANY, VMEM] + [ANY] * 5 + [VMEM, ANY, VMEM] + [ANY] * 9,
        [ANY] * 8,
        scratch(F32, (2 * rows, width))
        + scratch(
            BF16,
            (2 * rows, width),
            (2 * rows, width),
            (2 * rows, width),
            (2 * rows, q_width),
            (half_rows, 2 * kv_width),
            (2 * half_rows, 2 * kv_width),
            (2 * rows, q_width),
        )
        + scratch(F32, (half_rows, rows), (2 * half_rows, rows))
        + scratch(
            BF16,
            (4, piece, in_width),
            (q_width, width),
            (2 * thirds, share),
            (4, thirds, share),
            (4, share // 2, piece),
            (2 * rows, width),
        )
        + scratch(F32, (8, width), (2 * rows, width))
        + scratch(BF16, (2 * rows, width), (2 * rows, q_width), (width, 2 * rows), (HEAD_SIZE, 2 * half_rows))
        + scratch(F32, (half_rows, 2 * kv_width), (2 * half_rows, 2 * kv_width))
        + scratch(
            BF16,
            (half_rows, 2 * kv_width),
            (2, half_rows, 2 * kv_width),
            (3, 2, rows, 2 * kv_width),
            (4, rows, 2 * kv_width),
            (2 * rows, in_width),
            (2 * rows, width),
            (rows, width),
            (rows, width),
            (rows, width),
            (rows, width),
            gu_chunk,
            gu_chunk,
            halved((thirds, share)),
            halved((thirds, share)),
            (thirds, share),
            (thirds, share),
            (thirds, share),
            halved(dn_chunk),
            halved(dn_chunk),
            dn_chunk,
            dn_chunk,
            dn_chunk,
            dn_chunk,
            dn_chunk,
            *weight_scratch(q_half),
            *weight_scratch((thin, 2 * kv_width)),
            *weight_scratch(w_half),
            (2, rows, width),
            (2 * rows, width),
        )
        + scratch(F32, (8, in_width), (4, 8, piece), (4, 8, in_width), (8, 8, piece))
        + scratch(F32, *[(16, in_width)] * 4),
        limit=60,
    )(
        grad_normed_ffn,
        middle,
        cot_full,
        gains4,
        tok_rows,
        normed,
        query,
        kv_a,
        kv_b,
        logs,
        attended,
        tables,
        mask_a,
        mask_b,
        w_in_full,
        w_out_full,
        both_sum,
        both_late,
        down_half,
        result_sum,
        result_ahead,
    )
    steps = 8
    narrow = [gate_up, down_all, in_total, kv_total, out_total, result, grad_tokens, small_all]
    lines = [(q_width,), (kv_width,), (kv_width,), (piece,), (piece,)]
    wide = [
        (half_rows, piece),
        (half_rows, piece),
        (piece, q_width),
        (piece, kv_width),
        (piece, kv_width),
        (q_width, piece),
        (piece, hidden),
        (piece, hidden),
        (hidden, piece),
    ]

    def in_block(array):
        if array is small_all:
            return pl.BlockSpec(array.shape, lambda i: (0, 0, 0))
        if array.ndim == 3:
            return pl.BlockSpec((2, array.shape[1] // steps, array.shape[2]), lambda i: (0, i, 0))
        if array is down_all:
            return pl.BlockSpec((hidden // steps, piece), lambda i: (i, 0))
        return pl.BlockSpec((array.shape[0] // steps, array.shape[1]), lambda i: (i, 0))

    wide_out = pl.pallas_call(
        widen_kernel,
        grid=(steps,),
        out_shape=[jax.ShapeDtypeStruct(shape, F32) for shape in wide + lines],
        in_specs=[in_block(array) for array in narrow],
        out_specs=[pl.BlockSpec((shape[0] // steps, shape[1]), lambda i: (i, 0)) for shape in wide]
        + [pl.BlockSpec(shape, lambda i: (0,)) for shape in lines],
        compiler_params=pltpu.CompilerParams(vmem_limit_bytes=60 << 20),
    )(*narrow)
    result_w, tokens_w, query_w, key_w, value_w, out_w, gate_w, up_w, down_w, *flat = wide_out
    bias_q, bias_k, bias_v, gain_one, gain_two = flat
    return (
        result_w,
        tokens_w,
        gain_one,
        query_w,
        key_w,
        value_w,
        bias_q,
        bias_k,
        bias_v,
        out_w,
        gain_two,
        gate_w,
        up_w,
        down_w,
    )


def solution(mesh):
    placed = (
        P(("dp", "col"), "row"),
        P(("dp", "col"), "row"),
        P("dp", None),
        P("row"),
        P("row", "col"),
        P("row", "col"),
        P("row", "col"),
        P("col"),
        P("col"),
        P("col"),
        P("col", "row"),
        P("row"),
        P("row", "col"),
        P("row", "col"),
        P("col", "row"),
    )
    return jax.shard_map(
        on_device,
        mesh=mesh,
        in_specs=placed,
        out_specs=(
            P(("dp", "col"), "row"),
            P(("dp", "col"), "row"),
            P("row"),
            P("row", "col"),
            P("row", "col"),
            P("row", "col"),
            P("col"),
            P("col"),
            P("col"),
            P("col", "row"),
            P("row"),
            P("row", "col"),
            P("row", "col"),
            P("col", "row"),
        ),
        check_vma=False,
    )
```

```python
import math

import jax
import jax.numpy as jnp
from jax import lax
from jax.experimental import pallas as pl
from jax.experimental.pallas import tpu as pltpu
from jax.sharding import PartitionSpec as P

HEAD_SIZE = 128
EPS = 1e-06
THETA = 1000000.0
LANES = 128
MESH = pl.DeviceIdType.MESH
BF16 = jnp.bfloat16
F32 = jnp.float32
ANY = pl.BlockSpec(memory_space=pl.ANY)
VMEM = pl.BlockSpec(memory_space=pltpu.VMEM)

Z_STEP = 4
FRONT_COPIES = 77
FRONT_LOCAL = 27
BACK_COPIES = 145
BACK_LOCAL = 30


def here():
    return lax.axis_index("dp"), lax.axis_index("row"), lax.axis_index("col")


def flip_near(dp):
    return dp + 2 - 4 * ((dp // 2) % 2)


def pair_of(place, row=None):
    dp, own, col = place
    return flip_near(dp), own if row is None else row, 1 - col


def near_of(place, row=None):
    dp, own, col = place
    return flip_near(dp), own if row is None else row, col


def twin_of(place):
    dp, row, col = place
    return dp + 1 - 2 * (dp % 2), row, col


def along_z(place, step):
    dp, row, col = place
    return (dp + Z_STEP * step) % (4 * Z_STEP), row, col


def along_y(place, step):
    dp, row, col = place
    return dp, (row + step) % 4, col


def meet(peers):
    barrier = pltpu.get_barrier_semaphore()
    for peer in peers:
        pl.semaphore_signal(barrier, inc=1, device_id=peer, device_id_type=MESH)
    pl.semaphore_wait(barrier, len(peers))


class Mail:
    def __init__(self, send, recv):
        self.send, self.recv, self.count, self.sent = send, recv, 0, []

    def post(self, source, target, device):
        index = self.count
        self.count += 1
        copy = pltpu.make_async_remote_copy(
            src_ref=source,
            dst_ref=target,
            send_sem=self.send.at[index],
            recv_sem=self.recv.at[index],
            device_id=device,
            device_id_type=MESH,
        )
        copy.start()
        self.sent.append(copy)
        return copy

    def finish(self):
        assert self.count == self.send.shape[0], (self.count, self.send.shape)
        for copy in self.sent:
            copy.wait_send()


def talk(body, ident, copies, local, outs, in_specs, out_specs, scratch=(), limit=32):
    return pl.pallas_call(
        body,
        out_shape=[jax.ShapeDtypeStruct(*out) for out in outs],
        in_specs=in_specs,
        out_specs=out_specs,
        scratch_shapes=[
            *scratch,
            pltpu.SemaphoreType.DMA((copies,)),
            pltpu.SemaphoreType.DMA((copies,)),
            pltpu.SemaphoreType.DMA((max(local, 1),)),
        ],
        compiler_params=pltpu.CompilerParams(
            collective_id=ident, has_side_effects=True, vmem_limit_bytes=limit << 20
        ),
    )


def front_kernel(
    tok,
    cot,
    lens_in,
    gain_attn,
    gain_ffn,
    bias_q,
    bias_k,
    bias_v,
    wq,
    wk,
    wv,
    wo,
    wg,
    wu,
    wd,
    tok_out,
    cot_full,
    gains_out,
    normed_t,
    query,
    kva_out,
    kvb_out,
    logs,
    attended_t,
    tables,
    middle,
    turned_a,
    turned_b,
    normed_ffn,
    w_in_out,
    w_out_out,
    wgu_full,
    wd_full,
    keys_a_t,
    keys_b_t,
    normed,
    attended,
    lens,
    gains,
    tok_v,
    lens_v,
    gains_v,
    w_in,
    w_out,
    gu_own,
    wd_own,
    blank_gu,
    blank_wd,
    kv,
    kva,
    kvb,
    bias_a,
    bias_b,
    branch,
    branch_in,
    send,
    recv,
    local,
):
    place = here()
    dp, row, col = place
    z, core = dp // Z_STEP, dp % 2
    twin, pair, up, down = twin_of(place), pair_of(place), along_z(place, 1), along_z(place, 3)
    right, left, near = along_y(place, 1), along_y(place, 3), near_of(place)
    meet(
        [along_y(place, s) for s in (1, 2, 3)]
        + [near_of(place, (row + s) % 4) for s in range(4)]
        + [pair, twin, up, down]
    )
    mail = Mail(send, recv)
    kept = []

    def keep(source, target):
        kept.append(pltpu.make_async_copy(source, target, local.at[len(kept)]))
        kept[-1].start()
        return len(kept) - 1

    def kept_wait(index):
        kept[index].wait()
        kept[index] = None

    def even(start, size):
        return pl.ds(pl.multiple_of(start, 16), size)

    rows, piece = tok.shape[0] // 4, tok.shape[1]
    width = 4 * piece
    own_rows = even(col * rows, rows)
    spot = even(row * rows, rows)

    def spread(source, target):
        got = []
        for step in range(4):
            part = source.at[even(((row + step) % 4) * rows, rows), :]
            lanes = pl.ds(((4 - step) % 4) * piece, piece)
            if step:
                got.append(mail.post(part, target.at[own_rows, lanes], along_y(place, step)))
            else:
                mine = keep(part, target.at[own_rows, lanes])
        return got, mine

    tokens = spread(tok, tok_v)
    lens[...] = jnp.zeros_like(lens)
    lens[0:1, 0 : lens_in.shape[1]] = lens_in[...]
    gains[...] = jnp.zeros_like(gains)
    gains[0:1, :] = gain_attn[...].reshape(1, piece)
    gains[1:2, :] = gain_ffn[...].reshape(1, piece)
    lens_got = mail.post(lens, lens_v.at[col], pair)
    lens_kept = keep(lens, lens_v.at[col])
    gains_kept = keep(gains, gains_v.at[0])
    gains_got = [mail.post(gains, gains_v.at[4 - s], along_y(place, s)) for s in (1, 2, 3)]

    q_width, kv_width = wq.shape[1], wk.shape[1]
    stages = [
        keep(wq, w_in.at[0, :, pl.ds(0, q_width)]),
        keep(wk, w_in.at[0, :, pl.ds(q_width, kv_width)]),
        keep(wv, w_in.at[0, :, pl.ds(q_width + kv_width, kv_width)]),
        keep(wo, w_out.at[:, pl.ds(0, piece)]),
    ]
    share = wd_own.shape[0]
    thin = piece // 2
    sure = share - LANES
    take = pl.multiple_of(z * share, LANES)
    big = []
    for k in range(2):
        for i, source in enumerate((wg, wu)):
            from_rows = pl.ds(k * thin, thin)
            big.append(keep(source.at[from_rows, pl.ds(take, sure)], gu_own.at[k, :, pl.ds(i * share, sure)]))
    big.append(keep(wd.at[pl.ds(take, sure), :], wd_own.at[pl.ds(0, sure), :]))
    blank_gu[...] = jnp.zeros_like(blank_gu)
    blank_wd[...] = jnp.zeros_like(blank_wd)
    first_edge = len(kept)
    edges = []
    for k in range(2):
        for i, source in enumerate((wg, wu)):
            target = gu_own.at[k, :, pl.ds(i * share + sure, LANES)]
            edges.append((source, pl.ds(k * thin, thin), None, target, blank_gu))
    edges.append((wd, None, slice(None), wd_own.at[pl.ds(sure, LANES), :], blank_wd))

    def edge(index, last):
        source, from_rows, _, target, blank = edges[index]
        if last:
            origin = blank
        elif from_rows is None:
            origin = source.at[pl.ds(pl.multiple_of(take + sure, LANES), LANES), :]
        else:
            origin = source.at[from_rows, pl.ds(pl.multiple_of(take + sure, LANES), LANES)]
        return pltpu.make_async_copy(origin, target, local.at[first_edge + index])

    @pl.when(z < 3)
    def _():
        for index in range(len(edges)):
            edge(index, False).start()

    @pl.when(z == 3)
    def _():
        for index in range(len(edges)):
            edge(index, True).start()

    for index in range(len(edges)):
        kept.append(edge(index, True))
        big.append(first_edge + index)

    q_rows, o_rows = thin // 4, w_out.shape[0] // 8

    def in_part(j, owner_z):
        return w_in.at[j, even(core * thin + owner_z * q_rows, q_rows), :]

    def in_parts(owner_z):
        return w_in.at[pl.ds(1, 3), even(core * thin + owner_z * q_rows, q_rows), :]

    def in_side(owner_z, side):
        lanes = pl.ds(side * (w_in.shape[2] // 2), w_in.shape[2] // 2)
        return w_in.at[pl.ds(1, 3), even(core * thin + owner_z * q_rows, q_rows), lanes]

    def out_part(j, owner_z):
        return w_out.at[even(core * 4 * o_rows + owner_z * o_rows, o_rows), pl.ds(j * piece, piece)]

    def out_parts(owner_z):
        return w_out.at[even(core * 4 * o_rows + owner_z * o_rows, o_rows), pl.ds(piece, 3 * piece)]

    def out_side(owner_z, side):
        start = core * 4 * o_rows + owner_z * o_rows + side * (o_rows // 2)
        return w_out.at[even(start, o_rows // 2), pl.ds(piece, 3 * piece)]

    for index in stages:
        kept_wait(index)
    in_got = [mail.post(in_part(0, z), in_part(4 - step, z), along_y(place, step)) for step in (1, 3, 2)]

    def to_pair(spreading, target):
        got, mine = spreading
        kept_wait(mine)
        for copy in got:
            copy.wait_recv()
        return mail.post(target.at[own_rows, :], target.at[own_rows, :], pair)

    tokens_pair = to_pair(tokens, tok_v)
    shares = []

    def give(part):
        shares.append(mail.post(part, part, twin))

    def z_first(side):
        copies = {}
        for turn in range(2):
            copies["u", turn] = mail.post(side(z, turn), side(z, turn), up)
            copies["d", 1 - turn] = mail.post(side(z, 1 - turn), side(z, 1 - turn), down)
        return copies

    below, above, across = (z + 3) % 4, (z + 1) % 4, (z + 2) % 4

    def z_second(side, whole, copies):
        copies["u", 0].wait_recv()
        far_up = mail.post(side(below, 0), side(below, 0), up)
        copies["d", 1].wait_recv()
        far_down = mail.post(side(above, 1), side(above, 1), down)
        copies["u", 1].wait_recv()
        give(whole(below))
        copies["d", 0].wait_recv()
        give(whole(above))
        return far_up, far_down

    def z_third(whole, copies):
        for copy in copies:
            copy.wait_recv()
        give(whole(across))

    for copy in in_got:
        copy.wait_recv()
    in_z = z_first(in_side)
    give(in_parts(z))
    out_got = [mail.post(out_part(0, z), out_part(4 - step, z), along_y(place, step)) for step in (1, 3, 2)]
    cotangents = spread(cot, cot_full.at[0])
    for index in big:
        kept_wait(index)
    x_lo = (dp // 2) % 2
    gu_half, wd_half = thin // 4, share // 4

    def gu_part(j, which=None, owner=x_lo):
        start, size = (0, 2 * gu_half) if which is None else (which * gu_half, gu_half)
        return wgu_full.at[j, core, even(owner * 2 * gu_half + start, size), :]

    def gu_whole(j):
        return wgu_full.at[j, core]

    def wd_part(j, which=None):
        start, size = (0, 2 * wd_half) if which is None else (which * wd_half, wd_half)
        return wd_full.at[even(core * 2 * wd_half + start, size), pl.ds(j * piece, piece)]

    def gu_source(which):
        return gu_own.at[core, even((x_lo * 2 + which) * gu_half, gu_half), :]

    def wd_source(which):
        return wd_own.at[even((core * 2 + which) * wd_half, wd_half), :]

    y_ring, near_gu, twins = {}, [], []

    def y_start(name, source, part):
        for turn in range(2):
            y_ring[name, "r", turn] = mail.post(source(turn), part(3, turn), right)
            y_ring[name, "l", 1 - turn] = mail.post(source(1 - turn), part(1, 1 - turn), left)

    def y_forward(name, part):
        y_ring[name, "r", 0].wait_recv()
        y_ring[name, "fr"] = mail.post(part(3, 0), part(2, 0), right)
        y_ring[name, "l", 1].wait_recv()
        y_ring[name, "fl"] = mail.post(part(1, 1), part(2, 1), left)

    def y_share(name, part, queue, device):
        y_ring[name, "r", 1].wait_recv()
        queue.append(mail.post(part(3), part(3), device))
        y_ring[name, "l", 0].wait_recv()
        queue.append(mail.post(part(1), part(1), device))

    def y_end(name, part, queue, device):
        y_ring[name, "fr"].wait_recv()
        y_ring[name, "fl"].wait_recv()
        queue.append(mail.post(part(2), part(2), device))


    kept_wait(lens_kept)
    lens_got.wait_recv()
    half_rows = 4 * rows

    def segment_of(which, index):
        end_0 = lens_v[which, 0:1, 0:1]
        end_1 = end_0 + lens_v[which, 0:1, 1:2]
        past_0 = (index >= end_0).astype(jnp.int32)
        past_1 = (index >= end_1).astype(jnp.int32)
        start = jnp.where(past_1 > 0, end_1, jnp.where(past_0 > 0, end_0, 0))
        return past_0 + past_1, start

    lane = lax.broadcasted_iota(jnp.int32, (rows, HEAD_SIZE), 1)
    half_lane = jnp.where(lane >= HEAD_SIZE // 2, lane - HEAD_SIZE // 2, lane).astype(F32)
    inverse = jnp.exp(half_lane * (-2.0 * math.log(THETA) / HEAD_SIZE))
    for which, mask, mask_t, key_count in ((0, bias_a, turned_a, half_rows), (1, bias_b, turned_b, 2 * half_rows)):
        index = lax.broadcasted_iota(jnp.int32, (rows, HEAD_SIZE), 0) + (row * rows + which * half_rows)
        _, start = segment_of(which, index)
        turn = (index - start).astype(F32) * inverse
        tables[0, which * rows : (which + 1) * rows, :] = jnp.cos(turn)
        sine = jnp.sin(turn)
        tables[1, which * rows : (which + 1) * rows, :] = jnp.where(lane >= HEAD_SIZE // 2, sine, -sine)
        at = lax.broadcasted_iota(jnp.int32, (rows, key_count), 0) + (row * rows + which * half_rows)
        keys = lax.broadcasted_iota(jnp.int32, (rows, key_count), 1)
        allowed = jnp.logical_and(segment_of(which, at)[0] == segment_of(which, keys)[0], keys <= at)
        mask[...] = jnp.where(allowed, 0.0, -1e30)
        at = lax.broadcasted_iota(jnp.int32, (key_count, rows), 1) + (row * rows + which * half_rows)
        keys = lax.broadcasted_iota(jnp.int32, (key_count, rows), 0)
        allowed = jnp.logical_and(segment_of(which, at)[0] == segment_of(which, keys)[0], keys <= at)
        mask_t[...] = jnp.where(allowed, 0.0, -1e30)

    kept_wait(gains_kept)
    for copy in gains_got:
        copy.wait_recv()
    keep(gains_v, gains_out)

    def normalise(value, which):
        scale = lax.rsqrt(jnp.sum(value * value, -1, keepdims=True) * (1.0 / width) + EPS)
        return [
            (value[:, j * piece : (j + 1) * piece] * scale * gains_v[j, which : which + 1, :]).astype(BF16)
            for j in range(4)
        ]

    def norm_rows(which):
        part = pl.ds(pl.multiple_of(which * rows, rows), rows)
        for j, block in enumerate(normalise(tok_v[part, :].astype(F32), 0)):
            normed[part, pl.ds(j * piece, piece)] = block

    norm_rows(col)
    for copy in out_got:
        copy.wait_recv()
    give(out_parts(z))
    y_start("gu", gu_source, gu_part)
    keep(gu_own, wgu_full.at[0])
    keep(wd_own, wd_full.at[:, pl.ds(0, piece)])
    in_far = z_second(in_side, in_parts, in_z)
    out_z = z_first(out_side)
    tokens_pair.wait_recv()
    keep(tok_v, tok_out)
    norm_rows(1 - col)
    cot_pair = to_pair(cotangents, cot_full.at[0])
    z_third(in_parts, in_far)
    for copy in shares:
        copy.wait_recv()
    shares.clear()
    keep(w_in, w_in_out)

    in_width = w_in.shape[2]

    def project(lanes, bias):
        weights = w_in[:, :, lanes]
        weights = weights.reshape(4 * weights.shape[1], weights.shape[2])
        return jnp.dot(normed[...], weights, preferred_element_type=F32) + bias

    def rotate(value):
        return value * tables[0] + pltpu.roll(value, HEAD_SIZE // 2, 1) * tables[1]

    key_value = project(slice(q_width, in_width), jnp.concatenate([bias_k[...].reshape(1, kv_width), bias_v[...].reshape(1, kv_width)], 1))
    kv[:, 0:kv_width] = rotate(key_value[:, 0:kv_width]).astype(BF16)
    kv[:, kv_width : 2 * kv_width] = key_value[:, kv_width : 2 * kv_width].astype(BF16)
    a_rows, b_rows = pl.ds(0, rows), pl.ds(rows, rows)
    high_spot = even(half_rows + row * rows, rows)
    a_got, b_got = [], []
    for step in (1, 2, 3):
        a_got.append(mail.post(kv.at[a_rows, :], kva.at[spot, :], along_y(place, step)))
    for step in range(4):
        b_got.append(mail.post(kv.at[a_rows, :], kvb.at[spot, :], near_of(place, (row + step) % 4)))
        if step:
            b_got.append(mail.post(kv.at[b_rows, :], kvb.at[high_spot, :], along_y(place, step)))
    kva[spot, :] = kv[a_rows, :]
    kvb[high_spot, :] = kv[b_rows, :]
    for first in range(0, q_width, 2 * HEAD_SIZE):
        value = project(slice(first, first + 2 * HEAD_SIZE), bias_q[first : first + 2 * HEAD_SIZE].reshape(1, 2 * HEAD_SIZE))
        for i in range(2):
            lanes = slice(first + i * HEAD_SIZE, first + (i + 1) * HEAD_SIZE)
            query[:, lanes] = rotate(value[:, i * HEAD_SIZE : (i + 1) * HEAD_SIZE]).astype(BF16)

    y_forward("gu", gu_part)
    y_share("gu", gu_part, near_gu, near)
    out_far = z_second(out_side, out_parts, out_z)
    heads = q_width // HEAD_SIZE
    factor = HEAD_SIZE ** (-0.5)

    def attend(half, keys, mask):
        part = slice(half * rows, (half + 1) * rows)

        @pl.loop(0, heads)
        def _(h):
            lanes = pl.ds(pl.multiple_of(h * HEAD_SIZE, LANES), HEAD_SIZE)
            raw = lax.dot_general(
                query[part, lanes], keys[:, 0:HEAD_SIZE], (((1,), (1,)), ((), ())), preferred_element_type=F32
            )
            scores = raw * factor + mask[...]
            peak = jnp.max(scores, -1, keepdims=True)
            raised = jnp.exp(scores - peak)
            total = jnp.sum(raised, -1, keepdims=True)
            probs = (raised * (1.0 / total)).astype(BF16)
            out = jnp.dot(probs, keys[:, HEAD_SIZE : 2 * HEAD_SIZE], preferred_element_type=F32)
            attended[part, lanes] = out.astype(BF16)
            logs[half * heads + h] = jnp.broadcast_to(peak + jnp.log(total), (rows, LANES)).T[0:8, :]

        for first in range(0, width, piece):
            lanes = slice(first, first + piece)
            branch[part, lanes] = jnp.dot(
                attended[part, :], w_out[:, lanes], preferred_element_type=F32
            ).astype(BF16)
        return mail.post(branch.at[part, :], branch_in.at[part, :], pair)

    def turn_over(source, target):
        for first in range(0, source.shape[1], LANES):
            target[first : first + LANES, :] = source[:, first : first + LANES].T

    def finish_half(half, copy):
        part = slice(half * rows, (half + 1) * rows)
        copy.wait_recv()
        value = tok_v[part, :].astype(F32) + (branch[part, :].astype(F32) + branch_in[part, :].astype(F32))
        middle[part, :] = value
        for j, block in enumerate(normalise(value, 1)):
            normed_ffn[part, j * piece : (j + 1) * piece] = block

    def z_part(slot, half):
        return cot_full.at[slot, pl.ds(half * rows, rows), :]

    def z_send():
        copies = {}
        for turn in range(2):
            copies["u", turn] = mail.post(z_part(0, turn), z_part(1, turn), up)
            copies["d", 1 - turn] = mail.post(z_part(0, 1 - turn), z_part(3, 1 - turn), down)
        return copies

    def z_forward(copies):
        copies["u", 0].wait_recv()
        far_up = mail.post(z_part(1, 0), z_part(2, 0), up)
        copies["d", 1].wait_recv()
        far_down = mail.post(z_part(3, 1), z_part(2, 1), down)
        return [copies["u", 1], copies["d", 0], far_up, far_down]

    cot_pair.wait_recv()
    cot_z = z_send()
    turn_over(normed, normed_t)
    for copy in a_got:
        copy.wait_recv()
    keep(kva, kva_out)
    z_third(out_parts, out_far)
    for copy in shares:
        copy.wait_recv()
    keep(w_out, w_out_out)
    swap_a = attend(0, kva, bias_a)
    for copy in b_got:
        copy.wait_recv()
    keep(kvb, kvb_out)
    y_start("wd", wd_source, wd_part)
    swap_b = attend(1, kvb, bias_b)
    y_end("gu", gu_part, near_gu, near)
    turn_over(attended, attended_t)
    for keys, target in ((kva, keys_a_t), (kvb, keys_b_t)):
        for first in range(0, keys.shape[0], LANES):
            target[:, first : first + LANES] = keys[first : first + LANES, 0:HEAD_SIZE].T
    finish_half(0, swap_a)
    y_forward("wd", wd_part)
    cot_last = z_forward(cot_z)
    y_share("wd", wd_part, twins, twin)
    finish_half(1, swap_b)
    for j, copy in zip((3, 1, 2), near_gu):
        copy.wait_recv()
        twins.append(mail.post(gu_whole(j), gu_whole(j), twin))
    y_end("wd", wd_part, twins, twin)
    for copy in cot_last:
        copy.wait_recv()
    for copy in twins:
        copy.wait_recv()
    for copy in kept:
        if copy is not None:
            copy.wait()
    mail.finish()


def ffn_kernel(
    normed,
    cot,
    wgu,
    wd,
    total,
    gu_sum,
    gu_late,
    dn_half,
    result_sum,
    result_ahead,
    x,
    cot_v,
    wgu_v,
    wd_v,
    gb,
    act,
    parts,
    turned,
    down_v,
    gu_in,
    dn_in,
    up1,
    down1,
    up2,
    down2,
    other,
    stage_up,
    stage_down,
    stage,
    res_up1,
    res_down1,
    res_up2,
    res_down2,
    gu_up1,
    gu_down1,
    gu_up2,
    gu_down2,
    send,
    recv,
    local,
):
    place = here()
    dp, row, col = place
    core = dp % 2
    up, down, pair, twin = along_z(place, 1), along_z(place, 3), pair_of(place), twin_of(place)
    right, left = along_y(place, 1), along_y(place, 3)
    meet([up, down, pair, twin, right, left])
    mail = Mail(send, recv)
    order = ((0, 0), (0, 1), (1, 0), (3, 1), (2, 0), (2, 1), (1, 1), (3, 0))
    spots = {half: i for i, half in enumerate(order)}
    rows = normed.shape[0] // 2
    size = rows // 2

    def block(ref, slot, half):
        return ref.at[pl.ds(spots[slot, half] * rows, rows), :]

    def halves(ref, half):
        return ref.at[pl.ds(half * rows, rows), :]

    kept = []

    def keep(source, target):
        kept.append(pltpu.make_async_copy(source, target, local.at[len(kept)]))
        kept[-1].start()
        return len(kept) - 1

    def kept_wait(index):
        kept[index].wait()
        kept[index] = None

    got = {}

    def z_start(which):
        got["u", which] = mail.post(halves(normed, which), block(x, 1, which), up)
        got["d", 1 - which] = mail.post(halves(normed, 1 - which), block(x, 3, 1 - which), down)

    z_start(0)
    share = wd.shape[0]
    early = [keep(normed, x.at[pl.ds(0, 2 * rows), :]), keep(wgu, wgu_v)]
    early.append(keep(cot.at[0], cot_v.at[pl.ds(0, 2 * rows), :]))
    early.append(keep(wd, wd_v))
    later = [keep(cot.at[slot, pl.ds(half * rows, rows), :], block(cot_v, slot, half)) for slot, half in order[2:]]
    width = normed.shape[1]
    piece = width // 4

    def dot_nt(left, right):
        return lax.dot_general(left, right, (((1,), (1,)), ((), ())), preferred_element_type=F32)

    def compute(c):
        part = slice(2 * rows * c, 2 * rows * (c + 1))
        for start, size in ((0, 512), (512, share - 512)):
            lanes, above = slice(start, start + size), slice(share + start, share + start + size)
            gate = jnp.dot(x[part, :], wgu_v[:, lanes], preferred_element_type=F32)
            value = jnp.dot(x[part, :], wgu_v[:, above], preferred_element_type=F32)
            grad = dot_nt(cot_v[part, :], wd_v[lanes, :])
            spread = 1.0 / (1.0 + jnp.exp(-gate))
            smooth = gate * spread
            act[part, lanes] = (smooth * value).astype(BF16)
            gb[part, lanes] = (grad * value * (spread * (1.0 + gate * (1.0 - spread)))).astype(BF16)
            gb[part, above] = (grad * smooth).astype(BF16)
        for m in range(3):
            lanes = slice(512 * m, 512 * (m + 1))
            parts[part, lanes] = dot_nt(gb[part, :], wgu_v[lanes, :]).astype(BF16)

    for index in early:
        kept_wait(index)
    compute(0)
    got["u", 0].wait_recv()
    far_up = mail.post(block(x, 1, 0), block(x, 2, 0), up)
    got["d", 1].wait_recv()
    far_down = mail.post(block(x, 3, 1), block(x, 2, 1), down)
    for index in later:
        kept_wait(index)
    compute(1)
    z_start(1)
    far_up.wait_recv()
    far_down.wait_recv()
    compute(2)
    first = {}
    for i in range(2):
        rows_i = pl.ds(i * size, size)
        first["u", i] = mail.post(block(parts, 2, 0).at[rows_i, :], up1.at[i], up)
        first["d", i] = mail.post(block(parts, 2, 1).at[rows_i, :], down1.at[i], down)
    got["u", 1].wait_recv()
    got["d", 0].wait_recv()
    compute(3)
    second = {
        ("d", 0): mail.post(block(parts, 1, 0), down2.at[0], down),
        ("u", 1): mail.post(block(parts, 3, 1), up2.at[1], up),
    }

    def turn_over(source, target):
        @pl.loop(0, source.shape[1] // LANES)
        def _(t):
            lanes = pl.ds(pl.multiple_of(t * LANES, LANES), LANES)
            target[lanes, :] = source[:, lanes].T

    def forward(i):
        rows_i = pl.ds(i * size, size)
        first["u", i].wait_recv()
        stage_up[i] = (block(parts, 3, 0).at[rows_i, :][...].astype(F32) + up1[i].astype(F32)).astype(BF16)
        second["u", 0, i] = mail.post(stage_up.at[i], up2.at[0, rows_i, :], up)
        first["d", i].wait_recv()
        stage_down[i] = (block(parts, 1, 1).at[rows_i, :][...].astype(F32) + down1[i].astype(F32)).astype(BF16)
        second["d", 1, i] = mail.post(stage_down.at[i], down2.at[1, rows_i, :], down)

    turn_over(x, turned)
    tile = 256
    tiles = 2 * share // tile

    def gu_tiles(first_tile, last_tile):
        @pl.loop(first_tile, last_tile)
        def _(n):
            lanes = pl.ds(pl.multiple_of(((n + (tiles // 2) * (1 - core)) % tiles) * tile, tile), tile)
            wgu_v[:, lanes] = jnp.dot(turned[...], gb[:, lanes], preferred_element_type=F32).astype(BF16)

    swaps = {}

    def settle(i):
        rows_i = pl.ds(i * size, size)
        if i == 0:
            second["d", 0].wait_recv()
            second["u", 1].wait_recv()
        second["u", 0, i].wait_recv()
        second["d", 1, i].wait_recv()
        for half in range(2):
            value = block(parts, 0, half).at[rows_i, :][...].astype(F32)
            value = value + up2[half, rows_i, :].astype(F32) + down2[half, rows_i, :].astype(F32)
            stage[half, rows_i, :] = value.astype(BF16)
            swaps[half, i] = mail.post(stage.at[half, rows_i, :], other.at[half, rows_i, :], pair)

    there = pl.ds(pl.multiple_of((1 - core) * share, LANES), share)
    mine = pl.ds(pl.multiple_of(core * share, LANES), share)
    gu_tiles(0, tiles // 2 + 1)
    shared = [
        mail.post(wgu_v.at[pl.ds(j * piece, piece), there], gu_in.at[j], twin) for j in range(4)
    ]
    forward(0)
    forward(1)
    gu_tiles(tiles // 2 + 1, tiles)
    for j in range(4):
        shared[j].wait_recv()
        gu_in[j] = (wgu_v[pl.ds(j * piece, piece), mine].astype(F32) + gu_in[j].astype(F32)).astype(BF16)

    def ring_y(i):
        height = piece // 3
        half = height // 2
        low, high = pl.ds(i * height, half), pl.ds(i * height + half, half)
        one, two, three, four = gu_up1.at[i], gu_down1.at[i], gu_up2.at[i], gu_down2.at[i]
        begin = (mail.post(gu_in.at[2, low, :], one, right), mail.post(gu_in.at[2, high, :], two, left))
        straight = [
            mail.post(gu_in.at[1, high, :], three.at[pl.ds(half, half), :], right),
            mail.post(gu_in.at[3, low, :], four.at[pl.ds(0, half), :], left),
        ]
        yield
        begin[0].wait_recv()
        one[...] = (gu_in[1, low, :].astype(F32) + one[...].astype(F32)).astype(BF16)
        straight.append(mail.post(one, three.at[pl.ds(0, half), :], right))
        begin[1].wait_recv()
        two[...] = (gu_in[3, high, :].astype(F32) + two[...].astype(F32)).astype(BF16)
        straight.append(mail.post(two, four.at[pl.ds(half, half), :], left))
        yield
        for copy in straight:
            copy.wait_recv()
        part = pl.ds(i * height, height)
        value = gu_in[0, part, :].astype(F32) + three[...].astype(F32) + four[...].astype(F32)
        gu_sum[part, :] = value.astype(BF16)
        yield

    rings = [ring_y(i) for i in range(2)]
    keep(gu_in.at[:, pl.ds(2 * (piece // 3), piece // 3), :], gu_late)
    for ring in rings:
        next(ring)
    for m in range(3):
        lanes = slice(512 * m, 512 * (m + 1))

        @pl.loop(0, 4)
        def _(c):
            part = pl.ds(pl.multiple_of(c * 2 * rows, 2 * rows), 2 * rows)
            down_v[part, lanes] = jnp.dot(act[part, :], wd_v[:, lanes], preferred_element_type=F32).astype(BF16)

    settle(0)
    settle(1)
    result = {
        "u1": mail.post(block(down_v, 2, 0), res_up1, up),
        "d1": mail.post(block(down_v, 2, 1), res_down1, down),
        "u2": mail.post(block(down_v, 3, 1), res_up2, up),
        "d2": mail.post(block(down_v, 1, 0), res_down2, down),
    }
    turn_over(act, turned)

    @pl.loop(0, width // tile)
    def _(n):
        lanes = pl.ds(pl.multiple_of(n * tile, tile), tile)
        wd_v[:, lanes] = jnp.dot(
            turned[0:share, :], cot_v[:, lanes], preferred_element_type=F32
        ).astype(BF16)

    half_share = share // 2
    rows_there = pl.ds(pl.multiple_of((1 - core) * half_share, 16), half_share)
    rows_mine = pl.ds(pl.multiple_of(core * half_share, 16), half_share)
    shared += [
        mail.post(wd_v.at[rows_there, pl.ds(j * piece, piece)], dn_in.at[j], twin) for j in range(4)
    ]
    for ring in rings:
        next(ring)
    for j in range(4):
        shared[4 + j].wait_recv()
        dn_in[j] = (wd_v[rows_mine, pl.ds(j * piece, piece)].astype(F32) + dn_in[j].astype(F32)).astype(BF16)
        keep(dn_in.at[j], dn_half.at[j])
    for half, i in ((0, 0), (1, 0), (0, 1), (1, 1)):
        rows_i = pl.ds(i * size, size)
        swaps[half, i].wait_recv()
        total[pl.ds(half * rows + i * size, size), :] = stage[half, rows_i, :].astype(F32) + other[
            half, rows_i, :
        ].astype(F32)
    next(rings[0])
    next(rings[1])
    for copy in result.values():
        copy.wait_recv()
    result_ahead[0] = (block(down_v, 3, 0)[...].astype(F32) + res_up1[...].astype(F32)).astype(BF16)
    result_ahead[1] = (block(down_v, 1, 1)[...].astype(F32) + res_down1[...].astype(F32)).astype(BF16)
    for half, theirs in ((0, res_down2), (1, res_up2)):
        value = block(down_v, 0, half)[...].astype(F32) + theirs[...].astype(F32)
        result_sum[pl.ds(half * rows, rows), :] = value.astype(BF16)
    for copy in kept:
        if copy is not None:
            copy.wait()
    mail.finish()


def back_kernel(
    total,
    middle,
    cot,
    gains,
    tok,
    normed,
    query,
    kv_a,
    kv_b,
    keys_a_t,
    keys_b_t,
    logs,
    attended,
    tables,
    turned_a,
    turned_b,
    w_in,
    w_out,
    gu,
    gl,
    dn,
    result_sum,
    ahead,
    gu_out,
    dn_out,
    in_out,
    kw_out,
    wo_out,
    grad_out,
    result_out,
    small_out,
    middle_v,
    cot_v,
    tok_v,
    normed_v,
    query_v,
    kva,
    kvb,
    kta,
    ktb,
    attended_v,
    turned_a_v,
    turned_b_v,
    w_in_v,
    w_out_v,
    gu_v,
    gl_v,
    dn_v,
    down_v,
    gain_rows,
    grad_middle,
    grad_low,
    grad_att,
    dkv_a,
    dkv_b,
    low_kv,
    own_kv,
    from_own,
    from_near,
    grad_pre,
    grad_part,
    grad_in,
    part_in,
    rows_out,
    result_rows,
    gu_n,
    gu_s,
    gl_up1,
    gl_down1,
    gl_up2,
    gl_down2,
    gl_y,
    dn_up1,
    dn_down1,
    dn_up2,
    dn_down2,
    dn_y,
    dn_n,
    dn_s,
    in_p,
    in_t,
    in_up1,
    in_down1,
    in_up2,
    in_down2,
    in_s,
    in_n,
    in_z,
    kw_p,
    kw_t,
    kw_up1,
    kw_down1,
    kw_up2,
    kw_down2,
    kw_s,
    kw_n,
    kw_z,
    wo_p,
    wo_t,
    wo_up1,
    wo_down1,
    wo_up2,
    wo_down2,
    wo_s,
    wo_n,
    wo_z,
    res_in,
    res_total,
    bias_own,
    gains_own,
    bias_in,
    gains_in,
    small_a,
    small_b,
    small_t,
    small_n,
    send,
    recv,
    local,
):
    place = here()
    dp, row, col = place
    core = dp % 2
    z = dp // Z_STEP
    twin, near, pair = twin_of(place), near_of(place), pair_of(place)
    up, down, far_z = along_z(place, 1), along_z(place, 3), along_z(place, 2)
    right, left = along_y(place, 1), along_y(place, 3)
    meet(
        [along_y(place, s) for s in (1, 2, 3)]
        + [near_of(place, (row + s) % 4) for s in range(4)]
        + [pair_of(place, (row + s) % 4) for s in range(4)]
        + [twin, up, down, far_z]
    )
    mail = Mail(send, recv)
    kept, arrivals = [], []

    def keep(source, target):
        kept.append(pltpu.make_async_copy(source, target, local.at[len(kept)]))
        kept[-1].start()
        return len(kept) - 1

    def kept_wait(index):
        if kept[index] is not None:
            kept[index].wait()
            kept[index] = None

    def even(start, size):
        return pl.ds(pl.multiple_of(start, 16), size)

    def plus(*values):
        result = values[0].astype(F32)
        for value in values[1:]:
            result = result + value.astype(F32)
        return result

    def dot_nt(left, right):
        return lax.dot_general(left, right, (((1,), (1,)), ((), ())), preferred_element_type=F32)

    rows = tok.shape[0] // 2
    width = tok.shape[1]
    piece = width // 4
    spot = even(row * rows, rows)
    own_rows, other_rows = even(col * rows, rows), even((1 - col) * rows, rows)

    def ffn_flow(i):
        if i < 2:
            height = gu.shape[0] // 2
            start = i * height
            theirs, done = gu_n.at[i], gu_s.at[i]
            mine = gu_v.at[pl.ds(start, height), :]
            swap = mail.post(gu.at[pl.ds(start, height), :], theirs, near)
            half = height // 2
            yield
            kept_wait(loads["gu"])
        else:
            if i == 2:
                held, loaded, name, height, start = gl, gl_v, "gl", gl.shape[1], 2 * gl.shape[1]
                mine, theirs, done = gl_y, gu_n.at[2], gu_s.at[2]
                one, two, three, four = gl_up1, gl_down1, gl_up2, gl_down2
            else:
                held, loaded, name, height, start = dn, dn_v, "dn", dn.shape[1], 0
                mine, theirs, done = dn_y, dn_n, dn_s
                one, two, three, four = dn_up1, dn_down1, dn_up2, dn_down2
            half = height // 2
            low, high = pl.ds(0, half), pl.ds(half, half)
            first = (mail.post(held.at[2, low, :], one, right), mail.post(held.at[2, high, :], two, left))
            straight = (
                mail.post(held.at[1, high, :], three.at[high, :], right),
                mail.post(held.at[3, low, :], four.at[low, :], left),
            )
            yield
            kept_wait(loads[name])
            first[0].wait_recv()
            one[...] = plus(loaded[1, low, :], one[...]).astype(BF16)
            last = [mail.post(one, three.at[low, :], right)]
            first[1].wait_recv()
            two[...] = plus(loaded[3, high, :], two[...]).astype(BF16)
            last.append(mail.post(two, four.at[high, :], left))
            yield
            for copy in straight + tuple(last):
                copy.wait_recv()
            mine[...] = plus(loaded[0], three[...], four[...]).astype(BF16)
            swap = mail.post(mine, theirs, near)
            yield
        swap.wait_recv()
        done[...] = plus(mine[...], theirs[...]).astype(BF16)

        def room(slot, which=None):
            begin, size = (start, height) if which is None else (start + which * half, half)
            if i < 3:
                share = gu_out.shape[2] // 4
                lanes = pl.ds(pl.multiple_of(slot * share, LANES), share)
                return gu_out.at[core, pl.ds(begin, size), lanes]
            return dn_out.at[even((slot * 2 + core) * height + begin, size), :]

        posts = {}
        for turn in range(2):
            for name, device, which in (("u", up, turn), ("d", down, 1 - turn)):
                posts[name, which] = mail.post(done.at[pl.ds(which * half, half), :], room(z, which), device)
        keep(done, room(z))
        arrivals.append(mail.post(done, room(z), twin))
        yield
        posts["u", 0].wait_recv()
        block = room((z + 3) % 4, 0)
        one_more = mail.post(block, block, up)
        posts["d", 1].wait_recv()
        block = room((z + 1) % 4, 1)
        two_more = mail.post(block, block, down)
        yield
        posts["u", 1].wait_recv()
        block = room((z + 3) % 4)
        arrivals.append(mail.post(block, block, twin))
        posts["d", 0].wait_recv()
        block = room((z + 1) % 4)
        arrivals.append(mail.post(block, block, twin))
        one_more.wait_recv()
        two_more.wait_recv()
        block = room((z + 2) % 4)
        arrivals.append(mail.post(block, block, twin))
        yield

    def weight_flow(part, t, up1, down1, up2, down2, total_h, theirs, quarter, out):
        height = t.shape[1]
        half = height // 2
        low, high = pl.ds(0, half), pl.ds(half, half)
        copy = mail.post(part.at[:, even((1 - core) * height, height), :], t, twin)
        yield
        copy.wait_recv()
        for j in range(4):
            t[j] = plus(part[j, even(core * height, height), :], t[j]).astype(BF16)
        first = (mail.post(t.at[2, low, :], up1, right), mail.post(t.at[2, high, :], down1, left))
        straight = (
            mail.post(t.at[1, high, :], up2.at[high, :], right),
            mail.post(t.at[3, low, :], down2.at[low, :], left),
        )
        yield
        first[0].wait_recv()
        up1[...] = plus(t[1, low, :], up1[...]).astype(BF16)
        last = [mail.post(up1, up2.at[low, :], right)]
        first[1].wait_recv()
        down1[...] = plus(t[3, high, :], down1[...]).astype(BF16)
        last.append(mail.post(down1, down2.at[high, :], left))
        yield
        for copy in straight + tuple(last):
            copy.wait_recv()
        total_h[...] = plus(t[0], up2[...], down2[...]).astype(BF16)
        swap = mail.post(total_h, theirs, near)
        yield
        swap.wait_recv()
        t[0] = plus(total_h[...], theirs[...]).astype(BF16)
        size = height // 4
        copies = []
        for step, device in ((1, up), (3, down), (2, far_z)):
            source = t.at[0, even(((z + step) % 4) * size, size), :]
            copies.append(mail.post(source, quarter.at[step - 1], device))
        yield
        for copy in copies:
            copy.wait_recv()
        mine = even(z * size, size)
        theirs[0:size, :] = plus(t[0, mine, :], quarter[0], quarter[1], quarter[2]).astype(BF16)
        place_of = lambda owner: out.at[even(core * height + owner * size, size), :]
        copies = [mail.post(theirs.at[0:size, :], place_of(z), device) for device in (up, down, far_z)]
        arrivals.append(mail.post(theirs.at[0:size, :], place_of(z), twin))
        keep(theirs.at[0:size, :], place_of(z))
        yield
        for copy in copies:
            copy.wait_recv()
        for step in (1, 2, 3):
            block = place_of((z + step) % 4)
            arrivals.append(mail.post(block, block, twin))
        yield

    def result_flow():
        copies = (mail.post(ahead.at[0], res_in.at[0], up), mail.post(ahead.at[1], res_in.at[1], down))
        yield
        kept_wait(loads["down"])
        for half, copy in enumerate(copies):
            copy.wait_recv()
            part = pl.ds(half * rows, rows)
            res_total[part, :] = plus(down_v[part, :], res_in[half]).astype(BF16)
        swap = mail.post(res_total.at[other_rows, :], part_in, pair)
        yield
        swap.wait_recv()
        result_rows[...] = (middle_v[own_rows, :] + plus(res_total[own_rows, :], part_in[...])).astype(BF16)
        yield
        spread(result_rows, result_out)
        yield

    def spread(source, target):
        for step in range(4):
            lanes = pl.ds(step * piece, piece)
            if step:
                arrivals.append(mail.post(source.at[:, lanes], target.at[spot, :], along_y(place, step)))
            else:
                keep(source.at[:, lanes], target.at[spot, :])

    flows = [ffn_flow(i) for i in range(4)]
    loads = {}
    for name, source, target in (
        ("middle", middle, middle_v),
        ("cot", cot.at[0], cot_v),
        ("w_out", w_out, w_out_v),
        ("attended", attended, attended_v),
        ("query", query, query_v),
        ("kva", kv_a, kva),
        ("kvb", kv_b, kvb),
        ("kta", keys_a_t, kta),
        ("ktb", keys_b_t, ktb),
        ("ta", turned_a, turned_a_v),
        ("tb", turned_b, turned_b_v),
        ("gu", gu, gu_v),
        ("w_in", w_in, w_in_v),
        ("normed", normed, normed_v),
        ("tok", tok, tok_v),
        ("dn", dn, dn_v),
        ("gl", gl, gl_v),
        ("down", result_sum, down_v),
    ):
        loads[name] = keep(source, target)
    result_steps = result_flow()
    next(flows[3])
    next(flows[1])
    for j in range(4):
        gain_rows[:, j * piece : (j + 1) * piece] = gains[j]

    def norm_back(stream, gain, incoming):
        scale = lax.rsqrt(jnp.sum(stream * stream, -1, keepdims=True) * (1.0 / width) + EPS)
        scaled = incoming * gain
        inner = jnp.sum(scaled * stream, -1, keepdims=True) * (1.0 / width)
        back = scale * scaled - stream * (scale * scale * scale * inner)
        return back, jnp.sum(incoming * stream * scale, 0, keepdims=True)

    kept_wait(loads["middle"])
    kept_wait(loads["cot"])
    gain_ffn_part = jnp.zeros((1, width), F32)
    for half in range(2):
        part = slice(half * rows, (half + 1) * rows)
        back, gain_part = norm_back(middle_v[part, :], gain_rows[1:2, :], total[part, :])
        value = cot_v[part, :].astype(F32) + back
        grad_middle[part, :] = value
        grad_low[part, :] = value.astype(BF16)
        gain_ffn_part = gain_ffn_part + gain_part
    gains_own[...] = jnp.zeros_like(gains_own)
    for j in range(4):
        gains_own[j, 1:2, :] = 0.5 * gain_ffn_part[:, j * piece : (j + 1) * piece]
    next(result_steps)
    kept_wait(loads["w_out"])
    q_width = w_out.shape[0]
    for first in range(0, q_width, 256):
        lanes = slice(first, first + 256)
        grad_att[:, lanes] = dot_nt(grad_low[...], w_out_v[lanes, :]).astype(BF16)

    kept_wait(loads["attended"])
    for j in range(4):
        wo_p[j] = jnp.dot(
            attended_v[...], grad_low[:, j * piece : (j + 1) * piece], preferred_element_type=F32
        ).astype(BF16)
    wo_steps = weight_flow(wo_p, wo_t, wo_up1, wo_down1, wo_up2, wo_down2, wo_s, wo_n, wo_z, wo_out)

    for name in ("query", "kva", "kvb", "kta", "ktb", "ta", "tb"):
        kept_wait(loads[name])
    heads = q_width // HEAD_SIZE
    factor = HEAD_SIZE ** (-0.5)

    def unrotate(value, half):
        part = slice(half * rows, (half + 1) * rows)
        return value * tables[0, part, :] + pltpu.roll(value * tables[1, part, :], HEAD_SIZE // 2, 1)

    def attend_back(half, keys, keys_t, mask, sums):
        part = slice(half * rows, (half + 1) * rows)
        sums[...] = jnp.zeros_like(sums)

        @pl.loop(0, heads)
        def _(h):
            lanes = pl.ds(pl.multiple_of(h * HEAD_SIZE, LANES), HEAD_SIZE)
            one, grad = query_v[part, lanes], grad_att[part, lanes]
            raw = dot_nt(keys[:, 0:HEAD_SIZE], one)
            probs = jnp.exp(raw * factor + mask[...] - logs[half * heads + h, 0:1, :])
            grad_probs = dot_nt(keys[:, HEAD_SIZE : 2 * HEAD_SIZE], grad)
            inner = jnp.sum(grad_probs * probs, 0, keepdims=True)
            grad_scores = (probs * (grad_probs - inner)).astype(BF16)
            sums[:, 0:HEAD_SIZE] += jnp.dot(grad_scores, one, preferred_element_type=F32)
            sums[:, HEAD_SIZE : 2 * HEAD_SIZE] += jnp.dot(probs.astype(BF16), grad, preferred_element_type=F32)
            grad_query = jnp.dot(keys_t[...], grad_scores, preferred_element_type=F32).T * factor
            grad_pre[part, lanes] = unrotate(grad_query, half).astype(BF16)

    def low_sums(sums, part):
        return (sums[part, 0:HEAD_SIZE] * factor).astype(BF16), sums[part, HEAD_SIZE : 2 * HEAD_SIZE].astype(BF16)

    next(wo_steps)
    next(flows[1])
    next(flows[2])
    next(result_steps)
    next(flows[1])
    next(flows[3])
    attend_back(1, kvb, ktb, turned_b_v, dkv_b)
    half_rows = kva.shape[0]
    low_part, high_part = slice(0, half_rows), slice(half_rows, 2 * half_rows)
    for target, sums, part in ((low_kv, dkv_b, low_part), (own_kv.at[1], dkv_b, high_part)):
        target[:, 0:HEAD_SIZE], target[:, HEAD_SIZE : 2 * HEAD_SIZE] = low_sums(sums, part)
    kv_got = []
    for step in range(4):
        other = (row + step) % 4
        part = even(other * rows, rows)
        kv_got.append(mail.post(low_kv.at[part, :], from_near.at[step], near_of(place, other)))
        if step:
            kv_got.append(mail.post(own_kv.at[1, part, :], from_own.at[step - 1, 1], along_y(place, step)))
    next(flows[0])
    attend_back(0, kva, kta, turned_a_v, dkv_a)
    target = own_kv.at[0]
    target[:, 0:HEAD_SIZE], target[:, HEAD_SIZE : 2 * HEAD_SIZE] = low_sums(dkv_a, low_part)
    for step in (1, 2, 3):
        part = even(((row + step) % 4) * rows, rows)
        kv_got.append(mail.post(own_kv.at[0, part, :], from_own.at[step - 1, 0], along_y(place, step)))
    next(flows[2])
    next(flows[3])
    next(wo_steps)
    kept_wait(loads["normed"])
    for j in range(4):
        in_p[j] = jnp.dot(
            normed_v[j * piece : (j + 1) * piece, :], grad_pre[:, 0:q_width], preferred_element_type=F32
        ).astype(BF16)
    in_steps = weight_flow(in_p, in_t, in_up1, in_down1, in_up2, in_down2, in_s, in_n, in_z, in_out)
    next(flows[3])
    next(flows[2])
    next(flows[0])
    next(in_steps)
    for copy in kv_got:
        copy.wait_recv()
    for half in range(2):
        part = slice(half * rows, (half + 1) * rows)
        value = own_kv[half, spot, :].astype(F32)
        for step in range(3):
            value = value + from_own[step, half].astype(F32)
        if half == 0:
            for step in range(4):
                value = value + from_near[step].astype(F32)
        grad_pre[part, q_width : q_width + HEAD_SIZE] = unrotate(value[:, 0:HEAD_SIZE], half).astype(BF16)
        grad_pre[part, q_width + HEAD_SIZE : q_width + 2 * HEAD_SIZE] = value[:, HEAD_SIZE : 2 * HEAD_SIZE].astype(
            BF16
        )
    next(wo_steps)
    next(in_steps)
    kept_wait(loads["w_in"])
    for j in range(4):
        grad_part[:, j * piece : (j + 1) * piece] = dot_nt(grad_pre[...], w_in_v[j]).astype(BF16)
    swap = mail.post(grad_part.at[other_rows, :], grad_in, pair)
    for j in range(4):
        kw_p[j] = jnp.dot(
            normed_v[j * piece : (j + 1) * piece, :], grad_pre[:, q_width:], preferred_element_type=F32
        ).astype(BF16)
    kw_steps = weight_flow(kw_p, kw_t, kw_up1, kw_down1, kw_up2, kw_down2, kw_s, kw_n, kw_z, kw_out)
    next(wo_steps)
    next(flows[2])
    next(kw_steps)
    next(result_steps)
    next(in_steps)
    next(kw_steps)
    bias_own[...] = jnp.zeros_like(bias_own)
    bias_own[0:1, :] = jnp.sum(grad_pre[...].astype(F32), 0, keepdims=True)
    next(wo_steps)
    kept_wait(loads["tok"])
    swap.wait_recv()
    back, gain_part = norm_back(
        tok_v[own_rows, :].astype(F32), gain_rows[0:1, :], plus(grad_part[own_rows, :], grad_in[...])
    )
    rows_out[...] = (grad_middle[own_rows, :] + back).astype(BF16)
    for j in range(4):
        gains_own[j, 0:1, :] = gain_part[:, j * piece : (j + 1) * piece]
    next(in_steps)
    next(flows[2])
    next(kw_steps)
    next(wo_steps)
    small_copies, small_kept = [], []
    for step in range(4):
        device = along_y(place, step)
        mine = gains_in.at[col * 4 + row]
        if step:
            small_copies.append(mail.post(bias_own, bias_in.at[row], device))
            small_copies.append(mail.post(gains_own.at[step], mine, device))
        else:
            small_kept.append(keep(bias_own, bias_in.at[row]))
            small_kept.append(keep(gains_own.at[step], mine))
        small_copies.append(mail.post(gains_own.at[step], mine, pair_of(place, (row + step) % 4)))
    spread(rows_out, grad_out)
    next(kw_steps)
    next(in_steps)
    for copy in small_copies:
        copy.wait_recv()
    for index in small_kept:
        kept_wait(index)
    small_a[...] = jnp.zeros_like(small_a)
    small_a[0:8, :] = bias_in[0] + bias_in[1] + bias_in[2] + bias_in[3]
    small_a[8:16, 0:piece] = (
        gains_in[0] + gains_in[1] + gains_in[2] + gains_in[3] + gains_in[4] + gains_in[5] + gains_in[6] + gains_in[7]
    )
    small_first = mail.post(small_a, small_t, twin)
    next(result_steps)
    next(kw_steps)
    small_first.wait_recv()
    small_b[...] = small_a[...] + small_t[...]
    small_second = mail.post(small_b, small_n, near)
    next(in_steps)
    next(flows[2])
    small_second.wait_recv()
    small_t[...] = small_b[...] + small_n[...]
    for device in (up, down, far_z):
        arrivals.append(mail.post(small_t, small_out.at[z], device))
    keep(small_t, small_out.at[z])
    next(wo_steps)
    next(kw_steps)
    next(in_steps)
    for steps in [*flows, wo_steps, in_steps, kw_steps, result_steps]:
        for _ in steps:
            pass
    for copy in arrivals:
        copy.wait_recv()
    for copy in kept:
        if copy is not None:
            copy.wait()
    mail.finish()


def widen_kernel(gate_up, down, w_in, w_kv, w_out, result, tokens, small, *outs):
    result_w, tokens_w, query_w, key_w, value_w, out_w, gate_w, up_w, down_w, *flat = outs
    total = small[0] + small[1] + small[2] + small[3]
    start = 0
    for line, out in zip((0, 0, 0, 8, 9), flat):
        start = 0 if line else start
        out[...] = total[line, start : start + out.shape[0]]
        start += out.shape[0]
    result_w[...] = result[...].astype(F32)
    tokens_w[...] = tokens[...].astype(F32)
    query_w[...] = w_in[...].astype(F32)
    key_w[...] = w_kv[:, : key_w.shape[1]].astype(F32)
    value_w[...] = w_kv[:, key_w.shape[1] :].astype(F32)
    out_w[...] = w_out[...].astype(F32)
    gate_w[...] = gate_up[0, :, : gate_w.shape[1]].astype(F32)
    up_w[...] = gate_up[1, :, : up_w.shape[1]].astype(F32)
    down_w[...] = down[...].astype(F32)


def on_device(
    tokens,
    cotangent,
    lengths,
    gain_attn,
    w_query,
    key_projection,
    value_projection,
    bias_query,
    key_bias_vector,
    value_bias_vector,
    w_out,
    gain_ffn,
    w_gate,
    w_up,
    w_down,
):
    half_rows, piece = tokens.shape
    width = 4 * piece
    rows = half_rows // 4
    q_width = w_query.shape[1]
    kv_width = key_projection.shape[1]
    heads = q_width // HEAD_SIZE
    hidden = w_gate.shape[1]
    share = -(-hidden // (4 * LANES)) * LANES

    in_width = q_width + 2 * kv_width
    thin = piece // 2
    (
        tok_rows,
        cot_full,
        gains4,
        normed_t,
        query,
        kv_a,
        kv_b,
        logs,
        attended_t,
        tables,
        middle,
        mask_a,
        mask_b,
        normed_ffn,
        w_in_full,
        w_out_full,
        w_gu_full,
        w_down_full,
        keys_a_t,
        keys_b_t,
    ) = talk(
        front_kernel,
        0,
        FRONT_COPIES,
        FRONT_LOCAL,
        [
            ((2 * rows, width), BF16),
            ((4, 2 * rows, width), BF16),
            ((4, 8, piece), F32),
            ((width, 2 * rows), BF16),
            ((2 * rows, q_width), BF16),
            ((half_rows, 2 * kv_width), BF16),
            ((2 * half_rows, 2 * kv_width), BF16),
            ((2 * heads, 8, rows), F32),
            ((q_width, 2 * rows), BF16),
            ((2, 2 * rows, HEAD_SIZE), F32),
            ((2 * rows, width), F32),
            ((half_rows, rows), F32),
            ((2 * half_rows, rows), F32),
            ((2 * rows, width), BF16),
            ((4, piece, in_width), BF16),
            ((q_width, width), BF16),
            ((4, 2, thin, 2 * share), BF16),
            ((share, width), BF16),
            ((HEAD_SIZE, half_rows), BF16),
            ((HEAD_SIZE, 2 * half_rows), BF16),
        ],
        [ANY] * 2 + [VMEM] * 6 + [ANY] * 7,
        [ANY] * 3 + [VMEM] * 2 + [ANY] * 2 + [VMEM] * 7 + [ANY] * 4 + [VMEM] * 2,
        [
            pltpu.VMEM((2 * rows, width), BF16),
            pltpu.VMEM((2 * rows, q_width), BF16),
            pltpu.VMEM((8, LANES), jnp.int32),
            pltpu.VMEM((8, piece), F32),
            pltpu.VMEM((2 * rows, width), BF16),
            pltpu.VMEM((2, 8, LANES), jnp.int32),
            pltpu.VMEM((4, 8, piece), F32),
            pltpu.VMEM((4, piece, in_width), BF16),
            pltpu.VMEM((q_width, width), BF16),
            pltpu.VMEM((2, thin, 2 * share), BF16),
            pltpu.VMEM((share, piece), BF16),
            pltpu.VMEM((thin, LANES), BF16),
            pltpu.VMEM((LANES, piece), BF16),
            pltpu.VMEM((2 * rows, 2 * kv_width), BF16),
            pltpu.VMEM((half_rows, 2 * kv_width), BF16),
            pltpu.VMEM((2 * half_rows, 2 * kv_width), BF16),
            pltpu.VMEM((rows, half_rows), F32),
            pltpu.VMEM((rows, 2 * half_rows), F32),
            pltpu.VMEM((2 * rows, width), BF16),
            pltpu.VMEM((2 * rows, width), BF16),
        ],
        limit=56,
    )(
        tokens,
        cotangent,
        lengths,
        gain_attn,
        gain_ffn,
        bias_query,
        key_bias_vector,
        value_bias_vector,
        w_query,
        key_projection,
        value_projection,
        w_out,
        w_gate,
        w_up,
        w_down,
    )

    w_both_full = w_gu_full.reshape(width, 2 * share)
    half_block = (2, rows, width)
    grad_normed_ffn, both_sum, both_late, down_half, result_sum, result_ahead = talk(
        ffn_kernel,
        4,
        44,
        15,
        [
            ((2 * rows, width), F32),
            ((2 * piece // 3, share), BF16),
            ((4, piece // 3, share), BF16),
            ((4, share // 2, piece), BF16),
            ((2 * rows, width), BF16),
            ((2, rows, width), BF16),
        ],
        [ANY] * 4,
        [VMEM, VMEM, ANY, ANY, VMEM, VMEM],
        [
            pltpu.VMEM(shape, BF16)
            for shape in (
                (8 * rows, width),
                (8 * rows, width),
                (width, 2 * share),
                (share, width),
                (8 * rows, 2 * share),
                (8 * rows, share),
                (8 * rows, width),
                (width, 8 * rows),
                (8 * rows, width),
                (4, piece, share),
                (4, share // 2, piece),
                (2, rows // 2, width),
                (2, rows // 2, width),
                half_block,
                half_block,
                half_block,
                (2, rows // 2, width),
                (2, rows // 2, width),
                half_block,
                (rows, width),
                (rows, width),
                (rows, width),
                (rows, width),
                (2, piece // 6, share),
                (2, piece // 6, share),
                (2, piece // 3, share),
                (2, piece // 3, share),
            )
        ],
        limit=60,
    )(normed_ffn, cot_full, w_both_full, w_down_full)
    thirds = piece // 3
    q_half, w_half = (thin, q_width), (q_width // 2, piece)
    gu_chunk, dn_chunk = (3, thirds, share), (share // 2, piece)

    def halved(shape):
        return (*shape[:-2], shape[-2] // 2, shape[-1])

    def weight_scratch(shape):
        return [
            (4, 2 * shape[0], shape[1]),
            (4, *shape),
            halved(shape),
            halved(shape),
            shape,
            shape,
            shape,
            shape,
            (3, shape[0] // 4, shape[1]),
        ]

    def scratch(kind, *shapes):
        return [pltpu.VMEM(shape, kind) for shape in shapes]

    gate_up, down_all, in_total, kv_total, out_total, grad_tokens, result, small_all = talk(
        back_kernel,
        8,
        BACK_COPIES,
        BACK_LOCAL,
        [
            ((2, piece, 4 * share), BF16),
            ((4 * share, piece), BF16),
            ((piece, q_width), BF16),
            ((piece, 2 * kv_width), BF16),
            ((q_width, piece), BF16),
            ((half_rows, piece), BF16),
            ((half_rows, piece), BF16),
            ((4, 16, in_width), F32),
        ],
        [VMEM, ANY, ANY, VMEM] + [ANY] * 7 + [VMEM, ANY, VMEM] + [ANY] * 9,
        [ANY] * 8,
        scratch(F32, (2 * rows, width))
        + scratch(
            BF16,
            (2 * rows, width),
            (2 * rows, width),
            (width, 2 * rows),
            (2 * rows, q_width),
            (half_rows, 2 * kv_width),
            (2 * half_rows, 2 * kv_width),
            (HEAD_SIZE, half_rows),
            (HEAD_SIZE, 2 * half_rows),
            (q_width, 2 * rows),
        )
        + scratch(F32, (half_rows, rows), (2 * half_rows, rows))
        + scratch(
            BF16,
            (4, piece, in_width),
            (q_width, width),
            (2 * thirds, share),
            (4, thirds, share),
            (4, share // 2, piece),
            (2 * rows, width),
        )
        + scratch(F32, (8, width), (2 * rows, width))
        + scratch(BF16, (2 * rows, width), (2 * rows, q_width))
        + scratch(F32, (half_rows, 2 * kv_width), (2 * half_rows, 2 * kv_width))
        + scratch(
            BF16,
            (half_rows, 2 * kv_width),
            (2, half_rows, 2 * kv_width),
            (3, 2, rows, 2 * kv_width),
            (4, rows, 2 * kv_width),
            (2 * rows, in_width),
            (2 * rows, width),
            (rows, width),
            (rows, width),
            (rows, width),
            (rows, width),
            gu_chunk,
            gu_chunk,
            halved((thirds, share)),
            halved((thirds, share)),
            (thirds, share),
            (thirds, share),
            (thirds, share),
            halved(dn_chunk),
            halved(dn_chunk),
            dn_chunk,
            dn_chunk,
            dn_chunk,
            dn_chunk,
            dn_chunk,
            *weight_scratch(q_half),
            *weight_scratch((thin, 2 * kv_width)),
            *weight_scratch(w_half),
            (2, rows, width),
            (2 * rows, width),
        )
        + scratch(F32, (8, in_width), (4, 8, piece), (4, 8, in_width), (8, 8, piece))
        + scratch(F32, *[(16, in_width)] * 4),
        limit=60,
    )(
        grad_normed_ffn,
        middle,
        cot_full,
        gains4,
        tok_rows,
        normed_t,
        query,
        kv_a,
        kv_b,
        keys_a_t,
        keys_b_t,
        logs,
        attended_t,
        tables,
        mask_a,
        mask_b,
        w_in_full,
        w_out_full,
        both_sum,
        both_late,
        down_half,
        result_sum,
        result_ahead,
    )
    steps = 8
    narrow = [gate_up, down_all, in_total, kv_total, out_total, result, grad_tokens, small_all]
    lines = [(q_width,), (kv_width,), (kv_width,), (piece,), (piece,)]
    wide = [
        (half_rows, piece),
        (half_rows, piece),
        (piece, q_width),
        (piece, kv_width),
        (piece, kv_width),
        (q_width, piece),
        (piece, hidden),
        (piece, hidden),
        (hidden, piece),
    ]

    def in_block(array):
        if array is small_all:
            return pl.BlockSpec(array.shape, lambda i: (0, 0, 0))
        if array.ndim == 3:
            return pl.BlockSpec((2, array.shape[1] // steps, array.shape[2]), lambda i: (0, i, 0))
        if array is down_all:
            return pl.BlockSpec((hidden // steps, piece), lambda i: (i, 0))
        return pl.BlockSpec((array.shape[0] // steps, array.shape[1]), lambda i: (i, 0))

    wide_out = pl.pallas_call(
        widen_kernel,
        grid=(steps,),
        out_shape=[jax.ShapeDtypeStruct(shape, F32) for shape in wide + lines],
        in_specs=[in_block(array) for array in narrow],
        out_specs=[pl.BlockSpec((shape[0] // steps, shape[1]), lambda i: (i, 0)) for shape in wide]
        + [pl.BlockSpec(shape, lambda i: (0,)) for shape in lines],
        compiler_params=pltpu.CompilerParams(vmem_limit_bytes=60 << 20),
    )(*narrow)
    result_w, tokens_w, query_w, key_w, value_w, out_w, gate_w, up_w, down_w, *flat = wide_out
    bias_q, bias_k, bias_v, gain_one, gain_two = flat
    return (
        result_w,
        tokens_w,
        gain_one,
        query_w,
        key_w,
        value_w,
        bias_q,
        bias_k,
        bias_v,
        out_w,
        gain_two,
        gate_w,
        up_w,
        down_w,
    )


def solution(mesh):
    placed = (
        P(("dp", "col"), "row"),
        P(("dp", "col"), "row"),
        P("dp", None),
        P("row"),
        P("row", "col"),
        P("row", "col"),
        P("row", "col"),
        P("col"),
        P("col"),
        P("col"),
        P("col", "row"),
        P("row"),
        P("row", "col"),
        P("row", "col"),
        P("col", "row"),
    )
    return jax.shard_map(
        on_device,
        mesh=mesh,
        in_specs=placed,
        out_specs=(
            P(("dp", "col"), "row"),
            P(("dp", "col"), "row"),
            P("row"),
            P("row", "col"),
            P("row", "col"),
            P("row", "col"),
            P("col"),
            P("col"),
            P("col"),
            P("col", "row"),
            P("row"),
            P("row", "col"),
            P("row", "col"),
            P("col", "row"),
        ),
        check_vma=False,
    )
```

```python
import math

import jax
import jax.numpy as jnp
from jax import lax
from jax.experimental import pallas as pl
from jax.experimental.pallas import tpu as pltpu
from jax.sharding import PartitionSpec as P

HEAD_SIZE = 128
EPS = 1e-06
THETA = 1000000.0
LANES = 128
MESH = pl.DeviceIdType.MESH
BF16 = jnp.bfloat16
F32 = jnp.float32
ANY = pl.BlockSpec(memory_space=pl.ANY)
VMEM = pl.BlockSpec(memory_space=pltpu.VMEM)

Z_STEP = 4
FRONT_COPIES = 77
FRONT_LOCAL = 27
BACK_COPIES = 145
BACK_LOCAL = 28


def here():
    return lax.axis_index("dp"), lax.axis_index("row"), lax.axis_index("col")


def flip_near(dp):
    return dp + 2 - 4 * ((dp // 2) % 2)


def pair_of(place, row=None):
    dp, own, col = place
    return flip_near(dp), own if row is None else row, 1 - col


def near_of(place, row=None):
    dp, own, col = place
    return flip_near(dp), own if row is None else row, col


def twin_of(place):
    dp, row, col = place
    return dp + 1 - 2 * (dp % 2), row, col


def along_z(place, step):
    dp, row, col = place
    return (dp + Z_STEP * step) % (4 * Z_STEP), row, col


def along_y(place, step):
    dp, row, col = place
    return dp, (row + step) % 4, col


def meet(peers):
    barrier = pltpu.get_barrier_semaphore()
    for peer in peers:
        pl.semaphore_signal(barrier, inc=1, device_id=peer, device_id_type=MESH)
    pl.semaphore_wait(barrier, len(peers))


class Mail:
    def __init__(self, send, recv):
        self.send, self.recv, self.count, self.sent = send, recv, 0, []

    def post(self, source, target, device):
        index = self.count
        self.count += 1
        copy = pltpu.make_async_remote_copy(
            src_ref=source,
            dst_ref=target,
            send_sem=self.send.at[index],
            recv_sem=self.recv.at[index],
            device_id=device,
            device_id_type=MESH,
        )
        copy.start()
        self.sent.append(copy)
        return copy

    def finish(self):
        assert self.count == self.send.shape[0], (self.count, self.send.shape)
        for copy in self.sent:
            copy.wait_send()


def talk(body, ident, copies, local, outs, in_specs, out_specs, scratch=(), limit=32):
    return pl.pallas_call(
        body,
        out_shape=[jax.ShapeDtypeStruct(*out) for out in outs],
        in_specs=in_specs,
        out_specs=out_specs,
        scratch_shapes=[
            *scratch,
            pltpu.SemaphoreType.DMA((copies,)),
            pltpu.SemaphoreType.DMA((copies,)),
            pltpu.SemaphoreType.DMA((max(local, 1),)),
        ],
        compiler_params=pltpu.CompilerParams(
            collective_id=ident, has_side_effects=True, vmem_limit_bytes=limit << 20
        ),
    )


def front_kernel(
    tok,
    cot,
    lens_in,
    gain_attn,
    gain_ffn,
    bias_q,
    bias_k,
    bias_v,
    wq,
    wk,
    wv,
    wo,
    wg,
    wu,
    wd,
    tok_out,
    cot_full,
    gains_out,
    normed,
    query,
    kva_out,
    kvb_out,
    logs,
    attended,
    tables,
    middle,
    turned_a,
    turned_b,
    normed_ffn,
    w_in_out,
    w_out_out,
    wgu_full,
    wd_full,
    lens,
    gains,
    tok_v,
    lens_v,
    gains_v,
    w_in,
    w_out,
    gu_own,
    wd_own,
    blank_gu,
    blank_wd,
    kv,
    kva,
    kvb,
    bias_a,
    bias_b,
    branch,
    branch_in,
    send,
    recv,
    local,
):
    place = here()
    dp, row, col = place
    z, core = dp // Z_STEP, dp % 2
    twin, pair, up, down = twin_of(place), pair_of(place), along_z(place, 1), along_z(place, 3)
    right, left, near = along_y(place, 1), along_y(place, 3), near_of(place)
    meet(
        [along_y(place, s) for s in (1, 2, 3)]
        + [near_of(place, (row + s) % 4) for s in range(4)]
        + [pair, twin, up, down]
    )
    mail = Mail(send, recv)
    kept = []

    def keep(source, target):
        kept.append(pltpu.make_async_copy(source, target, local.at[len(kept)]))
        kept[-1].start()
        return len(kept) - 1

    def kept_wait(index):
        kept[index].wait()
        kept[index] = None

    def even(start, size):
        return pl.ds(pl.multiple_of(start, 16), size)

    rows, piece = tok.shape[0] // 4, tok.shape[1]
    width = 4 * piece
    own_rows = even(col * rows, rows)
    spot = even(row * rows, rows)

    def spread(source, target):
        got = []
        for step in range(4):
            part = source.at[even(((row + step) % 4) * rows, rows), :]
            lanes = pl.ds(((4 - step) % 4) * piece, piece)
            if step:
                got.append(mail.post(part, target.at[own_rows, lanes], along_y(place, step)))
            else:
                mine = keep(part, target.at[own_rows, lanes])
        return got, mine

    tokens = spread(tok, tok_v)
    lens[...] = jnp.zeros_like(lens)
    lens[0:1, 0 : lens_in.shape[1]] = lens_in[...]
    gains[...] = jnp.zeros_like(gains)
    gains[0:1, :] = gain_attn[...].reshape(1, piece)
    gains[1:2, :] = gain_ffn[...].reshape(1, piece)
    lens_got = mail.post(lens, lens_v.at[col], pair)
    lens_kept = keep(lens, lens_v.at[col])
    gains_kept = keep(gains, gains_v.at[0])
    gains_got = [mail.post(gains, gains_v.at[4 - s], along_y(place, s)) for s in (1, 2, 3)]

    q_width, kv_width = wq.shape[1], wk.shape[1]
    stages = [
        keep(wq, w_in.at[0, :, pl.ds(0, q_width)]),
        keep(wk, w_in.at[0, :, pl.ds(q_width, kv_width)]),
        keep(wv, w_in.at[0, :, pl.ds(q_width + kv_width, kv_width)]),
        keep(wo, w_out.at[:, pl.ds(0, piece)]),
    ]
    share = wd_own.shape[0]
    thin = piece // 2
    sure = share - LANES
    take = pl.multiple_of(z * share, LANES)
    big = []
    for k in range(2):
        for i, source in enumerate((wg, wu)):
            from_rows = pl.ds(k * thin, thin)
            big.append(keep(source.at[from_rows, pl.ds(take, sure)], gu_own.at[k, :, pl.ds(i * share, sure)]))
    big.append(keep(wd.at[pl.ds(take, sure), :], wd_own.at[pl.ds(0, sure), :]))
    blank_gu[...] = jnp.zeros_like(blank_gu)
    blank_wd[...] = jnp.zeros_like(blank_wd)
    first_edge = len(kept)
    edges = []
    for k in range(2):
        for i, source in enumerate((wg, wu)):
            target = gu_own.at[k, :, pl.ds(i * share + sure, LANES)]
            edges.append((source, pl.ds(k * thin, thin), None, target, blank_gu))
    edges.append((wd, None, slice(None), wd_own.at[pl.ds(sure, LANES), :], blank_wd))

    def edge(index, last):
        source, from_rows, _, target, blank = edges[index]
        if last:
            origin = blank
        elif from_rows is None:
            origin = source.at[pl.ds(pl.multiple_of(take + sure, LANES), LANES), :]
        else:
            origin = source.at[from_rows, pl.ds(pl.multiple_of(take + sure, LANES), LANES)]
        return pltpu.make_async_copy(origin, target, local.at[first_edge + index])

    @pl.when(z < 3)
    def _():
        for index in range(len(edges)):
            edge(index, False).start()

    @pl.when(z == 3)
    def _():
        for index in range(len(edges)):
            edge(index, True).start()

    for index in range(len(edges)):
        kept.append(edge(index, True))
        big.append(first_edge + index)

    q_rows, o_rows = thin // 4, w_out.shape[0] // 8

    def in_part(j, owner_z):
        return w_in.at[j, even(core * thin + owner_z * q_rows, q_rows), :]

    def in_parts(owner_z):
        return w_in.at[pl.ds(1, 3), even(core * thin + owner_z * q_rows, q_rows), :]

    def in_side(owner_z, side):
        lanes = pl.ds(side * (w_in.shape[2] // 2), w_in.shape[2] // 2)
        return w_in.at[pl.ds(1, 3), even(core * thin + owner_z * q_rows, q_rows), lanes]

    def out_part(j, owner_z):
        return w_out.at[even(core * 4 * o_rows + owner_z * o_rows, o_rows), pl.ds(j * piece, piece)]

    def out_parts(owner_z):
        return w_out.at[even(core * 4 * o_rows + owner_z * o_rows, o_rows), pl.ds(piece, 3 * piece)]

    def out_side(owner_z, side):
        start = core * 4 * o_rows + owner_z * o_rows + side * (o_rows // 2)
        return w_out.at[even(start, o_rows // 2), pl.ds(piece, 3 * piece)]

    for index in stages:
        kept_wait(index)
    in_got = [mail.post(in_part(0, z), in_part(4 - step, z), along_y(place, step)) for step in (1, 3, 2)]

    def to_pair(spreading, target):
        got, mine = spreading
        kept_wait(mine)
        for copy in got:
            copy.wait_recv()
        return mail.post(target.at[own_rows, :], target.at[own_rows, :], pair)

    tokens_pair = to_pair(tokens, tok_v)
    shares = []

    def give(part):
        shares.append(mail.post(part, part, twin))

    def z_first(side):
        copies = {}
        for turn in range(2):
            copies["u", turn] = mail.post(side(z, turn), side(z, turn), up)
            copies["d", 1 - turn] = mail.post(side(z, 1 - turn), side(z, 1 - turn), down)
        return copies

    below, above, across = (z + 3) % 4, (z + 1) % 4, (z + 2) % 4

    def z_second(side, whole, copies):
        copies["u", 0].wait_recv()
        far_up = mail.post(side(below, 0), side(below, 0), up)
        copies["d", 1].wait_recv()
        far_down = mail.post(side(above, 1), side(above, 1), down)
        copies["u", 1].wait_recv()
        give(whole(below))
        copies["d", 0].wait_recv()
        give(whole(above))
        return far_up, far_down

    def z_third(whole, copies):
        for copy in copies:
            copy.wait_recv()
        give(whole(across))

    for copy in in_got:
        copy.wait_recv()
    in_z = z_first(in_side)
    give(in_parts(z))
    out_got = [mail.post(out_part(0, z), out_part(4 - step, z), along_y(place, step)) for step in (1, 3, 2)]
    cotangents = spread(cot, cot_full.at[0])
    for index in big:
        kept_wait(index)
    x_lo = (dp // 2) % 2
    gu_half, wd_half = thin // 4, share // 4

    def gu_part(j, which=None, owner=x_lo):
        start, size = (0, 2 * gu_half) if which is None else (which * gu_half, gu_half)
        return wgu_full.at[j, core, even(owner * 2 * gu_half + start, size), :]

    def gu_whole(j):
        return wgu_full.at[j, core]

    def wd_part(j, which=None):
        start, size = (0, 2 * wd_half) if which is None else (which * wd_half, wd_half)
        return wd_full.at[even(core * 2 * wd_half + start, size), pl.ds(j * piece, piece)]

    def gu_source(which):
        return gu_own.at[core, even((x_lo * 2 + which) * gu_half, gu_half), :]

    def wd_source(which):
        return wd_own.at[even((core * 2 + which) * wd_half, wd_half), :]

    y_ring, near_gu, twins = {}, [], []

    def y_start(name, source, part):
        for turn in range(2):
            y_ring[name, "r", turn] = mail.post(source(turn), part(3, turn), right)
            y_ring[name, "l", 1 - turn] = mail.post(source(1 - turn), part(1, 1 - turn), left)

    def y_forward(name, part):
        y_ring[name, "r", 0].wait_recv()
        y_ring[name, "fr"] = mail.post(part(3, 0), part(2, 0), right)
        y_ring[name, "l", 1].wait_recv()
        y_ring[name, "fl"] = mail.post(part(1, 1), part(2, 1), left)

    def y_share(name, part, queue, device):
        y_ring[name, "r", 1].wait_recv()
        queue.append(mail.post(part(3), part(3), device))
        y_ring[name, "l", 0].wait_recv()
        queue.append(mail.post(part(1), part(1), device))

    def y_end(name, part, queue, device):
        y_ring[name, "fr"].wait_recv()
        y_ring[name, "fl"].wait_recv()
        queue.append(mail.post(part(2), part(2), device))


    kept_wait(lens_kept)
    lens_got.wait_recv()
    half_rows = 4 * rows

    def segment_of(which, index):
        end_0 = lens_v[which, 0:1, 0:1]
        end_1 = end_0 + lens_v[which, 0:1, 1:2]
        past_0 = (index >= end_0).astype(jnp.int32)
        past_1 = (index >= end_1).astype(jnp.int32)
        start = jnp.where(past_1 > 0, end_1, jnp.where(past_0 > 0, end_0, 0))
        return past_0 + past_1, start

    lane = lax.broadcasted_iota(jnp.int32, (rows, HEAD_SIZE), 1)
    half_lane = jnp.where(lane >= HEAD_SIZE // 2, lane - HEAD_SIZE // 2, lane).astype(F32)
    inverse = jnp.exp(half_lane * (-2.0 * math.log(THETA) / HEAD_SIZE))
    for which, mask, mask_t, key_count in ((0, bias_a, turned_a, half_rows), (1, bias_b, turned_b, 2 * half_rows)):
        index = lax.broadcasted_iota(jnp.int32, (rows, HEAD_SIZE), 0) + (row * rows + which * half_rows)
        _, start = segment_of(which, index)
        turn = (index - start).astype(F32) * inverse
        tables[0, which * rows : (which + 1) * rows, :] = jnp.cos(turn)
        sine = jnp.sin(turn)
        tables[1, which * rows : (which + 1) * rows, :] = jnp.where(lane >= HEAD_SIZE // 2, sine, -sine)
        at = lax.broadcasted_iota(jnp.int32, (rows, key_count), 0) + (row * rows + which * half_rows)
        keys = lax.broadcasted_iota(jnp.int32, (rows, key_count), 1)
        allowed = jnp.logical_and(segment_of(which, at)[0] == segment_of(which, keys)[0], keys <= at)
        mask[...] = jnp.where(allowed, 0.0, -1e30)
        at = lax.broadcasted_iota(jnp.int32, (key_count, rows), 1) + (row * rows + which * half_rows)
        keys = lax.broadcasted_iota(jnp.int32, (key_count, rows), 0)
        allowed = jnp.logical_and(segment_of(which, at)[0] == segment_of(which, keys)[0], keys <= at)
        mask_t[...] = jnp.where(allowed, 0.0, -1e30)

    kept_wait(gains_kept)
    for copy in gains_got:
        copy.wait_recv()
    keep(gains_v, gains_out)

    def normalise(value, which):
        scale = lax.rsqrt(jnp.sum(value * value, -1, keepdims=True) * (1.0 / width) + EPS)
        return [
            (value[:, j * piece : (j + 1) * piece] * scale * gains_v[j, which : which + 1, :]).astype(BF16)
            for j in range(4)
        ]

    def norm_rows(which):
        part = pl.ds(pl.multiple_of(which * rows, rows), rows)
        for j, block in enumerate(normalise(tok_v[part, :].astype(F32), 0)):
            normed[part, pl.ds(j * piece, piece)] = block

    norm_rows(col)
    for copy in out_got:
        copy.wait_recv()
    give(out_parts(z))
    y_start("gu", gu_source, gu_part)
    keep(gu_own, wgu_full.at[0])
    keep(wd_own, wd_full.at[:, pl.ds(0, piece)])
    in_far = z_second(in_side, in_parts, in_z)
    out_z = z_first(out_side)
    tokens_pair.wait_recv()
    keep(tok_v, tok_out)
    norm_rows(1 - col)
    cot_pair = to_pair(cotangents, cot_full.at[0])
    z_third(in_parts, in_far)
    for copy in shares:
        copy.wait_recv()
    shares.clear()
    keep(w_in, w_in_out)

    in_width = w_in.shape[2]

    def project(lanes, bias):
        weights = w_in[:, :, lanes]
        weights = weights.reshape(4 * weights.shape[1], weights.shape[2])
        return jnp.dot(normed[...], weights, preferred_element_type=F32) + bias

    def rotate(value):
        return value * tables[0] + pltpu.roll(value, HEAD_SIZE // 2, 1) * tables[1]

    key_value = project(slice(q_width, in_width), jnp.concatenate([bias_k[...].reshape(1, kv_width), bias_v[...].reshape(1, kv_width)], 1))
    kv[:, 0:kv_width] = rotate(key_value[:, 0:kv_width]).astype(BF16)
    kv[:, kv_width : 2 * kv_width] = key_value[:, kv_width : 2 * kv_width].astype(BF16)
    a_rows, b_rows = pl.ds(0, rows), pl.ds(rows, rows)
    high_spot = even(half_rows + row * rows, rows)
    a_got, b_got = [], []
    for step in (1, 2, 3):
        a_got.append(mail.post(kv.at[a_rows, :], kva.at[spot, :], along_y(place, step)))
    for step in range(4):
        b_got.append(mail.post(kv.at[a_rows, :], kvb.at[spot, :], near_of(place, (row + step) % 4)))
        if step:
            b_got.append(mail.post(kv.at[b_rows, :], kvb.at[high_spot, :], along_y(place, step)))
    kva[spot, :] = kv[a_rows, :]
    kvb[high_spot, :] = kv[b_rows, :]
    for first in range(0, q_width, 2 * HEAD_SIZE):
        value = project(slice(first, first + 2 * HEAD_SIZE), bias_q[first : first + 2 * HEAD_SIZE].reshape(1, 2 * HEAD_SIZE))
        for i in range(2):
            lanes = slice(first + i * HEAD_SIZE, first + (i + 1) * HEAD_SIZE)
            query[:, lanes] = rotate(value[:, i * HEAD_SIZE : (i + 1) * HEAD_SIZE]).astype(BF16)

    y_forward("gu", gu_part)
    y_share("gu", gu_part, near_gu, near)
    out_far = z_second(out_side, out_parts, out_z)
    heads = q_width // HEAD_SIZE
    factor = HEAD_SIZE ** (-0.5)

    def attend(half, keys, mask):
        part = slice(half * rows, (half + 1) * rows)

        @pl.loop(0, heads)
        def _(h):
            lanes = pl.ds(pl.multiple_of(h * HEAD_SIZE, LANES), HEAD_SIZE)
            raw = lax.dot_general(
                query[part, lanes], keys[:, 0:HEAD_SIZE], (((1,), (1,)), ((), ())), preferred_element_type=F32
            )
            scores = raw * factor + mask[...]
            peak = jnp.max(scores, -1, keepdims=True)
            raised = jnp.exp(scores - peak)
            total = jnp.sum(raised, -1, keepdims=True)
            probs = (raised * (1.0 / total)).astype(BF16)
            out = jnp.dot(probs, keys[:, HEAD_SIZE : 2 * HEAD_SIZE], preferred_element_type=F32)
            attended[part, lanes] = out.astype(BF16)
            logs[half * heads + h] = jnp.broadcast_to(peak + jnp.log(total), (rows, LANES)).T[0:8, :]

        for first in range(0, width, piece):
            lanes = slice(first, first + piece)
            branch[part, lanes] = jnp.dot(
                attended[part, :], w_out[:, lanes], preferred_element_type=F32
            ).astype(BF16)
        return mail.post(branch.at[part, :], branch_in.at[part, :], pair)

    def finish_half(half, copy):
        part = slice(half * rows, (half + 1) * rows)
        copy.wait_recv()
        value = tok_v[part, :].astype(F32) + (branch[part, :].astype(F32) + branch_in[part, :].astype(F32))
        middle[part, :] = value
        for j, block in enumerate(normalise(value, 1)):
            normed_ffn[part, j * piece : (j + 1) * piece] = block

    def z_part(slot, half):
        return cot_full.at[slot, pl.ds(half * rows, rows), :]

    def z_send():
        copies = {}
        for turn in range(2):
            copies["u", turn] = mail.post(z_part(0, turn), z_part(1, turn), up)
            copies["d", 1 - turn] = mail.post(z_part(0, 1 - turn), z_part(3, 1 - turn), down)
        return copies

    def z_forward(copies):
        copies["u", 0].wait_recv()
        far_up = mail.post(z_part(1, 0), z_part(2, 0), up)
        copies["d", 1].wait_recv()
        far_down = mail.post(z_part(3, 1), z_part(2, 1), down)
        return [copies["u", 1], copies["d", 0], far_up, far_down]

    cot_pair.wait_recv()
    cot_z = z_send()
    for copy in a_got:
        copy.wait_recv()
    keep(kva, kva_out)
    z_third(out_parts, out_far)
    for copy in shares:
        copy.wait_recv()
    keep(w_out, w_out_out)
    swap_a = attend(0, kva, bias_a)
    for copy in b_got:
        copy.wait_recv()
    keep(kvb, kvb_out)
    y_start("wd", wd_source, wd_part)
    swap_b = attend(1, kvb, bias_b)
    y_end("gu", gu_part, near_gu, near)
    finish_half(0, swap_a)
    y_forward("wd", wd_part)
    cot_last = z_forward(cot_z)
    y_share("wd", wd_part, twins, twin)
    finish_half(1, swap_b)
    for j, copy in zip((3, 1, 2), near_gu):
        copy.wait_recv()
        twins.append(mail.post(gu_whole(j), gu_whole(j), twin))
    y_end("wd", wd_part, twins, twin)
    for copy in cot_last:
        copy.wait_recv()
    for copy in twins:
        copy.wait_recv()
    for copy in kept:
        if copy is not None:
            copy.wait()
    mail.finish()


def ffn_kernel(
    normed,
    cot,
    wgu,
    wd,
    total,
    gu_sum,
    gu_late,
    dn_half,
    result_sum,
    result_ahead,
    x,
    cot_v,
    wgu_v,
    wd_v,
    gb,
    act,
    parts,
    turned,
    down_v,
    gu_in,
    dn_in,
    up1,
    down1,
    up2,
    down2,
    other,
    stage_up,
    stage_down,
    stage,
    res_up1,
    res_down1,
    res_up2,
    res_down2,
    gu_up1,
    gu_down1,
    gu_up2,
    gu_down2,
    send,
    recv,
    local,
):
    place = here()
    dp, row, col = place
    core = dp % 2
    up, down, pair, twin = along_z(place, 1), along_z(place, 3), pair_of(place), twin_of(place)
    right, left = along_y(place, 1), along_y(place, 3)
    meet([up, down, pair, twin, right, left])
    mail = Mail(send, recv)
    order = ((0, 0), (0, 1), (1, 0), (3, 1), (2, 0), (2, 1), (1, 1), (3, 0))
    spots = {half: i for i, half in enumerate(order)}
    rows = normed.shape[0] // 2
    size = rows // 2

    def block(ref, slot, half):
        return ref.at[pl.ds(spots[slot, half] * rows, rows), :]

    def halves(ref, half):
        return ref.at[pl.ds(half * rows, rows), :]

    kept = []

    def keep(source, target):
        kept.append(pltpu.make_async_copy(source, target, local.at[len(kept)]))
        kept[-1].start()
        return len(kept) - 1

    def kept_wait(index):
        kept[index].wait()
        kept[index] = None

    got = {}

    def z_start(which):
        got["u", which] = mail.post(halves(normed, which), block(x, 1, which), up)
        got["d", 1 - which] = mail.post(halves(normed, 1 - which), block(x, 3, 1 - which), down)

    z_start(0)
    share = wd.shape[0]
    early = [keep(normed, x.at[pl.ds(0, 2 * rows), :]), keep(wgu, wgu_v)]
    early.append(keep(cot.at[0], cot_v.at[pl.ds(0, 2 * rows), :]))
    early.append(keep(wd, wd_v))
    later = [keep(cot.at[slot, pl.ds(half * rows, rows), :], block(cot_v, slot, half)) for slot, half in order[2:]]
    width = normed.shape[1]
    piece = width // 4

    def dot_nt(left, right):
        return lax.dot_general(left, right, (((1,), (1,)), ((), ())), preferred_element_type=F32)

    def compute(c):
        part = slice(2 * rows * c, 2 * rows * (c + 1))
        for start, size in ((0, 512), (512, share - 512)):
            lanes, above = slice(start, start + size), slice(share + start, share + start + size)
            gate = jnp.dot(x[part, :], wgu_v[:, lanes], preferred_element_type=F32)
            value = jnp.dot(x[part, :], wgu_v[:, above], preferred_element_type=F32)
            grad = dot_nt(cot_v[part, :], wd_v[lanes, :])
            spread = 1.0 / (1.0 + jnp.exp(-gate))
            smooth = gate * spread
            act[part, lanes] = (smooth * value).astype(BF16)
            gb[part, lanes] = (grad * value * (spread * (1.0 + gate * (1.0 - spread)))).astype(BF16)
            gb[part, above] = (grad * smooth).astype(BF16)
        for m in range(3):
            lanes = slice(512 * m, 512 * (m + 1))
            parts[part, lanes] = dot_nt(gb[part, :], wgu_v[lanes, :]).astype(BF16)

    for index in early:
        kept_wait(index)
    compute(0)
    got["u", 0].wait_recv()
    far_up = mail.post(block(x, 1, 0), block(x, 2, 0), up)
    got["d", 1].wait_recv()
    far_down = mail.post(block(x, 3, 1), block(x, 2, 1), down)
    for index in later:
        kept_wait(index)
    compute(1)
    z_start(1)
    far_up.wait_recv()
    far_down.wait_recv()
    compute(2)
    first = {}
    for i in range(2):
        rows_i = pl.ds(i * size, size)
        first["u", i] = mail.post(block(parts, 2, 0).at[rows_i, :], up1.at[i], up)
        first["d", i] = mail.post(block(parts, 2, 1).at[rows_i, :], down1.at[i], down)
    got["u", 1].wait_recv()
    got["d", 0].wait_recv()
    compute(3)
    second = {
        ("d", 0): mail.post(block(parts, 1, 0), down2.at[0], down),
        ("u", 1): mail.post(block(parts, 3, 1), up2.at[1], up),
    }

    def turn_over(source, target):
        @pl.loop(0, source.shape[1] // LANES)
        def _(t):
            lanes = pl.ds(pl.multiple_of(t * LANES, LANES), LANES)
            target[lanes, :] = source[:, lanes].T

    def forward(i):
        rows_i = pl.ds(i * size, size)
        first["u", i].wait_recv()
        stage_up[i] = (block(parts, 3, 0).at[rows_i, :][...] + up1[i])
        second["u", 0, i] = mail.post(stage_up.at[i], up2.at[0, rows_i, :], up)
        first["d", i].wait_recv()
        stage_down[i] = (block(parts, 1, 1).at[rows_i, :][...] + down1[i])
        second["d", 1, i] = mail.post(stage_down.at[i], down2.at[1, rows_i, :], down)

    turn_over(x, turned)
    tile = 256
    tiles = 2 * share // tile

    def gu_tiles(first_tile, last_tile):
        @pl.loop(first_tile, last_tile)
        def _(n):
            lanes = pl.ds(pl.multiple_of(((n + (tiles // 2) * (1 - core)) % tiles) * tile, tile), tile)
            wgu_v[:, lanes] = jnp.dot(turned[...], gb[:, lanes], preferred_element_type=F32).astype(BF16)

    swaps = {}

    def settle(i):
        rows_i = pl.ds(i * size, size)
        if i == 0:
            second["d", 0].wait_recv()
            second["u", 1].wait_recv()
        second["u", 0, i].wait_recv()
        second["d", 1, i].wait_recv()
        for half in range(2):
            value = block(parts, 0, half).at[rows_i, :][...].astype(F32)
            value = value + up2[half, rows_i, :].astype(F32) + down2[half, rows_i, :].astype(F32)
            stage[half, rows_i, :] = value.astype(BF16)
            swaps[half, i] = mail.post(stage.at[half, rows_i, :], other.at[half, rows_i, :], pair)

    there = pl.ds(pl.multiple_of((1 - core) * share, LANES), share)
    mine = pl.ds(pl.multiple_of(core * share, LANES), share)
    gu_tiles(0, tiles // 2 + 1)
    shared = [
        mail.post(wgu_v.at[pl.ds(j * piece, piece), there], gu_in.at[j], twin) for j in range(4)
    ]
    forward(0)
    forward(1)
    gu_tiles(tiles // 2 + 1, tiles)
    for j in range(4):
        shared[j].wait_recv()
        gu_in[j] = (wgu_v[pl.ds(j * piece, piece), mine] + gu_in[j])

    def ring_y(i):
        height = piece // 3
        half = height // 2
        low, high = pl.ds(i * height, half), pl.ds(i * height + half, half)
        one, two, three, four = gu_up1.at[i], gu_down1.at[i], gu_up2.at[i], gu_down2.at[i]
        begin = (mail.post(gu_in.at[2, low, :], one, right), mail.post(gu_in.at[2, high, :], two, left))
        straight = [
            mail.post(gu_in.at[1, high, :], three.at[pl.ds(half, half), :], right),
            mail.post(gu_in.at[3, low, :], four.at[pl.ds(0, half), :], left),
        ]
        yield
        begin[0].wait_recv()
        one[...] = (gu_in[1, low, :] + one[...])
        straight.append(mail.post(one, three.at[pl.ds(0, half), :], right))
        begin[1].wait_recv()
        two[...] = (gu_in[3, high, :] + two[...])
        straight.append(mail.post(two, four.at[pl.ds(half, half), :], left))
        yield
        for copy in straight:
            copy.wait_recv()
        part = pl.ds(i * height, height)
        value = gu_in[0, part, :].astype(F32) + three[...].astype(F32) + four[...].astype(F32)
        gu_sum[part, :] = value.astype(BF16)
        yield

    rings = [ring_y(i) for i in range(2)]
    keep(gu_in.at[:, pl.ds(2 * (piece // 3), piece // 3), :], gu_late)
    for ring in rings:
        next(ring)
    for m in range(3):
        lanes = slice(512 * m, 512 * (m + 1))

        @pl.loop(0, 4)
        def _(c):
            part = pl.ds(pl.multiple_of(c * 2 * rows, 2 * rows), 2 * rows)
            down_v[part, lanes] = jnp.dot(act[part, :], wd_v[:, lanes], preferred_element_type=F32).astype(BF16)

    settle(0)
    settle(1)
    result = {
        "u1": mail.post(block(down_v, 2, 0), res_up1, up),
        "d1": mail.post(block(down_v, 2, 1), res_down1, down),
        "u2": mail.post(block(down_v, 3, 1), res_up2, up),
        "d2": mail.post(block(down_v, 1, 0), res_down2, down),
    }
    turn_over(act, turned)

    @pl.loop(0, width // tile)
    def _(n):
        lanes = pl.ds(pl.multiple_of(n * tile, tile), tile)
        wd_v[:, lanes] = jnp.dot(
            turned[0:share, :], cot_v[:, lanes], preferred_element_type=F32
        ).astype(BF16)

    half_share = share // 2
    rows_there = pl.ds(pl.multiple_of((1 - core) * half_share, 16), half_share)
    rows_mine = pl.ds(pl.multiple_of(core * half_share, 16), half_share)
    shared += [
        mail.post(wd_v.at[rows_there, pl.ds(j * piece, piece)], dn_in.at[j], twin) for j in range(4)
    ]
    for ring in rings:
        next(ring)
    for j in range(4):
        shared[4 + j].wait_recv()
        dn_in[j] = (wd_v[rows_mine, pl.ds(j * piece, piece)] + dn_in[j])
        keep(dn_in.at[j], dn_half.at[j])
    for half, i in ((0, 0), (1, 0), (0, 1), (1, 1)):
        rows_i = pl.ds(i * size, size)
        swaps[half, i].wait_recv()
        total[pl.ds(half * rows + i * size, size), :] = stage[half, rows_i, :].astype(F32) + other[
            half, rows_i, :
        ].astype(F32)
    next(rings[0])
    next(rings[1])
    for copy in result.values():
        copy.wait_recv()
    result_ahead[0] = (block(down_v, 3, 0)[...] + res_up1[...])
    result_ahead[1] = (block(down_v, 1, 1)[...] + res_down1[...])
    for half, theirs in ((0, res_down2), (1, res_up2)):
        value = block(down_v, 0, half)[...].astype(F32) + theirs[...].astype(F32)
        result_sum[pl.ds(half * rows, rows), :] = value.astype(BF16)
    for copy in kept:
        if copy is not None:
            copy.wait()
    mail.finish()


def back_kernel(
    total,
    middle,
    cot,
    gains,
    tok,
    normed,
    query,
    kv_a,
    kv_b,
    logs,
    attended,
    tables,
    turned_a,
    turned_b,
    w_in,
    w_out,
    gu,
    gl,
    dn,
    result_sum,
    ahead,
    gu_out,
    dn_out,
    in_out,
    kw_out,
    wo_out,
    grad_out,
    result_out,
    small_out,
    middle_v,
    cot_v,
    tok_v,
    normed_v,
    query_v,
    kva,
    kvb,
    attended_v,
    turned_a_v,
    turned_b_v,
    w_in_v,
    w_out_v,
    gu_v,
    gl_v,
    dn_v,
    down_v,
    gain_rows,
    grad_middle,
    grad_low,
    grad_att,
    flat,
    keys_t,
    dkv_a,
    dkv_b,
    low_kv,
    own_kv,
    from_own,
    from_near,
    grad_pre,
    grad_part,
    grad_in,
    part_in,
    rows_out,
    result_rows,
    gu_n,
    gu_s,
    gl_up1,
    gl_down1,
    gl_up2,
    gl_down2,
    gl_y,
    dn_up1,
    dn_down1,
    dn_up2,
    dn_down2,
    dn_y,
    dn_n,
    dn_s,
    in_p,
    in_t,
    in_up1,
    in_down1,
    in_up2,
    in_down2,
    in_s,
    in_n,
    in_z,
    kw_p,
    kw_t,
    kw_up1,
    kw_down1,
    kw_up2,
    kw_down2,
    kw_s,
    kw_n,
    kw_z,
    wo_p,
    wo_t,
    wo_up1,
    wo_down1,
    wo_up2,
    wo_down2,
    wo_s,
    wo_n,
    wo_z,
    res_in,
    res_total,
    bias_own,
    gains_own,
    bias_in,
    gains_in,
    small_a,
    small_b,
    small_t,
    small_n,
    send,
    recv,
    local,
):
    place = here()
    dp, row, col = place
    core = dp % 2
    z = dp // Z_STEP
    twin, near, pair = twin_of(place), near_of(place), pair_of(place)
    up, down, far_z = along_z(place, 1), along_z(place, 3), along_z(place, 2)
    right, left = along_y(place, 1), along_y(place, 3)
    meet(
        [along_y(place, s) for s in (1, 2, 3)]
        + [near_of(place, (row + s) % 4) for s in range(4)]
        + [pair_of(place, (row + s) % 4) for s in range(4)]
        + [twin, up, down, far_z]
    )
    mail = Mail(send, recv)
    kept, arrivals = [], []

    def keep(source, target):
        kept.append(pltpu.make_async_copy(source, target, local.at[len(kept)]))
        kept[-1].start()
        return len(kept) - 1

    def kept_wait(index):
        if kept[index] is not None:
            kept[index].wait()
            kept[index] = None

    def even(start, size):
        return pl.ds(pl.multiple_of(start, 16), size)

    def plus(*values):
        result = values[0].astype(F32)
        for value in values[1:]:
            result = result + value.astype(F32)
        return result

    def dot_nt(left, right):
        return lax.dot_general(left, right, (((1,), (1,)), ((), ())), preferred_element_type=F32)

    rows = tok.shape[0] // 2
    width = tok.shape[1]
    piece = width // 4
    spot = even(row * rows, rows)
    own_rows, other_rows = even(col * rows, rows), even((1 - col) * rows, rows)

    def ffn_flow(i):
        if i < 2:
            height = gu.shape[0] // 2
            start = i * height
            theirs, done = gu_n.at[i], gu_s.at[i]
            mine = gu_v.at[pl.ds(start, height), :]
            swap = mail.post(gu.at[pl.ds(start, height), :], theirs, near)
            half = height // 2
            yield
            kept_wait(loads["gu"])
        else:
            if i == 2:
                held, loaded, name, height, start = gl, gl_v, "gl", gl.shape[1], 2 * gl.shape[1]
                mine, theirs, done = gl_y, gu_n.at[2], gu_s.at[2]
                one, two, three, four = gl_up1, gl_down1, gl_up2, gl_down2
            else:
                held, loaded, name, height, start = dn, dn_v, "dn", dn.shape[1], 0
                mine, theirs, done = dn_y, dn_n, dn_s
                one, two, three, four = dn_up1, dn_down1, dn_up2, dn_down2
            half = height // 2
            low, high = pl.ds(0, half), pl.ds(half, half)
            first = (mail.post(held.at[2, low, :], one, right), mail.post(held.at[2, high, :], two, left))
            straight = (
                mail.post(held.at[1, high, :], three.at[high, :], right),
                mail.post(held.at[3, low, :], four.at[low, :], left),
            )
            yield
            kept_wait(loads[name])
            first[0].wait_recv()
            one[...] = (loaded[1, low, :] + one[...])
            last = [mail.post(one, three.at[low, :], right)]
            first[1].wait_recv()
            two[...] = (loaded[3, high, :] + two[...])
            last.append(mail.post(two, four.at[high, :], left))
            yield
            for copy in straight + tuple(last):
                copy.wait_recv()
            mine[...] = plus(loaded[0], three[...], four[...]).astype(BF16)
            swap = mail.post(mine, theirs, near)
            yield
        swap.wait_recv()
        done[...] = (mine[...] + theirs[...])

        def room(slot, which=None):
            begin, size = (start, height) if which is None else (start + which * half, half)
            if i < 3:
                share = gu_out.shape[2] // 4
                lanes = pl.ds(pl.multiple_of(slot * share, LANES), share)
                return gu_out.at[core, pl.ds(begin, size), lanes]
            return dn_out.at[even((slot * 2 + core) * height + begin, size), :]

        posts = {}
        for turn in range(2):
            for name, device, which in (("u", up, turn), ("d", down, 1 - turn)):
                posts[name, which] = mail.post(done.at[pl.ds(which * half, half), :], room(z, which), device)
        keep(done, room(z))
        arrivals.append(mail.post(done, room(z), twin))
        yield
        posts["u", 0].wait_recv()
        block = room((z + 3) % 4, 0)
        one_more = mail.post(block, block, up)
        posts["d", 1].wait_recv()
        block = room((z + 1) % 4, 1)
        two_more = mail.post(block, block, down)
        yield
        posts["u", 1].wait_recv()
        block = room((z + 3) % 4)
        arrivals.append(mail.post(block, block, twin))
        posts["d", 0].wait_recv()
        block = room((z + 1) % 4)
        arrivals.append(mail.post(block, block, twin))
        one_more.wait_recv()
        two_more.wait_recv()
        block = room((z + 2) % 4)
        arrivals.append(mail.post(block, block, twin))
        yield

    def weight_flow(part, t, up1, down1, up2, down2, total_h, theirs, quarter, out):
        height = t.shape[1]
        half = height // 2
        low, high = pl.ds(0, half), pl.ds(half, half)
        copy = mail.post(part.at[:, even((1 - core) * height, height), :], t, twin)
        yield
        copy.wait_recv()
        for j in range(4):
            t[j] = (part[j, even(core * height, height), :] + t[j])
        first = (mail.post(t.at[2, low, :], up1, right), mail.post(t.at[2, high, :], down1, left))
        straight = (
            mail.post(t.at[1, high, :], up2.at[high, :], right),
            mail.post(t.at[3, low, :], down2.at[low, :], left),
        )
        yield
        first[0].wait_recv()
        up1[...] = (t[1, low, :] + up1[...])
        last = [mail.post(up1, up2.at[low, :], right)]
        first[1].wait_recv()
        down1[...] = (t[3, high, :] + down1[...])
        last.append(mail.post(down1, down2.at[high, :], left))
        yield
        for copy in straight + tuple(last):
            copy.wait_recv()
        total_h[...] = plus(t[0], up2[...], down2[...]).astype(BF16)
        swap = mail.post(total_h, theirs, near)
        yield
        swap.wait_recv()
        t[0] = (total_h[...] + theirs[...])
        size = height // 4
        copies = []
        for step, device in ((1, up), (3, down), (2, far_z)):
            source = t.at[0, even(((z + step) % 4) * size, size), :]
            copies.append(mail.post(source, quarter.at[step - 1], device))
        yield
        for copy in copies:
            copy.wait_recv()
        mine = even(z * size, size)
        theirs[0:size, :] = plus(t[0, mine, :], quarter[0], quarter[1], quarter[2]).astype(BF16)
        place_of = lambda owner: out.at[even(core * height + owner * size, size), :]
        copies = [mail.post(theirs.at[0:size, :], place_of(z), device) for device in (up, down, far_z)]
        arrivals.append(mail.post(theirs.at[0:size, :], place_of(z), twin))
        keep(theirs.at[0:size, :], place_of(z))
        yield
        for copy in copies:
            copy.wait_recv()
        for step in (1, 2, 3):
            block = place_of((z + step) % 4)
            arrivals.append(mail.post(block, block, twin))
        yield

    def result_flow():
        copies = (mail.post(ahead.at[0], res_in.at[0], up), mail.post(ahead.at[1], res_in.at[1], down))
        yield
        kept_wait(loads["down"])
        for half, copy in enumerate(copies):
            copy.wait_recv()
            part = pl.ds(half * rows, rows)
            res_total[part, :] = (down_v[part, :] + res_in[half])
        swap = mail.post(res_total.at[other_rows, :], part_in, pair)
        yield
        swap.wait_recv()
        result_rows[...] = (middle_v[own_rows, :] + plus(res_total[own_rows, :], part_in[...])).astype(BF16)
        yield
        spread(result_rows, result_out)
        yield

    def spread(source, target):
        for step in range(4):
            lanes = pl.ds(step * piece, piece)
            if step:
                arrivals.append(mail.post(source.at[:, lanes], target.at[spot, :], along_y(place, step)))
            else:
                keep(source.at[:, lanes], target.at[spot, :])

    flows = [ffn_flow(i) for i in range(4)]
    loads = {}
    for name, source, target in (
        ("middle", middle, middle_v),
        ("cot", cot.at[0], cot_v),
        ("w_out", w_out, w_out_v),
        ("attended", attended, attended_v),
        ("query", query, query_v),
        ("kva", kv_a, kva),
        ("kvb", kv_b, kvb),
        ("ta", turned_a, turned_a_v),
        ("tb", turned_b, turned_b_v),
        ("gu", gu, gu_v),
        ("w_in", w_in, w_in_v),
        ("normed", normed, normed_v),
        ("tok", tok, tok_v),
        ("dn", dn, dn_v),
        ("gl", gl, gl_v),
        ("down", result_sum, down_v),
    ):
        loads[name] = keep(source, target)
    result_steps = result_flow()
    next(flows[3])
    next(flows[1])
    for j in range(4):
        gain_rows[:, j * piece : (j + 1) * piece] = gains[j]

    def norm_back(stream, gain, incoming):
        scale = lax.rsqrt(jnp.sum(stream * stream, -1, keepdims=True) * (1.0 / width) + EPS)
        scaled = incoming * gain
        inner = jnp.sum(scaled * stream, -1, keepdims=True) * (1.0 / width)
        back = scale * scaled - stream * (scale * scale * scale * inner)
        return back, jnp.sum(incoming * stream * scale, 0, keepdims=True)

    kept_wait(loads["middle"])
    kept_wait(loads["cot"])
    gain_ffn_part = jnp.zeros((1, width), F32)
    for half in range(2):
        part = slice(half * rows, (half + 1) * rows)
        back, gain_part = norm_back(middle_v[part, :], gain_rows[1:2, :], total[part, :])
        value = cot_v[part, :].astype(F32) + back
        grad_middle[part, :] = value
        grad_low[part, :] = value.astype(BF16)
        gain_ffn_part = gain_ffn_part + gain_part
    gains_own[...] = jnp.zeros_like(gains_own)
    for j in range(4):
        gains_own[j, 1:2, :] = 0.5 * gain_ffn_part[:, j * piece : (j + 1) * piece]
    next(result_steps)
    kept_wait(loads["w_out"])
    q_width = w_out.shape[0]
    for first in range(0, q_width, 256):
        lanes = slice(first, first + 256)
        grad_att[:, lanes] = dot_nt(grad_low[...], w_out_v[lanes, :]).astype(BF16)

    def turn_over(source, target, count):
        for t in range(count):
            lanes = slice(t * LANES, (t + 1) * LANES)
            target[lanes, 0 : source.shape[0]] = source[:, lanes].T

    next(flows[0])
    next(flows[3])
    kept_wait(loads["attended"])
    turn_over(attended_v, flat, q_width // LANES)
    for j in range(4):
        wo_p[j] = jnp.dot(
            flat[0:q_width, :], grad_low[:, j * piece : (j + 1) * piece], preferred_element_type=F32
        ).astype(BF16)
    wo_steps = weight_flow(wo_p, wo_t, wo_up1, wo_down1, wo_up2, wo_down2, wo_s, wo_n, wo_z, wo_out)

    for name in ("query", "kva", "kvb", "ta", "tb"):
        kept_wait(loads[name])
    heads = q_width // HEAD_SIZE
    factor = HEAD_SIZE ** (-0.5)

    def unrotate(value, half):
        part = slice(half * rows, (half + 1) * rows)
        return value * tables[0, part, :] + pltpu.roll(value * tables[1, part, :], HEAD_SIZE // 2, 1)

    def attend_back(half, keys, mask, sums):
        part = slice(half * rows, (half + 1) * rows)
        count = keys.shape[0]
        for t in range(count // LANES):
            lanes = slice(t * LANES, (t + 1) * LANES)
            keys_t[:, lanes] = keys[lanes, 0:HEAD_SIZE].T
        sums[...] = jnp.zeros_like(sums)

        @pl.loop(0, heads)
        def _(h):
            lanes = pl.ds(pl.multiple_of(h * HEAD_SIZE, LANES), HEAD_SIZE)
            one, grad = query_v[part, lanes], grad_att[part, lanes]
            raw = dot_nt(keys[:, 0:HEAD_SIZE], one)
            probs = jnp.exp(raw * factor + mask[...] - logs[half * heads + h, 0:1, :])
            grad_probs = dot_nt(keys[:, HEAD_SIZE : 2 * HEAD_SIZE], grad)
            inner = jnp.sum(grad_probs * probs, 0, keepdims=True)
            grad_scores = (probs * (grad_probs - inner)).astype(BF16)
            sums[:, 0:HEAD_SIZE] += jnp.dot(grad_scores, one, preferred_element_type=F32)
            sums[:, HEAD_SIZE : 2 * HEAD_SIZE] += jnp.dot(probs.astype(BF16), grad, preferred_element_type=F32)
            grad_query = jnp.dot(keys_t[:, 0:count], grad_scores, preferred_element_type=F32).T * factor
            grad_pre[part, lanes] = unrotate(grad_query, half).astype(BF16)

    def low_sums(sums, part):
        return (sums[part, 0:HEAD_SIZE] * factor).astype(BF16), sums[part, HEAD_SIZE : 2 * HEAD_SIZE].astype(BF16)

    next(wo_steps)
    next(flows[1])
    next(flows[2])
    next(result_steps)
    next(flows[1])
    next(flows[3])
    attend_back(1, kvb, turned_b_v, dkv_b)
    half_rows = kva.shape[0]
    low_part, high_part = slice(0, half_rows), slice(half_rows, 2 * half_rows)
    for target, sums, part in ((low_kv, dkv_b, low_part), (own_kv.at[1], dkv_b, high_part)):
        target[:, 0:HEAD_SIZE], target[:, HEAD_SIZE : 2 * HEAD_SIZE] = low_sums(sums, part)
    kv_got = []
    for step in range(4):
        other = (row + step) % 4
        part = even(other * rows, rows)
        kv_got.append(mail.post(low_kv.at[part, :], from_near.at[step], near_of(place, other)))
        if step:
            kv_got.append(mail.post(own_kv.at[1, part, :], from_own.at[step - 1, 1], along_y(place, step)))
    next(flows[0])
    attend_back(0, kva, turned_a_v, dkv_a)
    target = own_kv.at[0]
    target[:, 0:HEAD_SIZE], target[:, HEAD_SIZE : 2 * HEAD_SIZE] = low_sums(dkv_a, low_part)
    for step in (1, 2, 3):
        part = even(((row + step) % 4) * rows, rows)
        kv_got.append(mail.post(own_kv.at[0, part, :], from_own.at[step - 1, 0], along_y(place, step)))
    next(flows[2])
    next(flows[3])
    next(wo_steps)
    kept_wait(loads["normed"])
    turn_over(normed_v, flat, width // LANES)
    for j in range(4):
        in_p[j] = jnp.dot(
            flat[j * piece : (j + 1) * piece, :], grad_pre[:, 0:q_width], preferred_element_type=F32
        ).astype(BF16)
    in_steps = weight_flow(in_p, in_t, in_up1, in_down1, in_up2, in_down2, in_s, in_n, in_z, in_out)
    next(flows[3])
    next(flows[2])
    next(flows[0])
    next(in_steps)
    for copy in kv_got:
        copy.wait_recv()
    for half in range(2):
        part = slice(half * rows, (half + 1) * rows)
        value = own_kv[half, spot, :].astype(F32)
        for step in range(3):
            value = value + from_own[step, half].astype(F32)
        if half == 0:
            for step in range(4):
                value = value + from_near[step].astype(F32)
        grad_pre[part, q_width : q_width + HEAD_SIZE] = unrotate(value[:, 0:HEAD_SIZE], half).astype(BF16)
        grad_pre[part, q_width + HEAD_SIZE : q_width + 2 * HEAD_SIZE] = value[:, HEAD_SIZE : 2 * HEAD_SIZE].astype(
            BF16
        )
    next(wo_steps)
    next(in_steps)
    kept_wait(loads["w_in"])
    for j in range(4):
        grad_part[:, j * piece : (j + 1) * piece] = dot_nt(grad_pre[...], w_in_v[j]).astype(BF16)
    swap = mail.post(grad_part.at[other_rows, :], grad_in, pair)
    for j in range(4):
        kw_p[j] = jnp.dot(
            flat[j * piece : (j + 1) * piece, :], grad_pre[:, q_width:], preferred_element_type=F32
        ).astype(BF16)
    kw_steps = weight_flow(kw_p, kw_t, kw_up1, kw_down1, kw_up2, kw_down2, kw_s, kw_n, kw_z, kw_out)
    next(wo_steps)
    next(flows[2])
    next(kw_steps)
    next(result_steps)
    next(in_steps)
    next(kw_steps)
    bias_own[...] = jnp.zeros_like(bias_own)
    bias_own[0:1, :] = jnp.sum(grad_pre[...].astype(F32), 0, keepdims=True)
    next(wo_steps)
    kept_wait(loads["tok"])
    swap.wait_recv()
    back, gain_part = norm_back(
        tok_v[own_rows, :].astype(F32), gain_rows[0:1, :], plus(grad_part[own_rows, :], grad_in[...])
    )
    rows_out[...] = (grad_middle[own_rows, :] + back).astype(BF16)
    for j in range(4):
        gains_own[j, 0:1, :] = gain_part[:, j * piece : (j + 1) * piece]
    next(in_steps)
    next(flows[2])
    next(kw_steps)
    next(wo_steps)
    small_copies, small_kept = [], []
    for step in range(4):
        device = along_y(place, step)
        mine = gains_in.at[col * 4 + row]
        if step:
            small_copies.append(mail.post(bias_own, bias_in.at[row], device))
            small_copies.append(mail.post(gains_own.at[step], mine, device))
        else:
            small_kept.append(keep(bias_own, bias_in.at[row]))
            small_kept.append(keep(gains_own.at[step], mine))
        small_copies.append(mail.post(gains_own.at[step], mine, pair_of(place, (row + step) % 4)))
    spread(rows_out, grad_out)
    next(kw_steps)
    next(in_steps)
    for copy in small_copies:
        copy.wait_recv()
    for index in small_kept:
        kept_wait(index)
    small_a[...] = jnp.zeros_like(small_a)
    small_a[0:8, :] = bias_in[0] + bias_in[1] + bias_in[2] + bias_in[3]
    small_a[8:16, 0:piece] = (
        gains_in[0] + gains_in[1] + gains_in[2] + gains_in[3] + gains_in[4] + gains_in[5] + gains_in[6] + gains_in[7]
    )
    small_first = mail.post(small_a, small_t, twin)
    next(result_steps)
    next(kw_steps)
    small_first.wait_recv()
    small_b[...] = small_a[...] + small_t[...]
    small_second = mail.post(small_b, small_n, near)
    next(in_steps)
    next(flows[2])
    small_second.wait_recv()
    small_t[...] = small_b[...] + small_n[...]
    for device in (up, down, far_z):
        arrivals.append(mail.post(small_t, small_out.at[z], device))
    keep(small_t, small_out.at[z])
    next(wo_steps)
    next(kw_steps)
    next(in_steps)
    for steps in [*flows, wo_steps, in_steps, kw_steps, result_steps]:
        for _ in steps:
            pass
    for copy in arrivals:
        copy.wait_recv()
    for copy in kept:
        if copy is not None:
            copy.wait()
    mail.finish()


def widen_kernel(gate_up, down, w_in, w_kv, w_out, result, tokens, small, *outs):
    result_w, tokens_w, query_w, key_w, value_w, out_w, gate_w, up_w, down_w, *flat = outs
    total = small[0] + small[1] + small[2] + small[3]
    start = 0
    for line, out in zip((0, 0, 0, 8, 9), flat):
        start = 0 if line else start
        out[...] = total[line, start : start + out.shape[0]]
        start += out.shape[0]
    result_w[...] = result[...].astype(F32)
    tokens_w[...] = tokens[...].astype(F32)
    query_w[...] = w_in[...].astype(F32)
    key_w[...] = w_kv[:, : key_w.shape[1]].astype(F32)
    value_w[...] = w_kv[:, key_w.shape[1] :].astype(F32)
    out_w[...] = w_out[...].astype(F32)
    gate_w[...] = gate_up[0, :, : gate_w.shape[1]].astype(F32)
    up_w[...] = gate_up[1, :, : up_w.shape[1]].astype(F32)
    down_w[...] = down[...].astype(F32)


def on_device(
    tokens,
    cotangent,
    lengths,
    gain_attn,
    w_query,
    key_projection,
    value_projection,
    bias_query,
    key_bias_vector,
    value_bias_vector,
    w_out,
    gain_ffn,
    w_gate,
    w_up,
    w_down,
):
    half_rows, piece = tokens.shape
    width = 4 * piece
    rows = half_rows // 4
    q_width = w_query.shape[1]
    kv_width = key_projection.shape[1]
    heads = q_width // HEAD_SIZE
    hidden = w_gate.shape[1]
    share = -(-hidden // (4 * LANES)) * LANES

    in_width = q_width + 2 * kv_width
    thin = piece // 2
    (
        tok_rows,
        cot_full,
        gains4,
        normed,
        query,
        kv_a,
        kv_b,
        logs,
        attended,
        tables,
        middle,
        mask_a,
        mask_b,
        normed_ffn,
        w_in_full,
        w_out_full,
        w_gu_full,
        w_down_full,
    ) = talk(
        front_kernel,
        0,
        FRONT_COPIES,
        FRONT_LOCAL,
        [
            ((2 * rows, width), BF16),
            ((4, 2 * rows, width), BF16),
            ((4, 8, piece), F32),
            ((2 * rows, width), BF16),
            ((2 * rows, q_width), BF16),
            ((half_rows, 2 * kv_width), BF16),
            ((2 * half_rows, 2 * kv_width), BF16),
            ((2 * heads, 8, rows), F32),
            ((2 * rows, q_width), BF16),
            ((2, 2 * rows, HEAD_SIZE), F32),
            ((2 * rows, width), F32),
            ((half_rows, rows), F32),
            ((2 * half_rows, rows), F32),
            ((2 * rows, width), BF16),
            ((4, piece, in_width), BF16),
            ((q_width, width), BF16),
            ((4, 2, thin, 2 * share), BF16),
            ((share, width), BF16),
        ],
        [ANY] * 2 + [VMEM] * 6 + [ANY] * 7,
        [ANY] * 3 + [VMEM] * 2 + [ANY] * 2 + [VMEM] * 7 + [ANY] * 4,
        [
            pltpu.VMEM((8, LANES), jnp.int32),
            pltpu.VMEM((8, piece), F32),
            pltpu.VMEM((2 * rows, width), BF16),
            pltpu.VMEM((2, 8, LANES), jnp.int32),
            pltpu.VMEM((4, 8, piece), F32),
            pltpu.VMEM((4, piece, in_width), BF16),
            pltpu.VMEM((q_width, width), BF16),
            pltpu.VMEM((2, thin, 2 * share), BF16),
            pltpu.VMEM((share, piece), BF16),
            pltpu.VMEM((thin, LANES), BF16),
            pltpu.VMEM((LANES, piece), BF16),
            pltpu.VMEM((2 * rows, 2 * kv_width), BF16),
            pltpu.VMEM((half_rows, 2 * kv_width), BF16),
            pltpu.VMEM((2 * half_rows, 2 * kv_width), BF16),
            pltpu.VMEM((rows, half_rows), F32),
            pltpu.VMEM((rows, 2 * half_rows), F32),
            pltpu.VMEM((2 * rows, width), BF16),
            pltpu.VMEM((2 * rows, width), BF16),
        ],
        limit=56,
    )(
        tokens,
        cotangent,
        lengths,
        gain_attn,
        gain_ffn,
        bias_query,
        key_bias_vector,
        value_bias_vector,
        w_query,
        key_projection,
        value_projection,
        w_out,
        w_gate,
        w_up,
        w_down,
    )

    w_both_full = w_gu_full.reshape(width, 2 * share)
    half_block = (2, rows, width)
    grad_normed_ffn, both_sum, both_late, down_half, result_sum, result_ahead = talk(
        ffn_kernel,
        4,
        44,
        15,
        [
            ((2 * rows, width), F32),
            ((2 * piece // 3, share), BF16),
            ((4, piece // 3, share), BF16),
            ((4, share // 2, piece), BF16),
            ((2 * rows, width), BF16),
            ((2, rows, width), BF16),
        ],
        [ANY] * 4,
        [VMEM, VMEM, ANY, ANY, VMEM, VMEM],
        [
            pltpu.VMEM(shape, BF16)
            for shape in (
                (8 * rows, width),
                (8 * rows, width),
                (width, 2 * share),
                (share, width),
                (8 * rows, 2 * share),
                (8 * rows, share),
                (8 * rows, width),
                (width, 8 * rows),
                (8 * rows, width),
                (4, piece, share),
                (4, share // 2, piece),
                (2, rows // 2, width),
                (2, rows // 2, width),
                half_block,
                half_block,
                half_block,
                (2, rows // 2, width),
                (2, rows // 2, width),
                half_block,
                (rows, width),
                (rows, width),
                (rows, width),
                (rows, width),
                (2, piece // 6, share),
                (2, piece // 6, share),
                (2, piece // 3, share),
                (2, piece // 3, share),
            )
        ],
        limit=60,
    )(normed_ffn, cot_full, w_both_full, w_down_full)
    thirds = piece // 3
    q_half, w_half = (thin, q_width), (q_width // 2, piece)
    gu_chunk, dn_chunk = (3, thirds, share), (share // 2, piece)

    def halved(shape):
        return (*shape[:-2], shape[-2] // 2, shape[-1])

    def weight_scratch(shape):
        return [
            (4, 2 * shape[0], shape[1]),
            (4, *shape),
            halved(shape),
            halved(shape),
            shape,
            shape,
            shape,
            shape,
            (3, shape[0] // 4, shape[1]),
        ]

    def scratch(kind, *shapes):
        return [pltpu.VMEM(shape, kind) for shape in shapes]

    gate_up, down_all, in_total, kv_total, out_total, grad_tokens, result, small_all = talk(
        back_kernel,
        8,
        BACK_COPIES,
        BACK_LOCAL,
        [
            ((2, piece, 4 * share), BF16),
            ((4 * share, piece), BF16),
            ((piece, q_width), BF16),
            ((piece, 2 * kv_width), BF16),
            ((q_width, piece), BF16),
            ((half_rows, piece), BF16),
            ((half_rows, piece), BF16),
            ((4, 16, in_width), F32),
        ],
        [VMEM, ANY, ANY, VMEM] + [ANY] * 5 + [VMEM, ANY, VMEM] + [ANY] * 9,
        [ANY] * 8,
        scratch(F32, (2 * rows, width))
        + scratch(
            BF16,
            (2 * rows, width),
            (2 * rows, width),
            (2 * rows, width),
            (2 * rows, q_width),
            (half_rows, 2 * kv_width),
            (2 * half_rows, 2 * kv_width),
            (2 * rows, q_width),
        )
        + scratch(F32, (half_rows, rows), (2 * half_rows, rows))
        + scratch(
            BF16,
            (4, piece, in_width),
            (q_width, width),
            (2 * thirds, share),
            (4, thirds, share),
            (4, share // 2, piece),
            (2 * rows, width),
        )
        + scratch(F32, (8, width), (2 * rows, width))
        + scratch(BF16, (2 * rows, width), (2 * rows, q_width), (width, 2 * rows), (HEAD_SIZE, 2 * half_rows))
        + scratch(F32, (half_rows, 2 * kv_width), (2 * half_rows, 2 * kv_width))
        + scratch(
            BF16,
            (half_rows, 2 * kv_width),
            (2, half_rows, 2 * kv_width),
            (3, 2, rows, 2 * kv_width),
            (4, rows, 2 * kv_width),
            (2 * rows, in_width),
            (2 * rows, width),
            (rows, width),
            (rows, width),
            (rows, width),
            (rows, width),
            gu_chunk,
            gu_chunk,
            halved((thirds, share)),
            halved((thirds, share)),
            (thirds, share),
            (thirds, share),
            (thirds, share),
            halved(dn_chunk),
            halved(dn_chunk),
            dn_chunk,
            dn_chunk,
            dn_chunk,
            dn_chunk,
            dn_chunk,
            *weight_scratch(q_half),
            *weight_scratch((thin, 2 * kv_width)),
            *weight_scratch(w_half),
            (2, rows, width),
            (2 * rows, width),
        )
        + scratch(F32, (8, in_width), (4, 8, piece), (4, 8, in_width), (8, 8, piece))
        + scratch(F32, *[(16, in_width)] * 4),
        limit=60,
    )(
        grad_normed_ffn,
        middle,
        cot_full,
        gains4,
        tok_rows,
        normed,
        query,
        kv_a,
        kv_b,
        logs,
        attended,
        tables,
        mask_a,
        mask_b,
        w_in_full,
        w_out_full,
        both_sum,
        both_late,
        down_half,
        result_sum,
        result_ahead,
    )
    steps = 8
    narrow = [gate_up, down_all, in_total, kv_total, out_total, result, grad_tokens, small_all]
    lines = [(q_width,), (kv_width,), (kv_width,), (piece,), (piece,)]
    wide = [
        (half_rows, piece),
        (half_rows, piece),
        (piece, q_width),
        (piece, kv_width),
        (piece, kv_width),
        (q_width, piece),
        (piece, hidden),
        (piece, hidden),
        (hidden, piece),
    ]

    def in_block(array):
        if array is small_all:
            return pl.BlockSpec(array.shape, lambda i: (0, 0, 0))
        if array.ndim == 3:
            return pl.BlockSpec((2, array.shape[1] // steps, array.shape[2]), lambda i: (0, i, 0))
        if array is down_all:
            return pl.BlockSpec((hidden // steps, piece), lambda i: (i, 0))
        return pl.BlockSpec((array.shape[0] // steps, array.shape[1]), lambda i: (i, 0))

    wide_out = pl.pallas_call(
        widen_kernel,
        grid=(steps,),
        out_shape=[jax.ShapeDtypeStruct(shape, F32) for shape in wide + lines],
        in_specs=[in_block(array) for array in narrow],
        out_specs=[pl.BlockSpec((shape[0] // steps, shape[1]), lambda i: (i, 0)) for shape in wide]
        + [pl.BlockSpec(shape, lambda i: (0,)) for shape in lines],
        compiler_params=pltpu.CompilerParams(vmem_limit_bytes=60 << 20),
    )(*narrow)
    result_w, tokens_w, query_w, key_w, value_w, out_w, gate_w, up_w, down_w, *flat = wide_out
    bias_q, bias_k, bias_v, gain_one, gain_two = flat
    return (
        result_w,
        tokens_w,
        gain_one,
        query_w,
        key_w,
        value_w,
        bias_q,
        bias_k,
        bias_v,
        out_w,
        gain_two,
        gate_w,
        up_w,
        down_w,
    )


def solution(mesh):
    placed = (
        P(("dp", "col"), "row"),
        P(("dp", "col"), "row"),
        P("dp", None),
        P("row"),
        P("row", "col"),
        P("row", "col"),
        P("row", "col"),
        P("col"),
        P("col"),
        P("col"),
        P("col", "row"),
        P("row"),
        P("row", "col"),
        P("row", "col"),
        P("col", "row"),
    )
    return jax.shard_map(
        on_device,
        mesh=mesh,
        in_specs=placed,
        out_specs=(
            P(("dp", "col"), "row"),
            P(("dp", "col"), "row"),
            P("row"),
            P("row", "col"),
            P("row", "col"),
            P("row", "col"),
            P("col"),
            P("col"),
            P("col"),
            P("col", "row"),
            P("row"),
            P("row", "col"),
            P("row", "col"),
            P("col", "row"),
        ),
        check_vma=False,
    )
```
